32 devices in a mesh: dp: 8 (over z, y), mp: 4 (over x, core).
Axes of the slice: x: 2, y: 2, z: 4, core: 2. Of those that a mesh axis runs over, the one named last changes fastest.
Arguments:
- text_tokens: bfloat16 [2048, 768], P('dp'), may hold values from -6 to 6
- segment_ids: int32 [2048], P('dp'), may hold values from 0 to 191, as said below
- labels: int32 [192], P('dp'), may hold values from 0 to 191, each once
- image_tokens: bfloat16 [9600, 768], P('dp'), may hold values from -6 to 6
- image_gain_one: float32 [768], replicated, may hold values from 0.5 to 1.5
- image_bias_one: float32 [768], replicated, may hold values from -4 to 4
- image_qkv: bfloat16 [768, 3, 768], P(None, None, 'mp'), may hold values from -0.21875 to 0.21875
- image_out: bfloat16 [768, 768], P('mp'), may hold values from -0.875 to 0.875
- image_gain_two: float32 [768], replicated, may hold values from 0.5 to 1.5
- image_bias_two: float32 [768], replicated, may hold values from -4 to 4
- image_up: bfloat16 [768, 3072], P(None, 'mp'), may hold values from -0.21875 to 0.21875
- image_up_bias: float32 [3072], P('mp'), may hold values from -6 to 6
- image_down: bfloat16 [3072, 768], P('mp'), may hold values from -0.109375 to 0.109375
- text_gain_one: float32 [768], replicated, may hold values from 0.5 to 1.5
- text_bias_one: float32 [768], replicated, may hold values from -4 to 4
- text_qkv: bfloat16 [768, 3, 768], P(None, None, 'mp'), may hold values from -0.21875 to 0.21875
- text_out: bfloat16 [768, 768], P('mp'), may hold values from -0.625 to 0.625
- text_gain_two: float32 [768], replicated, may hold values from 0.5 to 1.5
- text_bias_two: float32 [768], replicated, may hold values from -4 to 4
- text_up: bfloat16 [768, 3072], P(None, 'mp'), may hold values from -0.21875 to 0.21875
- text_up_bias: float32 [3072], P('mp'), may hold values from -6 to 6
- text_down: bfloat16 [3072, 768], P('mp'), may hold values from -0.109375 to 0.109375
Outputs:
- pair_loss: float32 [192], P('dp')
- text_grad: float32 [2048, 768], P('dp')
- grad_gain_one: float32 [768], replicated
- grad_bias_one: float32 [768], replicated
- grad_qkv: float32 [768, 3, 768], P(None, None, 'mp')
- grad_out: float32 [768, 768], P('mp')
- grad_gain_two: float32 [768], replicated
- grad_bias_two: float32 [768], replicated
- grad_up: float32 [768, 3072], P(None, 'mp')
- grad_up_bias: float32 [3072], P('mp')
- grad_down: float32 [3072, 768], P('mp')
The draws below stay inside these ranges and needn't reach their ends.
Inputs may be any that keep to these rules, and one draw needn't show every extreme that they name: `segment_ids`: each packed row of 64 tokens holds exactly 6 whole captions one after another; captions are numbered row after row, so the rows of one index of dp hold captions of that index only. `labels`: each image number appears once.
All inputs are finite; a program needn't handle non-finite values.
Results may differ from the reference program's by a relative error of at most 0.033.
Values may be sent and summed in bfloat16 or wider, within the bound.
A program may use at most 128 MiB of HBM per device.

```python
import jax
import jax.numpy as jnp
from jax import lax

D = 768
HEADS = 12
HEAD = 64
FF = 3072
IMG_LEN = 50
ROW_LEN = 64
CAP_ROW = 6
TEXT_ROWS = 32
TOKENS = 2048
PAIRS_DEV = 24
PAIRS = 192
N_DP = 8


def draw_segment_ids(key, part):
    key = jax.random.fold_in(key, 7)
    row_keys = jax.random.split(key, TEXT_ROWS)

    def one_row(row_key):
        cuts = jax.random.permutation(row_key, ROW_LEN - 1)[:CAP_ROW - 1] + 1
        cuts = jnp.sort(cuts)
        places = jnp.arange(ROW_LEN)
        return jnp.sum((places[:, None] >= cuts[None, :]).astype(jnp.int32), axis=1)
    within = jax.vmap(one_row)(row_keys)
    starts = jnp.arange(TEXT_ROWS, dtype=jnp.int32)[:, None] * CAP_ROW
    return (within + starts).reshape(TEXT_ROWS * ROW_LEN).astype(jnp.int32)


def block_levels(own_key, extent, pieces, least, top_value):
    level = 1.0
    for axis_at, shards_of in pieces:
        draws = jax.random.uniform(jax.random.fold_in(jax.random.fold_in(own_key, 6), axis_at), (shards_of,), jnp.float32, least / len(pieces), top_value / len(pieces))
        level = level * jnp.repeat(jnp.exp(draws), extent[axis_at] // shards_of).reshape((-1,) + (1,) * (len(extent) - 1 - axis_at))
    return level


def normal_values(key, shape, spread, reach, pieces=(), held_as=jnp.bfloat16):
    level = block_levels(key, shape, pieces, -0.22, 0.18) if pieces else 1.0
    values = jax.random.normal(key, shape, jnp.float32) * spread * level
    return jnp.minimum(jnp.maximum(values, -reach), reach).astype(held_as)


def setup_inputs(seed: int = 0) -> dict:
    key_of = jax.random.split(jax.random.key(seed), 23)
    return {
        "text_tokens": normal_values(key_of[0], (TOKENS, D), 1.0, 6.0, ((0, 8),)),
        "segment_ids": draw_segment_ids(jax.random.fold_in(key_of[22], 71), 0),
        "labels": jax.random.permutation(key_of[2], PAIRS).astype(jnp.int32),
        "image_tokens": normal_values(key_of[3], (PAIRS * IMG_LEN, D), 1.0, 6.0, ((0, 8),)),
        "image_gain_one": jnp.clip(1.0 + 0.1 * jax.random.normal(key_of[4], (D,), jnp.float32), 0.5, 1.5),
        "image_bias_one": normal_values(key_of[5], (D,), 0.3, 4.0, (), jnp.float32),
        "image_qkv": normal_values(key_of[6], (D, 3, D), D ** -0.5, 0.21875, ((2, 4),)),
        "image_out": normal_values(key_of[7], (D, D), (D // 16) ** -0.5, 0.875, ((0, 4),)),
        "image_gain_two": jnp.clip(1.0 + 0.1 * jax.random.normal(key_of[8], (D,), jnp.float32), 0.5, 1.5),
        "image_bias_two": normal_values(key_of[9], (D,), 0.3, 4.0, (), jnp.float32),
        "image_up": normal_values(key_of[10], (D, FF), D ** -0.5, 0.21875, ((1, 4),)),
        "image_up_bias": normal_values(key_of[11], (FF,), 0.5, 6.0, ((0, 4),), jnp.float32),
        "image_down": normal_values(key_of[12], (FF, D), FF ** -0.5, 0.109375, ((0, 4),)),
        "text_gain_one": jnp.clip(1.0 + 0.1 * jax.random.normal(key_of[13], (D,), jnp.float32), 0.5, 1.5),
        "text_bias_one": normal_values(key_of[14], (D,), 0.3, 4.0, (), jnp.float32),
        "text_qkv": normal_values(key_of[15], (D, 3, D), D ** -0.5, 0.21875, ((2, 4),)),
        "text_out": normal_values(key_of[16], (D, D), (D // 8) ** -0.5, 0.625, ((0, 4),)),
        "text_gain_two": jnp.clip(1.0 + 0.1 * jax.random.normal(key_of[17], (D,), jnp.float32), 0.5, 1.5),
        "text_bias_two": normal_values(key_of[18], (D,), 0.3, 4.0, (), jnp.float32),
        "text_up": normal_values(key_of[19], (D, FF), D ** -0.5, 0.21875, ((1, 4),)),
        "text_up_bias": normal_values(key_of[20], (FF,), 0.5, 6.0, ((0, 4),), jnp.float32),
        "text_down": normal_values(key_of[21], (FF, D), FF ** -0.5, 0.109375, ((0, 4),)),
    }


@jax.custom_vjp
def low(v):
    return lax.optimization_barrier(v.astype(jnp.bfloat16)).astype(jnp.float32)

@jax.custom_vjp
def low_back(v):
    return v

def low_keep(v):
    return (low(v), None)

def low_pass(kept, grad):
    return (grad,)

def back_keep(v):
    return (v, None)

def back_low(kept, grad):
    return (low(grad),)
low.defvjp(low_keep, low_pass)
low_back.defvjp(back_keep, back_low)

def matmul(left, right):
    return jnp.dot(left, right, precision=lax.Precision.HIGHEST)

def layer_norm(values, gain, shift_bias):
    center = values - lax.optimization_barrier(jnp.mean(values, axis=-1, keepdims=True))
    factor = lax.rsqrt(lax.optimization_barrier(jnp.mean(center * center, axis=-1, keepdims=True)) + 1e-05)
    return center * factor * gain + shift_bias

def unit(rows):
    return rows * lax.rsqrt(lax.optimization_barrier(jnp.sum(rows * rows, axis=-1, keepdims=True)) + 1e-06)

def block(stream, params, seq_len, segments):
    gain_one, bias_one, w_qkv, w_out, gain_two, bias_two, w_up, b_up, w_down = params
    count = stream.shape[0]
    normed = low(layer_norm(stream, gain_one, bias_one))
    mixed = jnp.einsum('td,dke->tke', normed, w_qkv, precision=lax.Precision.HIGHEST)
    mixed = low(low_back(mixed)).reshape(count // seq_len, seq_len, 3, HEADS, HEAD)
    queries = mixed[:, :, 0]
    keys = mixed[:, :, 1]
    values = mixed[:, :, 2]
    scale = HEAD ** (-0.5)
    scores = jnp.einsum('sqhe,skhe->shqk', queries, keys, precision=lax.Precision.HIGHEST) * scale
    scores = low_back(scores)
    if segments is not None:
        grouped = segments.reshape(count // seq_len, seq_len)
        places = jnp.arange(seq_len)
        allowed = (grouped[:, :, None] == grouped[:, None, :]) & (places[None, None, :] <= places[None, :, None])
        scores = jnp.where(allowed[:, None], scores, -1e+30)
    probs = jax.nn.softmax(scores, axis=-1)
    context = jnp.einsum('shqk,skhe->sqhe', low(probs), values, precision=lax.Precision.HIGHEST)
    context = low(low_back(context)).reshape(count, HEADS * HEAD)
    middle = stream + low_back(matmul(context, w_out))
    normed_two = low(layer_norm(middle, gain_two, bias_two))
    hidden = low_back(matmul(normed_two, w_up) + b_up)
    active = low(jax.nn.gelu(hidden, approximate=False))
    return middle + low_back(matmul(active, w_down))

def reference(text_tokens, segment_ids, labels, image_tokens, image_gain_one, image_bias_one, image_qkv, image_out, image_gain_two, image_bias_two, image_up, image_up_bias, image_down, text_gain_one, text_bias_one, text_qkv, text_out, text_gain_two, text_bias_two, text_up, text_up_bias, text_down):
    f32 = jnp.float32
    image_params = (image_gain_one.astype(f32), image_bias_one.astype(f32), image_qkv.astype(f32), image_out.astype(f32), image_gain_two.astype(f32), image_bias_two.astype(f32), image_up.astype(f32), image_up_bias.astype(f32), image_down.astype(f32))
    text_params = (text_gain_one.astype(f32), text_bias_one.astype(f32), text_qkv.astype(f32), text_out.astype(f32), text_gain_two.astype(f32), text_bias_two.astype(f32), text_up.astype(f32), text_up_bias.astype(f32), text_down.astype(f32))
    groups = image_tokens.astype(f32).reshape(N_DP, PAIRS_DEV * IMG_LEN, D)

    def image_group(group):
        result = block(group, image_params, IMG_LEN, None)
        return result.reshape(PAIRS_DEV, IMG_LEN, D)[:, 0]
    image_embed = low(unit(lax.map(image_group, groups).reshape(PAIRS, D)))
    ends = jnp.concatenate([segment_ids[1:] != segment_ids[:-1], jnp.array([True])])

    def objective(stream, params):
        final = block(stream, params, ROW_LEN, segment_ids)
        pooled = jax.ops.segment_sum(jnp.where(ends[:, None], final, 0.0), segment_ids, num_segments=PAIRS)
        text_embed = low(unit(pooled))
        logits = low_back(64.0 * matmul(text_embed, image_embed.T))
        row_terms = jax.nn.logsumexp(logits, axis=1)
        col_terms = jax.nn.logsumexp(logits, axis=0)
        positive = jnp.take_along_axis(logits, labels[:, None].astype(jnp.int32), axis=1)[:, 0]
        pair_terms = 0.5 * (row_terms + col_terms) - positive
        return (jnp.sum(pair_terms), pair_terms)
    total, pullback, pair_loss = jax.vjp(objective, text_tokens.astype(f32), text_params, has_aux=True)
    grad_stream, grads = pullback(jnp.ones_like(total))
    return (pair_loss, grad_stream, grads[0], grads[1], grads[2], grads[3], grads[4], grads[5], grads[6], grads[7], grads[8])
```

```python
import jax
import jax.numpy as jnp
from jax import lax
from jax.sharding import PartitionSpec as P

HEAD = 64
IMG_LEN = 50
F32 = jnp.float32
BF16 = jnp.bfloat16


def dot(a, b):
    return lax.dot_general(a, b, (((1,), (0,)), ((), ())), preferred_element_type=F32)


def dot_nt(a, b):
    return lax.dot_general(a, b, (((1,), (1,)), ((), ())), preferred_element_type=F32)


def dot_tn(a, b):
    return lax.dot_general(a, b, (((0,), (0,)), ((), ())), preferred_element_type=F32)


def normalized(values):
    center = values - jnp.mean(values, axis=-1, keepdims=True)
    factor = lax.rsqrt(jnp.mean(center * center, axis=-1, keepdims=True) + 1e-05)
    return center * factor, factor


def norm_back(grad, hat, factor, gain):
    scaled = grad * gain
    along = jnp.mean(scaled * hat, axis=-1, keepdims=True)
    return factor * (scaled - jnp.mean(scaled, axis=-1, keepdims=True) - hat * along)


def unit(rows):
    return rows * lax.rsqrt(jnp.sum(rows * rows, axis=-1, keepdims=True) + 1e-06)


def gelu_parts(hidden):
    cdf = 0.5 * (1.0 + lax.erf(hidden * 0.7071067811865476))
    slope = cdf + hidden * jnp.exp(-0.5 * hidden * hidden) * 0.3989422804014327
    return hidden * cdf, slope


def head_blocks(rows, width):
    lanes = lax.broadcasted_iota(jnp.int32, (1, width), 1)
    return jnp.concatenate(
        [
            jnp.where((lanes >= h * HEAD) & (lanes < (h + 1) * HEAD), rows, 0.0)
            for h in range(width // HEAD)
        ],
        axis=0,
    )


def head_pick(blocks, width):
    heads = width // HEAD
    count = blocks.shape[0] // heads
    lanes = lax.broadcasted_iota(jnp.int32, (1, width), 1)
    total = jnp.zeros((count, width), F32)
    for h in range(heads):
        own = (lanes >= h * HEAD) & (lanes < (h + 1) * HEAD)
        total = total + jnp.where(own, blocks[h * count : (h + 1) * count], 0.0)
    return total


def attend(normed_rows, normed, allowed, weights):
    width = weights.shape[1]
    heads = width // HEAD
    queries = dot_nt(normed_rows, weights[0]).astype(BF16)
    folded = dot(head_blocks(queries.astype(F32), width).astype(BF16), weights[1]).astype(BF16)
    scores = dot_nt(folded, normed) * HEAD**-0.5
    scores = jnp.where(jnp.concatenate([allowed] * heads, axis=0), scores, -1e30)
    expo = jnp.exp(scores - jnp.max(scores, axis=-1, keepdims=True))
    probs = expo / jnp.sum(expo, axis=-1, keepdims=True)
    mixed = dot(probs.astype(BF16), normed).astype(BF16)
    context = head_pick(dot_nt(mixed, weights[2]), width).astype(BF16)
    return queries, folded, probs, mixed, context


def plain_device(
    text_tokens,
    segment_ids,
    labels,
    image_tokens,
    image_gain_one,
    image_bias_one,
    image_qkv,
    image_out,
    image_gain_two,
    image_bias_two,
    image_up,
    image_up_bias,
    image_down,
    text_gain_one,
    text_bias_one,
    text_qkv,
    text_out,
    text_gain_two,
    text_bias_two,
    text_up,
    text_up_bias,
    text_down,
):
    rank = lax.axis_index("dp")
    pairs = labels.shape[0]
    tokens = segment_ids.shape[0]
    width = text_out.shape[0]
    heads = width // HEAD
    features = text_tokens.shape[1]
    image_weights = jnp.transpose(image_qkv, (1, 2, 0))
    text_weights = jnp.transpose(text_qkv, (1, 2, 0))

    image_x = image_tokens.astype(F32)
    image_n = (normalized(image_x)[0] * image_gain_one + image_bias_one).astype(BF16)
    image_first = image_x.reshape(pairs, IMG_LEN, features)[:, 0]
    first_n = (normalized(image_first)[0] * image_gain_one + image_bias_one).astype(BF16)
    owner = lax.broadcasted_iota(jnp.int32, (pairs, pairs * IMG_LEN), 0)
    place = lax.broadcasted_iota(jnp.int32, (pairs, pairs * IMG_LEN), 1)
    inside = (place >= owner * IMG_LEN) & (place < (owner + 1) * IMG_LEN)
    image_context = attend(first_n, image_n, inside, image_weights)[4]

    text_x = text_tokens.astype(F32)
    hat_one, factor_one = normalized(text_x)
    normed = (hat_one * text_gain_one + text_bias_one).astype(BF16)
    captions = rank * pairs + jnp.arange(pairs)
    mine = segment_ids[None, :] == captions[:, None]
    spot = lax.broadcasted_iota(jnp.int32, (pairs, tokens), 1)
    last = jnp.max(jnp.where(mine, spot, -1), axis=1, keepdims=True)
    pick = (spot == last).astype(BF16)
    normed_last = dot(pick, normed).astype(BF16)
    queries, folded, probs, mixed, context = attend(normed_last, normed, mine, text_weights)

    attended = jnp.concatenate([dot(image_context, image_out), dot(context, text_out)], axis=0)
    attended = lax.psum(attended.astype(BF16), "mp").astype(F32)
    middle = jnp.concatenate([image_first, dot(pick, text_tokens)], axis=0) + attended
    hat_two, factor_two = normalized(middle)
    image_n2 = (hat_two[:pairs] * image_gain_two + image_bias_two).astype(BF16)
    normed_two = (hat_two[pairs:] * text_gain_two + text_bias_two).astype(BF16)
    image_active = gelu_parts(dot(image_n2, image_up) + image_up_bias)[0].astype(BF16)
    active, slope = gelu_parts(dot(normed_two, text_up) + text_up_bias)
    active = active.astype(BF16)
    branch = jnp.concatenate([dot(image_active, image_down), dot(active, text_down)], axis=0)
    final = middle + lax.psum(branch.astype(BF16), "mp").astype(F32)

    everyone = lax.all_gather(final.astype(BF16), "dp").astype(F32)
    total = everyone.shape[0] * pairs
    image_low = unit(everyone[:, :pairs].reshape(total, features)).astype(BF16)
    pooled = final[pairs:]
    text_low = unit(everyone[:, pairs:].reshape(total, features)).astype(BF16)
    logits = 64.0 * dot_nt(text_low, image_low)
    column_lse = jax.nn.logsumexp(logits, axis=0)
    own = lax.dynamic_slice_in_dim(logits, rank * pairs, pairs, axis=0)
    row_lse = jax.nn.logsumexp(own, axis=1)
    own_columns = lax.dynamic_slice_in_dim(column_lse, rank * pairs, pairs)
    onehot = (labels[:, None] == jnp.arange(total)[None, :]).astype(F32)
    pair_loss = 0.5 * (row_lse + own_columns) - jnp.sum(own * onehot, axis=1)
    grad_logits = (
        0.5 * (jnp.exp(own - row_lse[:, None]) + jnp.exp(own - column_lse[None, :])) - onehot
    )
    grad_embed = 64.0 * dot(grad_logits.astype(BF16), image_low)
    scale = lax.rsqrt(jnp.sum(pooled * pooled, axis=-1, keepdims=True) + 1e-06)
    text_unit = pooled * scale
    grad_final = scale * (
        grad_embed - text_unit * jnp.sum(text_unit * grad_embed, axis=-1, keepdims=True)
    )

    final_low = grad_final.astype(BF16)
    grad_hidden = (dot_nt(final_low, text_down) * slope).astype(BF16)
    grad_normed_two = lax.psum(dot_nt(grad_hidden, text_up).astype(BF16), "mp").astype(F32)
    hat_two = hat_two[pairs:]
    grad_middle = grad_final + norm_back(grad_normed_two, hat_two, factor_two[pairs:], text_gain_two)
    middle_low = grad_middle.astype(BF16)
    grad_context = dot_nt(middle_low, text_out).astype(BF16)
    grad_folded = dot(head_blocks(grad_context.astype(F32), width).astype(BF16), text_weights[2])
    grad_folded = grad_folded.astype(BF16)
    grad_probs = dot_nt(grad_folded, normed)
    grad_scores = probs * (grad_probs - jnp.sum(grad_probs * probs, axis=-1, keepdims=True))
    grad_scores = (grad_scores * HEAD**-0.5).astype(BF16)
    mixed_back = dot(grad_scores, normed).astype(BF16)
    grad_queries = head_pick(dot_nt(mixed_back, text_weights[1]), width).astype(BF16)
    grad_normed = dot_tn(grad_scores, folded) + dot_tn(probs.astype(BF16), grad_folded)
    grad_normed = grad_normed + dot_tn(pick, dot(grad_queries, text_weights[0]).astype(BF16))
    grad_normed = lax.psum(grad_normed.astype(BF16), "mp").astype(F32)
    text_grad = norm_back(grad_normed, hat_one, factor_one, text_gain_one)
    text_grad = text_grad + dot_tn(pick, middle_low)

    vectors = jnp.concatenate(
        [
            jnp.sum(grad_normed * hat_one, axis=0),
            jnp.sum(grad_normed, axis=0),
            jnp.sum(grad_normed_two * hat_two, axis=0),
            jnp.sum(grad_normed_two, axis=0),
            jnp.sum(grad_hidden.astype(F32), axis=0),
        ]
    )
    vectors = jnp.sum(lax.all_gather(vectors, "dp"), axis=0)
    cuts = [features, 2 * features, 3 * features, 4 * features]
    gain_one, bias_one, gain_two, bias_two, up_bias = jnp.split(vectors, cuts)

    def by_head(blocks):
        return [blocks[h * pairs : (h + 1) * pairs] for h in range(heads)]

    pieces = [active, final_low, normed_two, grad_hidden, context, middle_low, normed_last]
    pieces += [grad_queries, queries, grad_context] + by_head(mixed_back) + by_head(mixed)
    sent = lax.all_gather(jnp.concatenate(pieces, axis=1), "dp").reshape(total, -1)
    got = []
    at = 0
    for piece in pieces:
        got.append(sent[:, at : at + piece.shape[1]])
        at += piece.shape[1]
    active, final_low, normed_two, grad_hidden, context, middle_low, normed_last = got[:7]
    grad_queries, queries, grad_context = got[7:10]
    mixed_back = got[10 : 10 + heads]
    mixed = got[10 + heads :]

    def per_head(rows, blocks):
        return jnp.concatenate(
            [dot_tn(rows[:, h * HEAD : (h + 1) * HEAD], blocks[h]) for h in range(heads)], axis=0
        )

    grad_qkv = jnp.stack(
        [
            dot_tn(grad_queries, normed_last),
            per_head(queries, mixed_back),
            per_head(grad_context, mixed),
        ]
    )
    return (
        pair_loss,
        text_grad,
        gain_one,
        bias_one,
        jnp.transpose(grad_qkv, (2, 0, 1)),
        dot_tn(context, middle_low),
        gain_two,
        bias_two,
        dot_tn(normed_two, grad_hidden),
        up_bias,
        dot_tn(active, final_low),
    )


def solution(mesh):
    placed = (
        P("dp", None),
        P("dp"),
        P("dp"),
        P("dp", None),
        P(),
        P(),
        P(None, None, "mp"),
        P("mp", None),
        P(),
        P(),
        P(None, "mp"),
        P("mp"),
        P("mp", None),
        P(),
        P(),
        P(None, None, "mp"),
        P("mp", None),
        P(),
        P(),
        P(None, "mp"),
        P("mp"),
        P("mp", None),
    )
    return jax.shard_map(
        plain_device,
        mesh=mesh,
        in_specs=placed,
        out_specs=(
            P("dp"),
            P("dp", None),
            P(),
            P(),
            P(None, None, "mp"),
            P("mp", None),
            P(),
            P(),
            P(None, "mp"),
            P("mp"),
            P("mp", None),
        ),
        check_vma=False,
    )
```

```python
import functools

import jax
import jax.numpy as jnp
from jax import lax
from jax.experimental import pallas as pl
from jax.experimental.pallas import tpu as pltpu
from jax.sharding import PartitionSpec as P

HEAD = 64
IMG_LEN = 50
F32 = jnp.float32
BF16 = jnp.bfloat16


def dot(a, b):
    return lax.dot_general(a, b, (((1,), (0,)), ((), ())), preferred_element_type=F32)


def dot_nt(a, b):
    return lax.dot_general(a, b, (((1,), (1,)), ((), ())), preferred_element_type=F32)


def dot_tn(a, b):
    return lax.dot_general(a, b, (((0,), (0,)), ((), ())), preferred_element_type=F32)


def normalized(values):
    center = values - jnp.mean(values, axis=-1, keepdims=True)
    factor = lax.rsqrt(jnp.mean(center * center, axis=-1, keepdims=True) + 1e-05)
    return center * factor, factor


def norm_back(grad, hat, factor, gain):
    scaled = grad * gain
    along = jnp.mean(scaled * hat, axis=-1, keepdims=True)
    return factor * (scaled - jnp.mean(scaled, axis=-1, keepdims=True) - hat * along)


def unit(rows):
    return rows * lax.rsqrt(jnp.sum(rows * rows, axis=-1, keepdims=True) + 1e-06)


def gelu_parts(hidden):
    cdf = 0.5 * (1.0 + lax.erf(hidden * 0.7071067811865476))
    slope = cdf + hidden * jnp.exp(-0.5 * hidden * hidden) * 0.3989422804014327
    return hidden * cdf, slope


def head_blocks(rows, width):
    lanes = lax.broadcasted_iota(jnp.int32, (1, width), 1)
    return jnp.concatenate(
        [
            jnp.where((lanes >= h * HEAD) & (lanes < (h + 1) * HEAD), rows, 0.0)
            for h in range(width // HEAD)
        ],
        axis=0,
    )


def head_pick(blocks, width):
    heads = width // HEAD
    count = blocks.shape[0] // heads
    lanes = lax.broadcasted_iota(jnp.int32, (1, width), 1)
    total = jnp.zeros((count, width), F32)
    for h in range(heads):
        own = (lanes >= h * HEAD) & (lanes < (h + 1) * HEAD)
        total = total + jnp.where(own, blocks[h * count : (h + 1) * count], 0.0)
    return total


def attend(normed_rows, normed, allowed, weights):
    width = weights.shape[1]
    heads = width // HEAD
    queries = dot_nt(normed_rows, weights[0]).astype(BF16)
    folded = dot(head_blocks(queries.astype(F32), width).astype(BF16), weights[1]).astype(BF16)
    scores = dot_nt(folded, normed) * HEAD**-0.5
    scores = jnp.where(jnp.concatenate([allowed] * heads, axis=0), scores, -1e30)
    expo = jnp.exp(scores - jnp.max(scores, axis=-1, keepdims=True))
    probs = expo / jnp.sum(expo, axis=-1, keepdims=True)
    mixed = dot(probs.astype(BF16), normed).astype(BF16)
    context = head_pick(dot_nt(mixed, weights[2]), width).astype(BF16)
    return queries, folded, probs, mixed, context


def plain_device(
    text_tokens,
    segment_ids,
    labels,
    image_tokens,
    image_gain_one,
    image_bias_one,
    image_qkv,
    image_out,
    image_gain_two,
    image_bias_two,
    image_up,
    image_up_bias,
    image_down,
    text_gain_one,
    text_bias_one,
    text_qkv,
    text_out,
    text_gain_two,
    text_bias_two,
    text_up,
    text_up_bias,
    text_down,
):
    rank = lax.axis_index("dp")
    pairs = labels.shape[0]
    tokens = segment_ids.shape[0]
    width = text_out.shape[0]
    heads = width // HEAD
    features = text_tokens.shape[1]
    image_weights = jnp.transpose(image_qkv, (1, 2, 0))
    text_weights = jnp.transpose(text_qkv, (1, 2, 0))

    image_x = image_tokens.astype(F32)
    image_n = (normalized(image_x)[0] * image_gain_one + image_bias_one).astype(BF16)
    image_first = image_x.reshape(pairs, IMG_LEN, features)[:, 0]
    first_n = (normalized(image_first)[0] * image_gain_one + image_bias_one).astype(BF16)
    owner = lax.broadcasted_iota(jnp.int32, (pairs, pairs * IMG_LEN), 0)
    place = lax.broadcasted_iota(jnp.int32, (pairs, pairs * IMG_LEN), 1)
    inside = (place >= owner * IMG_LEN) & (place < (owner + 1) * IMG_LEN)
    image_context = attend(first_n, image_n, inside, image_weights)[4]

    text_x = text_tokens.astype(F32)
    hat_one, factor_one = normalized(text_x)
    normed = (hat_one * text_gain_one + text_bias_one).astype(BF16)
    captions = rank * pairs + jnp.arange(pairs)
    mine = segment_ids[None, :] == captions[:, None]
    spot = lax.broadcasted_iota(jnp.int32, (pairs, tokens), 1)
    last = jnp.max(jnp.where(mine, spot, -1), axis=1, keepdims=True)
    pick = (spot == last).astype(BF16)
    normed_last = dot(pick, normed).astype(BF16)
    queries, folded, probs, mixed, context = attend(normed_last, normed, mine, text_weights)

    attended = jnp.concatenate([dot(image_context, image_out), dot(context, text_out)], axis=0)
    attended = lax.psum(attended.astype(BF16), "mp").astype(F32)
    middle = jnp.concatenate([image_first, dot(pick, text_tokens)], axis=0) + attended
    hat_two, factor_two = normalized(middle)
    image_n2 = (hat_two[:pairs] * image_gain_two + image_bias_two).astype(BF16)
    normed_two = (hat_two[pairs:] * text_gain_two + text_bias_two).astype(BF16)
    image_active = gelu_parts(dot(image_n2, image_up) + image_up_bias)[0].astype(BF16)
    active, slope = gelu_parts(dot(normed_two, text_up) + text_up_bias)
    active = active.astype(BF16)
    branch = jnp.concatenate([dot(image_active, image_down), dot(active, text_down)], axis=0)
    final = middle + lax.psum(branch.astype(BF16), "mp").astype(F32)

    everyone = lax.all_gather(final.astype(BF16), "dp").astype(F32)
    total = everyone.shape[0] * pairs
    image_low = unit(everyone[:, :pairs].reshape(total, features)).astype(BF16)
    pooled = final[pairs:]
    text_low = unit(everyone[:, pairs:].reshape(total, features)).astype(BF16)
    logits = 64.0 * dot_nt(text_low, image_low)
    column_lse = jax.nn.logsumexp(logits, axis=0)
    own = lax.dynamic_slice_in_dim(logits, rank * pairs, pairs, axis=0)
    row_lse = jax.nn.logsumexp(own, axis=1)
    own_columns = lax.dynamic_slice_in_dim(column_lse, rank * pairs, pairs)
    onehot = (labels[:, None] == jnp.arange(total)[None, :]).astype(F32)
    pair_loss = 0.5 * (row_lse + own_columns) - jnp.sum(own * onehot, axis=1)
    grad_logits = (
        0.5 * (jnp.exp(own - row_lse[:, None]) + jnp.exp(own - column_lse[None, :])) - onehot
    )
    grad_embed = 64.0 * dot(grad_logits.astype(BF16), image_low)
    scale = lax.rsqrt(jnp.sum(pooled * pooled, axis=-1, keepdims=True) + 1e-06)
    text_unit = pooled * scale
    grad_final = scale * (
        grad_embed - text_unit * jnp.sum(text_unit * grad_embed, axis=-1, keepdims=True)
    )

    final_low = grad_final.astype(BF16)
    grad_hidden = (dot_nt(final_low, text_down) * slope).astype(BF16)
    grad_normed_two = lax.psum(dot_nt(grad_hidden, text_up).astype(BF16), "mp").astype(F32)
    hat_two = hat_two[pairs:]
    grad_middle = grad_final + norm_back(grad_normed_two, hat_two, factor_two[pairs:], text_gain_two)
    middle_low = grad_middle.astype(BF16)
    grad_context = dot_nt(middle_low, text_out).astype(BF16)
    grad_folded = dot(head_blocks(grad_context.astype(F32), width).astype(BF16), text_weights[2])
    grad_folded = grad_folded.astype(BF16)
    grad_probs = dot_nt(grad_folded, normed)
    grad_scores = probs * (grad_probs - jnp.sum(grad_probs * probs, axis=-1, keepdims=True))
    grad_scores = (grad_scores * HEAD**-0.5).astype(BF16)
    mixed_back = dot(grad_scores, normed).astype(BF16)
    grad_queries = head_pick(dot_nt(mixed_back, text_weights[1]), width).astype(BF16)
    grad_normed = dot_tn(grad_scores, folded) + dot_tn(probs.astype(BF16), grad_folded)
    grad_normed = grad_normed + dot_tn(pick, dot(grad_queries, text_weights[0]).astype(BF16))
    grad_normed = lax.psum(grad_normed.astype(BF16), "mp").astype(F32)
    text_grad = norm_back(grad_normed, hat_one, factor_one, text_gain_one)
    text_grad = text_grad + dot_tn(pick, middle_low)

    vectors = jnp.concatenate(
        [
            jnp.sum(grad_normed * hat_one, axis=0),
            jnp.sum(grad_normed, axis=0),
            jnp.sum(grad_normed_two * hat_two, axis=0),
            jnp.sum(grad_normed_two, axis=0),
            jnp.sum(grad_hidden.astype(F32), axis=0),
        ]
    )
    vectors = jnp.sum(lax.all_gather(vectors, "dp"), axis=0)
    cuts = [features, 2 * features, 3 * features, 4 * features]
    gain_one, bias_one, gain_two, bias_two, up_bias = jnp.split(vectors, cuts)

    def by_head(blocks):
        return [blocks[h * pairs : (h + 1) * pairs] for h in range(heads)]

    pieces = [active, final_low, normed_two, grad_hidden, context, middle_low, normed_last]
    pieces += [grad_queries, queries, grad_context] + by_head(mixed_back) + by_head(mixed)
    sent = lax.all_gather(jnp.concatenate(pieces, axis=1), "dp").reshape(total, -1)
    got = []
    at = 0
    for piece in pieces:
        got.append(sent[:, at : at + piece.shape[1]])
        at += piece.shape[1]
    active, final_low, normed_two, grad_hidden, context, middle_low, normed_last = got[:7]
    grad_queries, queries, grad_context = got[7:10]
    mixed_back = got[10 : 10 + heads]
    mixed = got[10 + heads :]

    def per_head(rows, blocks):
        return jnp.concatenate(
            [dot_tn(rows[:, h * HEAD : (h + 1) * HEAD], blocks[h]) for h in range(heads)], axis=0
        )

    grad_qkv = jnp.stack(
        [
            dot_tn(grad_queries, normed_last),
            per_head(queries, mixed_back),
            per_head(grad_context, mixed),
        ]
    )
    return (
        pair_loss,
        text_grad,
        gain_one,
        bias_one,
        jnp.transpose(grad_qkv, (2, 0, 1)),
        dot_tn(context, middle_low),
        gain_two,
        bias_two,
        dot_tn(normed_two, grad_hidden),
        up_bias,
        dot_tn(active, final_low),
    )


MESH = pl.DeviceIdType.MESH


def to_tall(rows):
    half = rows.shape[1] // 2
    return jnp.concatenate([rows[:, :half], rows[:, half:]], axis=0).astype(BF16)


def from_tall(tall):
    count = tall.shape[0] // 2
    wide = tall.astype(F32)
    return jnp.concatenate([wide[:count], wide[count:]], axis=1)


def from_tall_all(ref, n_dp):
    talls = [ref[i].astype(F32) for i in range(n_dp)]
    count = talls[0].shape[0] // 2
    left = jnp.concatenate([t[:count] for t in talls], axis=0)
    right = jnp.concatenate([t[count:] for t in talls], axis=0)
    return jnp.concatenate([left, right], axis=1)


def column_of(row, count):
    shape = (count, row.shape[1])
    same = lax.broadcasted_iota(jnp.int32, shape, 0) == lax.broadcasted_iota(jnp.int32, shape, 1)
    return jnp.sum(jnp.where(same, row, 0), axis=1, keepdims=True)


def caption_masks(seg, first, count):
    captions = first + lax.broadcasted_iota(jnp.int32, (count, seg.shape[1]), 0)
    mine = seg == captions
    spot = lax.broadcasted_iota(jnp.int32, (count, seg.shape[1]), 1)
    last = jnp.max(jnp.where(mine, spot, -1), axis=1, keepdims=True)
    return mine, (spot == last).astype(F32).astype(BF16)


def softmax_rows(scores, allowed):
    scores = jnp.where(allowed, scores, -1e30)
    expo = jnp.exp(scores - jnp.max(scores, axis=-1, keepdims=True))
    return expo / jnp.sum(expo, axis=-1, keepdims=True)


def stats_pack(top, bottom):
    pieces = []
    for row in (top, bottom):
        pieces += [row[:, at : at + 128] for at in range(0, row.shape[1], 128)]
    rows = len(pieces)
    pieces.append(jnp.zeros((-rows % 8, 128), F32))
    return jnp.concatenate(pieces, axis=0)


def stats_unpack(packed, features):
    per = features // 128
    top = jnp.concatenate([packed[i : i + 1] for i in range(per)], axis=1)
    bottom = jnp.concatenate([packed[per + i : per + i + 1] for i in range(per)], axis=1)
    return top, bottom


def step_kernel(
    sizes,
    text_hbm,
    image_hbm,
    iw_hbm,
    io_hbm,
    iu_hbm,
    id_hbm,
    tw_hbm,
    to_hbm,
    tu_hbm,
    td_hbm,
    seg_ref,
    lab_ref,
    ig1_ref,
    ib1_ref,
    ig2_ref,
    ib2_ref,
    iub_ref,
    tg1_ref,
    tb1_ref,
    tg2_ref,
    tb2_ref,
    tub_ref,
    act_o,
    fin_o,
    n2_o,
    gh_o,
    ctx_o,
    mid_o,
    nsel_o,
    dq_o,
    q_o,
    gctx_o,
    xk_o,
    xv_o,
    tg_o,
    vec_o,
    loss_o,
    xi,
    ni,
    iw,
    io,
    iu,
    idn,
    tw,
    to,
    tu,
    td,
    tok,
    nall,
    ids,
    ar,
    gat,
    fq,
    fg,
    fd,
    stm,
    std,
    wide_a,
    wide_b,
    wide_c,
    fold,
    probs_all,
    load_sem,
    img_sem,
    tz_s,
    ty_s,
    tc_s,
    tz_r,
    ty_r,
    tc_r,
    ar_s,
    ar_r,
    g_s,
    g_f,
    g_r,
    f_s,
    f_r,
    sm_s,
    sm_r,
):
    n_dp, n_mp, pairs, tokens, features, width = sizes
    heads = width // HEAD
    half_dp = n_dp // 2
    total = n_dp * pairs
    scale = HEAD**-0.5
    d = lax.axis_index("dp")
    m = lax.axis_index("mp")
    core = lax.rem(m, 2)
    hi = lax.div(d, 2)
    lo = lax.rem(d, 2)
    partner = (d, m + 1 - 2 * core)
    beside = (hi * 2 + 1 - lo, m)

    chunk = img_sem.shape[0]
    chunk_rows = xi.shape[0] // chunk

    def image_load(k):
        rows = pl.ds(k * chunk_rows, chunk_rows)
        return pltpu.make_async_copy(image_hbm.at[rows], xi.at[rows], img_sem.at[k])

    loads = {}
    order = [
        ("text", text_hbm, tok.at[d]),
        ("iw", iw_hbm, iw),
        ("io", io_hbm, io),
        ("tw", tw_hbm, tw),
        ("to", to_hbm, to),
        ("iu", iu_hbm, iu),
        ("id", id_hbm, idn),
        ("tu", tu_hbm, tu),
        ("td", td_hbm, td),
    ]
    for k in range(chunk):
        image_load(k).start()
    for at, (name, src, dst) in enumerate(order):
        loads[name] = pltpu.make_async_copy(src, dst, load_sem.at[at])
        loads[name].start()

    barrier = pltpu.get_barrier_semaphore()
    for i in range(1, n_mp):
        pl.semaphore_signal(
            barrier, inc=1, device_id=(d, lax.rem(m + i, n_mp)), device_id_type=MESH
        )

    @pl.loop(1, n_dp)
    def _(i):
        pl.semaphore_signal(
            barrier, inc=1, device_id=(lax.rem(d + i, n_dp), m), device_id_type=MESH
        )

    def remote(src, dst, send, recv, device):
        return pltpu.make_async_remote_copy(
            src_ref=src,
            dst_ref=dst,
            send_sem=send,
            recv_sem=recv,
            device_id=device,
            device_id_type=MESH,
        )

    def mp_send(buf, send, recv):
        for i in range(1, n_mp):
            remote(
                buf.at[m], buf.at[m], send.at[i], recv.at[i], (d, lax.rem(m + i, n_mp))
            ).start()

    def mp_recv(buf, send, recv):
        for i in range(1, n_mp):
            slot = buf.at[lax.rem(m + n_mp - i, n_mp)]
            remote(slot, slot, send.at[i], recv.at[i], partner).wait_recv()

    def mp_drain(buf, send, recv):
        for i in range(1, n_mp):
            remote(buf.at[m], buf.at[m], send.at[i], recv.at[i], partner).wait_send()

    def split(mine, body):
        for k in range(half_dp - 1):
            body(2 * k + (2 - core if mine else 1 + core))

        @pl.when(core == (1 if mine else 0))
        def _():
            body(2 * half_dp - 1)

    def dp_send(at):
        buf, send, recv = gat.at[at], g_s.at[at], g_r.at[at]

        def body(i):
            remote(
                buf.at[d], buf.at[d], send.at[i], recv.at[i], (lax.rem(d + i, n_dp), m)
            ).start()

        split(True, body)

    def dp_slot(buf, i):
        return buf.at[lax.rem(d + n_dp - i, n_dp)]

    def dp_forward(at, buf=None, send=None, recv=None, fwd=None):
        buf, recv, fwd = gat.at[at], g_r.at[at], g_f.at[at]

        def body(i):
            slot = dp_slot(buf, i)
            remote(slot, slot, fwd.at[i], recv.at[i], partner).wait_recv()
            remote(slot, slot, fwd.at[i], recv.at[i], partner).start()

        split(True, body)

    def dp_recv(at):
        buf, recv, fwd = gat.at[at], g_r.at[at], g_f.at[at]

        def body(i):
            slot = dp_slot(buf, i)
            remote(slot, slot, fwd.at[i], recv.at[i], partner).wait_recv()

        split(False, body)

    def dp_drain(at):
        buf, send, recv, fwd = gat.at[at], g_s.at[at], g_r.at[at], g_f.at[at]

        def body(i):
            slot = buf.at[d]
            remote(slot, slot, send.at[i], recv.at[i], partner).wait_send()
            remote(slot, slot, fwd.at[i], recv.at[i], partner).wait_send()

        split(True, body)

    def split_hi(mine, body):
        for k in range(half_dp // 2 - 1):
            body(2 * k + (2 - core if mine else 1 + core))

        @pl.when(core == (1 if mine else 0))
        def _():
            body(half_dp - 1)

    def tok_slot(i, across):
        return tok.at[lax.rem(hi + half_dp - i, half_dp) * 2 + (1 - lo if across else lo)]

    def tok_start():
        def body(i):
            slot = tok.at[d]
            to_dev = (lax.rem(hi + i, half_dp) * 2 + lo, m)
            remote(slot, slot, tz_s.at[i], tz_r.at[i], to_dev).start()

        split_hi(True, body)

        @pl.when(core == 0)
        def _():
            remote(tok.at[d], tok.at[d], ty_s.at[0], ty_r.at[0], beside).start()

    def tok_second():
        def body(i):
            slot = tok_slot(i, False)
            remote(slot, slot, tz_s.at[i], tz_r.at[i], partner).wait_recv()
            remote(slot, slot, ty_s.at[i], ty_r.at[i], beside).start()
            remote(slot, slot, tc_s.at[i], tc_r.at[i], partner).start()

        split_hi(True, body)

    def tok_third():
        def body(i):
            slot = tok_slot(i, True)
            at = half_dp + i
            remote(slot, slot, ty_s.at[i], ty_r.at[i], partner).wait_recv()
            remote(slot, slot, tc_s.at[at], tc_r.at[at], partner).start()

        split_hi(True, body)

        @pl.when(core == 0)
        def _():
            body(0)

    def tok_last():
        def body(i):
            slot = tok_slot(i, False)
            remote(slot, slot, tc_s.at[i], tc_r.at[i], partner).wait_recv()
            slot = tok_slot(i, True)
            at = half_dp + i
            remote(slot, slot, tc_s.at[at], tc_r.at[at], partner).wait_recv()

        split_hi(False, body)

        @pl.when(core == 1)
        def _():
            slot = tok_slot(0, True)
            at = half_dp
            remote(slot, slot, tc_s.at[at], tc_r.at[at], partner).wait_recv()

    def tok_drain():
        def body(i):
            slot = tok.at[d]
            at = half_dp + i
            remote(slot, slot, tz_s.at[i], tz_r.at[i], partner).wait_send()
            remote(slot, slot, ty_s.at[i], ty_r.at[i], partner).wait_send()
            remote(slot, slot, tc_s.at[i], tc_r.at[i], partner).wait_send()
            remote(slot, slot, tc_s.at[at], tc_r.at[at], partner).wait_send()

        split_hi(True, body)

        @pl.when(core == 0)
        def _():
            slot = tok.at[d]
            remote(slot, slot, ty_s.at[0], ty_r.at[0], partner).wait_send()
            at = half_dp
            remote(slot, slot, tc_s.at[at], tc_r.at[at], partner).wait_send()

    def attend_rows(queries, normed, allowed, weights):
        stacked = head_blocks(queries.astype(F32), width).astype(BF16)
        folded = dot(stacked, weights[1]).astype(BF16)
        scores = dot_nt(folded, normed) * scale
        probs = softmax_rows(scores, allowed)
        mixed = dot(probs.astype(BF16), normed).astype(BF16)
        context = head_pick(dot_nt(mixed, weights[2]), width).astype(BF16)
        return folded, probs, context

    gain, shift = ig1_ref[...], ib1_ref[...]

    @pl.loop(0, chunk)
    def _(k):
        image_load(k).wait()
        rows = pl.ds(pl.multiple_of(k * chunk_rows, 16), chunk_rows)
        hat = normalized(xi[rows, :].astype(F32))[0]
        ni[rows, :] = (hat * gain + shift).astype(BF16)

    firsts = [i * IMG_LEN for i in range(pairs)]
    image_first = jnp.concatenate([xi[r : r + 1, :].astype(F32) for r in firsts], axis=0)
    first_n = (normalized(image_first)[0] * gain + shift).astype(BF16)
    loads["iw"].wait()
    image_q = dot_nt(first_n, iw[0]).astype(BF16)
    shape = (pairs, xi.shape[0])
    place = lax.broadcasted_iota(jnp.int32, shape, 1)
    begin = lax.broadcasted_iota(jnp.int32, shape, 0) * IMG_LEN
    inside = jnp.concatenate([(place >= begin) & (place < begin + IMG_LEN)] * heads, axis=0)
    image_context = attend_rows(image_q, ni[...], inside, iw)[2]
    loads["io"].wait()
    ar[0, m] = to_tall(dot(image_context, io[...]))

    ids[d, 0:1, :] = seg_ref[...]
    ids[d, 1:2, 0:pairs] = lab_ref[...]
    loads["text"].wait()
    pl.semaphore_wait(barrier, n_mp - 1 + n_dp - 1)
    mp_send(ar.at[0], ar_s.at[0], ar_r.at[0])
    tok_start()

    @pl.loop(1, n_dp)
    def _(i):
        remote(
            ids.at[d], ids.at[d], sm_s.at[i], sm_r.at[i], (lax.rem(d + i, n_dp), m)
        ).start()

    x = tok[d].astype(F32)
    hat_one, factor_one = normalized(x)
    normed = (hat_one * tg1_ref[...] + tb1_ref[...]).astype(BF16)
    mine, pick = caption_masks(seg_ref[...], d * pairs, pairs)
    allowed = jnp.concatenate([mine] * heads, axis=0)
    loads["tw"].wait()
    queries = dot_nt(dot(pick, normed).astype(BF16), tw[0]).astype(BF16)
    folded, probs, context = attend_rows(queries, normed, allowed, tw)
    loads["to"].wait()
    ar[1, m] = to_tall(dot(context, to[...]))
    mp_send(ar.at[1], ar_s.at[1], ar_r.at[1])
    text_last = dot(pick, tok[d])

    def head_rows(blocks):
        return [
            jnp.sum(blocks[h * pairs : (h + 1) * pairs], axis=0, keepdims=True)
            for h in range(heads)
        ]

    def padded(rows, small, count):
        zeros = jnp.zeros((8 - len(small), tokens), F32)
        foot = jnp.concatenate(small + [zeros], axis=0)
        foot = jnp.concatenate([foot, jnp.zeros((8, features - tokens), F32)], axis=1)
        return jnp.concatenate([rows, foot], axis=0)[:count].astype(BF16)

    fq[m] = padded(folded.astype(F32), head_rows(probs), fq.shape[1])
    mp_send(fq, f_s.at[0], f_r.at[0])

    def summed(at):
        mp_recv(ar.at[at], ar_s.at[at], ar_r.at[at])
        full = ar[at, 0].astype(F32)
        for i in range(1, n_mp):
            full = full + ar[at, i].astype(F32)
        count = full.shape[0] // 2
        return jnp.concatenate([full[:count], full[count:]], axis=1)

    image_middle = image_first + summed(0)
    image_n2 = (normalized(image_middle)[0] * ig2_ref[...] + ib2_ref[...]).astype(BF16)
    loads["iu"].wait()
    image_active = gelu_parts(dot(image_n2, iu[...]) + iub_ref[...])[0].astype(BF16)
    loads["id"].wait()
    ar[2, m] = to_tall(dot(image_active, idn[...]))
    mp_send(ar.at[2], ar_s.at[2], ar_r.at[2])

    middle = text_last + summed(1)
    gat[0, d] = to_tall(middle)
    dp_send(0)
    gain_two = tg2_ref[...]
    hat_two, factor_two = normalized(middle)
    normed_two = (hat_two * gain_two + tb2_ref[...]).astype(BF16)
    loads["tu"].wait()
    active = gelu_parts(dot(normed_two, tu[...]) + tub_ref[...])[0].astype(BF16)
    loads["td"].wait()
    ar[3, m] = to_tall(dot(active, td[...]))
    mp_send(ar.at[3], ar_s.at[3], ar_r.at[3])

    gat[1, d] = to_tall(unit(image_middle + summed(2)))
    dp_send(1)
    gat[2, d] = to_tall(middle + summed(3))
    dp_send(2)

    dp_forward(0)
    tok_second()
    dp_recv(0)
    middle_all = from_tall_all(gat.at[0], n_dp)
    hat_all, factor_all = normalized(middle_all)
    wide_a[...] = hat_all
    n2_all = (hat_all * gain_two + tb2_ref[...]).astype(BF16)
    n2_o[...] = n2_all
    act_all, slope_all = gelu_parts(dot(n2_all, tu[...]) + tub_ref[...])
    act_o[...] = act_all.astype(BF16)
    wide_b[...] = slope_all

    dp_forward(1)
    tok_third()
    dp_forward(2)

    @pl.loop(1, n_dp)
    def _(i):
        slot = dp_slot(ids, i)
        remote(slot, slot, sm_s.at[i], sm_r.at[i], partner).wait_recv()

    labels = jnp.concatenate([column_of(ids[i, 1:2, 0:128], pairs) for i in range(n_dp)], axis=0)
    onehot = (labels == lax.broadcasted_iota(jnp.int32, (total, total), 1)).astype(F32)
    dp_recv(1)
    dp_recv(2)

    image_low = from_tall_all(gat.at[1], n_dp).astype(BF16)
    pooled = from_tall_all(gat.at[2], n_dp)
    shrink = lax.rsqrt(jnp.sum(pooled * pooled, axis=-1, keepdims=True) + 1e-06)
    text_unit = pooled * shrink
    logits = 64.0 * dot_nt(text_unit.astype(BF16), image_low)
    row_top = jnp.max(logits, axis=1, keepdims=True)
    row_lse = row_top + jnp.log(jnp.sum(jnp.exp(logits - row_top), axis=1, keepdims=True))
    col_top = jnp.max(logits, axis=0, keepdims=True)
    col_lse = col_top + jnp.log(jnp.sum(jnp.exp(logits - col_top), axis=0, keepdims=True))
    grad_logits = 0.5 * (jnp.exp(logits - row_lse) + jnp.exp(logits - col_lse)) - onehot
    grad_embed = 64.0 * dot(grad_logits.astype(BF16), image_low)
    along = jnp.sum(text_unit * grad_embed, axis=-1, keepdims=True)
    grad_final = shrink * (grad_embed - text_unit * along)
    final_low = grad_final.astype(BF16)
    fin_o[...] = final_low
    wide_c[...] = grad_final
    grad_hidden = dot_nt(final_low, td[...]) * wide_b[...]
    gh_o[...] = grad_hidden.astype(BF16)
    wide_b[...] = grad_hidden
    own = pl.ds(pl.multiple_of(d * pairs, 8), pairs)
    ar[4, m] = to_tall(dot_nt(wide_b[own, :].astype(BF16), tu[...]))
    mp_send(ar.at[4], ar_s.at[4], ar_r.at[4])

    positive = jnp.sum(logits * onehot, axis=1, keepdims=True)
    pair_loss = 0.5 * (row_lse + column_of(col_lse, total)) - positive
    shape = (total, loss_o.shape[1])
    spot = lax.broadcasted_iota(jnp.int32, shape, 1)
    here = lax.broadcasted_iota(jnp.int32, shape, 0) == d * pairs + spot
    loss_o[...] = jnp.sum(jnp.where(here, pair_loss, 0.0), axis=0, keepdims=True)
    up_bias = jnp.sum(gh_o[...].astype(F32), axis=0, keepdims=True)

    tok_last()
    twice = 2 * pairs

    def pair_masks(j):
        seg = jnp.concatenate([ids[2 * j, 0:1, :], ids[2 * j + 1, 0:1, :]], axis=1)
        return caption_masks(seg, j * twice, twice)

    @pl.loop(0, half_dp)
    def _(j):
        rows = pl.ds(pl.multiple_of(j * twice, 16), twice)
        both = tok[pl.ds(2 * j, 2)].reshape(2 * tokens, features).astype(F32)
        hat = normalized(both)[0]
        low = (hat * tg1_ref[...] + tb1_ref[...]).astype(BF16)
        nall[j] = low
        nsel_o[rows, :] = dot(pair_masks(j)[1], low).astype(BF16)

    q_all = dot_nt(nsel_o[...], tw[0]).astype(BF16)
    q_o[...] = q_all
    fold[...] = dot(head_blocks(q_all.astype(F32), width).astype(BF16), tw[1]).astype(BF16).reshape(
        heads, total, features
    )

    @pl.loop(0, half_dp)
    def _(j):
        rows = pl.ds(pl.multiple_of(j * twice, 16), twice)
        low = nall[j]
        blocks = jnp.concatenate([fold[h, rows, :] for h in range(heads)], axis=0)
        mask = jnp.concatenate([pair_masks(j)[0]] * heads, axis=0)
        both = softmax_rows(dot_nt(blocks, low) * scale, mask)
        probs_all[j] = both
        mixed = dot(both.astype(BF16), low).astype(BF16)
        for h in range(heads):
            xv_o[h, rows, :] = mixed[h * twice : (h + 1) * twice]

    ctx_o[...] = head_pick(
        dot_nt(xv_o[...].reshape(heads * total, features), tw[2]), width
    ).astype(BF16)

    grad_n2 = summed(4)
    gat[3, d] = to_tall(grad_n2)
    dp_send(3)
    grad_middle = wide_c[own, :] + norm_back(grad_n2, hat_two, factor_two, gain_two)
    middle_low = grad_middle.astype(BF16)
    grad_context = dot_nt(middle_low, to[...]).astype(BF16)
    grad_folded = dot(head_blocks(grad_context.astype(F32), width).astype(BF16), tw[2])
    fg[m] = padded(grad_folded, [], fg.shape[1])
    mp_send(fg, f_s.at[1], f_r.at[1])
    grad_probs = dot_nt(grad_folded.astype(BF16), normed)
    grad_scores = probs * (grad_probs - jnp.sum(grad_probs * probs, axis=-1, keepdims=True))
    scaled = grad_scores * scale
    mixed_back = dot(scaled.astype(BF16), normed).astype(BF16)
    grad_queries = head_pick(dot_nt(mixed_back, tw[1]), width).astype(BF16)
    fd[m] = padded(dot(grad_queries, tw[0]), head_rows(scaled), fd.shape[1])
    mp_send(fd, f_s.at[2], f_r.at[2])

    def spread(slots, ref, at):
        parts = []
        for i in slots:
            foot = ref[i, at : at + 8, 0:tokens].astype(F32)
            for h in range(heads):
                parts.append(jnp.where(mine, foot[h : h + 1], 0.0))
            parts.append(jnp.zeros((8, tokens), F32))
        return jnp.concatenate(parts, axis=0).astype(BF16)

    def first_norm_grad(slots, sources):
        folds, backs, rests = sources
        place_low = jnp.concatenate(
            [jnp.concatenate([pick.astype(F32), jnp.zeros((8, tokens), F32)], axis=0)] * len(slots),
            axis=0,
        ).astype(BF16)
        grads = dot_tn(spread(slots, fd, pairs), folds)
        grads = grads + dot_tn(spread(slots, fq, pairs * heads), backs)
        return grads + dot_tn(place_low, rests)

    part = first_norm_grad([m], (fq[m], fg[m], fd[m]))
    stm[m] = stats_pack(
        jnp.sum(part * hat_one, axis=0, keepdims=True), jnp.sum(part, axis=0, keepdims=True)
    )
    mp_send(stm, f_s.at[3], f_r.at[3])

    dp_forward(3)
    mp_recv(stm, f_s.at[3], f_r.at[3])
    own_stats = stm[0]
    for i in range(1, n_mp):
        own_stats = own_stats + stm[i]
    std[d] = own_stats

    @pl.loop(1, n_dp)
    def _(i):
        remote(
            std.at[d], std.at[d], sm_s.at[n_dp + i], sm_r.at[n_dp + i], (lax.rem(d + i, n_dp), m)
        ).start()

    dp_recv(3)
    grad_all = from_tall_all(gat.at[3], n_dp)
    hat_all = wide_a[...]
    back_all = norm_back(grad_all, hat_all, factor_all, gain_two)
    mid_all = (wide_c[...] + back_all).astype(BF16)
    mid_o[...] = mid_all
    gain_two_grad = jnp.sum(grad_all * hat_all, axis=0, keepdims=True)
    bias_two_grad = jnp.sum(grad_all, axis=0, keepdims=True)
    gctx_all = dot_nt(mid_all, to[...]).astype(BF16)
    gctx_o[...] = gctx_all
    fold[...] = dot(
        head_blocks(gctx_all.astype(F32), width).astype(BF16), tw[2]
    ).astype(BF16).reshape(heads, total, features)

    @pl.loop(0, half_dp)
    def _(j):
        rows = pl.ds(pl.multiple_of(j * twice, 16), twice)
        low = nall[j]
        blocks = jnp.concatenate([fold[h, rows, :] for h in range(heads)], axis=0)
        grads = dot_nt(blocks, low)
        both = probs_all[j]
        grads = both * (grads - jnp.sum(grads * both, axis=-1, keepdims=True)) * scale
        mixed = dot(grads.astype(BF16), low).astype(BF16)
        for h in range(heads):
            xk_o[h, rows, :] = mixed[h * twice : (h + 1) * twice]

    dq_o[...] = head_pick(
        dot_nt(xk_o[...].reshape(heads * total, features), tw[1]), width
    ).astype(BF16)

    for at, buf in ((0, fq), (1, fg), (2, fd)):
        mp_recv(buf, f_s.at[at], f_r.at[at])
    flat = [ref[...].reshape(n_mp * ref.shape[1], features) for ref in (fq, fg, fd)]
    grad_normed = first_norm_grad(list(range(n_mp)), flat)
    text_grad = norm_back(grad_normed, hat_one, factor_one, tg1_ref[...])
    tg_o[...] = text_grad + dot_tn(pick, middle_low)

    @pl.loop(1, n_dp)
    def _(i):
        slot = dp_slot(std, i)
        remote(slot, slot, sm_s.at[n_dp + i], sm_r.at[n_dp + i], partner).wait_recv()

    stats = std[0]
    for i in range(1, n_dp):
        stats = stats + std[i]
    gain_one_grad, bias_one_grad = stats_unpack(stats, features)
    vec_o[...] = jnp.concatenate(
        [gain_one_grad, bias_one_grad, gain_two_grad, bias_two_grad, up_bias]
        + [jnp.zeros((3, features), F32)],
        axis=0,
    )

    for at in range(ar.shape[0]):
        mp_drain(ar.at[at], ar_s.at[at], ar_r.at[at])
    for at, buf in enumerate((fq, fg, fd, stm)):
        mp_drain(buf, f_s.at[at], f_r.at[at])
    for at in range(gat.shape[0]):
        dp_drain(at)
    tok_drain()

    @pl.loop(1, n_dp)
    def _(i):
        remote(ids.at[d], ids.at[d], sm_s.at[i], sm_r.at[i], partner).wait_send()
        at = n_dp + i
        remote(std.at[d], std.at[d], sm_s.at[at], sm_r.at[at], partner).wait_send()


def weights_kernel(
    act,
    fin,
    n2,
    gh,
    ctx,
    mid,
    nsel,
    dq,
    q,
    gctx,
    xk,
    xv,
    tg,
    vec,
    loss,
    tg_out,
    qkv_out,
    out_out,
    up_out,
    down_out,
    loss_out,
    g1_out,
    b1_out,
    g2_out,
    b2_out,
    ub_out,
    qkv_buf,
    out_buf,
    up_buf,
    down_buf,
    sem,
):
    heads, total, features = xk.shape
    width = q.shape[1]
    started = []

    def ship(src, dst):
        copy = pltpu.make_async_copy(src, dst, sem.at[len(started)])
        copy.start()
        started.append(copy)

    ship(tg, tg_out)
    step = 256
    for left, right, buf, dst in (
        (act, fin, down_buf, down_out),
        (n2, gh, up_buf, up_out),
    ):
        for at in range(0, features, step):
            rows = pl.ds(at, step)
            buf[rows, :] = dot_tn(left[:, at : at + step], right[...])
            ship(buf.at[rows], dst.at[rows])
    out_buf[...] = dot_tn(ctx[...], mid[...])
    ship(out_buf, out_out)
    qkv_buf[0] = dot_tn(dq[...], nsel[...])
    ship(qkv_buf.at[0], qkv_out.at[0])
    for at, rows, blocks in ((1, q, xk), (2, gctx, xv)):
        stacked = head_blocks(rows[...].astype(F32), width).astype(BF16)
        qkv_buf[at] = dot_tn(stacked, blocks[...].reshape(heads * total, features))
        ship(qkv_buf.at[at], qkv_out.at[at])
    for at, dst in enumerate((g1_out, b1_out, g2_out, b2_out, ub_out)):
        dst[...] = vec[at : at + 1, :]
    loss_out[...] = loss[:, 0 : loss_out.shape[1]]
    for copy in started:
        copy.wait()


def kernel_device(
    n_dp,
    n_mp,
    text_tokens,
    segment_ids,
    labels,
    image_tokens,
    image_gain_one,
    image_bias_one,
    image_qkv,
    image_out,
    image_gain_two,
    image_bias_two,
    image_up,
    image_up_bias,
    image_down,
    text_gain_one,
    text_bias_one,
    text_qkv,
    text_out,
    text_gain_two,
    text_bias_two,
    text_up,
    text_up_bias,
    text_down,
):
    pairs = labels.shape[0]
    tokens, features = text_tokens.shape
    width = text_out.shape[0]
    hidden = text_up.shape[1]
    heads = width // HEAD
    total = n_dp * pairs
    half_dp = n_dp // 2
    vmem = pltpu.VMEM
    whole = pl.BlockSpec(memory_space=pltpu.VMEM)
    anywhere = pl.BlockSpec(memory_space=pl.ANY)

    def row(vector):
        return vector.reshape(1, vector.shape[0])

    def sems(*shape):
        return pltpu.SemaphoreType.DMA(shape)

    outs = [
        ((total, hidden), BF16),
        ((total, features), BF16),
        ((total, features), BF16),
        ((total, hidden), BF16),
        ((total, width), BF16),
        ((total, features), BF16),
        ((total, features), BF16),
        ((total, width), BF16),
        ((total, width), BF16),
        ((total, width), BF16),
        ((heads, total, features), BF16),
        ((heads, total, features), BF16),
        ((tokens, features), F32),
        ((8, features), F32),
        ((1, 128), F32),
    ]
    tall = (2 * pairs, features // 2)
    fold_rows = heads * pairs + 8
    factors = pl.pallas_call(
        functools.partial(step_kernel, (n_dp, n_mp, pairs, tokens, features, width)),
        out_shape=[vmem(shape, dtype) for shape, dtype in outs],
        in_specs=[anywhere] * 10 + [whole] * 12,
        out_specs=[whole] * len(outs),
        scratch_shapes=[
            vmem(image_tokens.shape, BF16),
            vmem(image_tokens.shape, BF16),
            vmem((3, width, features), BF16),
            vmem(image_out.shape, BF16),
            vmem(image_up.shape, BF16),
            vmem(image_down.shape, BF16),
            vmem((3, width, features), BF16),
            vmem(text_out.shape, BF16),
            vmem(text_up.shape, BF16),
            vmem(text_down.shape, BF16),
            vmem((n_dp, tokens, features), BF16),
            vmem((half_dp, 2 * tokens, features), BF16),
            vmem((n_dp, 8, tokens), jnp.int32),
            vmem((5, n_mp) + tall, BF16),
            vmem((4, n_dp) + tall, BF16),
            vmem((n_mp, fold_rows, features), BF16),
            vmem((n_mp, fold_rows, features), BF16),
            vmem((n_mp, pairs + 8, features), BF16),
            vmem((n_mp, 16, 128), F32),
            vmem((n_dp, 16, 128), F32),
            vmem((total, features), F32),
            vmem((total, hidden), F32),
            vmem((total, features), F32),
            vmem((heads, total, features), BF16),
            vmem((half_dp, heads * 2 * pairs, 2 * tokens), F32),
            sems(9),
            sems(5),
            sems(half_dp),
            sems(half_dp),
            sems(n_dp),
            sems(half_dp),
            sems(half_dp),
            sems(n_dp),
            sems(5, n_mp),
            sems(5, n_mp),
            sems(4, n_dp),
            sems(4, n_dp),
            sems(4, n_dp),
            sems(4, n_mp),
            sems(4, n_mp),
            sems(2 * n_dp),
            sems(2 * n_dp),
        ],
        compiler_params=pltpu.CompilerParams(
            collective_id=0, has_side_effects=True, vmem_limit_bytes=48 * 2**20
        ),
        name="step",
    )(
        text_tokens,
        image_tokens,
        jnp.transpose(image_qkv, (1, 2, 0)),
        image_out,
        image_up,
        image_down,
        jnp.transpose(text_qkv, (1, 2, 0)),
        text_out,
        text_up,
        text_down,
        row(segment_ids),
        row(labels),
        row(image_gain_one),
        row(image_bias_one),
        row(image_gain_two),
        row(image_bias_two),
        row(image_up_bias),
        row(text_gain_one),
        row(text_bias_one),
        row(text_gain_two),
        row(text_bias_two),
        row(text_up_bias),
    )
    vector = jax.ShapeDtypeStruct((1, features), F32)
    results = pl.pallas_call(
        weights_kernel,
        out_shape=[
            jax.ShapeDtypeStruct((tokens, features), F32),
            jax.ShapeDtypeStruct((3, width, features), F32),
            jax.ShapeDtypeStruct((width, features), F32),
            jax.ShapeDtypeStruct((features, hidden), F32),
            jax.ShapeDtypeStruct((hidden, features), F32),
            jax.ShapeDtypeStruct((1, pairs), F32),
            vector,
            vector,
            vector,
            vector,
            jax.ShapeDtypeStruct((1, hidden), F32),
        ],
        in_specs=[whole] * len(outs),
        out_specs=[anywhere] * 5 + [whole] * 6,
        scratch_shapes=[
            vmem((3, width, features), F32),
            vmem((width, features), F32),
            vmem((features, hidden), F32),
            vmem((hidden, features), F32),
            sems(16),
        ],
        compiler_params=pltpu.CompilerParams(vmem_limit_bytes=32 * 2**20),
        name="weights",
    )(*[pltpu.with_memory_space_constraint(factor, pltpu.VMEM) for factor in factors])
    text_grad, qkv, out, up, down, loss, gain_one, bias_one, gain_two, bias_two, up_bias = results
    return (
        loss.reshape(pairs),
        text_grad,
        gain_one.reshape(features),
        bias_one.reshape(features),
        jnp.transpose(qkv, (2, 0, 1)),
        out,
        gain_two.reshape(features),
        bias_two.reshape(features),
        up,
        up_bias.reshape(hidden),
        down,
    )


def solution(mesh):
    placed = (
        P("dp", None),
        P("dp"),
        P("dp"),
        P("dp", None),
        P(),
        P(),
        P(None, None, "mp"),
        P("mp", None),
        P(),
        P(),
        P(None, "mp"),
        P("mp"),
        P("mp", None),
        P(),
        P(),
        P(None, None, "mp"),
        P("mp", None),
        P(),
        P(),
        P(None, "mp"),
        P("mp"),
        P("mp", None),
    )
    n_dp, n_mp = mesh.shape["dp"], mesh.shape["mp"]
    body = plain_device
    if n_dp <= 16:
        body = functools.partial(kernel_device, n_dp, n_mp)
    return jax.shard_map(
        body,
        mesh=mesh,
        in_specs=placed,
        out_specs=(
            P("dp"),
            P("dp", None),
            P(),
            P(),
            P(None, None, "mp"),
            P("mp", None),
            P(),
            P(),
            P(None, "mp"),
            P("mp"),
            P("mp", None),
        ),
        check_vma=False,
    )
```

```python
import functools

import jax
import jax.numpy as jnp
from jax import lax
from jax.experimental import pallas as pl
from jax.experimental.pallas import tpu as pltpu
from jax.sharding import PartitionSpec as P

HEAD = 64
IMG_LEN = 50
F32 = jnp.float32
BF16 = jnp.bfloat16


def dot(a, b):
    return lax.dot_general(a, b, (((1,), (0,)), ((), ())), preferred_element_type=F32)


def dot_nt(a, b):
    return lax.dot_general(a, b, (((1,), (1,)), ((), ())), preferred_element_type=F32)


def dot_tn(a, b):
    return lax.dot_general(a, b, (((0,), (0,)), ((), ())), preferred_element_type=F32)


def normalized(values):
    center = values - jnp.mean(values, axis=-1, keepdims=True)
    factor = lax.rsqrt(jnp.mean(center * center, axis=-1, keepdims=True) + 1e-05)
    return center * factor, factor


def norm_back(grad, hat, factor, gain):
    scaled = grad * gain
    along = jnp.mean(scaled * hat, axis=-1, keepdims=True)
    return factor * (scaled - jnp.mean(scaled, axis=-1, keepdims=True) - hat * along)


def unit(rows):
    return rows * lax.rsqrt(jnp.sum(rows * rows, axis=-1, keepdims=True) + 1e-06)


def gelu_parts(hidden):
    cdf = 0.5 * (1.0 + lax.erf(hidden * 0.7071067811865476))
    slope = cdf + hidden * jnp.exp(-0.5 * hidden * hidden) * 0.3989422804014327
    return hidden * cdf, slope


def head_blocks(rows, width):
    lanes = lax.broadcasted_iota(jnp.int32, (1, width), 1)
    return jnp.concatenate(
        [
            jnp.where((lanes >= h * HEAD) & (lanes < (h + 1) * HEAD), rows, 0.0)
            for h in range(width // HEAD)
        ],
        axis=0,
    )


def head_pick(blocks, width):
    heads = width // HEAD
    count = blocks.shape[0] // heads
    lanes = lax.broadcasted_iota(jnp.int32, (1, width), 1)
    total = jnp.zeros((count, width), F32)
    for h in range(heads):
        own = (lanes >= h * HEAD) & (lanes < (h + 1) * HEAD)
        total = total + jnp.where(own, blocks[h * count : (h + 1) * count], 0.0)
    return total


def attend(normed_rows, normed, allowed, weights):
    width = weights.shape[1]
    heads = width // HEAD
    queries = dot_nt(normed_rows, weights[0]).astype(BF16)
    folded = dot(head_blocks(queries.astype(F32), width).astype(BF16), weights[1]).astype(BF16)
    scores = dot_nt(folded, normed) * HEAD**-0.5
    scores = jnp.where(jnp.concatenate([allowed] * heads, axis=0), scores, -1e30)
    expo = jnp.exp(scores - jnp.max(scores, axis=-1, keepdims=True))
    probs = expo / jnp.sum(expo, axis=-1, keepdims=True)
    mixed = dot(probs.astype(BF16), normed).astype(BF16)
    context = head_pick(dot_nt(mixed, weights[2]), width).astype(BF16)
    return queries, folded, probs, mixed, context


def plain_device(
    text_tokens,
    segment_ids,
    labels,
    image_tokens,
    image_gain_one,
    image_bias_one,
    image_qkv,
    image_out,
    image_gain_two,
    image_bias_two,
    image_up,
    image_up_bias,
    image_down,
    text_gain_one,
    text_bias_one,
    text_qkv,
    text_out,
    text_gain_two,
    text_bias_two,
    text_up,
    text_up_bias,
    text_down,
):
    rank = lax.axis_index("dp")
    pairs = labels.shape[0]
    tokens = segment_ids.shape[0]
    width = text_out.shape[0]
    heads = width // HEAD
    features = text_tokens.shape[1]
    image_weights = jnp.transpose(image_qkv, (1, 2, 0))
    text_weights = jnp.transpose(text_qkv, (1, 2, 0))

    image_x = image_tokens.astype(F32)
    image_n = (normalized(image_x)[0] * image_gain_one + image_bias_one).astype(BF16)
    image_first = image_x.reshape(pairs, IMG_LEN, features)[:, 0]
    first_n = (normalized(image_first)[0] * image_gain_one + image_bias_one).astype(BF16)
    owner = lax.broadcasted_iota(jnp.int32, (pairs, pairs * IMG_LEN), 0)
    place = lax.broadcasted_iota(jnp.int32, (pairs, pairs * IMG_LEN), 1)
    inside = (place >= owner * IMG_LEN) & (place < (owner + 1) * IMG_LEN)
    image_context = attend(first_n, image_n, inside, image_weights)[4]

    text_x = text_tokens.astype(F32)
    hat_one, factor_one = normalized(text_x)
    normed = (hat_one * text_gain_one + text_bias_one).astype(BF16)
    captions = rank * pairs + jnp.arange(pairs)
    mine = segment_ids[None, :] == captions[:, None]
    spot = lax.broadcasted_iota(jnp.int32, (pairs, tokens), 1)
    last = jnp.max(jnp.where(mine, spot, -1), axis=1, keepdims=True)
    pick = (spot == last).astype(BF16)
    normed_last = dot(pick, normed).astype(BF16)
    queries, folded, probs, mixed, context = attend(normed_last, normed, mine, text_weights)

    attended = jnp.concatenate([dot(image_context, image_out), dot(context, text_out)], axis=0)
    attended = lax.psum(attended.astype(BF16), "mp").astype(F32)
    middle = jnp.concatenate([image_first, dot(pick, text_tokens)], axis=0) + attended
    hat_two, factor_two = normalized(middle)
    image_n2 = (hat_two[:pairs] * image_gain_two + image_bias_two).astype(BF16)
    normed_two = (hat_two[pairs:] * text_gain_two + text_bias_two).astype(BF16)
    image_active = gelu_parts(dot(image_n2, image_up) + image_up_bias)[0].astype(BF16)
    active, slope = gelu_parts(dot(normed_two, text_up) + text_up_bias)
    active = active.astype(BF16)
    branch = jnp.concatenate([dot(image_active, image_down), dot(active, text_down)], axis=0)
    final = middle + lax.psum(branch.astype(BF16), "mp").astype(F32)

    everyone = lax.all_gather(final.astype(BF16), "dp").astype(F32)
    total = everyone.shape[0] * pairs
    image_low = unit(everyone[:, :pairs].reshape(total, features)).astype(BF16)
    pooled = final[pairs:]
    text_low = unit(everyone[:, pairs:].reshape(total, features)).astype(BF16)
    logits = 64.0 * dot_nt(text_low, image_low)
    column_lse = jax.nn.logsumexp(logits, axis=0)
    own = lax.dynamic_slice_in_dim(logits, rank * pairs, pairs, axis=0)
    row_lse = jax.nn.logsumexp(own, axis=1)
    own_columns = lax.dynamic_slice_in_dim(column_lse, rank * pairs, pairs)
    onehot = (labels[:, None] == jnp.arange(total)[None, :]).astype(F32)
    pair_loss = 0.5 * (row_lse + own_columns) - jnp.sum(own * onehot, axis=1)
    grad_logits = (
        0.5 * (jnp.exp(own - row_lse[:, None]) + jnp.exp(own - column_lse[None, :])) - onehot
    )
    grad_embed = 64.0 * dot(grad_logits.astype(BF16), image_low)
    scale = lax.rsqrt(jnp.sum(pooled * pooled, axis=-1, keepdims=True) + 1e-06)
    text_unit = pooled * scale
    grad_final = scale * (
        grad_embed - text_unit * jnp.sum(text_unit * grad_embed, axis=-1, keepdims=True)
    )

    final_low = grad_final.astype(BF16)
    grad_hidden = (dot_nt(final_low, text_down) * slope).astype(BF16)
    grad_normed_two = lax.psum(dot_nt(grad_hidden, text_up).astype(BF16), "mp").astype(F32)
    hat_two = hat_two[pairs:]
    grad_middle = grad_final + norm_back(grad_normed_two, hat_two, factor_two[pairs:], text_gain_two)
    middle_low = grad_middle.astype(BF16)
    grad_context = dot_nt(middle_low, text_out).astype(BF16)
    grad_folded = dot(head_blocks(grad_context.astype(F32), width).astype(BF16), text_weights[2])
    grad_folded = grad_folded.astype(BF16)
    grad_probs = dot_nt(grad_folded, normed)
    grad_scores = probs * (grad_probs - jnp.sum(grad_probs * probs, axis=-1, keepdims=True))
    grad_scores = (grad_scores * HEAD**-0.5).astype(BF16)
    mixed_back = dot(grad_scores, normed).astype(BF16)
    grad_queries = head_pick(dot_nt(mixed_back, text_weights[1]), width).astype(BF16)
    grad_normed = dot_tn(grad_scores, folded) + dot_tn(probs.astype(BF16), grad_folded)
    grad_normed = grad_normed + dot_tn(pick, dot(grad_queries, text_weights[0]).astype(BF16))
    grad_normed = lax.psum(grad_normed.astype(BF16), "mp").astype(F32)
    text_grad = norm_back(grad_normed, hat_one, factor_one, text_gain_one)
    text_grad = text_grad + dot_tn(pick, middle_low)

    vectors = jnp.concatenate(
        [
            jnp.sum(grad_normed * hat_one, axis=0),
            jnp.sum(grad_normed, axis=0),
            jnp.sum(grad_normed_two * hat_two, axis=0),
            jnp.sum(grad_normed_two, axis=0),
            jnp.sum(grad_hidden.astype(F32), axis=0),
        ]
    )
    vectors = jnp.sum(lax.all_gather(vectors, "dp"), axis=0)
    cuts = [features, 2 * features, 3 * features, 4 * features]
    gain_one, bias_one, gain_two, bias_two, up_bias = jnp.split(vectors, cuts)

    def by_head(blocks):
        return [blocks[h * pairs : (h + 1) * pairs] for h in range(heads)]

    pieces = [active, final_low, normed_two, grad_hidden, context, middle_low, normed_last]
    pieces += [grad_queries, queries, grad_context] + by_head(mixed_back) + by_head(mixed)
    sent = lax.all_gather(jnp.concatenate(pieces, axis=1), "dp").reshape(total, -1)
    got = []
    at = 0
    for piece in pieces:
        got.append(sent[:, at : at + piece.shape[1]])
        at += piece.shape[1]
    active, final_low, normed_two, grad_hidden, context, middle_low, normed_last = got[:7]
    grad_queries, queries, grad_context = got[7:10]
    mixed_back = got[10 : 10 + heads]
    mixed = got[10 + heads :]

    def per_head(rows, blocks):
        return jnp.concatenate(
            [dot_tn(rows[:, h * HEAD : (h + 1) * HEAD], blocks[h]) for h in range(heads)], axis=0
        )

    grad_qkv = jnp.stack(
        [
            dot_tn(grad_queries, normed_last),
            per_head(queries, mixed_back),
            per_head(grad_context, mixed),
        ]
    )
    return (
        pair_loss,
        text_grad,
        gain_one,
        bias_one,
        jnp.transpose(grad_qkv, (2, 0, 1)),
        dot_tn(context, middle_low),
        gain_two,
        bias_two,
        dot_tn(normed_two, grad_hidden),
        up_bias,
        dot_tn(active, final_low),
    )


MESH = pl.DeviceIdType.MESH
TOKEN_SHARE = 64


def to_tall(rows):
    half = rows.shape[1] // 2
    return jnp.concatenate([rows[:, :half], rows[:, half:]], axis=0).astype(BF16)


def from_tall(tall):
    count = tall.shape[0] // 2
    wide = tall.astype(F32)
    return jnp.concatenate([wide[:count], wide[count:]], axis=1)


def from_tall_all(ref, n_dp):
    talls = [ref[i].astype(F32) for i in range(n_dp)]
    count = talls[0].shape[0] // 2
    left = jnp.concatenate([t[:count] for t in talls], axis=0)
    right = jnp.concatenate([t[count:] for t in talls], axis=0)
    return jnp.concatenate([left, right], axis=1)


def column_of(row, count):
    shape = (count, row.shape[1])
    same = lax.broadcasted_iota(jnp.int32, shape, 0) == lax.broadcasted_iota(jnp.int32, shape, 1)
    return jnp.sum(jnp.where(same, row, 0), axis=1, keepdims=True)


def caption_masks(seg, first, count):
    captions = first + lax.broadcasted_iota(jnp.int32, (count, seg.shape[1]), 0)
    mine = seg == captions
    spot = lax.broadcasted_iota(jnp.int32, (count, seg.shape[1]), 1)
    last = jnp.max(jnp.where(mine, spot, -1), axis=1, keepdims=True)
    return mine, (spot == last).astype(F32).astype(BF16)


def softmax_rows(scores, allowed):
    scores = jnp.where(allowed, scores, -1e30)
    expo = jnp.exp(scores - jnp.max(scores, axis=-1, keepdims=True))
    return expo / jnp.sum(expo, axis=-1, keepdims=True)


def stats_pack(rows):
    pieces = []
    for row in rows:
        pieces += [row[:, at : at + 128] for at in range(0, row.shape[1], 128)]
    pieces.append(jnp.zeros((-len(pieces) % 8 or 8, 128), F32))
    return jnp.concatenate(pieces, axis=0)


def stats_unpack(packed, count, features):
    per = features // 128
    return [
        jnp.concatenate([packed[at * per + i : at * per + i + 1] for i in range(per)], axis=1)
        for at in range(count)
    ]


def step_kernel(
    sizes,
    text_hbm,
    image_hbm,
    iw_hbm,
    io_hbm,
    iu_hbm,
    id_hbm,
    tw_hbm,
    to_hbm,
    tu_hbm,
    td_hbm,
    seg_hbm,
    lab_hbm,
    ig1_hbm,
    ib1_hbm,
    ig2_hbm,
    ib2_hbm,
    iub_hbm,
    tg1_hbm,
    tb1_hbm,
    tg2_hbm,
    tb2_hbm,
    tub_hbm,
    act_o,
    fin_o,
    n2_o,
    gh_o,
    ctx_o,
    mid_o,
    nsel_o,
    dq_o,
    q_o,
    gctx_o,
    xk_o,
    xv_o,
    tg_o,
    vec_o,
    loss_o,
    xt,
    xi,
    ni,
    iw,
    io,
    iu,
    idn,
    tw,
    to,
    tu,
    td,
    seg_ref,
    lab_ref,
    ig1_ref,
    ib1_ref,
    ig2_ref,
    ib2_ref,
    iub_ref,
    tg1_ref,
    tb1_ref,
    tg2_ref,
    tb2_ref,
    tub_ref,
    tok,
    ids,
    prow,
    drow,
    stm,
    std,
    ar,
    gat,
    fq,
    fg,
    fd,
    wide_b,
    wide_c,
    load_sem,
    img_sem,
    tz_s,
    tz_r,
    ty_s,
    ty_r,
    tc_s,
    tc_r,
    tx_s,
    tx_r,
    tf_s,
    tf_r,
    ar_s,
    ar_r,
    g_s,
    g_f,
    g_r,
    f_s,
    f_r,
    sm_s,
    sm_r,
):
    n_dp, n_mp, pairs, tokens, features, width = sizes
    heads = width // HEAD
    half_dp = n_dp // 2
    total = n_dp * pairs
    scale = HEAD**-0.5
    d = lax.axis_index("dp")
    m = lax.axis_index("mp")
    core = lax.rem(m, 2)
    side = lax.div(m, 2)
    hi = lax.div(d, 2)
    lo = lax.rem(d, 2)
    partner = (d, m + 1 - 2 * core)
    across = (d, lax.rem(m + 2, 4))
    beside = (hi * 2 + 1 - lo, m)

    chunk = img_sem.shape[0]
    chunk_rows = xi.shape[0] // chunk

    def image_load(k):
        rows = pl.ds(k * chunk_rows, chunk_rows)
        return pltpu.make_async_copy(image_hbm.at[rows], xi.at[rows], img_sem.at[k])

    loads = {}

    def load(name, src, dst):
        loads[name] = pltpu.make_async_copy(src, dst, load_sem.at[len(loads)])
        loads[name].start()

    load("text", text_hbm, xt)
    load("tg1", tg1_hbm, tg1_ref)
    load("tb1", tb1_hbm, tb1_ref)
    load("seg", seg_hbm, seg_ref)
    load("lab", lab_hbm, lab_ref)
    load("ig1", ig1_hbm, ig1_ref)
    load("ib1", ib1_hbm, ib1_ref)
    for k in range(chunk):
        image_load(k).start()
    load("iw", iw_hbm, iw)
    load("io", io_hbm, io)
    load("tw", tw_hbm, tw)
    load("to", to_hbm, to)
    load("ig2", ig2_hbm, ig2_ref)
    load("ib2", ib2_hbm, ib2_ref)
    load("iub", iub_hbm, iub_ref)
    load("tg2", tg2_hbm, tg2_ref)
    load("tb2", tb2_hbm, tb2_ref)
    load("tub", tub_hbm, tub_ref)
    load("iu", iu_hbm, iu)
    load("id", id_hbm, idn)
    load("tu", tu_hbm, tu)
    load("td", td_hbm, td)

    def vector(name, ref):
        loads[name].wait()
        return ref[...].reshape(1, ref.shape[0])

    barrier = pltpu.get_barrier_semaphore()
    for i in range(1, n_mp):
        pl.semaphore_signal(
            barrier, inc=1, device_id=(d, lax.rem(m + i, n_mp)), device_id_type=MESH
        )

    @pl.loop(1, n_dp)
    def _(i):
        pl.semaphore_signal(
            barrier, inc=1, device_id=(lax.rem(d + i, n_dp), m), device_id_type=MESH
        )

    def remote(src, dst, send, recv, device):
        return pltpu.make_async_remote_copy(
            src_ref=src,
            dst_ref=dst,
            send_sem=send,
            recv_sem=recv,
            device_id=device,
            device_id_type=MESH,
        )

    def mp_send(buf, send, recv):
        for i in range(1, n_mp):
            remote(
                buf.at[m], buf.at[m], send.at[i], recv.at[i], (d, lax.rem(m + i, n_mp))
            ).start()

    def mp_recv(buf, send, recv):
        for i in range(1, n_mp):
            slot = buf.at[lax.rem(m + n_mp - i, n_mp)]
            remote(slot, slot, send.at[i], recv.at[i], partner).wait_recv()

    def mp_drain(buf, send, recv):
        for i in range(1, n_mp):
            remote(buf.at[m], buf.at[m], send.at[i], recv.at[i], partner).wait_send()

    def far_send(buf, send, recv):
        slot = buf.at[m]
        remote(slot, slot, send.at[2], recv.at[2], across).start()
        remote(slot, slot, send.at[1], recv.at[1], partner).start()

    def far_pass(buf, send, recv):
        slot = buf.at[lax.rem(m + 2, 4)]
        remote(slot, slot, send.at[3], recv.at[2], partner).wait_recv()
        remote(slot, slot, send.at[3], recv.at[3], partner).start()

    def far_recv(buf, send, recv):
        slot = buf.at[m]
        for i in (1, 3):
            remote(slot, slot, send.at[i], recv.at[i], partner).wait_recv()

    def split(mine, body):
        for k in range(half_dp - 1):
            body(2 * k + (2 - core if mine else 1 + core))

        @pl.when(core == (1 if mine else 0))
        def _():
            body(2 * half_dp - 1)

    def dp_slot(buf, i):
        return buf.at[lax.rem(d + n_dp - i, n_dp)]

    def dp_send(at):
        buf, send, recv = gat.at[at], g_s.at[at], g_r.at[at]

        def body(i):
            remote(
                buf.at[d], buf.at[d], send.at[i], recv.at[i], (lax.rem(d + i, n_dp), m)
            ).start()

        split(True, body)

    def dp_forward(at):
        buf, recv, fwd = gat.at[at], g_r.at[at], g_f.at[at]

        def body(i):
            slot = dp_slot(buf, i)
            remote(slot, slot, fwd.at[i], recv.at[i], partner).wait_recv()
            remote(slot, slot, fwd.at[i], recv.at[i], partner).start()

        split(True, body)

    def dp_recv(at):
        buf, recv, fwd = gat.at[at], g_r.at[at], g_f.at[at]

        def body(i):
            slot = dp_slot(buf, i)
            remote(slot, slot, fwd.at[i], recv.at[i], partner).wait_recv()

        split(False, body)

    def dp_drain(at):
        buf, send, recv, fwd = gat.at[at], g_s.at[at], g_r.at[at], g_f.at[at]

        def body(i):
            slot = buf.at[d]
            remote(slot, slot, send.at[i], recv.at[i], partner).wait_send()
            remote(slot, slot, fwd.at[i], recv.at[i], partner).wait_send()

        split(True, body)

    def small_send(at, buf):
        @pl.loop(1, n_dp)
        def _(i):
            remote(
                buf.at[d],
                buf.at[d],
                sm_s.at[at, i],
                sm_r.at[at, i],
                (lax.rem(d + i, n_dp), m),
            ).start()

    def small_recv(at, buf):
        @pl.loop(1, n_dp)
        def _(i):
            slot = dp_slot(buf, i)
            remote(slot, slot, sm_s.at[at, i], sm_r.at[at, i], partner).wait_recv()

    def small_drain(at, buf):
        @pl.loop(1, n_dp)
        def _(i):
            remote(buf.at[d], buf.at[d], sm_s.at[at, i], sm_r.at[at, i], partner).wait_send()

    shared = TOKEN_SHARE * tokens // 256
    kept = tokens - shared

    def split_hi(mine, body):
        for k in range(half_dp // 2 - 1):
            body(2 * k + (2 - core if mine else 1 + core))

        @pl.when(core == (1 if mine else 0))
        def _():
            body(half_dp - 1)

    def split_both(mine, body):
        def near(i):
            body(i, lax.rem(hi + half_dp - i, half_dp) * 2 + lo)

        def far(i):
            body(half_dp + i, lax.rem(hi + half_dp - i, half_dp) * 2 + 1 - lo)

        split_hi(mine, near)
        split_hi(mine, far)

        @pl.when(core == (0 if mine else 1))
        def _():
            far(0)

    def kept_rows(slot):
        return tok.at[slot, pl.ds(pl.multiple_of(side * shared, 16), kept)]

    def given_rows(slot):
        return tok.at[slot, pl.ds(pl.multiple_of(side * kept, 16), shared)]

    def taken_rows(slot):
        return tok.at[slot, pl.ds(pl.multiple_of((1 - side) * kept, 16), shared)]

    def tok_start():
        rows = kept_rows(d)

        def body(i):
            to_dev = (lax.rem(hi + i, half_dp) * 2 + lo, m)
            remote(rows, rows, tz_s.at[i], tz_r.at[i], to_dev).start()

        split_hi(True, body)

        @pl.when(core == 0)
        def _():
            remote(rows, rows, ty_s.at[0], ty_r.at[0], beside).start()

    def tok_second():
        def body(i):
            rows = kept_rows(lax.rem(hi + half_dp - i, half_dp) * 2 + lo)
            remote(rows, rows, tz_s.at[i], tz_r.at[i], partner).wait_recv()
            remote(rows, rows, ty_s.at[i], ty_r.at[i], beside).start()
            remote(rows, rows, tc_s.at[i], tc_r.at[i], partner).start()

        split_hi(True, body)

    def tok_third():
        def body(i):
            rows = kept_rows(lax.rem(hi + half_dp - i, half_dp) * 2 + 1 - lo)
            at = half_dp + i
            remote(rows, rows, ty_s.at[i], ty_r.at[i], partner).wait_recv()
            remote(rows, rows, tc_s.at[at], tc_r.at[at], partner).start()

        split_hi(True, body)

        @pl.when(core == 0)
        def _():
            body(0)

    def tok_near_across():
        def body(i):
            rows = given_rows(lax.rem(hi + half_dp - i, half_dp) * 2 + lo)
            remote(rows, rows, tx_s.at[i], tx_r.at[i], across).start()

        if shared:
            split_hi(True, body)

    def tok_far_across():
        def body(i):
            rows = given_rows(lax.rem(hi + half_dp - i, half_dp) * 2 + 1 - lo)
            at = half_dp + i
            remote(rows, rows, tx_s.at[at], tx_r.at[at], across).start()

        if shared:
            split_hi(True, body)

            @pl.when(core == 0)
            def _():
                body(0)

    def tok_pass():
        def body(at, slot):
            rows = taken_rows(slot)
            remote(rows, rows, tx_s.at[at], tx_r.at[at], partner).wait_recv()
            remote(rows, rows, tf_s.at[at], tf_r.at[at], partner).start()

        if shared:
            split_both(True, body)

    def tok_last():
        def body(at, slot):
            rows = kept_rows(slot)
            remote(rows, rows, tc_s.at[at], tc_r.at[at], partner).wait_recv()
            if shared:
                rows = taken_rows(slot)
                remote(rows, rows, tf_s.at[at], tf_r.at[at], partner).wait_recv()

        split_both(False, body)

    def tok_drain():
        rows = kept_rows(d)

        def body(at, slot):
            remote(rows, rows, tc_s.at[at], tc_r.at[at], partner).wait_send()
            if shared:
                few = taken_rows(d)
                remote(few, few, tx_s.at[at], tx_r.at[at], partner).wait_send()
                remote(few, few, tf_s.at[at], tf_r.at[at], partner).wait_send()

        split_both(True, body)

        def both(i):
            remote(rows, rows, tz_s.at[i], tz_r.at[i], partner).wait_send()
            remote(rows, rows, ty_s.at[i], ty_r.at[i], partner).wait_send()

        split_hi(True, both)

        @pl.when(core == 0)
        def _():
            remote(rows, rows, ty_s.at[0], ty_r.at[0], partner).wait_send()

    def attend_rows(queries, normed, allowed, weights):
        stacked = head_blocks(queries.astype(F32), width).astype(BF16)
        folded = dot(stacked, weights[1]).astype(BF16)
        scores = dot_nt(folded, normed) * scale
        probs = softmax_rows(scores, allowed)
        mixed = dot(probs.astype(BF16), normed).astype(BF16)
        context = head_pick(dot_nt(mixed, weights[2]), width).astype(BF16)
        return folded, probs, context

    loads["text"].wait()
    gain_one = vector("tg1", tg1_ref)
    hat_one, factor_one = normalized(xt[...].astype(F32))
    tok[d] = (hat_one * gain_one + vector("tb1", tb1_ref)).astype(BF16)
    seg = vector("seg", seg_ref)
    ids[d, 0:1, :] = seg
    ids[d, 1:2, 0:pairs] = vector("lab", lab_ref)
    pl.semaphore_wait(barrier, n_mp - 1 + n_dp - 1)
    tok_start()
    small_send(0, ids)

    gain, shift = vector("ig1", ig1_ref), vector("ib1", ib1_ref)

    @pl.loop(0, chunk)
    def _(k):
        image_load(k).wait()
        rows = pl.ds(pl.multiple_of(k * chunk_rows, 16), chunk_rows)
        hat = normalized(xi[rows, :].astype(F32))[0]
        ni[rows, :] = (hat * gain + shift).astype(BF16)

    firsts = [i * IMG_LEN for i in range(pairs)]
    image_first = jnp.concatenate([xi[r : r + 1, :].astype(F32) for r in firsts], axis=0)
    first_n = (normalized(image_first)[0] * gain + shift).astype(BF16)
    loads["iw"].wait()
    image_q = dot_nt(first_n, iw[0]).astype(BF16)
    shape = (pairs, xi.shape[0])
    place = lax.broadcasted_iota(jnp.int32, shape, 1)
    begin = lax.broadcasted_iota(jnp.int32, shape, 0) * IMG_LEN
    inside = jnp.concatenate([(place >= begin) & (place < begin + IMG_LEN)] * heads, axis=0)
    image_context = attend_rows(image_q, ni[...], inside, iw)[2]
    loads["io"].wait()
    ar[0, m] = to_tall(dot(image_context, io[...]))
    mp_send(ar.at[0], ar_s.at[0], ar_r.at[0])

    normed = tok[d]
    mine, pick = caption_masks(seg, d * pairs, pairs)
    allowed = jnp.concatenate([mine] * heads, axis=0)
    loads["tw"].wait()
    queries = dot_nt(dot(pick, normed).astype(BF16), tw[0]).astype(BF16)
    folded, probs, context = attend_rows(queries, normed, allowed, tw)
    loads["to"].wait()
    ar[1, m] = to_tall(dot(context, to[...]))
    mp_send(ar.at[1], ar_s.at[1], ar_r.at[1])
    text_last = dot(pick, xt[...])

    def head_rows(blocks):
        rows = [
            jnp.sum(blocks[h * pairs : (h + 1) * pairs], axis=0, keepdims=True)
            for h in range(heads)
        ]
        return jnp.concatenate(rows + [jnp.zeros((8 - heads, tokens), F32)], axis=0)

    def padded(rows, foot):
        foot = jnp.concatenate([foot, jnp.zeros((8, features - tokens), F32)], axis=1)
        return jnp.concatenate([rows, foot], axis=0).astype(BF16)

    no_foot = jnp.zeros((8, tokens), F32)
    prob_rows = head_rows(probs)
    prow[d] = prob_rows
    small_send(1, prow)
    fq[m] = padded(folded.astype(F32), prob_rows)
    far_send(fq, f_s.at[0], f_r.at[0])

    def summed(at):
        mp_recv(ar.at[at], ar_s.at[at], ar_r.at[at])
        full = ar[at, 0].astype(F32)
        for i in range(1, n_mp):
            full = full + ar[at, i].astype(F32)
        count = full.shape[0] // 2
        return jnp.concatenate([full[:count], full[count:]], axis=1)

    image_middle = image_first + summed(0)
    gain, shift = vector("ig2", ig2_ref), vector("ib2", ib2_ref)
    image_n2 = (normalized(image_middle)[0] * gain + shift).astype(BF16)
    loads["iu"].wait()
    image_hidden = dot(image_n2, iu[...]) + vector("iub", iub_ref)
    image_active = gelu_parts(image_hidden)[0].astype(BF16)
    loads["id"].wait()
    ar[2, m] = to_tall(dot(image_active, idn[...]))
    mp_send(ar.at[2], ar_s.at[2], ar_r.at[2])

    middle = text_last + summed(1)
    gat[0, d] = to_tall(middle)
    dp_send(0)
    gain_two, shift_two = vector("tg2", tg2_ref), vector("tb2", tb2_ref)
    hat_two, factor_two = normalized(middle)
    normed_two = (hat_two * gain_two + shift_two).astype(BF16)
    loads["tu"].wait()
    up_shift = vector("tub", tub_ref)
    active = gelu_parts(dot(normed_two, tu[...]) + up_shift)[0].astype(BF16)
    loads["td"].wait()
    ar[3, m] = to_tall(dot(active, td[...]))
    mp_send(ar.at[3], ar_s.at[3], ar_r.at[3])

    gat[1, d] = to_tall(unit(image_middle + summed(2)))
    dp_send(1)
    gat[2, d] = to_tall(middle + summed(3))
    dp_send(2)

    dp_forward(0)
    tok_second()
    tok_near_across()
    far_pass(fq, f_s.at[0], f_r.at[0])
    small_recv(0, ids)
    labels = jnp.concatenate([column_of(ids[i, 1:2, 0:128], pairs) for i in range(n_dp)], axis=0)
    onehot = (labels == lax.broadcasted_iota(jnp.int32, (total, total), 1)).astype(F32)
    dp_recv(0)
    middle_all = from_tall_all(gat.at[0], n_dp)
    n2_all = (normalized(middle_all)[0] * gain_two + shift_two).astype(BF16)
    n2_o[...] = n2_all
    act_all, slope_all = gelu_parts(dot(n2_all, tu[...]) + up_shift)
    act_o[...] = act_all.astype(BF16)
    wide_b[...] = slope_all
    dp_forward(1)
    dp_forward(2)
    dp_recv(1)
    dp_recv(2)

    image_low = from_tall_all(gat.at[1], n_dp).astype(BF16)
    pooled = from_tall_all(gat.at[2], n_dp)
    shrink = lax.rsqrt(jnp.sum(pooled * pooled, axis=-1, keepdims=True) + 1e-06)
    text_unit = pooled * shrink
    logits = 64.0 * dot_nt(text_unit.astype(BF16), image_low)
    row_top = jnp.max(logits, axis=1, keepdims=True)
    row_lse = row_top + jnp.log(jnp.sum(jnp.exp(logits - row_top), axis=1, keepdims=True))
    col_top = jnp.max(logits, axis=0, keepdims=True)
    col_lse = col_top + jnp.log(jnp.sum(jnp.exp(logits - col_top), axis=0, keepdims=True))
    grad_logits = 0.5 * (jnp.exp(logits - row_lse) + jnp.exp(logits - col_lse)) - onehot
    grad_embed = 64.0 * dot(grad_logits.astype(BF16), image_low)
    along = jnp.sum(text_unit * grad_embed, axis=-1, keepdims=True)
    grad_final = shrink * (grad_embed - text_unit * along)
    final_low = grad_final.astype(BF16)
    fin_o[...] = final_low
    wide_c[...] = grad_final
    grad_hidden = dot_nt(final_low, td[...]) * wide_b[...]
    gh_o[...] = grad_hidden.astype(BF16)
    wide_b[...] = grad_hidden
    own = pl.ds(pl.multiple_of(d * pairs, 8), pairs)
    ar[4, m] = to_tall(dot_nt(wide_b[own, :].astype(BF16), tu[...]))
    mp_send(ar.at[4], ar_s.at[4], ar_r.at[4])

    tok_third()
    tok_far_across()
    positive = jnp.sum(logits * onehot, axis=1, keepdims=True)
    pair_loss = 0.5 * (row_lse + column_of(col_lse, total)) - positive
    shape = (total, loss_o.shape[1])
    spot = lax.broadcasted_iota(jnp.int32, shape, 1)
    here = lax.broadcasted_iota(jnp.int32, shape, 0) == d * pairs + spot
    loss_o[...] = jnp.sum(jnp.where(here, pair_loss, 0.0), axis=0, keepdims=True)
    up_bias = jnp.sum(gh_o[...].astype(F32), axis=0, keepdims=True)

    grad_n2 = summed(4)
    grad_middle = wide_c[own, :] + norm_back(grad_n2, hat_two, factor_two, gain_two)
    gat[3, d] = to_tall(grad_middle)
    dp_send(3)
    middle_low = grad_middle.astype(BF16)
    grad_context = dot_nt(middle_low, to[...]).astype(BF16)
    grad_folded = dot(head_blocks(grad_context.astype(F32), width).astype(BF16), tw[2])
    fg[m] = padded(grad_folded, no_foot)
    far_send(fg, f_s.at[1], f_r.at[1])
    grad_probs = dot_nt(grad_folded.astype(BF16), normed)
    grad_scores = probs * (grad_probs - jnp.sum(grad_probs * probs, axis=-1, keepdims=True))
    scaled = grad_scores * scale
    score_rows = head_rows(scaled)
    drow[d] = score_rows
    small_send(2, drow)
    mixed_back = dot(scaled.astype(BF16), normed).astype(BF16)
    grad_queries = head_pick(dot_nt(mixed_back, tw[1]), width).astype(BF16)
    fd[m] = padded(dot(grad_queries, tw[0]), score_rows)
    far_send(fd, f_s.at[2], f_r.at[2])

    def spread(slots, ref, at):
        parts = []
        for i in slots:
            foot = ref[i, at : at + 8, 0:tokens].astype(F32)
            for h in range(heads):
                parts.append(jnp.where(mine, foot[h : h + 1], 0.0))
            parts.append(jnp.zeros((8, tokens), F32))
        return jnp.concatenate(parts, axis=0).astype(BF16)

    def first_norm_grad(slots, sources):
        folds, backs, rests = sources
        place_low = jnp.concatenate(
            [jnp.concatenate([pick.astype(F32), jnp.zeros((8, tokens), F32)], axis=0)] * len(slots),
            axis=0,
        ).astype(BF16)
        grads = dot_tn(spread(slots, fd, pairs), folds)
        grads = grads + dot_tn(spread(slots, fq, pairs * heads), backs)
        return grads + dot_tn(place_low, rests)

    part = first_norm_grad([m], (fq[m], fg[m], fd[m]))
    stm[m] = stats_pack(
        [jnp.sum(part * hat_one, axis=0, keepdims=True), jnp.sum(part, axis=0, keepdims=True)]
    )
    mp_send(stm, f_s.at[3], f_r.at[3])
    stats_two = [
        jnp.sum(grad_n2 * hat_two, axis=0, keepdims=True),
        jnp.sum(grad_n2, axis=0, keepdims=True),
    ]

    tok_pass()
    small_recv(1, prow)
    tok_last()
    twice = 2 * pairs

    def pair_of(j, rows_ref):
        seg = jnp.concatenate([ids[2 * j, 0:1, :], ids[2 * j + 1, 0:1, :]], axis=1)
        here, picks = caption_masks(seg, j * twice, twice)
        values = jnp.concatenate([rows_ref[2 * j], rows_ref[2 * j + 1]], axis=1)
        parts = [jnp.where(here, values[h : h + 1], 0.0) for h in range(heads)]
        low = tok[2 * j : 2 * j + 2].reshape(2 * tokens, features)
        return jnp.concatenate(parts, axis=0).astype(BF16), picks, low

    for j in range(half_dp):
        values, picks, low = pair_of(j, prow)
        rows = slice(j * twice, (j + 1) * twice)
        mixed = dot(values, low).astype(BF16)
        for h in range(heads):
            xv_o[h, rows, :] = mixed[h * twice : (h + 1) * twice]
        nsel_o[rows, :] = dot(picks, low).astype(BF16)

    far_pass(fg, f_s.at[1], f_r.at[1])
    far_pass(fd, f_s.at[2], f_r.at[2])
    dp_forward(3)
    mp_recv(stm, f_s.at[3], f_r.at[3])
    own_stats = stm[0]
    for i in range(1, n_mp):
        own_stats = own_stats + stm[i]
    std[d] = stats_pack(stats_unpack(own_stats, 2, features) + stats_two)
    small_send(3, std)
    q_o[...] = dot_nt(nsel_o[...], tw[0]).astype(BF16)
    ctx_o[...] = head_pick(
        dot_nt(xv_o[...].reshape(heads * total, features), tw[2]), width
    ).astype(BF16)

    small_recv(2, drow)
    for j in range(half_dp):
        values, picks, low = pair_of(j, drow)
        rows = slice(j * twice, (j + 1) * twice)
        mixed = dot(values, low).astype(BF16)
        for h in range(heads):
            xk_o[h, rows, :] = mixed[h * twice : (h + 1) * twice]
    dq_o[...] = head_pick(
        dot_nt(xk_o[...].reshape(heads * total, features), tw[1]), width
    ).astype(BF16)
    dp_recv(3)
    mid_all = from_tall_all(gat.at[3], n_dp).astype(BF16)
    mid_o[...] = mid_all
    gctx_o[...] = dot_nt(mid_all, to[...]).astype(BF16)

    for at, buf in ((0, fq), (1, fg), (2, fd)):
        far_recv(buf, f_s.at[at], f_r.at[at])
    flat = [ref[...].reshape(n_mp * ref.shape[1], features) for ref in (fq, fg, fd)]
    grad_normed = first_norm_grad(list(range(n_mp)), flat)
    text_grad = norm_back(grad_normed, hat_one, factor_one, gain_one)
    tg_o[...] = text_grad + dot_tn(pick, middle_low)

    small_recv(3, std)
    stats = std[0]
    for i in range(1, n_dp):
        stats = stats + std[i]
    vec_o[...] = jnp.concatenate(
        stats_unpack(stats, 4, features) + [up_bias, jnp.zeros((3, features), F32)], axis=0
    )

    for at in range(ar.shape[0]):
        mp_drain(ar.at[at], ar_s.at[at], ar_r.at[at])
    for at, buf in enumerate((fq, fg, fd, stm)):
        mp_drain(buf, f_s.at[at], f_r.at[at])
    for at in range(gat.shape[0]):
        dp_drain(at)
    for at, buf in enumerate((ids, prow, drow, std)):
        small_drain(at, buf)
    tok_drain()


def weights_kernel(
    act,
    fin,
    n2,
    gh,
    ctx,
    mid,
    nsel,
    dq,
    q,
    gctx,
    xk,
    xv,
    tg,
    vec,
    loss,
    tg_out,
    qkv_out,
    out_out,
    up_out,
    down_out,
    loss_out,
    g1_out,
    b1_out,
    g2_out,
    b2_out,
    ub_out,
    qkv_buf,
    out_buf,
    up_buf,
    down_buf,
    sem,
):
    heads, total, features = xk.shape
    width = q.shape[1]
    started = []

    def ship(src, dst):
        copy = pltpu.make_async_copy(src, dst, sem.at[len(started)])
        copy.start()
        started.append(copy)

    ship(tg, tg_out)
    step = 256
    for left, right, buf, dst in (
        (act, fin, down_buf, down_out),
        (n2, gh, up_buf, up_out),
    ):
        for at in range(0, features, step):
            rows = pl.ds(at, step)
            buf[rows, :] = dot_tn(left[:, at : at + step], right[...])
            ship(buf.at[rows], dst.at[rows])
    out_buf[...] = dot_tn(ctx[...], mid[...])
    ship(out_buf, out_out)
    qkv_buf[0] = dot_tn(dq[...], nsel[...])
    ship(qkv_buf.at[0], qkv_out.at[0])
    for at, rows, blocks in ((1, q, xk), (2, gctx, xv)):
        stacked = head_blocks(rows[...].astype(F32), width).astype(BF16)
        qkv_buf[at] = dot_tn(stacked, blocks[...].reshape(heads * total, features))
        ship(qkv_buf.at[at], qkv_out.at[at])
    for at, dst in enumerate((g1_out, b1_out, g2_out, b2_out, ub_out)):
        dst[...] = vec[at, :]
    loss_out[...] = loss[0, 0 : loss_out.shape[0]]
    for copy in started:
        copy.wait()


def kernel_device(
    n_dp,
    n_mp,
    text_tokens,
    segment_ids,
    labels,
    image_tokens,
    image_gain_one,
    image_bias_one,
    image_qkv,
    image_out,
    image_gain_two,
    image_bias_two,
    image_up,
    image_up_bias,
    image_down,
    text_gain_one,
    text_bias_one,
    text_qkv,
    text_out,
    text_gain_two,
    text_bias_two,
    text_up,
    text_up_bias,
    text_down,
):
    pairs = labels.shape[0]
    tokens, features = text_tokens.shape
    width = text_out.shape[0]
    hidden = text_up.shape[1]
    heads = width // HEAD
    total = n_dp * pairs
    half_dp = n_dp // 2
    vmem = pltpu.VMEM
    whole = pl.BlockSpec(memory_space=pltpu.VMEM)
    anywhere = pl.BlockSpec(memory_space=pl.ANY)

    def sems(*shape):
        return pltpu.SemaphoreType.DMA(shape)

    outs = [
        ((total, hidden), BF16),
        ((total, features), BF16),
        ((total, features), BF16),
        ((total, hidden), BF16),
        ((total, width), BF16),
        ((total, features), BF16),
        ((total, features), BF16),
        ((total, width), BF16),
        ((total, width), BF16),
        ((total, width), BF16),
        ((heads, total, features), BF16),
        ((heads, total, features), BF16),
        ((tokens, features), F32),
        ((8, features), F32),
        ((1, 128), F32),
    ]
    tall = (2 * pairs, features // 2)
    fold_rows = heads * pairs + 8
    vectors = (
        segment_ids,
        labels,
        image_gain_one,
        image_bias_one,
        image_gain_two,
        image_bias_two,
        image_up_bias,
        text_gain_one,
        text_bias_one,
        text_gain_two,
        text_bias_two,
        text_up_bias,
    )
    operands = (
        text_tokens,
        image_tokens,
        jnp.transpose(image_qkv, (1, 2, 0)),
        image_out,
        image_up,
        image_down,
        jnp.transpose(text_qkv, (1, 2, 0)),
        text_out,
        text_up,
        text_down,
    ) + vectors
    factors = pl.pallas_call(
        functools.partial(step_kernel, (n_dp, n_mp, pairs, tokens, features, width)),
        out_shape=[vmem(shape, dtype) for shape, dtype in outs],
        in_specs=[anywhere] * len(operands),
        out_specs=[whole] * len(outs),
        scratch_shapes=[
            vmem(text_tokens.shape, BF16),
            vmem(image_tokens.shape, BF16),
            vmem(image_tokens.shape, BF16),
            vmem((3, width, features), BF16),
            vmem(image_out.shape, BF16),
            vmem(image_up.shape, BF16),
            vmem(image_down.shape, BF16),
            vmem((3, width, features), BF16),
            vmem(text_out.shape, BF16),
            vmem(text_up.shape, BF16),
            vmem(text_down.shape, BF16),
        ]
        + [vmem(array.shape, array.dtype) for array in vectors]
        + [
            vmem((n_dp, tokens, features), BF16),
            vmem((n_dp, 8, tokens), jnp.int32),
            vmem((n_dp, 8, tokens), F32),
            vmem((n_dp, 8, tokens), F32),
            vmem((n_mp, 16, 128), F32),
            vmem((n_dp, 32, 128), F32),
            vmem((5, n_mp) + tall, BF16),
            vmem((4, n_dp) + tall, BF16),
            vmem((n_mp, fold_rows, features), BF16),
            vmem((n_mp, fold_rows, features), BF16),
            vmem((n_mp, pairs + 8, features), BF16),
            vmem((total, hidden), F32),
            vmem((total, features), F32),
            sems(22),
            sems(5),
        ]
        + [sems(half_dp)] * 4
        + [sems(n_dp)] * 6
        + [
            sems(5, n_mp),
            sems(5, n_mp),
            sems(4, n_dp),
            sems(4, n_dp),
            sems(4, n_dp),
            sems(4, n_mp),
            sems(4, n_mp),
            sems(4, n_dp),
            sems(4, n_dp),
        ],
        compiler_params=pltpu.CompilerParams(
            collective_id=0, has_side_effects=True, vmem_limit_bytes=48 * 2**20
        ),
        name="step",
    )(*[pltpu.with_memory_space_constraint(operand, pltpu.HBM) for operand in operands])
    vector = jax.ShapeDtypeStruct((features,), F32)
    results = pl.pallas_call(
        weights_kernel,
        out_shape=[
            jax.ShapeDtypeStruct((tokens, features), F32),
            jax.ShapeDtypeStruct((3, width, features), F32),
            jax.ShapeDtypeStruct((width, features), F32),
            jax.ShapeDtypeStruct((features, hidden), F32),
            jax.ShapeDtypeStruct((hidden, features), F32),
            jax.ShapeDtypeStruct((pairs,), F32),
            vector,
            vector,
            vector,
            vector,
            jax.ShapeDtypeStruct((hidden,), F32),
        ],
        in_specs=[whole] * len(outs),
        out_specs=[anywhere] * 5 + [whole] * 6,
        scratch_shapes=[
            vmem((3, width, features), F32),
            vmem((width, features), F32),
            vmem((features, hidden), F32),
            vmem((hidden, features), F32),
            sems(16),
        ],
        compiler_params=pltpu.CompilerParams(vmem_limit_bytes=32 * 2**20),
        name="weights",
    )(*[pltpu.with_memory_space_constraint(factor, pltpu.VMEM) for factor in factors])
    text_grad, qkv, out, up, down, loss, gain_one, bias_one, gain_two, bias_two, up_bias = results
    return (
        loss,
        text_grad,
        gain_one,
        bias_one,
        jnp.transpose(qkv, (2, 0, 1)),
        out,
        gain_two,
        bias_two,
        up,
        up_bias,
        down,
    )


def solution(mesh):
    placed = (
        P("dp", None),
        P("dp"),
        P("dp"),
        P("dp", None),
        P(),
        P(),
        P(None, None, "mp"),
        P("mp", None),
        P(),
        P(),
        P(None, "mp"),
        P("mp"),
        P("mp", None),
        P(),
        P(),
        P(None, None, "mp"),
        P("mp", None),
        P(),
        P(),
        P(None, "mp"),
        P("mp"),
        P("mp", None),
    )
    n_dp, n_mp = mesh.shape["dp"], mesh.shape["mp"]
    body = plain_device
    if n_dp <= 16 and n_dp % 4 == 0 and n_mp == 4:
        body = functools.partial(kernel_device, n_dp, n_mp)
    return jax.shard_map(
        body,
        mesh=mesh,
        in_specs=placed,
        out_specs=(
            P("dp"),
            P("dp", None),
            P(),
            P(),
            P(None, None, "mp"),
            P("mp", None),
            P(),
            P(),
            P(None, "mp"),
            P("mp"),
            P("mp", None),
        ),
        check_vma=False,
    )
```

```python
import functools

import jax
import jax.numpy as jnp
from jax import lax
from jax.experimental import pallas as pl
from jax.experimental.pallas import tpu as pltpu
from jax.sharding import PartitionSpec as P

HEAD = 64
IMG_LEN = 50
F32 = jnp.float32
BF16 = jnp.bfloat16


def dot(a, b):
    return lax.dot_general(a, b, (((1,), (0,)), ((), ())), preferred_element_type=F32)


def dot_nt(a, b):
    return lax.dot_general(a, b, (((1,), (1,)), ((), ())), preferred_element_type=F32)


def dot_tn(a, b):
    return lax.dot_general(a, b, (((0,), (0,)), ((), ())), preferred_element_type=F32)


def normalized(values):
    center = values - jnp.mean(values, axis=-1, keepdims=True)
    factor = lax.rsqrt(jnp.mean(center * center, axis=-1, keepdims=True) + 1e-05)
    return center * factor, factor


def norm_back(grad, hat, factor, gain):
    scaled = grad * gain
    along = jnp.mean(scaled * hat, axis=-1, keepdims=True)
    return factor * (scaled - jnp.mean(scaled, axis=-1, keepdims=True) - hat * along)


def unit(rows):
    return rows * lax.rsqrt(jnp.sum(rows * rows, axis=-1, keepdims=True) + 1e-06)


def gelu_parts(hidden):
    cdf = 0.5 * (1.0 + lax.erf(hidden * 0.7071067811865476))
    slope = cdf + hidden * jnp.exp(-0.5 * hidden * hidden) * 0.3989422804014327
    return hidden * cdf, slope


def head_blocks(rows, width):
    lanes = lax.broadcasted_iota(jnp.int32, (1, width), 1)
    return jnp.concatenate(
        [
            jnp.where((lanes >= h * HEAD) & (lanes < (h + 1) * HEAD), rows, 0.0)
            for h in range(width // HEAD)
        ],
        axis=0,
    )


def head_pick(blocks, width):
    heads = width // HEAD
    count = blocks.shape[0] // heads
    lanes = lax.broadcasted_iota(jnp.int32, (1, width), 1)
    total = jnp.zeros((count, width), F32)
    for h in range(heads):
        own = (lanes >= h * HEAD) & (lanes < (h + 1) * HEAD)
        total = total + jnp.where(own, blocks[h * count : (h + 1) * count], 0.0)
    return total


def attend(normed_rows, normed, allowed, weights):
    width = weights.shape[1]
    heads = width // HEAD
    queries = dot_nt(normed_rows, weights[0]).astype(BF16)
    folded = dot(head_blocks(queries.astype(F32), width).astype(BF16), weights[1]).astype(BF16)
    scores = dot_nt(folded, normed) * HEAD**-0.5
    scores = jnp.where(jnp.concatenate([allowed] * heads, axis=0), scores, -1e30)
    expo = jnp.exp(scores - jnp.max(scores, axis=-1, keepdims=True))
    probs = expo / jnp.sum(expo, axis=-1, keepdims=True)
    mixed = dot(probs.astype(BF16), normed).astype(BF16)
    context = head_pick(dot_nt(mixed, weights[2]), width).astype(BF16)
    return queries, folded, probs, mixed, context


def plain_device(
    text_tokens,
    segment_ids,
    labels,
    image_tokens,
    image_gain_one,
    image_bias_one,
    image_qkv,
    image_out,
    image_gain_two,
    image_bias_two,
    image_up,
    image_up_bias,
    image_down,
    text_gain_one,
    text_bias_one,
    text_qkv,
    text_out,
    text_gain_two,
    text_bias_two,
    text_up,
    text_up_bias,
    text_down,
):
    rank = lax.axis_index("dp")
    pairs = labels.shape[0]
    tokens = segment_ids.shape[0]
    width = text_out.shape[0]
    heads = width // HEAD
    features = text_tokens.shape[1]
    image_weights = jnp.transpose(image_qkv, (1, 2, 0))
    text_weights = jnp.transpose(text_qkv, (1, 2, 0))

    image_x = image_tokens.astype(F32)
    image_n = (normalized(image_x)[0] * image_gain_one + image_bias_one).astype(BF16)
    image_first = image_x.reshape(pairs, IMG_LEN, features)[:, 0]
    first_n = (normalized(image_first)[0] * image_gain_one + image_bias_one).astype(BF16)
    owner = lax.broadcasted_iota(jnp.int32, (pairs, pairs * IMG_LEN), 0)
    place = lax.broadcasted_iota(jnp.int32, (pairs, pairs * IMG_LEN), 1)
    inside = (place >= owner * IMG_LEN) & (place < (owner + 1) * IMG_LEN)
    image_context = attend(first_n, image_n, inside, image_weights)[4]

    text_x = text_tokens.astype(F32)
    hat_one, factor_one = normalized(text_x)
    normed = (hat_one * text_gain_one + text_bias_one).astype(BF16)
    captions = rank * pairs + jnp.arange(pairs)
    mine = segment_ids[None, :] == captions[:, None]
    spot = lax.broadcasted_iota(jnp.int32, (pairs, tokens), 1)
    last = jnp.max(jnp.where(mine, spot, -1), axis=1, keepdims=True)
    pick = (spot == last).astype(BF16)
    normed_last = dot(pick, normed).astype(BF16)
    queries, folded, probs, mixed, context = attend(normed_last, normed, mine, text_weights)

    attended = jnp.concatenate([dot(image_context, image_out), dot(context, text_out)], axis=0)
    attended = lax.psum(attended.astype(BF16), "mp").astype(F32)
    middle = jnp.concatenate([image_first, dot(pick, text_tokens)], axis=0) + attended
    hat_two, factor_two = normalized(middle)
    image_n2 = (hat_two[:pairs] * image_gain_two + image_bias_two).astype(BF16)
    normed_two = (hat_two[pairs:] * text_gain_two + text_bias_two).astype(BF16)
    image_active = gelu_parts(dot(image_n2, image_up) + image_up_bias)[0].astype(BF16)
    active, slope = gelu_parts(dot(normed_two, text_up) + text_up_bias)
    active = active.astype(BF16)
    branch = jnp.concatenate([dot(image_active, image_down), dot(active, text_down)], axis=0)
    final = middle + lax.psum(branch.astype(BF16), "mp").astype(F32)

    everyone = lax.all_gather(final.astype(BF16), "dp").astype(F32)
    total = everyone.shape[0] * pairs
    image_low = unit(everyone[:, :pairs].reshape(total, features)).astype(BF16)
    pooled = final[pairs:]
    text_low = unit(everyone[:, pairs:].reshape(total, features)).astype(BF16)
    logits = 64.0 * dot_nt(text_low, image_low)
    column_lse = jax.nn.logsumexp(logits, axis=0)
    own = lax.dynamic_slice_in_dim(logits, rank * pairs, pairs, axis=0)
    row_lse = jax.nn.logsumexp(own, axis=1)
    own_columns = lax.dynamic_slice_in_dim(column_lse, rank * pairs, pairs)
    onehot = (labels[:, None] == jnp.arange(total)[None, :]).astype(F32)
    pair_loss = 0.5 * (row_lse + own_columns) - jnp.sum(own * onehot, axis=1)
    grad_logits = (
        0.5 * (jnp.exp(own - row_lse[:, None]) + jnp.exp(own - column_lse[None, :])) - onehot
    )
    grad_embed = 64.0 * dot(grad_logits.astype(BF16), image_low)
    scale = lax.rsqrt(jnp.sum(pooled * pooled, axis=-1, keepdims=True) + 1e-06)
    text_unit = pooled * scale
    grad_final = scale * (
        grad_embed - text_unit * jnp.sum(text_unit * grad_embed, axis=-1, keepdims=True)
    )

    final_low = grad_final.astype(BF16)
    grad_hidden = (dot_nt(final_low, text_down) * slope).astype(BF16)
    grad_normed_two = lax.psum(dot_nt(grad_hidden, text_up).astype(BF16), "mp").astype(F32)
    hat_two = hat_two[pairs:]
    grad_middle = grad_final + norm_back(grad_normed_two, hat_two, factor_two[pairs:], text_gain_two)
    middle_low = grad_middle.astype(BF16)
    grad_context = dot_nt(middle_low, text_out).astype(BF16)
    grad_folded = dot(head_blocks(grad_context.astype(F32), width).astype(BF16), text_weights[2])
    grad_folded = grad_folded.astype(BF16)
    grad_probs = dot_nt(grad_folded, normed)
    grad_scores = probs * (grad_probs - jnp.sum(grad_probs * probs, axis=-1, keepdims=True))
    grad_scores = (grad_scores * HEAD**-0.5).astype(BF16)
    mixed_back = dot(grad_scores, normed).astype(BF16)
    grad_queries = head_pick(dot_nt(mixed_back, text_weights[1]), width).astype(BF16)
    grad_normed = dot_tn(grad_scores, folded) + dot_tn(probs.astype(BF16), grad_folded)
    grad_normed = grad_normed + dot_tn(pick, dot(grad_queries, text_weights[0]).astype(BF16))
    grad_normed = lax.psum(grad_normed.astype(BF16), "mp").astype(F32)
    text_grad = norm_back(grad_normed, hat_one, factor_one, text_gain_one)
    text_grad = text_grad + dot_tn(pick, middle_low)

    vectors = jnp.concatenate(
        [
            jnp.sum(grad_normed * hat_one, axis=0),
            jnp.sum(grad_normed, axis=0),
            jnp.sum(grad_normed_two * hat_two, axis=0),
            jnp.sum(grad_normed_two, axis=0),
            jnp.sum(grad_hidden.astype(F32), axis=0),
        ]
    )
    vectors = jnp.sum(lax.all_gather(vectors, "dp"), axis=0)
    cuts = [features, 2 * features, 3 * features, 4 * features]
    gain_one, bias_one, gain_two, bias_two, up_bias = jnp.split(vectors, cuts)

    def by_head(blocks):
        return [blocks[h * pairs : (h + 1) * pairs] for h in range(heads)]

    pieces = [active, final_low, normed_two, grad_hidden, context, middle_low, normed_last]
    pieces += [grad_queries, queries, grad_context] + by_head(mixed_back) + by_head(mixed)
    sent = lax.all_gather(jnp.concatenate(pieces, axis=1), "dp").reshape(total, -1)
    got = []
    at = 0
    for piece in pieces:
        got.append(sent[:, at : at + piece.shape[1]])
        at += piece.shape[1]
    active, final_low, normed_two, grad_hidden, context, middle_low, normed_last = got[:7]
    grad_queries, queries, grad_context = got[7:10]
    mixed_back = got[10 : 10 + heads]
    mixed = got[10 + heads :]

    def per_head(rows, blocks):
        return jnp.concatenate(
            [dot_tn(rows[:, h * HEAD : (h + 1) * HEAD], blocks[h]) for h in range(heads)], axis=0
        )

    grad_qkv = jnp.stack(
        [
            dot_tn(grad_queries, normed_last),
            per_head(queries, mixed_back),
            per_head(grad_context, mixed),
        ]
    )
    return (
        pair_loss,
        text_grad,
        gain_one,
        bias_one,
        jnp.transpose(grad_qkv, (2, 0, 1)),
        dot_tn(context, middle_low),
        gain_two,
        bias_two,
        dot_tn(normed_two, grad_hidden),
        up_bias,
        dot_tn(active, final_low),
    )


MESH = pl.DeviceIdType.MESH
TOKEN_PARTS = 2
STEPS = {
    0: (("start", 0), ("start", 1)),
    3: (("second", 0), ("near", 0)),
    4: (("second", 1), ("near", 1)),
    5: (("third", 0), ("far", 0), ("pass", 0)),
    6: (("third", 1), ("far", 1), ("pass", 1)),
    8: (("last", 0), ("last", 1)),
}


def to_tall(rows):
    half = rows.shape[1] // 2
    return jnp.concatenate([rows[:, :half], rows[:, half:]], axis=0).astype(BF16)


def from_tall(tall):
    count = tall.shape[0] // 2
    wide = tall.astype(F32)
    return jnp.concatenate([wide[:count], wide[count:]], axis=1)


def column_of(row, count):
    shape = (count, row.shape[1])
    same = lax.broadcasted_iota(jnp.int32, shape, 0) == lax.broadcasted_iota(jnp.int32, shape, 1)
    return jnp.sum(jnp.where(same, row, 0), axis=1, keepdims=True)


def caption_masks(seg, first, count):
    captions = first + lax.broadcasted_iota(jnp.int32, (count, seg.shape[1]), 0)
    mine = seg == captions
    spot = lax.broadcasted_iota(jnp.int32, (count, seg.shape[1]), 1)
    last = jnp.max(jnp.where(mine, spot, -1), axis=1, keepdims=True)
    return mine, (spot == last).astype(F32).astype(BF16)


def softmax_rows(scores, allowed):
    scores = jnp.where(allowed, scores, -1e30)
    expo = jnp.exp(scores - jnp.max(scores, axis=-1, keepdims=True))
    return expo / jnp.sum(expo, axis=-1, keepdims=True)


def stats_pack(rows):
    pieces = []
    for row in rows:
        pieces += [row[:, at : at + 128] for at in range(0, row.shape[1], 128)]
    if len(pieces) % 8:
        pieces.append(jnp.zeros((-len(pieces) % 8, 128), F32))
    return jnp.concatenate(pieces, axis=0)


def stats_unpack(packed, count, features):
    per = features // 128
    return [
        jnp.concatenate([packed[at * per + i : at * per + i + 1] for i in range(per)], axis=1)
        for at in range(count)
    ]


def step_kernel(
    sizes,
    text_hbm,
    image_hbm,
    iw_hbm,
    io_hbm,
    iu_hbm,
    id_hbm,
    tw_hbm,
    to_hbm,
    tu_hbm,
    td_hbm,
    seg_hbm,
    lab_hbm,
    ig1_hbm,
    ib1_hbm,
    ig2_hbm,
    ib2_hbm,
    iub_hbm,
    tg1_hbm,
    tb1_hbm,
    tg2_hbm,
    tb2_hbm,
    tub_hbm,
    act_o,
    fin_o,
    n2_o,
    gh_o,
    ctx_o,
    mid_o,
    nsel_o,
    dq_o,
    q_o,
    gctx_o,
    xk_o,
    xv_o,
    tg_o,
    vec_o,
    loss_o,
    xt,
    xi,
    ni,
    iw,
    io,
    iu,
    idn,
    tw,
    to,
    tu,
    td,
    seg_ref,
    lab_ref,
    ig1_ref,
    ib1_ref,
    ig2_ref,
    ib2_ref,
    iub_ref,
    tg1_ref,
    tb1_ref,
    tg2_ref,
    tb2_ref,
    tub_ref,
    tok,
    ids,
    prow,
    stm,
    std,
    ar,
    gat,
    fq,
    fg,
    fd,
    load_sem,
    img_sem,
    t_s,
    tz_r,
    ty_r,
    tx_r,
    tl_r,
    ar_s,
    ar_r,
    g_s,
    g_r,
    g_f,
    g_c,
    f_s,
    f_x,
    f_c,
    st_s,
    st_r,
    sm_s,
    sm_r,
):
    n_dp, n_mp, pairs, tokens, features, width = sizes
    heads = width // HEAD
    half_dp = n_dp // 2
    total = n_dp * pairs
    scale = HEAD**-0.5
    d = lax.axis_index("dp")
    m = lax.axis_index("mp")
    core = lax.rem(m, 2)
    side = lax.div(m, 2)
    hi = lax.div(d, 2)
    lo = lax.rem(d, 2)
    partner = (d, m + 1 - 2 * core)
    across = (d, lax.rem(m + 2, 4))
    beside = (hi * 2 + 1 - lo, m)

    chunk = img_sem.shape[0]
    chunk_rows = xi.shape[0] // chunk

    def image_load(k):
        rows = pl.ds(k * chunk_rows, chunk_rows)
        return pltpu.make_async_copy(image_hbm.at[rows], xi.at[rows], img_sem.at[k])

    loads = {}

    def load(name, src, dst):
        loads[name] = pltpu.make_async_copy(src, dst, load_sem.at[len(loads)])
        loads[name].start()

    load("text", text_hbm, xt)
    load("tg1", tg1_hbm, tg1_ref)
    load("tb1", tb1_hbm, tb1_ref)
    load("seg", seg_hbm, seg_ref)
    load("lab", lab_hbm, lab_ref)
    load("ig1", ig1_hbm, ig1_ref)
    load("ib1", ib1_hbm, ib1_ref)
    for k in range(chunk):
        image_load(k).start()
    load("iw", iw_hbm, iw)
    load("io", io_hbm, io)
    load("ig2", ig2_hbm, ig2_ref)
    load("ib2", ib2_hbm, ib2_ref)
    load("iub", iub_hbm, iub_ref)
    load("tg2", tg2_hbm, tg2_ref)
    load("tb2", tb2_hbm, tb2_ref)
    load("tub", tub_hbm, tub_ref)

    def vector(name, ref):
        loads[name].wait()
        return ref[...].reshape(1, ref.shape[0])

    barrier = pltpu.get_barrier_semaphore()
    for i in range(1, n_mp):
        pl.semaphore_signal(
            barrier, inc=1, device_id=(d, lax.rem(m + i, n_mp)), device_id_type=MESH
        )

    @pl.loop(1, n_dp)
    def _(i):
        pl.semaphore_signal(
            barrier, inc=1, device_id=(lax.rem(d + i, n_dp), m), device_id_type=MESH
        )

    def remote(src, dst, send, recv, device):
        return pltpu.make_async_remote_copy(
            src_ref=src,
            dst_ref=dst,
            send_sem=send,
            recv_sem=recv,
            device_id=device,
            device_id_type=MESH,
        )

    def mp_send(buf, send, recv):
        for i in range(1, n_mp):
            remote(buf.at[m], buf.at[m], send, recv, (d, lax.rem(m + i, n_mp))).start()

    def mp_recv(buf, send, recv):
        slots = buf.at[pl.ds(0, n_mp - 1)]
        remote(slots, slots, send, recv, partner).wait_recv()

    def mp_drain(buf, send, recv):
        slots = buf.at[pl.ds(0, n_mp - 1)]
        remote(slots, slots, send, recv, partner).wait_send()

    def far_send(buf, at):
        slot = buf.at[m]
        remote(slot, slot, f_s.at[at], f_x.at[at], across).start()
        remote(slot, slot, f_s.at[at], f_c.at[at], partner).start()

    def far_pass(buf, at):
        slot = buf.at[lax.rem(m + 2, 4)]
        remote(slot, slot, f_s.at[at], f_x.at[at], partner).wait_recv()
        remote(slot, slot, f_s.at[at], f_c.at[at], partner).start()

    def far_recv(buf, at):
        slots = buf.at[pl.ds(0, 2)]
        remote(slots, slots, f_s.at[at], f_c.at[at], partner).wait_recv()

    def far_drain(buf, at):
        slots = buf.at[pl.ds(0, 3)]
        remote(slots, slots, f_s.at[at], f_c.at[at], partner).wait_send()

    def on_core(which):
        return pl.when(core == which)

    def dp_send(at):
        slot = gat.at[at, lo, hi]
        other = lo + core * (1 - 2 * lo)

        def send(k):
            to_dev = (lax.rem(hi + k, half_dp) * 2 + other, m)
            remote(slot, slot, g_s.at[at], g_r.at[at], to_dev).start()

        for k in range(1, half_dp):
            send(k)
        on_core(1)(lambda: send(0))

    def dp_forward(at):
        @on_core(1)
        def _():
            slots = gat.at[at, 1 - lo]
            remote(slots, slots, g_f.at[at], g_r.at[at], partner).wait_recv()
            remote(slots, slots, g_f.at[at], g_c.at[at], partner).start()

        @on_core(0)
        def _():
            slots = gat.at[at, 0, pl.ds(0, half_dp - 1)]
            remote(slots, slots, g_f.at[at], g_r.at[at], partner).wait_recv()
            for k in range(1, half_dp):
                slot = gat.at[at, lo, lax.rem(hi + k, half_dp)]
                remote(slot, slot, g_f.at[at], g_c.at[at], partner).start()

    def dp_wait(at, first, wait):
        for which in (0, 1):

            @on_core(which)
            def _(which=which):
                slots = gat.at[at, 0, pl.ds(0, half_dp - (1 if which == first else 0))]
                wait(slots)

    def dp_recv(at):
        dp_wait(
            at,
            1,
            lambda slots: remote(slots, slots, g_f.at[at], g_c.at[at], partner).wait_recv(),
        )

    def dp_drain(at):
        def wait(slots):
            remote(slots, slots, g_s.at[at], g_c.at[at], partner).wait_send()
            remote(slots, slots, g_f.at[at], g_c.at[at], partner).wait_send()

        dp_wait(at, 0, wait)

    def gathered(at):
        talls = [gat[at, i % 2, i // 2].astype(F32) for i in range(n_dp)]
        left = jnp.concatenate([t[:pairs] for t in talls], axis=0)
        right = jnp.concatenate([t[pairs:] for t in talls], axis=0)
        return jnp.concatenate([left, right], axis=1)

    def small_send(at, buf):
        @pl.loop(1, n_dp)
        def _(i):
            to_dev = (lax.rem(d + i, n_dp), m)
            remote(buf.at[d], buf.at[d], sm_s.at[at], sm_r.at[at], to_dev).start()

    def small_recv(at, buf):
        slots = buf.at[pl.ds(0, n_dp - 1)]
        remote(slots, slots, sm_s.at[at], sm_r.at[at], partner).wait_recv()

    def small_drain(at, buf):
        slots = buf.at[pl.ds(0, n_dp - 1)]
        remote(slots, slots, sm_s.at[at], sm_r.at[at], partner).wait_send()

    part_rows = tokens // (2 * TOKEN_PARTS)

    def split_hi(mine, body):
        for k in range(half_dp // 2 - 1):
            body(2 * k + (2 - core if mine else 1 + core))

        @pl.when(core == (1 if mine else 0))
        def _():
            body(half_dp - 1)

    def near_slot(i):
        return lax.rem(hi + half_dp - i, half_dp) * 2 + lo

    def far_slot(i):
        return lax.rem(hi + half_dp - i, half_dp) * 2 + 1 - lo

    def split_far(mine, body):
        split_hi(mine, lambda i: body(half_dp + i, far_slot(i)))

        @pl.when(core == (0 if mine else 1))
        def _():
            body(half_dp, far_slot(0))

    def split_near(mine, body):
        split_hi(mine, lambda i: body(i, near_slot(i)))

    def rows_of(slot, part, which):
        start = (which * TOKEN_PARTS + part) * part_rows
        return tok.at[slot, pl.ds(pl.multiple_of(start, 16), part_rows)]

    def tok_push(rows, recv, device):
        remote(rows, rows, t_s.at[0], recv, device).start()

    def tok_wait(recv, counts):
        for which in (0, 1):
            if counts[which]:

                @on_core(which)
                def _(which=which):
                    rows = tok.at[0, pl.ds(0, counts[which] * part_rows)]
                    remote(rows, rows, t_s.at[0], recv, partner).wait_recv()

    quarter = half_dp // 2
    near_counts = (quarter - 1, quarter)
    far_counts = (quarter, quarter)

    def tok_start(part):
        rows = rows_of(d, part, side)

        def body(i):
            tok_push(rows, tz_r.at[part], (lax.rem(hi + i, half_dp) * 2 + lo, m))

        split_hi(True, body)
        on_core(0)(lambda: tok_push(rows, ty_r.at[part], beside))

    def tok_second(part):
        tok_wait(tz_r.at[part], near_counts)

        def body(i, slot):
            rows = rows_of(slot, part, side)
            tok_push(rows, ty_r.at[part], beside)
            tok_push(rows, tl_r.at[0], partner)

        split_near(True, body)

    def tok_third(part):
        tok_wait(ty_r.at[part], far_counts)
        split_far(True, lambda at, slot: tok_push(rows_of(slot, part, side), tl_r.at[0], partner))

    def tok_near(part):
        split_near(
            True, lambda at, slot: tok_push(rows_of(slot, part, side), tx_r.at[part, 0], across)
        )

    def tok_far(part):
        split_far(
            True, lambda at, slot: tok_push(rows_of(slot, part, side), tx_r.at[part, 1], across)
        )

    def tok_pass_near(part):
        tok_wait(tx_r.at[part, 0], near_counts)
        split_near(
            True, lambda at, slot: tok_push(rows_of(slot, part, 1 - side), tl_r.at[0], partner)
        )

    def tok_pass_far(part):
        tok_wait(tx_r.at[part, 1], far_counts)
        split_far(
            True, lambda at, slot: tok_push(rows_of(slot, part, 1 - side), tl_r.at[0], partner)
        )

    def tok_last():
        for which, count in ((0, 2 * quarter), (1, 2 * quarter - 1)):

            @on_core(which)
            def _(count=count):
                slots = tok.at[pl.ds(0, count)]
                remote(slots, slots, t_s.at[0], tl_r.at[0], partner).wait_recv()

    def tok_drain():
        for which, count in ((0, n_dp - 2), (1, n_dp)):

            @on_core(which)
            def _(count=count):
                slots = tok.at[pl.ds(0, count)]
                remote(slots, slots, t_s.at[0], tl_r.at[0], partner).wait_send()

    def token_steps(at):
        steps = {
            "start": tok_start,
            "second": tok_second,
            "third": tok_third,
            "near": tok_near,
            "far": tok_far,
            "pass": tok_pass_near,
            "last": tok_pass_far,
        }
        for name, part in STEPS.get(at, ()):
            steps[name](part)

    def attend_rows(queries, normed, allowed, weights):
        stacked = head_blocks(queries.astype(F32), width).astype(BF16)
        folded = dot(stacked, weights[1]).astype(BF16)
        scores = dot_nt(folded, normed) * scale
        probs = softmax_rows(scores, allowed)
        mixed = dot(probs.astype(BF16), normed).astype(BF16)
        context = head_pick(dot_nt(mixed, weights[2]), width).astype(BF16)
        return folded, probs, context

    loads["text"].wait()
    gain_one = vector("tg1", tg1_ref)
    hat_one, factor_one = normalized(xt[...].astype(F32))
    tok[d] = (hat_one * gain_one + vector("tb1", tb1_ref)).astype(BF16)
    seg = vector("seg", seg_ref)
    seg_rows = tokens // 128
    for i in range(seg_rows):
        ids[d, i : i + 1, :] = seg[:, i * 128 : (i + 1) * 128]
    ids[d, seg_rows : seg_rows + 1, 0:pairs] = vector("lab", lab_ref)

    gain, shift = vector("ig1", ig1_ref), vector("ib1", ib1_ref)

    @pl.loop(0, chunk)
    def _(k):
        image_load(k).wait()
        rows = pl.ds(pl.multiple_of(k * chunk_rows, 16), chunk_rows)
        hat = normalized(xi[rows, :].astype(F32))[0]
        ni[rows, :] = (hat * gain + shift).astype(BF16)

    load("tw", tw_hbm, tw)
    load("to", to_hbm, to)
    load("iu", iu_hbm, iu)
    load("id", id_hbm, idn)
    load("tu", tu_hbm, tu)
    load("td", td_hbm, td)
    firsts = [i * IMG_LEN for i in range(pairs)]
    image_first = jnp.concatenate([xi[r : r + 1, :].astype(F32) for r in firsts], axis=0)
    first_n = (normalized(image_first)[0] * gain + shift).astype(BF16)
    loads["iw"].wait()
    image_q = dot_nt(first_n, iw[0]).astype(BF16)
    shape = (pairs, xi.shape[0])
    place = lax.broadcasted_iota(jnp.int32, shape, 1)
    begin = lax.broadcasted_iota(jnp.int32, shape, 0) * IMG_LEN
    inside = jnp.concatenate([(place >= begin) & (place < begin + IMG_LEN)] * heads, axis=0)
    image_context = attend_rows(image_q, ni[...], inside, iw)[2]
    loads["io"].wait()
    ar[0, m] = to_tall(dot(image_context, io[...]))

    pl.semaphore_wait(barrier, n_mp - 1 + n_dp - 1)
    mp_send(ar.at[0], ar_s.at[0], ar_r.at[0])
    token_steps(0)
    small_send(0, ids)

    normed = tok[d]
    mine, pick = caption_masks(seg, d * pairs, pairs)
    allowed = jnp.concatenate([mine] * heads, axis=0)
    loads["tw"].wait()
    queries = dot_nt(dot(pick, normed).astype(BF16), tw[0]).astype(BF16)
    folded, probs, context = attend_rows(queries, normed, allowed, tw)
    loads["to"].wait()
    ar[1, m] = to_tall(dot(context, to[...]))
    mp_send(ar.at[1], ar_s.at[1], ar_r.at[1])
    text_last = dot(pick, xt[...])

    def head_rows(blocks):
        rows = [
            jnp.sum(blocks[h * pairs : (h + 1) * pairs], axis=0, keepdims=True)
            for h in range(heads)
        ]
        return jnp.concatenate(rows + [jnp.zeros((8 - heads, tokens), F32)], axis=0)

    def padded(rows, foot):
        foot = jnp.concatenate([foot, jnp.zeros((8, features - tokens), F32)], axis=1)
        return jnp.concatenate([rows, foot], axis=0).astype(BF16)

    no_foot = jnp.zeros((8, tokens), F32)
    prob_rows = head_rows(probs)
    fq[m] = padded(folded.astype(F32), prob_rows)
    token_steps(1)

    def summed(at):
        mp_recv(ar.at[at], ar_s.at[at], ar_r.at[at])
        full = ar[at, 0].astype(F32)
        for i in range(1, n_mp):
            full = full + ar[at, i].astype(F32)
        count = full.shape[0] // 2
        return jnp.concatenate([full[:count], full[count:]], axis=1)

    image_middle = image_first + summed(0)
    gain, shift = vector("ig2", ig2_ref), vector("ib2", ib2_ref)
    image_n2 = (normalized(image_middle)[0] * gain + shift).astype(BF16)
    loads["iu"].wait()
    image_hidden = dot(image_n2, iu[...]) + vector("iub", iub_ref)
    image_active = gelu_parts(image_hidden)[0].astype(BF16)
    loads["id"].wait()
    ar[2, m] = to_tall(dot(image_active, idn[...]))
    mp_send(ar.at[2], ar_s.at[2], ar_r.at[2])
    token_steps(2)

    middle = text_last + summed(1)
    gat[0, lo, hi] = to_tall(middle)
    gain_two, shift_two = vector("tg2", tg2_ref), vector("tb2", tb2_ref)
    hat_two, factor_two = normalized(middle)
    normed_two = (hat_two * gain_two + shift_two).astype(BF16)
    loads["tu"].wait()
    up_shift = vector("tub", tub_ref)
    active, slope = gelu_parts(dot(normed_two, tu[...]) + up_shift)
    loads["td"].wait()
    ar[3, m] = to_tall(dot(active.astype(BF16), td[...]))
    mp_send(ar.at[3], ar_s.at[3], ar_r.at[3])
    token_steps(3)

    gat[1, lo, hi] = to_tall(unit(image_middle + summed(2)))
    dp_send(1)
    gat[2, lo, hi] = to_tall(middle + summed(3))
    dp_send(2)
    far_send(fq, 0)

    token_steps(4)
    dp_forward(1)
    dp_forward(2)
    dp_send(0)
    far_pass(fq, 0)
    token_steps(5)
    dp_recv(1)
    dp_recv(2)

    image_low = gathered(1).astype(BF16)

    def embedded(rows):
        shrink = lax.rsqrt(jnp.sum(rows * rows, axis=-1, keepdims=True) + 1e-06)
        text_unit = rows * shrink
        return shrink, text_unit, 64.0 * dot_nt(text_unit.astype(BF16), image_low)

    def final_grad(shrink, text_unit, logits, labels):
        lanes = lax.broadcasted_iota(jnp.int32, logits.shape, 1)
        onehot = (labels == lanes).astype(F32)
        top = jnp.max(logits, axis=1, keepdims=True)
        lse = top + jnp.log(jnp.sum(jnp.exp(logits - top), axis=1, keepdims=True))
        grads = 0.5 * (jnp.exp(logits - lse) + jnp.exp(logits - col_lse)) - onehot
        grads = 64.0 * dot(grads.astype(BF16), image_low)
        along = jnp.sum(text_unit * grads, axis=-1, keepdims=True)
        positive = jnp.sum(logits * onehot, axis=1, keepdims=True)
        return shrink * (grads - text_unit * along), lse, positive

    shrink_all, unit_all, logits = embedded(gathered(2))
    col_top = jnp.max(logits, axis=0, keepdims=True)
    col_lse = col_top + jnp.log(jnp.sum(jnp.exp(logits - col_top), axis=0, keepdims=True))
    own_labels = column_of(ids[d, seg_rows : seg_rows + 1, :], pairs)
    grad_final, own_lse, positive = final_grad(*embedded(from_tall(gat[2, lo, hi])), own_labels)
    grad_hidden = (dot_nt(grad_final.astype(BF16), td[...]) * slope).astype(BF16)
    ar[4, m] = to_tall(dot_nt(grad_hidden, tu[...]))
    mp_send(ar.at[4], ar_s.at[4], ar_r.at[4])

    token_steps(6)
    lanes = lax.broadcasted_iota(jnp.int32, (pairs, total), 1)
    mine_first = lax.broadcasted_iota(jnp.int32, (pairs, total), 0) + d * pairs
    own_col = jnp.sum(jnp.where(lanes == mine_first, col_lse, 0.0), axis=1, keepdims=True)
    pair_loss = 0.5 * (own_lse + own_col) - positive
    shape = (pairs, loss_o.shape[1])
    diagonal = lax.broadcasted_iota(jnp.int32, shape, 0) == lax.broadcasted_iota(
        jnp.int32, shape, 1
    )
    loss_o[...] = jnp.sum(jnp.where(diagonal, pair_loss, 0.0), axis=0, keepdims=True)
    small_recv(0, ids)
    labels = jnp.concatenate(
        [column_of(ids[i, seg_rows : seg_rows + 1, :], pairs) for i in range(n_dp)], axis=0
    )
    fin_o[...] = final_grad(shrink_all, unit_all, logits, labels)[0].astype(BF16)
    dp_forward(0)

    grad_n2 = summed(4)
    grad_middle = grad_final + norm_back(grad_n2, hat_two, factor_two, gain_two)
    gat[3, lo, hi] = to_tall(grad_middle)
    dp_send(3)
    middle_low = grad_middle.astype(BF16)
    grad_context = dot_nt(middle_low, to[...]).astype(BF16)
    grad_folded = dot(head_blocks(grad_context.astype(F32), width).astype(BF16), tw[2])
    fg[m] = padded(grad_folded, no_foot)
    grad_probs = dot_nt(grad_folded.astype(BF16), normed)
    grad_scores = probs * (grad_probs - jnp.sum(grad_probs * probs, axis=-1, keepdims=True))
    scaled = grad_scores * scale
    score_rows = head_rows(scaled)
    prow[d] = jnp.concatenate([prob_rows[:heads], score_rows[: 8 - heads]], axis=0)
    mixed_back = dot(scaled.astype(BF16), normed).astype(BF16)
    grad_queries = head_pick(dot_nt(mixed_back, tw[1]), width).astype(BF16)
    fd[m] = padded(dot(grad_queries, tw[0]), score_rows)

    def spread(slots, ref, at):
        parts = []
        for i in slots:
            foot = ref[i, at : at + 8, 0:tokens].astype(F32)
            for h in range(heads):
                parts.append(jnp.where(mine, foot[h : h + 1], 0.0))
            parts.append(jnp.zeros((8, tokens), F32))
        return jnp.concatenate(parts, axis=0).astype(BF16)

    def first_norm_grad(slots, sources):
        folds, backs, rests = sources
        place_low = jnp.concatenate(
            [jnp.concatenate([pick.astype(F32), jnp.zeros((8, tokens), F32)], axis=0)] * len(slots),
            axis=0,
        ).astype(BF16)
        grads = dot_tn(spread(slots, fd, pairs), folds)
        grads = grads + dot_tn(spread(slots, fq, pairs * heads), backs)
        return grads + dot_tn(place_low, rests)

    part = first_norm_grad([m], (fq[m], fg[m], fd[m]))
    stm[m] = stats_pack(
        [jnp.sum(part * hat_one, axis=0, keepdims=True), jnp.sum(part, axis=0, keepdims=True)]
    )
    mp_send(stm, st_s.at[0], st_r.at[0])
    far_send(fg, 1)
    far_send(fd, 2)
    small_send(1, prow)
    stats_two = [
        jnp.sum(grad_n2 * hat_two, axis=0, keepdims=True),
        jnp.sum(grad_n2, axis=0, keepdims=True),
    ]

    token_steps(7)
    dp_recv(0)
    n2_all = (normalized(gathered(0))[0] * gain_two + shift_two).astype(BF16)
    n2_o[...] = n2_all
    act_all, slope_all = gelu_parts(dot(n2_all, tu[...]) + up_shift)
    act_o[...] = act_all.astype(BF16)
    gh_o[...] = (dot_nt(fin_o[...], td[...]) * slope_all).astype(BF16)
    up_bias = jnp.sum(gh_o[...].astype(F32), axis=0, keepdims=True)
    mp_recv(stm, st_s.at[0], st_r.at[0])
    one = stm[0]
    for i in range(1, n_mp):
        one = one + stm[i]
    std[d] = stats_pack(stats_unpack(one, 2, features) + stats_two)
    small_send(2, std)
    dp_forward(3)
    far_pass(fg, 1)
    far_pass(fd, 2)
    token_steps(8)

    for at, buf in ((0, fq), (1, fg), (2, fd)):
        far_recv(buf, at)
    flat = [ref[...].reshape(n_mp * ref.shape[1], features) for ref in (fq, fg, fd)]
    grad_normed = first_norm_grad(list(range(n_mp)), flat)
    text_grad = norm_back(grad_normed, hat_one, factor_one, gain_one)
    tg_o[...] = text_grad + dot_tn(pick, middle_low)

    small_recv(1, prow)
    tok_last()
    twice = 2 * pairs
    for j in range(half_dp):
        seg = jnp.concatenate(
            [ids[i, k : k + 1, :] for i in (2 * j, 2 * j + 1) for k in range(seg_rows)], axis=1
        )
        here, picks = caption_masks(seg, j * twice, twice)
        values = jnp.concatenate([prow[2 * j], prow[2 * j + 1]], axis=1)
        parts = [jnp.where(here, values[h : h + 1], 0.0) for h in range(heads)]
        parts += [jnp.where(here, values[heads + h : heads + h + 1], 0.0) for h in range(heads)]
        parts = [part.astype(BF16) for part in parts] + [picks]
        low = tok[2 * j : 2 * j + 2].reshape(2 * tokens, features)
        mixed = dot(jnp.concatenate(parts, axis=0), low).astype(BF16)
        rows = slice(j * twice, (j + 1) * twice)
        for h in range(heads):
            xv_o[h, rows, :] = mixed[h * twice : (h + 1) * twice]
            xk_o[h, rows, :] = mixed[(heads + h) * twice : (heads + h + 1) * twice]
        nsel_o[rows, :] = mixed[2 * heads * twice :]
    q_o[...] = dot_nt(nsel_o[...], tw[0]).astype(BF16)
    ctx_o[...] = head_pick(
        dot_nt(xv_o[...].reshape(heads * total, features), tw[2]), width
    ).astype(BF16)
    dq_o[...] = head_pick(
        dot_nt(xk_o[...].reshape(heads * total, features), tw[1]), width
    ).astype(BF16)
    dp_recv(3)
    mid_all = gathered(3).astype(BF16)
    mid_o[...] = mid_all
    gctx_o[...] = dot_nt(mid_all, to[...]).astype(BF16)

    small_recv(2, std)
    stats = std[0]
    for i in range(1, n_dp):
        stats = stats + std[i]
    rows = stats_unpack(stats, 4, features)
    vec_o[...] = jnp.concatenate(rows + [up_bias, jnp.zeros((3, features), F32)], axis=0)

    for at in range(ar.shape[0]):
        mp_drain(ar.at[at], ar_s.at[at], ar_r.at[at])
    mp_drain(stm, st_s.at[0], st_r.at[0])
    for at, buf in enumerate((fq, fg, fd)):
        far_drain(buf, at)
    for at in range(gat.shape[0]):
        dp_drain(at)
    for at, buf in enumerate((ids, prow, std)):
        small_drain(at, buf)
    tok_drain()


def weights_kernel(
    act,
    fin,
    n2,
    gh,
    ctx,
    mid,
    nsel,
    dq,
    q,
    gctx,
    xk,
    xv,
    tg,
    vec,
    loss,
    tg_out,
    qkv_out,
    out_out,
    up_out,
    down_out,
    loss_out,
    g1_out,
    b1_out,
    g2_out,
    b2_out,
    ub_out,
    qkv_buf,
    out_buf,
    up_buf,
    down_buf,
    sem,
):
    heads, total, features = xk.shape
    width = q.shape[1]
    started = []

    def ship(src, dst):
        copy = pltpu.make_async_copy(src, dst, sem.at[len(started)])
        copy.start()
        started.append(copy)

    ship(tg, tg_out)
    step = 256
    for left, right, buf, dst in (
        (act, fin, down_buf, down_out),
        (n2, gh, up_buf, up_out),
    ):
        for at in range(0, features, step):
            rows = pl.ds(at, step)
            buf[rows, :] = dot_tn(left[:, at : at + step], right[...])
            ship(buf.at[rows], dst.at[rows])
    out_buf[...] = dot_tn(ctx[...], mid[...])
    ship(out_buf, out_out)
    qkv_buf[0] = dot_tn(dq[...], nsel[...])
    ship(qkv_buf.at[0], qkv_out.at[0])
    for at, rows, blocks in ((1, q, xk), (2, gctx, xv)):
        stacked = head_blocks(rows[...].astype(F32), width).astype(BF16)
        qkv_buf[at] = dot_tn(stacked, blocks[...].reshape(heads * total, features))
        ship(qkv_buf.at[at], qkv_out.at[at])
    for at, dst in enumerate((g1_out, b1_out, g2_out, b2_out, ub_out)):
        dst[...] = vec[at, :]
    loss_out[...] = loss[0, 0 : loss_out.shape[0]]
    for copy in started:
        copy.wait()


def kernel_device(
    n_dp,
    n_mp,
    text_tokens,
    segment_ids,
    labels,
    image_tokens,
    image_gain_one,
    image_bias_one,
    image_qkv,
    image_out,
    image_gain_two,
    image_bias_two,
    image_up,
    image_up_bias,
    image_down,
    text_gain_one,
    text_bias_one,
    text_qkv,
    text_out,
    text_gain_two,
    text_bias_two,
    text_up,
    text_up_bias,
    text_down,
):
    pairs = labels.shape[0]
    tokens, features = text_tokens.shape
    width = text_out.shape[0]
    hidden = text_up.shape[1]
    heads = width // HEAD
    total = n_dp * pairs
    half_dp = n_dp // 2
    vmem = pltpu.VMEM
    whole = pl.BlockSpec(memory_space=pltpu.VMEM)
    anywhere = pl.BlockSpec(memory_space=pl.ANY)

    def sems(*shape):
        return pltpu.SemaphoreType.DMA(shape)

    outs = [
        ((total, hidden), BF16),
        ((total, features), BF16),
        ((total, features), BF16),
        ((total, hidden), BF16),
        ((total, width), BF16),
        ((total, features), BF16),
        ((total, features), BF16),
        ((total, width), BF16),
        ((total, width), BF16),
        ((total, width), BF16),
        ((heads, total, features), BF16),
        ((heads, total, features), BF16),
        ((tokens, features), F32),
        ((8, features), F32),
        ((1, 128), F32),
    ]
    tall = (2 * pairs, features // 2)
    fold_rows = heads * pairs + 8
    vectors = (
        segment_ids,
        labels,
        image_gain_one,
        image_bias_one,
        image_gain_two,
        image_bias_two,
        image_up_bias,
        text_gain_one,
        text_bias_one,
        text_gain_two,
        text_bias_two,
        text_up_bias,
    )
    operands = (
        text_tokens,
        image_tokens,
        jnp.transpose(image_qkv, (1, 2, 0)),
        image_out,
        image_up,
        image_down,
        jnp.transpose(text_qkv, (1, 2, 0)),
        text_out,
        text_up,
        text_down,
    ) + vectors
    factors = pl.pallas_call(
        functools.partial(step_kernel, (n_dp, n_mp, pairs, tokens, features, width)),
        out_shape=[vmem(shape, dtype) for shape, dtype in outs],
        in_specs=[anywhere] * len(operands),
        out_specs=[whole] * len(outs),
        scratch_shapes=[
            vmem(text_tokens.shape, BF16),
            vmem(image_tokens.shape, BF16),
            vmem(image_tokens.shape, BF16),
            vmem((3, width, features), BF16),
            vmem(image_out.shape, BF16),
            vmem(image_up.shape, BF16),
            vmem(image_down.shape, BF16),
            vmem((3, width, features), BF16),
            vmem(text_out.shape, BF16),
            vmem(text_up.shape, BF16),
            vmem(text_down.shape, BF16),
        ]
        + [vmem(array.shape, array.dtype) for array in vectors]
        + [
            vmem((n_dp, tokens, features), BF16),
            vmem((n_dp, 8, 128), jnp.int32),
            vmem((n_dp, 8, tokens), F32),
            vmem((n_mp, 16, 128), F32),
            vmem((n_dp, 24, 128), F32),
            vmem((5, n_mp) + tall, BF16),
            vmem((4, 2, half_dp) + tall, BF16),
            vmem((n_mp, fold_rows, features), BF16),
            vmem((n_mp, fold_rows, features), BF16),
            vmem((n_mp, pairs + 8, features), BF16),
            sems(22),
            sems(5),
            sems(1),
            sems(TOKEN_PARTS),
            sems(TOKEN_PARTS),
            sems(TOKEN_PARTS, 2),
            sems(1),
            sems(5),
            sems(5),
            sems(4),
            sems(4),
            sems(4),
            sems(4),
            sems(3),
            sems(3),
            sems(3),
            sems(1),
            sems(1),
            sems(3),
            sems(3),
        ],
        compiler_params=pltpu.CompilerParams(
            collective_id=0, has_side_effects=True, vmem_limit_bytes=48 * 2**20
        ),
        name="step",
    )(*[pltpu.with_memory_space_constraint(operand, pltpu.HBM) for operand in operands])
    vector = jax.ShapeDtypeStruct((features,), F32)
    results = pl.pallas_call(
        weights_kernel,
        out_shape=[
            jax.ShapeDtypeStruct((tokens, features), F32),
            jax.ShapeDtypeStruct((3, width, features), F32),
            jax.ShapeDtypeStruct((width, features), F32),
            jax.ShapeDtypeStruct((features, hidden), F32),
            jax.ShapeDtypeStruct((hidden, features), F32),
            jax.ShapeDtypeStruct((pairs,), F32),
            vector,
            vector,
            vector,
            vector,
            jax.ShapeDtypeStruct((hidden,), F32),
        ],
        in_specs=[whole] * len(outs),
        out_specs=[anywhere] * 5 + [whole] * 6,
        scratch_shapes=[
            vmem((3, width, features), F32),
            vmem((width, features), F32),
            vmem((features, hidden), F32),
            vmem((hidden, features), F32),
            sems(16),
        ],
        compiler_params=pltpu.CompilerParams(vmem_limit_bytes=32 * 2**20),
        name="weights",
    )(*[pltpu.with_memory_space_constraint(factor, pltpu.VMEM) for factor in factors])
    text_grad, qkv, out, up, down, loss, gain_one, bias_one, gain_two, bias_two, up_bias = results
    return (
        loss,
        text_grad,
        gain_one,
        bias_one,
        jnp.transpose(qkv, (2, 0, 1)),
        out,
        gain_two,
        bias_two,
        up,
        up_bias,
        down,
    )


def solution(mesh):
    placed = (
        P("dp", None),
        P("dp"),
        P("dp"),
        P("dp", None),
        P(),
        P(),
        P(None, None, "mp"),
        P("mp", None),
        P(),
        P(),
        P(None, "mp"),
        P("mp"),
        P("mp", None),
        P(),
        P(),
        P(None, None, "mp"),
        P("mp", None),
        P(),
        P(),
        P(None, "mp"),
        P("mp"),
        P("mp", None),
    )
    n_dp, n_mp = mesh.shape["dp"], mesh.shape["mp"]
    body = plain_device
    if n_dp <= 16 and n_dp % 4 == 0 and n_mp == 4:
        body = functools.partial(kernel_device, n_dp, n_mp)
    return jax.shard_map(
        body,
        mesh=mesh,
        in_specs=placed,
        out_specs=(
            P("dp"),
            P("dp", None),
            P(),
            P(),
            P(None, None, "mp"),
            P("mp", None),
            P(),
            P(),
            P(None, "mp"),
            P("mp"),
            P("mp", None),
        ),
        check_vma=False,
    )
```

```python
import functools

import jax
import jax.numpy as jnp
from jax import lax
from jax.experimental import pallas as pl
from jax.experimental.pallas import tpu as pltpu
from jax.sharding import PartitionSpec as P

HEAD = 64
IMG_LEN = 50
F32 = jnp.float32
BF16 = jnp.bfloat16


def dot(a, b):
    return lax.dot_general(a, b, (((1,), (0,)), ((), ())), preferred_element_type=F32)


def dot_nt(a, b):
    return lax.dot_general(a, b, (((1,), (1,)), ((), ())), preferred_element_type=F32)


def dot_tn(a, b):
    return lax.dot_general(a, b, (((0,), (0,)), ((), ())), preferred_element_type=F32)


def normalized(values):
    center = values - jnp.mean(values, axis=-1, keepdims=True)
    factor = lax.rsqrt(jnp.mean(center * center, axis=-1, keepdims=True) + 1e-05)
    return center * factor, factor


def norm_back(grad, hat, factor, gain):
    scaled = grad * gain
    along = jnp.mean(scaled * hat, axis=-1, keepdims=True)
    return factor * (scaled - jnp.mean(scaled, axis=-1, keepdims=True) - hat * along)


def unit(rows):
    return rows * lax.rsqrt(jnp.sum(rows * rows, axis=-1, keepdims=True) + 1e-06)


def gelu_parts(hidden):
    cdf = 0.5 * (1.0 + lax.erf(hidden * 0.7071067811865476))
    slope = cdf + hidden * jnp.exp(-0.5 * hidden * hidden) * 0.3989422804014327
    return hidden * cdf, slope


def head_blocks(rows, width):
    lanes = lax.broadcasted_iota(jnp.int32, (1, width), 1)
    return jnp.concatenate(
        [
            jnp.where((lanes >= h * HEAD) & (lanes < (h + 1) * HEAD), rows, 0.0)
            for h in range(width // HEAD)
        ],
        axis=0,
    )


def head_pick(blocks, width):
    heads = width // HEAD
    count = blocks.shape[0] // heads
    lanes = lax.broadcasted_iota(jnp.int32, (1, width), 1)
    total = jnp.zeros((count, width), F32)
    for h in range(heads):
        own = (lanes >= h * HEAD) & (lanes < (h + 1) * HEAD)
        total = total + jnp.where(own, blocks[h * count : (h + 1) * count], 0.0)
    return total


def attend(normed_rows, normed, allowed, weights):
    width = weights.shape[1]
    heads = width // HEAD
    queries = dot_nt(normed_rows, weights[0]).astype(BF16)
    folded = dot(head_blocks(queries.astype(F32), width).astype(BF16), weights[1]).astype(BF16)
    scores = dot_nt(folded, normed) * HEAD**-0.5
    scores = jnp.where(jnp.concatenate([allowed] * heads, axis=0), scores, -1e30)
    expo = jnp.exp(scores - jnp.max(scores, axis=-1, keepdims=True))
    probs = expo / jnp.sum(expo, axis=-1, keepdims=True)
    mixed = dot(probs.astype(BF16), normed).astype(BF16)
    context = head_pick(dot_nt(mixed, weights[2]), width).astype(BF16)
    return queries, folded, probs, mixed, context


def plain_device(
    text_tokens,
    segment_ids,
    labels,
    image_tokens,
    image_gain_one,
    image_bias_one,
    image_qkv,
    image_out,
    image_gain_two,
    image_bias_two,
    image_up,
    image_up_bias,
    image_down,
    text_gain_one,
    text_bias_one,
    text_qkv,
    text_out,
    text_gain_two,
    text_bias_two,
    text_up,
    text_up_bias,
    text_down,
):
    rank = lax.axis_index("dp")
    pairs = labels.shape[0]
    tokens = segment_ids.shape[0]
    width = text_out.shape[0]
    heads = width // HEAD
    features = text_tokens.shape[1]
    image_weights = jnp.transpose(image_qkv, (1, 2, 0))
    text_weights = jnp.transpose(text_qkv, (1, 2, 0))

    image_x = image_tokens.astype(F32)
    image_n = (normalized(image_x)[0] * image_gain_one + image_bias_one).astype(BF16)
    image_first = image_x.reshape(pairs, IMG_LEN, features)[:, 0]
    first_n = (normalized(image_first)[0] * image_gain_one + image_bias_one).astype(BF16)
    owner = lax.broadcasted_iota(jnp.int32, (pairs, pairs * IMG_LEN), 0)
    place = lax.broadcasted_iota(jnp.int32, (pairs, pairs * IMG_LEN), 1)
    inside = (place >= owner * IMG_LEN) & (place < (owner + 1) * IMG_LEN)
    image_context = attend(first_n, image_n, inside, image_weights)[4]

    text_x = text_tokens.astype(F32)
    hat_one, factor_one = normalized(text_x)
    normed = (hat_one * text_gain_one + text_bias_one).astype(BF16)
    captions = rank * pairs + jnp.arange(pairs)
    mine = segment_ids[None, :] == captions[:, None]
    spot = lax.broadcasted_iota(jnp.int32, (pairs, tokens), 1)
    last = jnp.max(jnp.where(mine, spot, -1), axis=1, keepdims=True)
    pick = (spot == last).astype(BF16)
    normed_last = dot(pick, normed).astype(BF16)
    queries, folded, probs, mixed, context = attend(normed_last, normed, mine, text_weights)

    attended = jnp.concatenate([dot(image_context, image_out), dot(context, text_out)], axis=0)
    attended = lax.psum(attended.astype(BF16), "mp").astype(F32)
    middle = jnp.concatenate([image_first, dot(pick, text_tokens)], axis=0) + attended
    hat_two, factor_two = normalized(middle)
    image_n2 = (hat_two[:pairs] * image_gain_two + image_bias_two).astype(BF16)
    normed_two = (hat_two[pairs:] * text_gain_two + text_bias_two).astype(BF16)
    image_active = gelu_parts(dot(image_n2, image_up) + image_up_bias)[0].astype(BF16)
    active, slope = gelu_parts(dot(normed_two, text_up) + text_up_bias)
    active = active.astype(BF16)
    branch = jnp.concatenate([dot(image_active, image_down), dot(active, text_down)], axis=0)
    final = middle + lax.psum(branch.astype(BF16), "mp").astype(F32)

    everyone = lax.all_gather(final.astype(BF16), "dp").astype(F32)
    total = everyone.shape[0] * pairs
    image_low = unit(everyone[:, :pairs].reshape(total, features)).astype(BF16)
    pooled = final[pairs:]
    text_low = unit(everyone[:, pairs:].reshape(total, features)).astype(BF16)
    logits = 64.0 * dot_nt(text_low, image_low)
    column_lse = jax.nn.logsumexp(logits, axis=0)
    own = lax.dynamic_slice_in_dim(logits, rank * pairs, pairs, axis=0)
    row_lse = jax.nn.logsumexp(own, axis=1)
    own_columns = lax.dynamic_slice_in_dim(column_lse, rank * pairs, pairs)
    onehot = (labels[:, None] == jnp.arange(total)[None, :]).astype(F32)
    pair_loss = 0.5 * (row_lse + own_columns) - jnp.sum(own * onehot, axis=1)
    grad_logits = (
        0.5 * (jnp.exp(own - row_lse[:, None]) + jnp.exp(own - column_lse[None, :])) - onehot
    )
    grad_embed = 64.0 * dot(grad_logits.astype(BF16), image_low)
    scale = lax.rsqrt(jnp.sum(pooled * pooled, axis=-1, keepdims=True) + 1e-06)
    text_unit = pooled * scale
    grad_final = scale * (
        grad_embed - text_unit * jnp.sum(text_unit * grad_embed, axis=-1, keepdims=True)
    )

    final_low = grad_final.astype(BF16)
    grad_hidden = (dot_nt(final_low, text_down) * slope).astype(BF16)
    grad_normed_two = lax.psum(dot_nt(grad_hidden, text_up).astype(BF16), "mp").astype(F32)
    hat_two = hat_two[pairs:]
    grad_middle = grad_final + norm_back(grad_normed_two, hat_two, factor_two[pairs:], text_gain_two)
    middle_low = grad_middle.astype(BF16)
    grad_context = dot_nt(middle_low, text_out).astype(BF16)
    grad_folded = dot(head_blocks(grad_context.astype(F32), width).astype(BF16), text_weights[2])
    grad_folded = grad_folded.astype(BF16)
    grad_probs = dot_nt(grad_folded, normed)
    grad_scores = probs * (grad_probs - jnp.sum(grad_probs * probs, axis=-1, keepdims=True))
    grad_scores = (grad_scores * HEAD**-0.5).astype(BF16)
    mixed_back = dot(grad_scores, normed).astype(BF16)
    grad_queries = head_pick(dot_nt(mixed_back, text_weights[1]), width).astype(BF16)
    grad_normed = dot_tn(grad_scores, folded) + dot_tn(probs.astype(BF16), grad_folded)
    grad_normed = grad_normed + dot_tn(pick, dot(grad_queries, text_weights[0]).astype(BF16))
    grad_normed = lax.psum(grad_normed.astype(BF16), "mp").astype(F32)
    text_grad = norm_back(grad_normed, hat_one, factor_one, text_gain_one)
    text_grad = text_grad + dot_tn(pick, middle_low)

    vectors = jnp.concatenate(
        [
            jnp.sum(grad_normed * hat_one, axis=0),
            jnp.sum(grad_normed, axis=0),
            jnp.sum(grad_normed_two * hat_two, axis=0),
            jnp.sum(grad_normed_two, axis=0),
            jnp.sum(grad_hidden.astype(F32), axis=0),
        ]
    )
    vectors = jnp.sum(lax.all_gather(vectors, "dp"), axis=0)
    cuts = [features, 2 * features, 3 * features, 4 * features]
    gain_one, bias_one, gain_two, bias_two, up_bias = jnp.split(vectors, cuts)

    def by_head(blocks):
        return [blocks[h * pairs : (h + 1) * pairs] for h in range(heads)]

    pieces = [active, final_low, normed_two, grad_hidden, context, middle_low, normed_last]
    pieces += [grad_queries, queries, grad_context] + by_head(mixed_back) + by_head(mixed)
    sent = lax.all_gather(jnp.concatenate(pieces, axis=1), "dp").reshape(total, -1)
    got = []
    at = 0
    for piece in pieces:
        got.append(sent[:, at : at + piece.shape[1]])
        at += piece.shape[1]
    active, final_low, normed_two, grad_hidden, context, middle_low, normed_last = got[:7]
    grad_queries, queries, grad_context = got[7:10]
    mixed_back = got[10 : 10 + heads]
    mixed = got[10 + heads :]

    def per_head(rows, blocks):
        return jnp.concatenate(
            [dot_tn(rows[:, h * HEAD : (h + 1) * HEAD], blocks[h]) for h in range(heads)], axis=0
        )

    grad_qkv = jnp.stack(
        [
            dot_tn(grad_queries, normed_last),
            per_head(queries, mixed_back),
            per_head(grad_context, mixed),
        ]
    )
    return (
        pair_loss,
        text_grad,
        gain_one,
        bias_one,
        jnp.transpose(grad_qkv, (2, 0, 1)),
        dot_tn(context, middle_low),
        gain_two,
        bias_two,
        dot_tn(normed_two, grad_hidden),
        up_bias,
        dot_tn(active, final_low),
    )


MESH = pl.DeviceIdType.MESH
TOKEN_PARTS = 2
SHIP_PARTS = 4
STEPS = {
    0: (("start", 0), ("start", 1)),
    3: (("second", 0), ("near", 0)),
    4: (("second", 1), ("near", 1)),
    9: (("third", 0), ("far", 0), ("pass", 0)),
    6: (("third", 1), ("far", 1), ("pass", 1)),
    8: (("last", 0), ("last", 1)),
}


def to_tall(rows):
    half = rows.shape[1] // 2
    return jnp.concatenate([rows[:, :half], rows[:, half:]], axis=0).astype(BF16)


def from_tall(tall):
    count = tall.shape[0] // 2
    wide = tall.astype(F32)
    return jnp.concatenate([wide[:count], wide[count:]], axis=1)


def column_of(row, count):
    shape = (count, row.shape[1])
    same = lax.broadcasted_iota(jnp.int32, shape, 0) == lax.broadcasted_iota(jnp.int32, shape, 1)
    return jnp.sum(jnp.where(same, row, 0), axis=1, keepdims=True)


def caption_masks(seg, first, count):
    captions = first + lax.broadcasted_iota(jnp.int32, (count, seg.shape[1]), 0)
    mine = seg == captions
    spot = lax.broadcasted_iota(jnp.int32, (count, seg.shape[1]), 1)
    last = jnp.max(jnp.where(mine, spot, -1), axis=1, keepdims=True)
    return mine, (spot == last).astype(F32).astype(BF16)


def softmax_rows(scores, allowed):
    scores = jnp.where(allowed, scores, -1e30)
    expo = jnp.exp(scores - jnp.max(scores, axis=-1, keepdims=True))
    return expo / jnp.sum(expo, axis=-1, keepdims=True)


def stats_pack(rows):
    pieces = []
    for row in rows:
        pieces += [row[:, at : at + 128] for at in range(0, row.shape[1], 128)]
    if len(pieces) % 8:
        pieces.append(jnp.zeros((-len(pieces) % 8, 128), F32))
    return jnp.concatenate(pieces, axis=0)


def stats_unpack(packed, count, features):
    per = features // 128
    return [
        jnp.concatenate([packed[at * per + i : at * per + i + 1] for i in range(per)], axis=1)
        for at in range(count)
    ]


def step_kernel(
    sizes,
    text_hbm,
    image_hbm,
    iw_hbm,
    io_hbm,
    iu_hbm,
    id_hbm,
    tw_hbm,
    to_hbm,
    tu_hbm,
    td_hbm,
    seg_hbm,
    lab_hbm,
    ig1_hbm,
    ib1_hbm,
    ig2_hbm,
    ib2_hbm,
    iub_hbm,
    tg1_hbm,
    tb1_hbm,
    tg2_hbm,
    tb2_hbm,
    tub_hbm,
    up_o,
    down_o,
    tw,
    to,
    mid_o,
    nsel_o,
    xk_o,
    xv_o,
    tg_o,
    vec_o,
    loss_o,
    xt,
    xi,
    iw,
    io,
    iu,
    idn,
    tu,
    td,
    seg_ref,
    lab_ref,
    ig1_ref,
    ib1_ref,
    ig2_ref,
    ib2_ref,
    iub_ref,
    tg1_ref,
    tb1_ref,
    tg2_ref,
    tb2_ref,
    tub_ref,
    tok,
    ids,
    prow,
    stm,
    std,
    ar,
    gat,
    fq,
    fg,
    fd,
    load_sem,
    img_sem,
    t_s,
    tz_r,
    ty_r,
    tx_r,
    tl_r,
    ar_s,
    ar_r,
    g_s,
    g_r,
    g_f,
    g_c,
    f_s,
    f_x,
    f_c,
    st_s,
    st_r,
    sm_s,
    sm_r,
):
    n_dp, n_mp, pairs, tokens, features, width = sizes
    heads = width // HEAD
    half_dp = n_dp // 2
    total = n_dp * pairs
    scale = HEAD**-0.5
    d = lax.axis_index("dp")
    m = lax.axis_index("mp")
    core = lax.rem(m, 2)
    side = lax.div(m, 2)
    hi = lax.div(d, 2)
    lo = lax.rem(d, 2)
    partner = (d, m + 1 - 2 * core)
    across = (d, lax.rem(m + 2, 4))
    beside = (hi * 2 + 1 - lo, m)

    chunk = img_sem.shape[0]
    chunk_rows = xi.shape[0] // chunk

    def image_load(k):
        rows = pl.ds(k * chunk_rows, chunk_rows)
        return pltpu.make_async_copy(image_hbm.at[rows], xi.at[rows], img_sem.at[k])

    loads = {}

    def load(name, src, dst):
        loads[name] = pltpu.make_async_copy(src, dst, load_sem.at[len(loads)])
        loads[name].start()

    for k in range(chunk):
        image_load(k).start()
    load("ig1", ig1_hbm, ig1_ref)
    load("ib1", ib1_hbm, ib1_ref)
    load("iw", iw_hbm, iw)
    load("io", io_hbm, io)

    def vector(name, ref):
        loads[name].wait()
        return ref[...].reshape(1, ref.shape[0])

    barrier = pltpu.get_barrier_semaphore()
    for i in range(1, n_mp):
        pl.semaphore_signal(
            barrier, inc=1, device_id=(d, lax.rem(m + i, n_mp)), device_id_type=MESH
        )

    @pl.loop(1, n_dp)
    def _(i):
        pl.semaphore_signal(
            barrier, inc=1, device_id=(lax.rem(d + i, n_dp), m), device_id_type=MESH
        )

    load("text", text_hbm, xt)
    load("tg1", tg1_hbm, tg1_ref)
    load("tb1", tb1_hbm, tb1_ref)
    load("seg", seg_hbm, seg_ref)
    load("lab", lab_hbm, lab_ref)
    load("tw", tw_hbm, tw)
    load("to", to_hbm, to)
    load("ig2", ig2_hbm, ig2_ref)
    load("ib2", ib2_hbm, ib2_ref)
    load("iub", iub_hbm, iub_ref)
    load("iu", iu_hbm, iu)
    load("id", id_hbm, idn)
    load("tg2", tg2_hbm, tg2_ref)
    load("tb2", tb2_hbm, tb2_ref)
    load("tub", tub_hbm, tub_ref)
    load("tu", tu_hbm, tu)
    load("td", td_hbm, td)

    def remote(src, dst, send, recv, device):
        return pltpu.make_async_remote_copy(
            src_ref=src,
            dst_ref=dst,
            send_sem=send,
            recv_sem=recv,
            device_id=device,
            device_id_type=MESH,
        )

    def mp_send(buf, send, recv):
        for i in range(1, n_mp):
            remote(buf.at[m], buf.at[m], send, recv, (d, lax.rem(m + i, n_mp))).start()

    def mp_recv(buf, send, recv):
        slots = buf.at[pl.ds(0, n_mp - 1)]
        remote(slots, slots, send, recv, partner).wait_recv()

    def mp_drain(buf, send, recv):
        slots = buf.at[pl.ds(0, n_mp - 1)]
        remote(slots, slots, send, recv, partner).wait_send()

    def far_send(buf, at):
        slot = buf.at[m]
        remote(slot, slot, f_s.at[at], f_x.at[at], across).start()
        remote(slot, slot, f_s.at[at], f_c.at[at], partner).start()

    def far_pass(buf, at):
        slot = buf.at[lax.rem(m + 2, 4)]
        remote(slot, slot, f_s.at[at], f_x.at[at], partner).wait_recv()
        remote(slot, slot, f_s.at[at], f_c.at[at], partner).start()

    def far_recv(buf, at):
        slots = buf.at[pl.ds(0, 2)]
        remote(slots, slots, f_s.at[at], f_c.at[at], partner).wait_recv()

    def far_drain(buf, at):
        slots = buf.at[pl.ds(0, 3)]
        remote(slots, slots, f_s.at[at], f_c.at[at], partner).wait_send()

    def on_core(which):
        return pl.when(core == which)

    def dp_send(at):
        slot = gat.at[at, lo, hi]
        other = lo + core * (1 - 2 * lo)

        def send(k):
            to_dev = (lax.rem(hi + k, half_dp) * 2 + other, m)
            remote(slot, slot, g_s.at[at], g_r.at[at], to_dev).start()

        for k in range(1, half_dp):
            send(k)
        on_core(1)(lambda: send(0))

    def dp_forward(at):
        @on_core(1)
        def _():
            slots = gat.at[at, 1 - lo]
            remote(slots, slots, g_f.at[at], g_r.at[at], partner).wait_recv()
            remote(slots, slots, g_f.at[at], g_c.at[at], partner).start()

        @on_core(0)
        def _():
            slots = gat.at[at, 0, pl.ds(0, half_dp - 1)]
            remote(slots, slots, g_f.at[at], g_r.at[at], partner).wait_recv()
            for k in range(1, half_dp):
                slot = gat.at[at, lo, lax.rem(hi + k, half_dp)]
                remote(slot, slot, g_f.at[at], g_c.at[at], partner).start()

    def dp_wait(at, first, wait):
        for which in (0, 1):

            @on_core(which)
            def _(which=which):
                slots = gat.at[at, 0, pl.ds(0, half_dp - (1 if which == first else 0))]
                wait(slots)

    def dp_recv(at):
        dp_wait(
            at,
            1,
            lambda slots: remote(slots, slots, g_f.at[at], g_c.at[at], partner).wait_recv(),
        )

    def dp_drain(at):
        def wait(slots):
            remote(slots, slots, g_s.at[at], g_c.at[at], partner).wait_send()
            remote(slots, slots, g_f.at[at], g_c.at[at], partner).wait_send()

        dp_wait(at, 0, wait)

    def gathered(at):
        talls = [gat[at, i % 2, i // 2].astype(F32) for i in range(n_dp)]
        left = jnp.concatenate([t[:pairs] for t in talls], axis=0)
        right = jnp.concatenate([t[pairs:] for t in talls], axis=0)
        return jnp.concatenate([left, right], axis=1)

    def small_send(at, buf):
        @pl.loop(1, n_dp)
        def _(i):
            to_dev = (lax.rem(d + i, n_dp), m)
            remote(buf.at[d], buf.at[d], sm_s.at[at], sm_r.at[at], to_dev).start()

    def small_recv(at, buf):
        slots = buf.at[pl.ds(0, n_dp - 1)]
        remote(slots, slots, sm_s.at[at], sm_r.at[at], partner).wait_recv()

    def small_drain(at, buf):
        slots = buf.at[pl.ds(0, n_dp - 1)]
        remote(slots, slots, sm_s.at[at], sm_r.at[at], partner).wait_send()

    part_rows = tokens // (2 * TOKEN_PARTS)

    def split_hi(mine, body):
        for k in range(half_dp // 2 - 1):
            body(2 * k + (2 - core if mine else 1 + core))

        @pl.when(core == (1 if mine else 0))
        def _():
            body(half_dp - 1)

    def near_slot(i):
        return lax.rem(hi + half_dp - i, half_dp) * 2 + lo

    def far_slot(i):
        return lax.rem(hi + half_dp - i, half_dp) * 2 + 1 - lo

    def split_far(mine, body):
        split_hi(mine, lambda i: body(half_dp + i, far_slot(i)))

        @pl.when(core == (0 if mine else 1))
        def _():
            body(half_dp, far_slot(0))

    def split_near(mine, body):
        split_hi(mine, lambda i: body(i, near_slot(i)))

    def rows_of(slot, part, which):
        start = (which * TOKEN_PARTS + part) * part_rows
        return tok.at[slot, pl.ds(pl.multiple_of(start, 16), part_rows)]

    def tok_push(rows, recv, device):
        remote(rows, rows, t_s.at[0], recv, device).start()

    def tok_wait(recv, counts):
        for which in (0, 1):
            if counts[which]:

                @on_core(which)
                def _(which=which):
                    rows = tok.at[0, pl.ds(0, counts[which] * part_rows)]
                    remote(rows, rows, t_s.at[0], recv, partner).wait_recv()

    quarter = half_dp // 2
    near_counts = (quarter - 1, quarter)
    far_counts = (quarter, quarter)

    def tok_start(part):
        rows = rows_of(d, part, side)

        def body(i):
            tok_push(rows, tz_r.at[part], (lax.rem(hi + i, half_dp) * 2 + lo, m))

        split_hi(True, body)
        on_core(0)(lambda: tok_push(rows, ty_r.at[part], beside))

    def tok_second(part):
        tok_wait(tz_r.at[part], near_counts)

        def body(i, slot):
            rows = rows_of(slot, part, side)
            tok_push(rows, ty_r.at[part], beside)
            tok_push(rows, tl_r.at[0], partner)

        split_near(True, body)

    def tok_third(part):
        tok_wait(ty_r.at[part], far_counts)
        split_far(True, lambda at, slot: tok_push(rows_of(slot, part, side), tl_r.at[0], partner))

    def tok_near(part):
        split_near(
            True, lambda at, slot: tok_push(rows_of(slot, part, side), tx_r.at[part, 0], across)
        )

    def tok_far(part):
        split_far(
            True, lambda at, slot: tok_push(rows_of(slot, part, side), tx_r.at[part, 1], across)
        )

    def tok_pass_near(part):
        tok_wait(tx_r.at[part, 0], near_counts)
        split_near(
            True, lambda at, slot: tok_push(rows_of(slot, part, 1 - side), tl_r.at[0], partner)
        )

    def tok_pass_far(part):
        tok_wait(tx_r.at[part, 1], far_counts)
        split_far(
            True, lambda at, slot: tok_push(rows_of(slot, part, 1 - side), tl_r.at[0], partner)
        )

    def tok_last():
        for which, count in ((0, 2 * quarter), (1, 2 * quarter - 1)):

            @on_core(which)
            def _(count=count):
                slots = tok.at[pl.ds(0, count)]
                remote(slots, slots, t_s.at[0], tl_r.at[0], partner).wait_recv()

    def tok_drain():
        for which, count in ((0, n_dp - 2), (1, n_dp)):

            @on_core(which)
            def _(count=count):
                slots = tok.at[pl.ds(0, count)]
                remote(slots, slots, t_s.at[0], tl_r.at[0], partner).wait_send()

    def token_steps(at):
        steps = {
            "start": tok_start,
            "second": tok_second,
            "third": tok_third,
            "near": tok_near,
            "far": tok_far,
            "pass": tok_pass_near,
            "last": tok_pass_far,
        }
        for name, part in STEPS.get(at, ()):
            steps[name](part)

    def attend_rows(queries, normed, allowed, weights):
        stacked = head_blocks(queries.astype(F32), width).astype(BF16)
        folded = dot(stacked, weights[1]).astype(BF16)
        scores = dot_nt(folded, normed) * scale
        probs = softmax_rows(scores, allowed)
        mixed = dot(probs.astype(BF16), normed).astype(BF16)
        context = head_pick(dot_nt(mixed, weights[2]), width).astype(BF16)
        return folded, probs, context

    for k in range(chunk):
        image_load(k).wait()
    gain, shift = vector("ig1", ig1_ref), vector("ib1", ib1_ref)
    firsts = [i * IMG_LEN for i in range(pairs)]
    image_first = jnp.concatenate([xi[r : r + 1, :].astype(F32) for r in firsts], axis=0)
    first_n = (normalized(image_first)[0] * gain + shift).astype(BF16)
    loads["iw"].wait()
    image_q = dot_nt(first_n, iw[0])
    image_fold = dot(head_blocks(image_q, width).astype(BF16), iw[1])
    group = pairs // chunk
    shape = (group, chunk_rows)
    place = lax.broadcasted_iota(jnp.int32, shape, 1)
    begin = lax.broadcasted_iota(jnp.int32, shape, 0) * IMG_LEN
    inside = jnp.concatenate([(place >= begin) & (place < begin + IMG_LEN)] * heads, axis=0)
    image_mixed = []
    for k in range(chunk):
        hat = normalized(xi[k * chunk_rows : (k + 1) * chunk_rows, :].astype(F32))[0]
        low = (hat * gain + shift).astype(BF16)
        spots = [h * pairs + k * group for h in range(heads)]
        asked = jnp.concatenate([image_fold[at : at + group] for at in spots], axis=0)
        scores = dot_nt(asked.astype(BF16), low) * scale
        image_mixed.append(dot(softmax_rows(scores, inside).astype(BF16), low))
    image_mixed = jnp.concatenate(
        [mixed[h * group : (h + 1) * group] for h in range(heads) for mixed in image_mixed], axis=0
    )
    image_context = head_pick(dot_nt(image_mixed.astype(BF16), iw[2]), width).astype(BF16)
    loads["io"].wait()
    ar[0, m] = to_tall(dot(image_context, io[...]))

    pl.semaphore_wait(barrier, n_mp - 1 + n_dp - 1)
    mp_send(ar.at[0], ar_s.at[0], ar_r.at[0])

    loads["text"].wait()
    gain_one = vector("tg1", tg1_ref)
    hat_one, factor_one = normalized(xt[...].astype(F32))
    tok[d] = (hat_one * gain_one + vector("tb1", tb1_ref)).astype(BF16)
    token_steps(0)
    seg = vector("seg", seg_ref)
    seg_rows = tokens // 128
    for i in range(seg_rows):
        ids[d, i : i + 1, :] = seg[:, i * 128 : (i + 1) * 128]
    ids[d, seg_rows : seg_rows + 1, 0:pairs] = vector("lab", lab_ref)
    small_send(0, ids)

    normed = tok[d]
    mine, pick = caption_masks(seg, d * pairs, pairs)
    allowed = jnp.concatenate([mine] * heads, axis=0)
    loads["tw"].wait()
    queries = dot_nt(dot(pick, normed).astype(BF16), tw[0]).astype(BF16)
    folded, probs, context = attend_rows(queries, normed, allowed, tw)
    loads["to"].wait()
    ar[1, m] = to_tall(dot(context, to[...]))
    mp_send(ar.at[1], ar_s.at[1], ar_r.at[1])
    text_last = dot(pick, xt[...])

    def head_rows(blocks):
        rows = [
            jnp.sum(blocks[h * pairs : (h + 1) * pairs], axis=0, keepdims=True)
            for h in range(heads)
        ]
        return jnp.concatenate(rows + [jnp.zeros((8 - heads, tokens), F32)], axis=0)

    def padded(rows, foot):
        foot = jnp.concatenate([foot, jnp.zeros((8, features - tokens), F32)], axis=1)
        return jnp.concatenate([rows, foot], axis=0).astype(BF16)

    no_foot = jnp.zeros((8, tokens), F32)
    prob_rows = head_rows(probs)
    fq[m] = padded(folded.astype(F32), prob_rows)
    token_steps(1)

    def summed(at):
        mp_recv(ar.at[at], ar_s.at[at], ar_r.at[at])
        full = ar[at, 0].astype(F32)
        for i in range(1, n_mp):
            full = full + ar[at, i].astype(F32)
        count = full.shape[0] // 2
        return jnp.concatenate([full[:count], full[count:]], axis=1)

    image_middle = image_first + summed(0)
    gain, shift = vector("ig2", ig2_ref), vector("ib2", ib2_ref)
    image_n2 = (normalized(image_middle)[0] * gain + shift).astype(BF16)
    loads["iu"].wait()
    image_hidden = dot(image_n2, iu[...]) + vector("iub", iub_ref)
    image_active = gelu_parts(image_hidden)[0].astype(BF16)
    loads["id"].wait()
    ar[2, m] = to_tall(dot(image_active, idn[...]))
    mp_send(ar.at[2], ar_s.at[2], ar_r.at[2])
    token_steps(2)

    middle = text_last + summed(1)
    gat[0, lo, hi] = to_tall(middle)
    gain_two, shift_two = vector("tg2", tg2_ref), vector("tb2", tb2_ref)
    hat_two, factor_two = normalized(middle)
    normed_two = (hat_two * gain_two + shift_two).astype(BF16)
    loads["tu"].wait()
    up_shift = vector("tub", tub_ref)
    active, slope = gelu_parts(dot(normed_two, tu[...]) + up_shift)
    loads["td"].wait()
    ar[3, m] = to_tall(dot(active.astype(BF16), td[...]))
    mp_send(ar.at[3], ar_s.at[3], ar_r.at[3])
    token_steps(3)

    gat[1, lo, hi] = to_tall(unit(image_middle + summed(2)))
    dp_send(1)
    gat[2, lo, hi] = to_tall(middle + summed(3))
    dp_send(2)
    far_send(fq, 0)

    token_steps(4)
    dp_forward(1)
    token_steps(9)
    dp_forward(2)
    dp_send(0)
    far_pass(fq, 0)
    token_steps(5)
    dp_recv(1)
    dp_recv(2)

    image_low = gathered(1).astype(BF16)

    def embedded(rows):
        shrink = lax.rsqrt(jnp.sum(rows * rows, axis=-1, keepdims=True) + 1e-06)
        text_unit = rows * shrink
        return shrink, text_unit, 64.0 * dot_nt(text_unit.astype(BF16), image_low)

    def final_grad(shrink, text_unit, logits, labels):
        lanes = lax.broadcasted_iota(jnp.int32, logits.shape, 1)
        onehot = (labels == lanes).astype(F32)
        top = jnp.max(logits, axis=1, keepdims=True)
        lse = top + jnp.log(jnp.sum(jnp.exp(logits - top), axis=1, keepdims=True))
        grads = 0.5 * (jnp.exp(logits - lse) + jnp.exp(logits - col_lse)) - onehot
        grads = 64.0 * dot(grads.astype(BF16), image_low)
        along = jnp.sum(text_unit * grads, axis=-1, keepdims=True)
        positive = jnp.sum(logits * onehot, axis=1, keepdims=True)
        return shrink * (grads - text_unit * along), lse, positive

    shrink_all, unit_all, logits = embedded(gathered(2))
    col_top = jnp.max(logits, axis=0, keepdims=True)
    col_lse = col_top + jnp.log(jnp.sum(jnp.exp(logits - col_top), axis=0, keepdims=True))
    own_labels = column_of(ids[d, seg_rows : seg_rows + 1, :], pairs)
    grad_final, own_lse, positive = final_grad(*embedded(from_tall(gat[2, lo, hi])), own_labels)
    grad_hidden = (dot_nt(grad_final.astype(BF16), td[...]) * slope).astype(BF16)
    ar[4, m] = to_tall(dot_nt(grad_hidden, tu[...]))
    mp_send(ar.at[4], ar_s.at[4], ar_r.at[4])

    token_steps(6)
    lanes = lax.broadcasted_iota(jnp.int32, (pairs, total), 1)
    mine_first = lax.broadcasted_iota(jnp.int32, (pairs, total), 0) + d * pairs
    own_col = jnp.sum(jnp.where(lanes == mine_first, col_lse, 0.0), axis=1, keepdims=True)
    pair_loss = 0.5 * (own_lse + own_col) - positive
    shape = (pairs, loss_o.shape[1])
    diagonal = lax.broadcasted_iota(jnp.int32, shape, 0) == lax.broadcasted_iota(
        jnp.int32, shape, 1
    )
    loss_o[...] = jnp.sum(jnp.where(diagonal, pair_loss, 0.0), axis=0, keepdims=True)
    small_recv(0, ids)
    labels = jnp.concatenate(
        [column_of(ids[i, seg_rows : seg_rows + 1, :], pairs) for i in range(n_dp)], axis=0
    )
    fin_all = final_grad(shrink_all, unit_all, logits, labels)[0].astype(BF16)
    dp_forward(0)

    grad_n2 = summed(4)
    grad_middle = grad_final + norm_back(grad_n2, hat_two, factor_two, gain_two)
    gat[3, lo, hi] = to_tall(grad_middle)
    dp_send(3)
    middle_low = grad_middle.astype(BF16)
    grad_context = dot_nt(middle_low, to[...]).astype(BF16)
    grad_folded = dot(head_blocks(grad_context.astype(F32), width).astype(BF16), tw[2])
    fg[m] = padded(grad_folded, no_foot)
    grad_probs = dot_nt(grad_folded.astype(BF16), normed)
    grad_scores = probs * (grad_probs - jnp.sum(grad_probs * probs, axis=-1, keepdims=True))
    scaled = grad_scores * scale
    score_rows = head_rows(scaled)
    prow[d] = jnp.concatenate([prob_rows[:heads], score_rows[: 8 - heads]], axis=0)
    mixed_back = dot(scaled.astype(BF16), normed).astype(BF16)
    grad_queries = head_pick(dot_nt(mixed_back, tw[1]), width).astype(BF16)
    fd[m] = padded(dot(grad_queries, tw[0]), score_rows)

    def spread(slots, ref, at):
        parts = []
        for i in slots:
            foot = ref[i, at : at + 8, 0:tokens].astype(F32)
            for h in range(heads):
                parts.append(jnp.where(mine, foot[h : h + 1], 0.0))
            parts.append(jnp.zeros((8, tokens), F32))
        return jnp.concatenate(parts, axis=0).astype(BF16)

    def first_norm_grad(slots, sources):
        folds, backs, rests = sources
        place_low = jnp.concatenate(
            [jnp.concatenate([pick.astype(F32), jnp.zeros((8, tokens), F32)], axis=0)] * len(slots),
            axis=0,
        ).astype(BF16)
        grads = dot_tn(spread(slots, fd, pairs), folds)
        grads = grads + dot_tn(spread(slots, fq, pairs * heads), backs)
        return grads + dot_tn(place_low, rests)

    part = first_norm_grad([m], (fq[m], fg[m], fd[m]))
    stm[m] = stats_pack(
        [jnp.sum(part * hat_one, axis=0, keepdims=True), jnp.sum(part, axis=0, keepdims=True)]
    )
    mp_send(stm, st_s.at[0], st_r.at[0])
    far_send(fg, 1)
    far_send(fd, 2)
    small_send(1, prow)
    stats_two = [
        jnp.sum(grad_n2 * hat_two, axis=0, keepdims=True),
        jnp.sum(grad_n2, axis=0, keepdims=True),
    ]

    token_steps(7)
    dp_recv(0)
    n2_all = (normalized(gathered(0))[0] * gain_two + shift_two).astype(BF16)
    act_all, slope_all = gelu_parts(dot(n2_all, tu[...]) + up_shift)
    gh_all = (dot_nt(fin_all, td[...]) * slope_all).astype(BF16)
    up_bias = jnp.sum(gh_all.astype(F32), axis=0, keepdims=True)
    mp_recv(stm, st_s.at[0], st_r.at[0])
    one = stm[0]
    for i in range(1, n_mp):
        one = one + stm[i]
    std[d] = stats_pack(stats_unpack(one, 2, features) + stats_two)
    small_send(2, std)
    dp_forward(3)
    far_pass(fg, 1)
    far_pass(fd, 2)
    token_steps(8)
    up_o[...] = dot_tn(n2_all, gh_all)
    down_o[...] = dot_tn(act_all.astype(BF16), fin_all)

    for at, buf in ((0, fq), (1, fg), (2, fd)):
        far_recv(buf, at)
    flat = [ref[...].reshape(n_mp * ref.shape[1], features) for ref in (fq, fg, fd)]
    grad_normed = first_norm_grad(list(range(n_mp)), flat)
    text_grad = norm_back(grad_normed, hat_one, factor_one, gain_one)
    tg_o[...] = text_grad + dot_tn(pick, middle_low)

    small_recv(1, prow)
    tok_last()
    twice = 2 * pairs
    for j in range(half_dp):
        seg = jnp.concatenate(
            [ids[i, k : k + 1, :] for i in (2 * j, 2 * j + 1) for k in range(seg_rows)], axis=1
        )
        here, picks = caption_masks(seg, j * twice, twice)
        values = jnp.concatenate([prow[2 * j], prow[2 * j + 1]], axis=1)
        parts = [jnp.where(here, values[h : h + 1], 0.0) for h in range(heads)]
        parts += [jnp.where(here, values[heads + h : heads + h + 1], 0.0) for h in range(heads)]
        parts = [part.astype(BF16) for part in parts] + [picks]
        low = tok[2 * j : 2 * j + 2].reshape(2 * tokens, features)
        mixed = dot(jnp.concatenate(parts, axis=0), low).astype(BF16)
        rows = slice(j * twice, (j + 1) * twice)
        for h in range(heads):
            xv_o[h, rows, :] = mixed[h * twice : (h + 1) * twice]
            xk_o[h, rows, :] = mixed[(heads + h) * twice : (heads + h + 1) * twice]
        nsel_o[rows, :] = mixed[2 * heads * twice :]
    dp_recv(3)
    mid_o[...] = gathered(3).astype(BF16)

    small_recv(2, std)
    stats = std[0]
    for i in range(1, n_dp):
        stats = stats + std[i]
    rows = stats_unpack(stats, 4, features)
    vec_o[...] = jnp.concatenate(rows + [up_bias, jnp.zeros((3, features), F32)], axis=0)

    for at in range(ar.shape[0]):
        mp_drain(ar.at[at], ar_s.at[at], ar_r.at[at])
    mp_drain(stm, st_s.at[0], st_r.at[0])
    for at, buf in enumerate((fq, fg, fd)):
        far_drain(buf, at)
    for at in range(gat.shape[0]):
        dp_drain(at)
    for at, buf in enumerate((ids, prow, std)):
        small_drain(at, buf)
    tok_drain()


def weights_kernel(
    up,
    down,
    tw,
    to,
    mid,
    nsel,
    xk,
    xv,
    tg,
    vec,
    loss,
    tg_out,
    qkv_out,
    out_out,
    up_out,
    down_out,
    loss_out,
    g1_out,
    b1_out,
    g2_out,
    b2_out,
    ub_out,
    qkv_buf,
    out_buf,
    sem,
):
    heads, total, features = xk.shape
    width = to.shape[0]
    started = []

    def ship(src, dst):
        copy = pltpu.make_async_copy(src, dst, sem.at[len(started)])
        copy.start()
        started.append(copy)

    for src, dst in ((up, up_out), (down, down_out)):
        step = src.shape[0] // SHIP_PARTS
        for at in range(0, src.shape[0], step):
            rows = pl.ds(at, step)
            ship(src.at[rows], dst.at[rows])
    ship(tg, tg_out)
    flat_k = xk[...].reshape(heads * total, features)
    flat_v = xv[...].reshape(heads * total, features)
    queries = dot_nt(nsel[...], tw[0])
    grad_context = dot_nt(mid[...], to[...])
    for at, rows, flat in ((1, queries, flat_k), (2, grad_context, flat_v)):
        stacked = head_blocks(rows.astype(BF16).astype(F32), width).astype(BF16)
        qkv_buf[at] = dot_tn(stacked, flat)
        ship(qkv_buf.at[at], qkv_out.at[at])
    grad_queries = head_pick(dot_nt(flat_k, tw[1]), width).astype(BF16)
    qkv_buf[0] = dot_tn(grad_queries, nsel[...])
    ship(qkv_buf.at[0], qkv_out.at[0])
    context = head_pick(dot_nt(flat_v, tw[2]), width).astype(BF16)
    out_buf[...] = dot_tn(context, mid[...])
    ship(out_buf, out_out)
    for at, dst in enumerate((g1_out, b1_out, g2_out, b2_out, ub_out)):
        dst[...] = vec[at, :]
    loss_out[...] = loss[0, 0 : loss_out.shape[0]]
    for copy in started:
        copy.wait()


def kernel_device(
    n_dp,
    n_mp,
    text_tokens,
    segment_ids,
    labels,
    image_tokens,
    image_gain_one,
    image_bias_one,
    image_qkv,
    image_out,
    image_gain_two,
    image_bias_two,
    image_up,
    image_up_bias,
    image_down,
    text_gain_one,
    text_bias_one,
    text_qkv,
    text_out,
    text_gain_two,
    text_bias_two,
    text_up,
    text_up_bias,
    text_down,
):
    pairs = labels.shape[0]
    tokens, features = text_tokens.shape
    width = text_out.shape[0]
    hidden = text_up.shape[1]
    heads = width // HEAD
    total = n_dp * pairs
    half_dp = n_dp // 2
    vmem = pltpu.VMEM
    whole = pl.BlockSpec(memory_space=pltpu.VMEM)
    anywhere = pl.BlockSpec(memory_space=pl.ANY)

    def sems(*shape):
        return pltpu.SemaphoreType.DMA(shape)

    outs = [
        ((features, hidden), F32),
        ((hidden, features), F32),
        ((3, width, features), BF16),
        ((width, features), BF16),
        ((total, features), BF16),
        ((total, features), BF16),
        ((heads, total, features), BF16),
        ((heads, total, features), BF16),
        ((tokens, features), F32),
        ((8, features), F32),
        ((1, 128), F32),
    ]
    tall = (2 * pairs, features // 2)
    fold_rows = heads * pairs + 8
    vectors = (
        segment_ids,
        labels,
        image_gain_one,
        image_bias_one,
        image_gain_two,
        image_bias_two,
        image_up_bias,
        text_gain_one,
        text_bias_one,
        text_gain_two,
        text_bias_two,
        text_up_bias,
    )
    operands = (
        text_tokens,
        image_tokens,
        jnp.transpose(image_qkv, (1, 2, 0)),
        image_out,
        image_up,
        image_down,
        jnp.transpose(text_qkv, (1, 2, 0)),
        text_out,
        text_up,
        text_down,
    ) + vectors
    factors = pl.pallas_call(
        functools.partial(step_kernel, (n_dp, n_mp, pairs, tokens, features, width)),
        out_shape=[vmem(shape, dtype) for shape, dtype in outs],
        in_specs=[anywhere] * len(operands),
        out_specs=[whole] * len(outs),
        scratch_shapes=[
            vmem(text_tokens.shape, BF16),
            vmem(image_tokens.shape, BF16),
            vmem((3, width, features), BF16),
            vmem(image_out.shape, BF16),
            vmem(image_up.shape, BF16),
            vmem(image_down.shape, BF16),
            vmem(text_up.shape, BF16),
            vmem(text_down.shape, BF16),
        ]
        + [vmem(array.shape, array.dtype) for array in vectors]
        + [
            vmem((n_dp, tokens, features), BF16),
            vmem((n_dp, 8, 128), jnp.int32),
            vmem((n_dp, 8, tokens), F32),
            vmem((n_mp, 16, 128), F32),
            vmem((n_dp, 24, 128), F32),
            vmem((5, n_mp) + tall, BF16),
            vmem((4, 2, half_dp) + tall, BF16),
            vmem((n_mp, fold_rows, features), BF16),
            vmem((n_mp, fold_rows, features), BF16),
            vmem((n_mp, pairs + 8, features), BF16),
            sems(22),
            sems(pairs // 8),
            sems(1),
            sems(TOKEN_PARTS),
            sems(TOKEN_PARTS),
            sems(TOKEN_PARTS, 2),
            sems(1),
            sems(5),
            sems(5),
            sems(4),
            sems(4),
            sems(4),
            sems(4),
            sems(3),
            sems(3),
            sems(3),
            sems(1),
            sems(1),
            sems(3),
            sems(3),
        ],
        compiler_params=pltpu.CompilerParams(
            collective_id=0, has_side_effects=True, vmem_limit_bytes=48 * 2**20
        ),
        name="step",
    )(*[pltpu.with_memory_space_constraint(operand, pltpu.HBM) for operand in operands])
    vector = jax.ShapeDtypeStruct((features,), F32)
    results = pl.pallas_call(
        weights_kernel,
        out_shape=[
            jax.ShapeDtypeStruct((tokens, features), F32),
            jax.ShapeDtypeStruct((3, width, features), F32),
            jax.ShapeDtypeStruct((width, features), F32),
            jax.ShapeDtypeStruct((features, hidden), F32),
            jax.ShapeDtypeStruct((hidden, features), F32),
            jax.ShapeDtypeStruct((pairs,), F32),
            vector,
            vector,
            vector,
            vector,
            jax.ShapeDtypeStruct((hidden,), F32),
        ],
        in_specs=[whole] * len(outs),
        out_specs=[anywhere] * 5 + [whole] * 6,
        scratch_shapes=[
            vmem((3, width, features), F32),
            vmem((width, features), F32),
            sems(2 * SHIP_PARTS + 5),
        ],
        compiler_params=pltpu.CompilerParams(vmem_limit_bytes=32 * 2**20),
        name="weights",
    )(*[pltpu.with_memory_space_constraint(factor, pltpu.VMEM) for factor in factors])
    text_grad, qkv, out, up, down, loss, gain_one, bias_one, gain_two, bias_two, up_bias = results
    return (
        loss,
        text_grad,
        gain_one,
        bias_one,
        jnp.transpose(qkv, (2, 0, 1)),
        out,
        gain_two,
        bias_two,
        up,
        up_bias,
        down,
    )


def solution(mesh):
    placed = (
        P("dp", None),
        P("dp"),
        P("dp"),
        P("dp", None),
        P(),
        P(),
        P(None, None, "mp"),
        P("mp", None),
        P(),
        P(),
        P(None, "mp"),
        P("mp"),
        P("mp", None),
        P(),
        P(),
        P(None, None, "mp"),
        P("mp", None),
        P(),
        P(),
        P(None, "mp"),
        P("mp"),
        P("mp", None),
    )
    n_dp, n_mp = mesh.shape["dp"], mesh.shape["mp"]
    body = plain_device
    if n_dp <= 16 and n_dp % 4 == 0 and n_mp == 4:
        body = functools.partial(kernel_device, n_dp, n_mp)
    return jax.shard_map(
        body,
        mesh=mesh,
        in_specs=placed,
        out_specs=(
            P("dp"),
            P("dp", None),
            P(),
            P(),
            P(None, None, "mp"),
            P("mp", None),
            P(),
            P(),
            P(None, "mp"),
            P("mp"),
            P("mp", None),
        ),
        check_vma=False,
    )
```

```python
import functools

import jax
import jax.numpy as jnp
from jax import lax
from jax.experimental import pallas as pl
from jax.experimental.pallas import tpu as pltpu
from jax.sharding import PartitionSpec as P

HEAD = 64
IMG_LEN = 50
F32 = jnp.float32
BF16 = jnp.bfloat16


def dot(a, b):
    return lax.dot_general(a, b, (((1,), (0,)), ((), ())), preferred_element_type=F32)


def dot_nt(a, b):
    return lax.dot_general(a, b, (((1,), (1,)), ((), ())), preferred_element_type=F32)


def dot_tn(a, b):
    return lax.dot_general(a, b, (((0,), (0,)), ((), ())), preferred_element_type=F32)


def normalized(values):
    center = values - jnp.mean(values, axis=-1, keepdims=True)
    factor = lax.rsqrt(jnp.mean(center * center, axis=-1, keepdims=True) + 1e-05)
    return center * factor, factor


def norm_back(grad, hat, factor, gain):
    scaled = grad * gain
    along = jnp.mean(scaled * hat, axis=-1, keepdims=True)
    return factor * (scaled - jnp.mean(scaled, axis=-1, keepdims=True) - hat * along)


def unit(rows):
    return rows * lax.rsqrt(jnp.sum(rows * rows, axis=-1, keepdims=True) + 1e-06)


def gelu_parts(hidden):
    cdf = 0.5 * (1.0 + lax.erf(hidden * 0.7071067811865476))
    slope = cdf + hidden * jnp.exp(-0.5 * hidden * hidden) * 0.3989422804014327
    return hidden * cdf, slope


def head_blocks(rows, width):
    lanes = lax.broadcasted_iota(jnp.int32, (1, width), 1)
    return jnp.concatenate(
        [
            jnp.where((lanes >= h * HEAD) & (lanes < (h + 1) * HEAD), rows, 0.0)
            for h in range(width // HEAD)
        ],
        axis=0,
    )


def head_pick(blocks, width):
    heads = width // HEAD
    count = blocks.shape[0] // heads
    lanes = lax.broadcasted_iota(jnp.int32, (1, width), 1)
    total = jnp.zeros((count, width), F32)
    for h in range(heads):
        own = (lanes >= h * HEAD) & (lanes < (h + 1) * HEAD)
        total = total + jnp.where(own, blocks[h * count : (h + 1) * count], 0.0)
    return total


def attend(normed_rows, normed, allowed, weights):
    width = weights.shape[1]
    heads = width // HEAD
    queries = dot_nt(normed_rows, weights[0]).astype(BF16)
    folded = dot(head_blocks(queries.astype(F32), width).astype(BF16), weights[1]).astype(BF16)
    scores = dot_nt(folded, normed) * HEAD**-0.5
    scores = jnp.where(jnp.concatenate([allowed] * heads, axis=0), scores, -1e30)
    expo = jnp.exp(scores - jnp.max(scores, axis=-1, keepdims=True))
    probs = expo / jnp.sum(expo, axis=-1, keepdims=True)
    mixed = dot(probs.astype(BF16), normed).astype(BF16)
    context = head_pick(dot_nt(mixed, weights[2]), width).astype(BF16)
    return queries, folded, probs, mixed, context


def plain_device(
    text_tokens,
    segment_ids,
    labels,
    image_tokens,
    image_gain_one,
    image_bias_one,
    image_qkv,
    image_out,
    image_gain_two,
    image_bias_two,
    image_up,
    image_up_bias,
    image_down,
    text_gain_one,
    text_bias_one,
    text_qkv,
    text_out,
    text_gain_two,
    text_bias_two,
    text_up,
    text_up_bias,
    text_down,
):
    rank = lax.axis_index("dp")
    pairs = labels.shape[0]
    tokens = segment_ids.shape[0]
    width = text_out.shape[0]
    heads = width // HEAD
    features = text_tokens.shape[1]
    image_weights = jnp.transpose(image_qkv, (1, 2, 0))
    text_weights = jnp.transpose(text_qkv, (1, 2, 0))

    image_x = image_tokens.astype(F32)
    image_n = (normalized(image_x)[0] * image_gain_one + image_bias_one).astype(BF16)
    image_first = image_x.reshape(pairs, IMG_LEN, features)[:, 0]
    first_n = (normalized(image_first)[0] * image_gain_one + image_bias_one).astype(BF16)
    owner = lax.broadcasted_iota(jnp.int32, (pairs, pairs * IMG_LEN), 0)
    place = lax.broadcasted_iota(jnp.int32, (pairs, pairs * IMG_LEN), 1)
    inside = (place >= owner * IMG_LEN) & (place < (owner + 1) * IMG_LEN)
    image_context = attend(first_n, image_n, inside, image_weights)[4]

    text_x = text_tokens.astype(F32)
    hat_one, factor_one = normalized(text_x)
    normed = (hat_one * text_gain_one + text_bias_one).astype(BF16)
    captions = rank * pairs + jnp.arange(pairs)
    mine = segment_ids[None, :] == captions[:, None]
    spot = lax.broadcasted_iota(jnp.int32, (pairs, tokens), 1)
    last = jnp.max(jnp.where(mine, spot, -1), axis=1, keepdims=True)
    pick = (spot == last).astype(BF16)
    normed_last = dot(pick, normed).astype(BF16)
    queries, folded, probs, mixed, context = attend(normed_last, normed, mine, text_weights)

    attended = jnp.concatenate([dot(image_context, image_out), dot(context, text_out)], axis=0)
    attended = lax.psum(attended.astype(BF16), "mp").astype(F32)
    middle = jnp.concatenate([image_first, dot(pick, text_tokens)], axis=0) + attended
    hat_two, factor_two = normalized(middle)
    image_n2 = (hat_two[:pairs] * image_gain_two + image_bias_two).astype(BF16)
    normed_two = (hat_two[pairs:] * text_gain_two + text_bias_two).astype(BF16)
    image_active = gelu_parts(dot(image_n2, image_up) + image_up_bias)[0].astype(BF16)
    active, slope = gelu_parts(dot(normed_two, text_up) + text_up_bias)
    active = active.astype(BF16)
    branch = jnp.concatenate([dot(image_active, image_down), dot(active, text_down)], axis=0)
    final = middle + lax.psum(branch.astype(BF16), "mp").astype(F32)

    everyone = lax.all_gather(final.astype(BF16), "dp").astype(F32)
    total = everyone.shape[0] * pairs
    image_low = unit(everyone[:, :pairs].reshape(total, features)).astype(BF16)
    pooled = final[pairs:]
    text_low = unit(everyone[:, pairs:].reshape(total, features)).astype(BF16)
    logits = 64.0 * dot_nt(text_low, image_low)
    column_lse = jax.nn.logsumexp(logits, axis=0)
    own = lax.dynamic_slice_in_dim(logits, rank * pairs, pairs, axis=0)
    row_lse = jax.nn.logsumexp(own, axis=1)
    own_columns = lax.dynamic_slice_in_dim(column_lse, rank * pairs, pairs)
    onehot = (labels[:, None] == jnp.arange(total)[None, :]).astype(F32)
    pair_loss = 0.5 * (row_lse + own_columns) - jnp.sum(own * onehot, axis=1)
    grad_logits = (
        0.5 * (jnp.exp(own - row_lse[:, None]) + jnp.exp(own - column_lse[None, :])) - onehot
    )
    grad_embed = 64.0 * dot(grad_logits.astype(BF16), image_low)
    scale = lax.rsqrt(jnp.sum(pooled * pooled, axis=-1, keepdims=True) + 1e-06)
    text_unit = pooled * scale
    grad_final = scale * (
        grad_embed - text_unit * jnp.sum(text_unit * grad_embed, axis=-1, keepdims=True)
    )

    final_low = grad_final.astype(BF16)
    grad_hidden = (dot_nt(final_low, text_down) * slope).astype(BF16)
    grad_normed_two = lax.psum(dot_nt(grad_hidden, text_up).astype(BF16), "mp").astype(F32)
    hat_two = hat_two[pairs:]
    grad_middle = grad_final + norm_back(grad_normed_two, hat_two, factor_two[pairs:], text_gain_two)
    middle_low = grad_middle.astype(BF16)
    grad_context = dot_nt(middle_low, text_out).astype(BF16)
    grad_folded = dot(head_blocks(grad_context.astype(F32), width).astype(BF16), text_weights[2])
    grad_folded = grad_folded.astype(BF16)
    grad_probs = dot_nt(grad_folded, normed)
    grad_scores = probs * (grad_probs - jnp.sum(grad_probs * probs, axis=-1, keepdims=True))
    grad_scores = (grad_scores * HEAD**-0.5).astype(BF16)
    mixed_back = dot(grad_scores, normed).astype(BF16)
    grad_queries = head_pick(dot_nt(mixed_back, text_weights[1]), width).astype(BF16)
    grad_normed = dot_tn(grad_scores, folded) + dot_tn(probs.astype(BF16), grad_folded)
    grad_normed = grad_normed + dot_tn(pick, dot(grad_queries, text_weights[0]).astype(BF16))
    grad_normed = lax.psum(grad_normed.astype(BF16), "mp").astype(F32)
    text_grad = norm_back(grad_normed, hat_one, factor_one, text_gain_one)
    text_grad = text_grad + dot_tn(pick, middle_low)

    vectors = jnp.concatenate(
        [
            jnp.sum(grad_normed * hat_one, axis=0),
            jnp.sum(grad_normed, axis=0),
            jnp.sum(grad_normed_two * hat_two, axis=0),
            jnp.sum(grad_normed_two, axis=0),
            jnp.sum(grad_hidden.astype(F32), axis=0),
        ]
    )
    vectors = jnp.sum(lax.all_gather(vectors, "dp"), axis=0)
    cuts = [features, 2 * features, 3 * features, 4 * features]
    gain_one, bias_one, gain_two, bias_two, up_bias = jnp.split(vectors, cuts)

    def by_head(blocks):
        return [blocks[h * pairs : (h + 1) * pairs] for h in range(heads)]

    pieces = [active, final_low, normed_two, grad_hidden, context, middle_low, normed_last]
    pieces += [grad_queries, queries, grad_context] + by_head(mixed_back) + by_head(mixed)
    sent = lax.all_gather(jnp.concatenate(pieces, axis=1), "dp").reshape(total, -1)
    got = []
    at = 0
    for piece in pieces:
        got.append(sent[:, at : at + piece.shape[1]])
        at += piece.shape[1]
    active, final_low, normed_two, grad_hidden, context, middle_low, normed_last = got[:7]
    grad_queries, queries, grad_context = got[7:10]
    mixed_back = got[10 : 10 + heads]
    mixed = got[10 + heads :]

    def per_head(rows, blocks):
        return jnp.concatenate(
            [dot_tn(rows[:, h * HEAD : (h + 1) * HEAD], blocks[h]) for h in range(heads)], axis=0
        )

    grad_qkv = jnp.stack(
        [
            dot_tn(grad_queries, normed_last),
            per_head(queries, mixed_back),
            per_head(grad_context, mixed),
        ]
    )
    return (
        pair_loss,
        text_grad,
        gain_one,
        bias_one,
        jnp.transpose(grad_qkv, (2, 0, 1)),
        dot_tn(context, middle_low),
        gain_two,
        bias_two,
        dot_tn(normed_two, grad_hidden),
        up_bias,
        dot_tn(active, final_low),
    )


MESH = pl.DeviceIdType.MESH
TOKEN_PARTS = 2
SHIP_PARTS = 4
FIRST_FOLDS = 2
STEPS = {
    0: (("start", 0), ("start", 1)),
    3: (("second", 0), ("near", 0), ("own", 0)),
    4: (("second", 1), ("near", 1), ("own", 1)),
    9: (("third", 0), ("far", 0), ("pass", 0)),
    6: (("third", 1), ("far", 1), ("pass", 1)),
    8: (("last", 0), ("last", 1)),
}


def to_tall(rows):
    half = rows.shape[1] // 2
    return jnp.concatenate([rows[:, :half], rows[:, half:]], axis=0).astype(BF16)


def from_tall(tall):
    count = tall.shape[0] // 2
    wide = tall.astype(F32)
    return jnp.concatenate([wide[:count], wide[count:]], axis=1)


def column_of(row, count):
    shape = (count, row.shape[1])
    same = lax.broadcasted_iota(jnp.int32, shape, 0) == lax.broadcasted_iota(jnp.int32, shape, 1)
    return jnp.sum(jnp.where(same, row, 0), axis=1, keepdims=True)


def caption_masks(seg, first, count):
    captions = first + lax.broadcasted_iota(jnp.int32, (count, seg.shape[1]), 0)
    mine = seg == captions
    spot = lax.broadcasted_iota(jnp.int32, (count, seg.shape[1]), 1)
    last = jnp.max(jnp.where(mine, spot, -1), axis=1, keepdims=True)
    return mine, (spot == last).astype(F32).astype(BF16)


def softmax_rows(scores, allowed):
    scores = jnp.where(allowed, scores, -1e30)
    expo = jnp.exp(scores - jnp.max(scores, axis=-1, keepdims=True))
    return expo / jnp.sum(expo, axis=-1, keepdims=True)


def stats_pack(rows, multiple=8):
    pieces = []
    for row in rows:
        pieces += [row[:, at : at + 128] for at in range(0, row.shape[1], 128)]
    if len(pieces) % multiple:
        pieces.append(jnp.zeros((-len(pieces) % multiple, 128), F32))
    return jnp.concatenate(pieces, axis=0)


def stats_unpack(packed, count, features):
    per = features // 128
    return [
        jnp.concatenate([packed[at * per + i : at * per + i + 1] for i in range(per)], axis=1)
        for at in range(count)
    ]


def step_kernel(
    sizes,
    text_hbm,
    image_hbm,
    iw_hbm,
    io_hbm,
    iu_hbm,
    id_hbm,
    tw_hbm,
    to_hbm,
    tu_hbm,
    td_hbm,
    seg_hbm,
    lab_hbm,
    ig1_hbm,
    ib1_hbm,
    ig2_hbm,
    ib2_hbm,
    iub_hbm,
    tg1_hbm,
    tb1_hbm,
    tg2_hbm,
    tb2_hbm,
    tub_hbm,
    up_o,
    down_o,
    tw,
    to,
    mid_o,
    nsel_o,
    xk_o,
    xv_o,
    tg_o,
    vec_o,
    loss_o,
    xt,
    xi,
    iw,
    io,
    iu,
    idn,
    tu,
    td,
    seg_ref,
    lab_ref,
    ig1_ref,
    ib1_ref,
    ig2_ref,
    ib2_ref,
    iub_ref,
    tg1_ref,
    tb1_ref,
    tg2_ref,
    tb2_ref,
    tub_ref,
    tok,
    ids,
    prow,
    stm,
    std,
    ar,
    gat,
    fq,
    fg,
    fd,
    load_sem,
    img_sem,
    t_s,
    tz_r,
    ty_r,
    to_r,
    tx_r,
    tl_r,
    ar_s,
    ar_r,
    g_s,
    g_r,
    g_f,
    g_c,
    f_s,
    f_x,
    f_c,
    st_s,
    st_r,
    sm_s,
    sm_r,
):
    n_dp, n_mp, pairs, tokens, features, width = sizes
    heads = width // HEAD
    half_dp = n_dp // 2
    total = n_dp * pairs
    scale = HEAD**-0.5
    d = lax.axis_index("dp")
    m = lax.axis_index("mp")
    core = lax.rem(m, 2)
    side = lax.div(m, 2)
    hi = lax.div(d, 2)
    lo = lax.rem(d, 2)
    partner = (d, m + 1 - 2 * core)
    across = (d, lax.rem(m + 2, 4))
    beside = (hi * 2 + 1 - lo, m)

    chunk = img_sem.shape[0]
    chunk_rows = xi.shape[0] // chunk

    def image_load(k):
        rows = pl.ds(k * chunk_rows, chunk_rows)
        return pltpu.make_async_copy(image_hbm.at[rows], xi.at[rows], img_sem.at[k])

    loads = {}

    def load(name, src, dst):
        loads[name] = pltpu.make_async_copy(src, dst, load_sem.at[len(loads)])
        loads[name].start()

    for k in range(chunk):
        image_load(k).start()
    load("ig1", ig1_hbm, ig1_ref)
    load("ib1", ib1_hbm, ib1_ref)
    load("iw", iw_hbm, iw)
    load("io", io_hbm, io)

    def vector(name, ref):
        loads[name].wait()
        return ref[...].reshape(1, ref.shape[0])

    barrier = pltpu.get_barrier_semaphore()
    for i in range(1, n_mp):
        pl.semaphore_signal(
            barrier, inc=1, device_id=(d, lax.rem(m + i, n_mp)), device_id_type=MESH
        )

    @pl.loop(1, n_dp)
    def _(i):
        pl.semaphore_signal(
            barrier, inc=1, device_id=(lax.rem(d + i, n_dp), m), device_id_type=MESH
        )

    load("text", text_hbm, xt)
    load("tg1", tg1_hbm, tg1_ref)
    load("tb1", tb1_hbm, tb1_ref)
    load("seg", seg_hbm, seg_ref)
    load("lab", lab_hbm, lab_ref)
    load("tw", tw_hbm, tw)
    load("to", to_hbm, to)
    load("ig2", ig2_hbm, ig2_ref)
    load("ib2", ib2_hbm, ib2_ref)
    load("iub", iub_hbm, iub_ref)
    load("iu", iu_hbm, iu)
    load("id", id_hbm, idn)
    load("tg2", tg2_hbm, tg2_ref)
    load("tb2", tb2_hbm, tb2_ref)
    load("tub", tub_hbm, tub_ref)
    load("tu", tu_hbm, tu)
    load("td", td_hbm, td)

    def remote(src, dst, send, recv, device):
        return pltpu.make_async_remote_copy(
            src_ref=src,
            dst_ref=dst,
            send_sem=send,
            recv_sem=recv,
            device_id=device,
            device_id_type=MESH,
        )

    def mp_send(buf, send, recv):
        for i in range(1, n_mp):
            remote(buf.at[m], buf.at[m], send, recv, (d, lax.rem(m + i, n_mp))).start()

    def mp_recv(buf, send, recv):
        slots = buf.at[pl.ds(0, n_mp - 1)]
        remote(slots, slots, send, recv, partner).wait_recv()

    def mp_drain(buf, send, recv):
        slots = buf.at[pl.ds(0, n_mp - 1)]
        remote(slots, slots, send, recv, partner).wait_send()

    def far_send(at):
        buf, first, rows = far[at]
        slot = buf.at[m, pl.ds(first, rows)]
        remote(slot, slot, f_s.at[at], f_x.at[at], across).start()
        remote(slot, slot, f_s.at[at], f_c.at[at], partner).start()

    def far_pass(at):
        buf, first, rows = far[at]
        slot = buf.at[lax.rem(m + 2, 4), pl.ds(first, rows)]
        remote(slot, slot, f_s.at[at], f_x.at[at], partner).wait_recv()
        remote(slot, slot, f_s.at[at], f_c.at[at], partner).start()

    def far_recv(at):
        buf, first, rows = far[at]
        slots = buf.at[pl.ds(0, 2), pl.ds(first, rows)]
        remote(slots, slots, f_s.at[at], f_c.at[at], partner).wait_recv()

    def far_drain(at):
        buf, first, rows = far[at]
        slots = buf.at[pl.ds(0, 3), pl.ds(first, rows)]
        remote(slots, slots, f_s.at[at], f_c.at[at], partner).wait_send()

    split_row = FIRST_FOLDS * 16
    far = (
        (fq, 0, fq.shape[1]),
        (fg, 0, split_row),
        (fg, split_row, fg.shape[1] - split_row),
        (fd, 0, fd.shape[1]),
    )

    def on_core(which):
        return pl.when(core == which)

    def dp_send(at):
        slot = gat.at[at, lo, hi]
        other = lo + core * (1 - 2 * lo)

        def send(k):
            to_dev = (lax.rem(hi + k, half_dp) * 2 + other, m)
            remote(slot, slot, g_s.at[at], g_r.at[at], to_dev).start()

        for k in range(1, half_dp):
            send(k)
        on_core(1)(lambda: send(0))

    def dp_forward(at):
        @on_core(1)
        def _():
            slots = gat.at[at, 1 - lo]
            remote(slots, slots, g_f.at[at], g_r.at[at], partner).wait_recv()
            remote(slots, slots, g_f.at[at], g_c.at[at], partner).start()

        @on_core(0)
        def _():
            slots = gat.at[at, 0, pl.ds(0, half_dp - 1)]
            remote(slots, slots, g_f.at[at], g_r.at[at], partner).wait_recv()
            for k in range(1, half_dp):
                slot = gat.at[at, lo, lax.rem(hi + k, half_dp)]
                remote(slot, slot, g_f.at[at], g_c.at[at], partner).start()

    def dp_wait(at, first, wait):
        for which in (0, 1):

            @on_core(which)
            def _(which=which):
                slots = gat.at[at, 0, pl.ds(0, half_dp - (1 if which == first else 0))]
                wait(slots)

    def dp_recv(at):
        dp_wait(
            at,
            1,
            lambda slots: remote(slots, slots, g_f.at[at], g_c.at[at], partner).wait_recv(),
        )

    def dp_drain(at):
        def wait(slots):
            remote(slots, slots, g_s.at[at], g_c.at[at], partner).wait_send()
            remote(slots, slots, g_f.at[at], g_c.at[at], partner).wait_send()

        dp_wait(at, 0, wait)

    def gathered(at):
        talls = [gat[at, i % 2, i // 2].astype(F32) for i in range(n_dp)]
        left = jnp.concatenate([t[:pairs] for t in talls], axis=0)
        right = jnp.concatenate([t[pairs:] for t in talls], axis=0)
        return jnp.concatenate([left, right], axis=1)

    def small_send(at, buf):
        @pl.loop(1, n_dp)
        def _(i):
            to_dev = (lax.rem(d + i, n_dp), m)
            remote(buf.at[d], buf.at[d], sm_s.at[at], sm_r.at[at], to_dev).start()

    def small_recv(at, buf):
        slots = buf.at[pl.ds(0, n_dp - 1)]
        remote(slots, slots, sm_s.at[at], sm_r.at[at], partner).wait_recv()

    def small_drain(at, buf):
        slots = buf.at[pl.ds(0, n_dp - 1)]
        remote(slots, slots, sm_s.at[at], sm_r.at[at], partner).wait_send()

    part_rows = tokens // (2 * TOKEN_PARTS)

    def split_hi(mine, body):
        for k in range(half_dp // 2 - 1):
            body(2 * k + (2 - core if mine else 1 + core))

        @pl.when(core == (1 if mine else 0))
        def _():
            body(half_dp - 1)

    def near_slot(i):
        return lax.rem(hi + half_dp - i, half_dp) * 2 + lo

    def far_slot(i):
        return lax.rem(hi + half_dp - i, half_dp) * 2 + 1 - lo

    def split_far(body):
        split_hi(True, lambda i: body(far_slot(i)))

    def split_near(body):
        split_hi(True, lambda i: body(near_slot(i)))

    def rows_of(slot, part, which):
        start = (which * TOKEN_PARTS + part) * part_rows
        return tok.at[slot, pl.ds(pl.multiple_of(start, 16), part_rows)]

    def tok_push(rows, recv, device):
        remote(rows, rows, t_s.at[0], recv, device).start()

    def tok_wait(recv, counts):
        for which in (0, 1):
            if counts[which]:

                @on_core(which)
                def _(which=which):
                    rows = tok.at[0, pl.ds(0, counts[which] * part_rows)]
                    remote(rows, rows, t_s.at[0], recv, partner).wait_recv()

    quarter = half_dp // 2
    counts = (quarter - 1, quarter)

    def tok_start(part):
        rows = rows_of(d, part, side)

        def body(i):
            tok_push(rows, tz_r.at[part], (lax.rem(hi + i, half_dp) * 2 + lo, m))

        split_hi(True, body)

        @on_core(0)
        def _():
            for which in (0, 1):
                tok_push(rows_of(d, part, which), to_r.at[part], beside)

    def tok_own(part):
        tok_wait(to_r.at[part], (2, 0))

        @on_core(0)
        def _():
            for which in (0, 1):
                tok_push(rows_of(far_slot(0), part, which), tl_r.at[0], partner)

    def tok_second(part):
        tok_wait(tz_r.at[part], counts)

        def body(slot):
            rows = rows_of(slot, part, side)
            tok_push(rows, ty_r.at[part], beside)
            tok_push(rows, tl_r.at[0], partner)

        split_near(body)

    def tok_third(part):
        tok_wait(ty_r.at[part], counts)
        split_far(lambda slot: tok_push(rows_of(slot, part, side), tl_r.at[0], partner))

    def tok_near(part):
        split_near(lambda slot: tok_push(rows_of(slot, part, side), tx_r.at[part, 0], across))

    def tok_far(part):
        split_far(lambda slot: tok_push(rows_of(slot, part, side), tx_r.at[part, 1], across))

    def tok_pass_near(part):
        tok_wait(tx_r.at[part, 0], counts)
        split_near(lambda slot: tok_push(rows_of(slot, part, 1 - side), tl_r.at[0], partner))

    def tok_pass_far(part):
        tok_wait(tx_r.at[part, 1], counts)
        split_far(lambda slot: tok_push(rows_of(slot, part, 1 - side), tl_r.at[0], partner))

    def tok_last():
        for which, count in ((0, 2 * quarter), (1, 2 * quarter - 1)):

            @on_core(which)
            def _(count=count):
                slots = tok.at[pl.ds(0, count)]
                remote(slots, slots, t_s.at[0], tl_r.at[0], partner).wait_recv()

    def tok_drain():
        for which, count in ((0, n_dp - 2), (1, n_dp)):

            @on_core(which)
            def _(count=count):
                slots = tok.at[pl.ds(0, count)]
                remote(slots, slots, t_s.at[0], tl_r.at[0], partner).wait_send()

    def token_steps(at):
        steps = {
            "start": tok_start,
            "own": tok_own,
            "second": tok_second,
            "third": tok_third,
            "near": tok_near,
            "far": tok_far,
            "pass": tok_pass_near,
            "last": tok_pass_far,
        }
        for name, part in STEPS.get(at, ()):
            steps[name](part)

    def attend_rows(queries, normed, allowed, weights):
        stacked = head_blocks(queries.astype(F32), width).astype(BF16)
        folded = dot(stacked, weights[1]).astype(BF16)
        scores = dot_nt(folded, normed) * scale
        probs = softmax_rows(scores, allowed)
        mixed = dot(probs.astype(BF16), normed).astype(BF16)
        context = head_pick(dot_nt(mixed, weights[2]), width).astype(BF16)
        return folded, probs, context

    for k in range(chunk):
        image_load(k).wait()
    gain, shift = vector("ig1", ig1_ref), vector("ib1", ib1_ref)
    loads["iw"].wait()
    hats = [
        normalized(xi[k * chunk_rows : (k + 1) * chunk_rows, :].astype(F32))[0].astype(BF16)
        for k in range(chunk)
    ]
    firsts = [i * IMG_LEN for i in range(pairs)]
    image_first = jnp.concatenate([xi[r : r + 1, :].astype(F32) for r in firsts], axis=0)
    first_n = (normalized(image_first)[0] * gain + shift).astype(BF16)
    image_fold = dot(head_blocks(dot_nt(first_n, iw[0]), width).astype(BF16), iw[1])
    shifted = jnp.sum(image_fold * shift, axis=-1, keepdims=True)
    image_fold = image_fold * gain
    group = pairs // chunk
    shape = (group, chunk_rows)
    place = lax.broadcasted_iota(jnp.int32, shape, 1)
    begin = lax.broadcasted_iota(jnp.int32, shape, 0) * IMG_LEN
    inside = jnp.concatenate([(place >= begin) & (place < begin + IMG_LEN)] * heads, axis=0)

    def of_group(rows, k):
        spots = [h * pairs + k * group for h in range(heads)]
        return jnp.concatenate([rows[at : at + group] for at in spots], axis=0)

    image_scores = [
        (dot_nt(of_group(image_fold, k).astype(BF16), hats[k]) + of_group(shifted, k)) * scale
        for k in range(chunk)
    ]
    image_probs = [softmax_rows(scores, inside).astype(BF16) for scores in image_scores]
    image_mixed = [dot(image_probs[k], hats[k]) for k in range(chunk)]
    image_mixed = jnp.concatenate(
        [mixed[h * group : (h + 1) * group] for h in range(heads) for mixed in image_mixed], axis=0
    )
    image_mixed = image_mixed * gain + shift
    image_context = head_pick(dot_nt(image_mixed.astype(BF16), iw[2]), width).astype(BF16)
    loads["io"].wait()
    ar[0, m] = to_tall(dot(image_context, io[...]))

    pl.semaphore_wait(barrier, n_mp - 1 + n_dp - 1)
    mp_send(ar.at[0], ar_s.at[0], ar_r.at[0])

    loads["text"].wait()
    gain_one = vector("tg1", tg1_ref)
    hat_one, factor_one = normalized(xt[...].astype(F32))
    tok[d] = (hat_one * gain_one + vector("tb1", tb1_ref)).astype(BF16)
    token_steps(0)
    seg = vector("seg", seg_ref)
    seg_rows = tokens // 128
    for i in range(seg_rows):
        ids[d, i : i + 1, :] = seg[:, i * 128 : (i + 1) * 128]
    ids[d, seg_rows : seg_rows + 1, 0:pairs] = vector("lab", lab_ref)
    small_send(0, ids)

    normed = tok[d]
    mine, pick = caption_masks(seg, d * pairs, pairs)
    allowed = jnp.concatenate([mine] * heads, axis=0)
    loads["tw"].wait()
    queries = dot_nt(dot(pick, normed).astype(BF16), tw[0]).astype(BF16)
    folded, probs, context = attend_rows(queries, normed, allowed, tw)
    loads["to"].wait()
    ar[1, m] = to_tall(dot(context, to[...]))
    mp_send(ar.at[1], ar_s.at[1], ar_r.at[1])
    text_last = dot(pick, xt[...])

    def head_rows(blocks):
        rows = [
            jnp.sum(blocks[h * pairs : (h + 1) * pairs], axis=0, keepdims=True)
            for h in range(heads)
        ]
        return jnp.concatenate(rows + [jnp.zeros((8 - heads, tokens), F32)], axis=0)

    def padded(rows, foot):
        foot = jnp.concatenate([foot, jnp.zeros((8, features - tokens), F32)], axis=1)
        return jnp.concatenate([rows, foot], axis=0).astype(BF16)

    no_foot = jnp.zeros((8, tokens), F32)
    prob_rows = head_rows(probs)
    fq[m] = padded(folded.astype(F32), prob_rows)
    token_steps(1)

    def summed(at):
        mp_recv(ar.at[at], ar_s.at[at], ar_r.at[at])
        full = ar[at, 0].astype(F32)
        for i in range(1, n_mp):
            full = full + ar[at, i].astype(F32)
        count = full.shape[0] // 2
        return jnp.concatenate([full[:count], full[count:]], axis=1)

    image_middle = image_first + summed(0)
    gain, shift = vector("ig2", ig2_ref), vector("ib2", ib2_ref)
    image_n2 = (normalized(image_middle)[0] * gain + shift).astype(BF16)
    loads["iu"].wait()
    image_hidden = dot(image_n2, iu[...]) + vector("iub", iub_ref)
    image_active = gelu_parts(image_hidden)[0].astype(BF16)
    loads["id"].wait()
    ar[2, m] = to_tall(dot(image_active, idn[...]))
    mp_send(ar.at[2], ar_s.at[2], ar_r.at[2])
    token_steps(2)

    middle = text_last + summed(1)
    gat[0, lo, hi] = to_tall(middle)
    gain_two, shift_two = vector("tg2", tg2_ref), vector("tb2", tb2_ref)
    hat_two, factor_two = normalized(middle)
    normed_two = (hat_two * gain_two + shift_two).astype(BF16)
    loads["tu"].wait()
    up_shift = vector("tub", tub_ref)
    active, slope = gelu_parts(dot(normed_two, tu[...]) + up_shift)
    loads["td"].wait()
    ar[3, m] = to_tall(dot(active.astype(BF16), td[...]))
    mp_send(ar.at[3], ar_s.at[3], ar_r.at[3])
    token_steps(3)

    gat[1, lo, hi] = to_tall(unit(image_middle + summed(2)))
    dp_send(1)
    gat[2, lo, hi] = to_tall(middle + summed(3))
    dp_send(2)
    far_send(0)

    token_steps(4)
    dp_forward(1)
    token_steps(9)
    dp_forward(2)
    dp_send(0)
    far_pass(0)
    token_steps(5)
    dp_recv(1)
    image_low = gathered(1).astype(BF16)
    own_labels = column_of(ids[d, seg_rows : seg_rows + 1, :], pairs)
    dp_recv(2)


    def embedded(rows):
        shrink = lax.rsqrt(jnp.sum(rows * rows, axis=-1, keepdims=True) + 1e-06)
        text_unit = rows * shrink
        return shrink, text_unit, 64.0 * dot_nt(text_unit.astype(BF16), image_low)

    def final_grad(shrink, text_unit, logits, labels):
        lanes = lax.broadcasted_iota(jnp.int32, logits.shape, 1)
        onehot = (labels == lanes).astype(F32)
        top = jnp.max(logits, axis=1, keepdims=True)
        lse = top + jnp.log(jnp.sum(jnp.exp(logits - top), axis=1, keepdims=True))
        grads = 0.5 * (jnp.exp(logits - lse) + jnp.exp(logits - col_lse)) - onehot
        grads = 64.0 * dot(grads.astype(BF16), image_low)
        along = jnp.sum(text_unit * grads, axis=-1, keepdims=True)
        positive = jnp.sum(logits * onehot, axis=1, keepdims=True)
        return shrink * (grads - text_unit * along), lse, positive

    shrink_all, unit_all, logits = embedded(gathered(2))
    col_top = jnp.max(logits, axis=0, keepdims=True)
    col_lse = col_top + jnp.log(jnp.sum(jnp.exp(logits - col_top), axis=0, keepdims=True))
    grad_final, own_lse, positive = final_grad(*embedded(from_tall(gat[2, lo, hi])), own_labels)
    grad_hidden = (dot_nt(grad_final.astype(BF16), td[...]) * slope).astype(BF16)
    ar[4, m] = to_tall(dot_nt(grad_hidden, tu[...]))
    mp_send(ar.at[4], ar_s.at[4], ar_r.at[4])

    token_steps(6)
    lanes = lax.broadcasted_iota(jnp.int32, (pairs, total), 1)
    mine_first = lax.broadcasted_iota(jnp.int32, (pairs, total), 0) + d * pairs
    own_col = jnp.sum(jnp.where(lanes == mine_first, col_lse, 0.0), axis=1, keepdims=True)
    pair_loss = 0.5 * (own_lse + own_col) - positive
    shape = (pairs, loss_o.shape[1])
    diagonal = lax.broadcasted_iota(jnp.int32, shape, 0) == lax.broadcasted_iota(
        jnp.int32, shape, 1
    )
    loss_o[...] = jnp.sum(jnp.where(diagonal, pair_loss, 0.0), axis=0, keepdims=True)
    small_recv(0, ids)
    labels = jnp.concatenate(
        [column_of(ids[i, seg_rows : seg_rows + 1, :], pairs) for i in range(n_dp)], axis=0
    )
    fin_all = final_grad(shrink_all, unit_all, logits, labels)[0].astype(BF16)
    dp_forward(0)

    grad_n2 = summed(4)
    grad_middle = grad_final + norm_back(grad_n2, hat_two, factor_two, gain_two)
    gat[3, lo, hi] = to_tall(grad_middle)
    dp_send(3)
    middle_low = grad_middle.astype(BF16)
    grad_context = dot_nt(middle_low, to[...]).astype(BF16)
    grad_folded = dot(head_blocks(grad_context.astype(F32), width).astype(BF16), tw[2])
    fg[m] = padded(grad_folded, no_foot)
    far_send(1)
    grad_probs = dot_nt(grad_folded.astype(BF16), normed)
    grad_scores = probs * (grad_probs - jnp.sum(grad_probs * probs, axis=-1, keepdims=True))
    scaled = grad_scores * scale
    score_rows = head_rows(scaled)
    prow[d] = jnp.concatenate([prob_rows[:heads], score_rows[: 8 - heads]], axis=0)
    mixed_back = dot(scaled.astype(BF16), normed).astype(BF16)
    grad_queries = head_pick(dot_nt(mixed_back, tw[1]), width).astype(BF16)
    fd[m] = padded(dot(grad_queries, tw[0]), score_rows)

    def spread(slots, ref, at):
        parts = []
        for i in slots:
            foot = ref[i, at : at + 8, 0:tokens].astype(F32)
            for h in range(heads):
                parts.append(jnp.where(mine, foot[h : h + 1], 0.0))
            parts.append(jnp.zeros((8, tokens), F32))
        return jnp.concatenate(parts, axis=0).astype(BF16)

    def first_norm_grad(slots, sources):
        folds, backs, rests = sources
        place_low = jnp.concatenate(
            [jnp.concatenate([pick.astype(F32), jnp.zeros((8, tokens), F32)], axis=0)] * len(slots),
            axis=0,
        ).astype(BF16)
        grads = dot_tn(spread(slots, fd, pairs), folds)
        grads = grads + dot_tn(spread(slots, fq, pairs * heads), backs)
        return grads + dot_tn(place_low, rests)

    part = first_norm_grad([m], (fq[m], fg[m], fd[m]))
    stm[m] = stats_pack(
        [jnp.sum(part * hat_one, axis=0, keepdims=True), jnp.sum(part, axis=0, keepdims=True)]
    )
    mp_send(stm, st_s.at[0], st_r.at[0])
    far_send(2)
    far_send(3)
    small_send(1, prow)
    stats_two = [
        jnp.sum(grad_n2 * hat_two, axis=0, keepdims=True),
        jnp.sum(grad_n2, axis=0, keepdims=True),
    ]

    token_steps(7)
    dp_recv(0)
    n2_all = (normalized(gathered(0))[0] * gain_two + shift_two).astype(BF16)
    act_all, slope_all = gelu_parts(dot(n2_all, tu[...]) + up_shift)
    gh_all = (dot_nt(fin_all, td[...]) * slope_all).astype(BF16)
    up_bias = jnp.sum(gh_all.astype(F32), axis=0, keepdims=True)
    up_o[...] = dot_tn(n2_all, gh_all)
    down_o[...] = dot_tn(act_all.astype(BF16), fin_all)
    mp_recv(stm, st_s.at[0], st_r.at[0])
    one = stm[0]
    for i in range(1, n_mp):
        one = one + stm[i]
    std[d] = stats_pack(stats_unpack(one, 2, features) + stats_two, 16).astype(BF16)
    small_send(2, std)
    far_pass(1)
    far_pass(2)
    dp_forward(3)
    far_pass(3)
    token_steps(8)

    for at in range(len(far)):
        far_recv(at)
    flat = [ref[...].reshape(n_mp * ref.shape[1], features) for ref in (fq, fg, fd)]
    grad_normed = first_norm_grad(list(range(n_mp)), flat)
    text_grad = norm_back(grad_normed, hat_one, factor_one, gain_one)
    tg_o[...] = text_grad + dot_tn(pick, middle_low)

    small_recv(1, prow)
    tok_last()
    twice = 2 * pairs
    for j in range(half_dp):
        seg = jnp.concatenate(
            [ids[i, k : k + 1, :] for i in (2 * j, 2 * j + 1) for k in range(seg_rows)], axis=1
        )
        here, picks = caption_masks(seg, j * twice, twice)
        values = jnp.concatenate([prow[2 * j], prow[2 * j + 1]], axis=1)
        parts = [jnp.where(here, values[h : h + 1], 0.0) for h in range(heads)]
        parts += [jnp.where(here, values[heads + h : heads + h + 1], 0.0) for h in range(heads)]
        parts = [part.astype(BF16) for part in parts] + [picks]
        low = tok[2 * j : 2 * j + 2].reshape(2 * tokens, features)
        mixed = dot(jnp.concatenate(parts, axis=0), low).astype(BF16)
        rows = slice(j * twice, (j + 1) * twice)
        for h in range(heads):
            xv_o[h, rows, :] = mixed[h * twice : (h + 1) * twice]
            xk_o[h, rows, :] = mixed[(heads + h) * twice : (heads + h + 1) * twice]
        nsel_o[rows, :] = mixed[2 * heads * twice :]
    dp_recv(3)
    mid_o[...] = gathered(3).astype(BF16)

    small_recv(2, std)
    stats = std[0].astype(F32)
    for i in range(1, n_dp):
        stats = stats + std[i].astype(F32)
    rows = stats_unpack(stats, 4, features)
    vec_o[...] = jnp.concatenate(rows + [up_bias, jnp.zeros((3, features), F32)], axis=0)

    for at in range(ar.shape[0]):
        mp_drain(ar.at[at], ar_s.at[at], ar_r.at[at])
    mp_drain(stm, st_s.at[0], st_r.at[0])
    for at in range(len(far)):
        far_drain(at)
    for at in range(gat.shape[0]):
        dp_drain(at)
    for at, buf in enumerate((ids, prow, std)):
        small_drain(at, buf)
    tok_drain()


def weights_kernel(
    up,
    down,
    tw,
    to,
    mid,
    nsel,
    xk,
    xv,
    tg,
    vec,
    loss,
    tg_out,
    qkv_out,
    out_out,
    up_out,
    down_out,
    loss_out,
    g1_out,
    b1_out,
    g2_out,
    b2_out,
    ub_out,
    qkv_buf,
    out_buf,
    sem,
):
    heads, total, features = xk.shape
    width = to.shape[0]
    started = []

    def ship(src, dst):
        copy = pltpu.make_async_copy(src, dst, sem.at[len(started)])
        copy.start()
        started.append(copy)

    for src, dst in ((up, up_out), (down, down_out)):
        step = src.shape[0] // SHIP_PARTS
        for at in range(0, src.shape[0], step):
            rows = pl.ds(at, step)
            ship(src.at[rows], dst.at[rows])
    ship(tg, tg_out)
    flat_k = xk[...].reshape(heads * total, features)
    flat_v = xv[...].reshape(heads * total, features)
    queries = dot_nt(nsel[...], tw[0])
    grad_context = dot_nt(mid[...], to[...])
    for at, rows, flat in ((1, queries, flat_k), (2, grad_context, flat_v)):
        stacked = head_blocks(rows.astype(BF16).astype(F32), width).astype(BF16)
        qkv_buf[at] = dot_tn(stacked, flat)
        ship(qkv_buf.at[at], qkv_out.at[at])
    grad_queries = head_pick(dot_nt(flat_k, tw[1]), width).astype(BF16)
    qkv_buf[0] = dot_tn(grad_queries, nsel[...])
    ship(qkv_buf.at[0], qkv_out.at[0])
    context = head_pick(dot_nt(flat_v, tw[2]), width).astype(BF16)
    out_buf[...] = dot_tn(context, mid[...])
    ship(out_buf, out_out)
    for at, dst in enumerate((g1_out, b1_out, g2_out, b2_out, ub_out)):
        dst[...] = vec[at, :]
    loss_out[...] = loss[0, 0 : loss_out.shape[0]]
    for copy in started:
        copy.wait()


def kernel_device(
    n_dp,
    n_mp,
    text_tokens,
    segment_ids,
    labels,
    image_tokens,
    image_gain_one,
    image_bias_one,
    image_qkv,
    image_out,
    image_gain_two,
    image_bias_two,
    image_up,
    image_up_bias,
    image_down,
    text_gain_one,
    text_bias_one,
    text_qkv,
    text_out,
    text_gain_two,
    text_bias_two,
    text_up,
    text_up_bias,
    text_down,
):
    pairs = labels.shape[0]
    tokens, features = text_tokens.shape
    width = text_out.shape[0]
    hidden = text_up.shape[1]
    heads = width // HEAD
    total = n_dp * pairs
    half_dp = n_dp // 2
    vmem = pltpu.VMEM
    whole = pl.BlockSpec(memory_space=pltpu.VMEM)
    anywhere = pl.BlockSpec(memory_space=pl.ANY)

    def sems(*shape):
        return pltpu.SemaphoreType.DMA(shape)

    outs = [
        ((features, hidden), F32),
        ((hidden, features), F32),
        ((3, width, features), BF16),
        ((width, features), BF16),
        ((total, features), BF16),
        ((total, features), BF16),
        ((heads, total, features), BF16),
        ((heads, total, features), BF16),
        ((tokens, features), F32),
        ((8, features), F32),
        ((1, 128), F32),
    ]
    tall = (2 * pairs, features // 2)
    fold_rows = heads * pairs + 8
    vectors = (
        segment_ids,
        labels,
        image_gain_one,
        image_bias_one,
        image_gain_two,
        image_bias_two,
        image_up_bias,
        text_gain_one,
        text_bias_one,
        text_gain_two,
        text_bias_two,
        text_up_bias,
    )
    operands = (
        text_tokens,
        image_tokens,
        jnp.transpose(image_qkv, (1, 2, 0)),
        image_out,
        image_up,
        image_down,
        jnp.transpose(text_qkv, (1, 2, 0)),
        text_out,
        text_up,
        text_down,
    ) + vectors
    factors = pl.pallas_call(
        functools.partial(step_kernel, (n_dp, n_mp, pairs, tokens, features, width)),
        out_shape=[vmem(shape, dtype) for shape, dtype in outs],
        in_specs=[anywhere] * len(operands),
        out_specs=[whole] * len(outs),
        scratch_shapes=[
            vmem(text_tokens.shape, BF16),
            vmem(image_tokens.shape, BF16),
            vmem((3, width, features), BF16),
            vmem(image_out.shape, BF16),
            vmem(image_up.shape, BF16),
            vmem(image_down.shape, BF16),
            vmem(text_up.shape, BF16),
            vmem(text_down.shape, BF16),
        ]
        + [vmem(array.shape, array.dtype) for array in vectors]
        + [
            vmem((n_dp, tokens, features), BF16),
            vmem((n_dp, 8, 128), jnp.int32),
            vmem((n_dp, 8, tokens), F32),
            vmem((n_mp, 16, 128), F32),
            vmem((n_dp, 32, 128), BF16),
            vmem((5, n_mp) + tall, BF16),
            vmem((4, 2, half_dp) + tall, BF16),
            vmem((n_mp, fold_rows, features), BF16),
            vmem((n_mp, fold_rows, features), BF16),
            vmem((n_mp, pairs + 8, features), BF16),
            sems(22),
            sems(pairs // 8),
            sems(1),
            sems(TOKEN_PARTS),
            sems(TOKEN_PARTS),
            sems(TOKEN_PARTS),
            sems(TOKEN_PARTS, 2),
            sems(1),
            sems(5),
            sems(5),
            sems(4),
            sems(4),
            sems(4),
            sems(4),
            sems(4),
            sems(4),
            sems(4),
            sems(1),
            sems(1),
            sems(3),
            sems(3),
        ],
        compiler_params=pltpu.CompilerParams(
            collective_id=0, has_side_effects=True, vmem_limit_bytes=48 * 2**20
        ),
        name="step",
    )(*[pltpu.with_memory_space_constraint(operand, pltpu.HBM) for operand in operands])
    vector = jax.ShapeDtypeStruct((features,), F32)
    results = pl.pallas_call(
        weights_kernel,
        out_shape=[
            jax.ShapeDtypeStruct((tokens, features), F32),
            jax.ShapeDtypeStruct((3, width, features), F32),
            jax.ShapeDtypeStruct((width, features), F32),
            jax.ShapeDtypeStruct((features, hidden), F32),
            jax.ShapeDtypeStruct((hidden, features), F32),
            jax.ShapeDtypeStruct((pairs,), F32),
            vector,
            vector,
            vector,
            vector,
            jax.ShapeDtypeStruct((hidden,), F32),
        ],
        in_specs=[whole] * len(outs),
        out_specs=[anywhere] * 5 + [whole] * 6,
        scratch_shapes=[
            vmem((3, width, features), F32),
            vmem((width, features), F32),
            sems(2 * SHIP_PARTS + 5),
        ],
        compiler_params=pltpu.CompilerParams(vmem_limit_bytes=32 * 2**20),
        name="weights",
    )(*[pltpu.with_memory_space_constraint(factor, pltpu.VMEM) for factor in factors])
    text_grad, qkv, out, up, down, loss, gain_one, bias_one, gain_two, bias_two, up_bias = results
    return (
        loss,
        text_grad,
        gain_one,
        bias_one,
        jnp.transpose(qkv, (2, 0, 1)),
        out,
        gain_two,
        bias_two,
        up,
        up_bias,
        down,
    )


def solution(mesh):
    placed = (
        P("dp", None),
        P("dp"),
        P("dp"),
        P("dp", None),
        P(),
        P(),
        P(None, None, "mp"),
        P("mp", None),
        P(),
        P(),
        P(None, "mp"),
        P("mp"),
        P("mp", None),
        P(),
        P(),
        P(None, None, "mp"),
        P("mp", None),
        P(),
        P(),
        P(None, "mp"),
        P("mp"),
        P("mp", None),
    )
    n_dp, n_mp = mesh.shape["dp"], mesh.shape["mp"]
    body = plain_device
    if n_dp <= 16 and n_dp % 4 == 0 and n_mp == 4:
        body = functools.partial(kernel_device, n_dp, n_mp)
    return jax.shard_map(
        body,
        mesh=mesh,
        in_specs=placed,
        out_specs=(
            P("dp"),
            P("dp", None),
            P(),
            P(),
            P(None, None, "mp"),
            P("mp", None),
            P(),
            P(),
            P(None, "mp"),
            P("mp"),
            P("mp", None),
        ),
        check_vma=False,
    )
```

```python
import functools

import jax
import jax.numpy as jnp
from jax import lax
from jax.experimental import pallas as pl
from jax.experimental.pallas import tpu as pltpu
from jax.sharding import PartitionSpec as P

HEAD = 64
IMG_LEN = 50
F32 = jnp.float32
BF16 = jnp.bfloat16


def dot(a, b):
    return lax.dot_general(a, b, (((1,), (0,)), ((), ())), preferred_element_type=F32)


def dot_nt(a, b):
    return lax.dot_general(a, b, (((1,), (1,)), ((), ())), preferred_element_type=F32)


def dot_tn(a, b):
    return lax.dot_general(a, b, (((0,), (0,)), ((), ())), preferred_element_type=F32)


def normalized(values):
    center = values - jnp.mean(values, axis=-1, keepdims=True)
    factor = lax.rsqrt(jnp.mean(center * center, axis=-1, keepdims=True) + 1e-05)
    return center * factor, factor


def norm_back(grad, hat, factor, gain):
    scaled = grad * gain
    along = jnp.mean(scaled * hat, axis=-1, keepdims=True)
    return factor * (scaled - jnp.mean(scaled, axis=-1, keepdims=True) - hat * along)


def unit(rows):
    return rows * lax.rsqrt(jnp.sum(rows * rows, axis=-1, keepdims=True) + 1e-06)


def gelu_parts(hidden):
    cdf = 0.5 * (1.0 + lax.erf(hidden * 0.7071067811865476))
    slope = cdf + hidden * jnp.exp(-0.5 * hidden * hidden) * 0.3989422804014327
    return hidden * cdf, slope


def head_blocks(rows, width):
    lanes = lax.broadcasted_iota(jnp.int32, (1, width), 1)
    return jnp.concatenate(
        [
            jnp.where((lanes >= h * HEAD) & (lanes < (h + 1) * HEAD), rows, 0.0)
            for h in range(width // HEAD)
        ],
        axis=0,
    )


def head_pick(blocks, width):
    heads = width // HEAD
    count = blocks.shape[0] // heads
    lanes = lax.broadcasted_iota(jnp.int32, (1, width), 1)
    total = jnp.zeros((count, width), F32)
    for h in range(heads):
        own = (lanes >= h * HEAD) & (lanes < (h + 1) * HEAD)
        total = total + jnp.where(own, blocks[h * count : (h + 1) * count], 0.0)
    return total


def attend(normed_rows, normed, allowed, weights):
    width = weights.shape[1]
    heads = width // HEAD
    queries = dot_nt(normed_rows, weights[0]).astype(BF16)
    folded = dot(head_blocks(queries.astype(F32), width).astype(BF16), weights[1]).astype(BF16)
    scores = dot_nt(folded, normed) * HEAD**-0.5
    scores = jnp.where(jnp.concatenate([allowed] * heads, axis=0), scores, -1e30)
    expo = jnp.exp(scores - jnp.max(scores, axis=-1, keepdims=True))
    probs = expo / jnp.sum(expo, axis=-1, keepdims=True)
    mixed = dot(probs.astype(BF16), normed).astype(BF16)
    context = head_pick(dot_nt(mixed, weights[2]), width).astype(BF16)
    return queries, folded, probs, mixed, context


def plain_device(
    text_tokens,
    segment_ids,
    labels,
    image_tokens,
    image_gain_one,
    image_bias_one,
    image_qkv,
    image_out,
    image_gain_two,
    image_bias_two,
    image_up,
    image_up_bias,
    image_down,
    text_gain_one,
    text_bias_one,
    text_qkv,
    text_out,
    text_gain_two,
    text_bias_two,
    text_up,
    text_up_bias,
    text_down,
):
    rank = lax.axis_index("dp")
    pairs = labels.shape[0]
    tokens = segment_ids.shape[0]
    width = text_out.shape[0]
    heads = width // HEAD
    features = text_tokens.shape[1]
    image_weights = jnp.transpose(image_qkv, (1, 2, 0))
    text_weights = jnp.transpose(text_qkv, (1, 2, 0))

    image_x = image_tokens.astype(F32)
    image_n = (normalized(image_x)[0] * image_gain_one + image_bias_one).astype(BF16)
    image_first = image_x.reshape(pairs, IMG_LEN, features)[:, 0]
    first_n = (normalized(image_first)[0] * image_gain_one + image_bias_one).astype(BF16)
    owner = lax.broadcasted_iota(jnp.int32, (pairs, pairs * IMG_LEN), 0)
    place = lax.broadcasted_iota(jnp.int32, (pairs, pairs * IMG_LEN), 1)
    inside = (place >= owner * IMG_LEN) & (place < (owner + 1) * IMG_LEN)
    image_context = attend(first_n, image_n, inside, image_weights)[4]

    text_x = text_tokens.astype(F32)
    hat_one, factor_one = normalized(text_x)
    normed = (hat_one * text_gain_one + text_bias_one).astype(BF16)
    captions = rank * pairs + jnp.arange(pairs)
    mine = segment_ids[None, :] == captions[:, None]
    spot = lax.broadcasted_iota(jnp.int32, (pairs, tokens), 1)
    last = jnp.max(jnp.where(mine, spot, -1), axis=1, keepdims=True)
    pick = (spot == last).astype(BF16)
    normed_last = dot(pick, normed).astype(BF16)
    queries, folded, probs, mixed, context = attend(normed_last, normed, mine, text_weights)

    attended = jnp.concatenate([dot(image_context, image_out), dot(context, text_out)], axis=0)
    attended = lax.psum(attended.astype(BF16), "mp").astype(F32)
    middle = jnp.concatenate([image_first, dot(pick, text_tokens)], axis=0) + attended
    hat_two, factor_two = normalized(middle)
    image_n2 = (hat_two[:pairs] * image_gain_two + image_bias_two).astype(BF16)
    normed_two = (hat_two[pairs:] * text_gain_two + text_bias_two).astype(BF16)
    image_active = gelu_parts(dot(image_n2, image_up) + image_up_bias)[0].astype(BF16)
    active, slope = gelu_parts(dot(normed_two, text_up) + text_up_bias)
    active = active.astype(BF16)
    branch = jnp.concatenate([dot(image_active, image_down), dot(active, text_down)], axis=0)
    final = middle + lax.psum(branch.astype(BF16), "mp").astype(F32)

    everyone = lax.all_gather(final.astype(BF16), "dp").astype(F32)
    total = everyone.shape[0] * pairs
    image_low = unit(everyone[:, :pairs].reshape(total, features)).astype(BF16)
    pooled = final[pairs:]
    text_low = unit(everyone[:, pairs:].reshape(total, features)).astype(BF16)
    logits = 64.0 * dot_nt(text_low, image_low)
    column_lse = jax.nn.logsumexp(logits, axis=0)
    own = lax.dynamic_slice_in_dim(logits, rank * pairs, pairs, axis=0)
    row_lse = jax.nn.logsumexp(own, axis=1)
    own_columns = lax.dynamic_slice_in_dim(column_lse, rank * pairs, pairs)
    onehot = (labels[:, None] == jnp.arange(total)[None, :]).astype(F32)
    pair_loss = 0.5 * (row_lse + own_columns) - jnp.sum(own * onehot, axis=1)
    grad_logits = (
        0.5 * (jnp.exp(own - row_lse[:, None]) + jnp.exp(own - column_lse[None, :])) - onehot
    )
    grad_embed = 64.0 * dot(grad_logits.astype(BF16), image_low)
    scale = lax.rsqrt(jnp.sum(pooled * pooled, axis=-1, keepdims=True) + 1e-06)
    text_unit = pooled * scale
    grad_final = scale * (
        grad_embed - text_unit * jnp.sum(text_unit * grad_embed, axis=-1, keepdims=True)
    )

    final_low = grad_final.astype(BF16)
    grad_hidden = (dot_nt(final_low, text_down) * slope).astype(BF16)
    grad_normed_two = lax.psum(dot_nt(grad_hidden, text_up).astype(BF16), "mp").astype(F32)
    hat_two = hat_two[pairs:]
    grad_middle = grad_final + norm_back(grad_normed_two, hat_two, factor_two[pairs:], text_gain_two)
    middle_low = grad_middle.astype(BF16)
    grad_context = dot_nt(middle_low, text_out).astype(BF16)
    grad_folded = dot(head_blocks(grad_context.astype(F32), width).astype(BF16), text_weights[2])
    grad_folded = grad_folded.astype(BF16)
    grad_probs = dot_nt(grad_folded, normed)
    grad_scores = probs * (grad_probs - jnp.sum(grad_probs * probs, axis=-1, keepdims=True))
    grad_scores = (grad_scores * HEAD**-0.5).astype(BF16)
    mixed_back = dot(grad_scores, normed).astype(BF16)
    grad_queries = head_pick(dot_nt(mixed_back, text_weights[1]), width).astype(BF16)
    grad_normed = dot_tn(grad_scores, folded) + dot_tn(probs.astype(BF16), grad_folded)
    grad_normed = grad_normed + dot_tn(pick, dot(grad_queries, text_weights[0]).astype(BF16))
    grad_normed = lax.psum(grad_normed.astype(BF16), "mp").astype(F32)
    text_grad = norm_back(grad_normed, hat_one, factor_one, text_gain_one)
    text_grad = text_grad + dot_tn(pick, middle_low)

    vectors = jnp.concatenate(
        [
            jnp.sum(grad_normed * hat_one, axis=0),
            jnp.sum(grad_normed, axis=0),
            jnp.sum(grad_normed_two * hat_two, axis=0),
            jnp.sum(grad_normed_two, axis=0),
            jnp.sum(grad_hidden.astype(F32), axis=0),
        ]
    )
    vectors = jnp.sum(lax.all_gather(vectors, "dp"), axis=0)
    cuts = [features, 2 * features, 3 * features, 4 * features]
    gain_one, bias_one, gain_two, bias_two, up_bias = jnp.split(vectors, cuts)

    def by_head(blocks):
        return [blocks[h * pairs : (h + 1) * pairs] for h in range(heads)]

    pieces = [active, final_low, normed_two, grad_hidden, context, middle_low, normed_last]
    pieces += [grad_queries, queries, grad_context] + by_head(mixed_back) + by_head(mixed)
    sent = lax.all_gather(jnp.concatenate(pieces, axis=1), "dp").reshape(total, -1)
    got = []
    at = 0
    for piece in pieces:
        got.append(sent[:, at : at + piece.shape[1]])
        at += piece.shape[1]
    active, final_low, normed_two, grad_hidden, context, middle_low, normed_last = got[:7]
    grad_queries, queries, grad_context = got[7:10]
    mixed_back = got[10 : 10 + heads]
    mixed = got[10 + heads :]

    def per_head(rows, blocks):
        return jnp.concatenate(
            [dot_tn(rows[:, h * HEAD : (h + 1) * HEAD], blocks[h]) for h in range(heads)], axis=0
        )

    grad_qkv = jnp.stack(
        [
            dot_tn(grad_queries, normed_last),
            per_head(queries, mixed_back),
            per_head(grad_context, mixed),
        ]
    )
    return (
        pair_loss,
        text_grad,
        gain_one,
        bias_one,
        jnp.transpose(grad_qkv, (2, 0, 1)),
        dot_tn(context, middle_low),
        gain_two,
        bias_two,
        dot_tn(normed_two, grad_hidden),
        up_bias,
        dot_tn(active, final_low),
    )


MESH = pl.DeviceIdType.MESH
TOKEN_PARTS = 2
SHIP_PARTS = 4
FIRST_FOLDS = 2
STEPS = {
    0: (("start", 0), ("start", 1)),
    3: (("second", 0), ("near", 0), ("own", 0)),
    4: (("second", 1), ("near", 1), ("own", 1)),
    9: (("third", 0), ("far", 0), ("pass", 0)),
    6: (("third", 1), ("far", 1), ("pass", 1)),
    8: (("last", 0), ("last", 1)),
}


def to_tall(rows):
    half = rows.shape[1] // 2
    return jnp.concatenate([rows[:, :half], rows[:, half:]], axis=0).astype(BF16)


def from_tall(tall):
    count = tall.shape[0] // 2
    wide = tall.astype(F32)
    return jnp.concatenate([wide[:count], wide[count:]], axis=1)


def column_of(row, count):
    shape = (count, row.shape[1])
    same = lax.broadcasted_iota(jnp.int32, shape, 0) == lax.broadcasted_iota(jnp.int32, shape, 1)
    return jnp.sum(jnp.where(same, row, 0), axis=1, keepdims=True)


def caption_masks(seg, first, count):
    captions = first + lax.broadcasted_iota(jnp.int32, (count, seg.shape[1]), 0)
    mine = seg == captions
    spot = lax.broadcasted_iota(jnp.int32, (count, seg.shape[1]), 1)
    last = jnp.max(jnp.where(mine, spot, -1), axis=1, keepdims=True)
    return mine, (spot == last).astype(F32).astype(BF16)


def softmax_rows(scores, allowed):
    scores = jnp.where(allowed, scores, -1e30)
    expo = jnp.exp(scores - jnp.max(scores, axis=-1, keepdims=True))
    return expo / jnp.sum(expo, axis=-1, keepdims=True)


def stats_pack(rows, multiple=8):
    pieces = []
    for row in rows:
        pieces += [row[:, at : at + 128] for at in range(0, row.shape[1], 128)]
    if len(pieces) % multiple:
        pieces.append(jnp.zeros((-len(pieces) % multiple, 128), F32))
    return jnp.concatenate(pieces, axis=0)


def stats_unpack(packed, count, features):
    per = features // 128
    return [
        jnp.concatenate([packed[at * per + i : at * per + i + 1] for i in range(per)], axis=1)
        for at in range(count)
    ]


def step_kernel(
    sizes,
    text_hbm,
    image_hbm,
    iw_hbm,
    io_hbm,
    iu_hbm,
    id_hbm,
    tw_hbm,
    to_hbm,
    tu_hbm,
    td_hbm,
    seg_hbm,
    lab_hbm,
    ig1_hbm,
    ib1_hbm,
    ig2_hbm,
    ib2_hbm,
    iub_hbm,
    tg1_hbm,
    tb1_hbm,
    tg2_hbm,
    tb2_hbm,
    tub_hbm,
    up_o,
    down_o,
    tw,
    to,
    mid_o,
    nsel_o,
    xk_o,
    xv_o,
    tg_o,
    vec_o,
    loss_o,
    xt,
    xi,
    iw,
    io,
    iu,
    idn,
    tu,
    td,
    seg_ref,
    lab_ref,
    ig1_ref,
    ib1_ref,
    ig2_ref,
    ib2_ref,
    iub_ref,
    tg1_ref,
    tb1_ref,
    tg2_ref,
    tb2_ref,
    tub_ref,
    tok,
    ids,
    prow,
    drow,
    stm,
    std,
    ar,
    gat,
    fq,
    fg,
    fd,
    load_sem,
    img_sem,
    t_s,
    tz_r,
    ty_r,
    to_r,
    tx_r,
    tl_r,
    ar_s,
    ar_r,
    g_s,
    g_r,
    g_f,
    g_c,
    f_s,
    f_x,
    f_c,
    st_s,
    st_r,
    sm_s,
    sm_r,
):
    n_dp, n_mp, pairs, tokens, features, width = sizes
    heads = width // HEAD
    half_dp = n_dp // 2
    total = n_dp * pairs
    scale = HEAD**-0.5
    d = lax.axis_index("dp")
    m = lax.axis_index("mp")
    core = lax.rem(m, 2)
    side = lax.div(m, 2)
    hi = lax.div(d, 2)
    lo = lax.rem(d, 2)
    partner = (d, m + 1 - 2 * core)
    across = (d, lax.rem(m + 2, 4))
    beside = (hi * 2 + 1 - lo, m)

    chunk = img_sem.shape[0]
    chunk_rows = xi.shape[0] // chunk

    def image_load(k):
        rows = pl.ds(k * chunk_rows, chunk_rows)
        return pltpu.make_async_copy(image_hbm.at[rows], xi.at[rows], img_sem.at[k])

    loads = {}

    def load(name, src, dst):
        loads[name] = pltpu.make_async_copy(src, dst, load_sem.at[len(loads)])
        loads[name].start()

    for k in range(chunk):
        image_load(k).start()
    load("ig1", ig1_hbm, ig1_ref)
    load("ib1", ib1_hbm, ib1_ref)
    load("iw", iw_hbm, iw)
    load("io", io_hbm, io)

    def vector(name, ref):
        loads[name].wait()
        return ref[...].reshape(1, ref.shape[0])

    barrier = pltpu.get_barrier_semaphore()
    for i in range(1, n_mp):
        pl.semaphore_signal(
            barrier, inc=1, device_id=(d, lax.rem(m + i, n_mp)), device_id_type=MESH
        )

    @pl.loop(1, n_dp)
    def _(i):
        pl.semaphore_signal(
            barrier, inc=1, device_id=(lax.rem(d + i, n_dp), m), device_id_type=MESH
        )

    load("text", text_hbm, xt)
    load("tg1", tg1_hbm, tg1_ref)
    load("tb1", tb1_hbm, tb1_ref)
    load("seg", seg_hbm, seg_ref)
    load("lab", lab_hbm, lab_ref)
    load("tw", tw_hbm, tw)
    load("to", to_hbm, to)
    load("ig2", ig2_hbm, ig2_ref)
    load("ib2", ib2_hbm, ib2_ref)
    load("iub", iub_hbm, iub_ref)
    load("iu", iu_hbm, iu)
    load("id", id_hbm, idn)
    load("tg2", tg2_hbm, tg2_ref)
    load("tb2", tb2_hbm, tb2_ref)
    load("tub", tub_hbm, tub_ref)
    load("tu", tu_hbm, tu)
    load("td", td_hbm, td)

    def remote(src, dst, send, recv, device):
        return pltpu.make_async_remote_copy(
            src_ref=src,
            dst_ref=dst,
            send_sem=send,
            recv_sem=recv,
            device_id=device,
            device_id_type=MESH,
        )

    def mp_send(buf, send, recv):
        for i in range(1, n_mp):
            remote(buf.at[m], buf.at[m], send, recv, (d, lax.rem(m + i, n_mp))).start()

    def mp_recv(buf, send, recv):
        slots = buf.at[pl.ds(0, n_mp - 1)]
        remote(slots, slots, send, recv, partner).wait_recv()

    def mp_drain(buf, send, recv):
        slots = buf.at[pl.ds(0, n_mp - 1)]
        remote(slots, slots, send, recv, partner).wait_send()

    def far_send(at):
        buf, first, rows = far[at]
        slot = buf.at[m, pl.ds(first, rows)]
        remote(slot, slot, f_s.at[at], f_x.at[at], across).start()
        remote(slot, slot, f_s.at[at], f_c.at[at], partner).start()

    def far_pass(at):
        buf, first, rows = far[at]
        slot = buf.at[lax.rem(m + 2, 4), pl.ds(first, rows)]
        remote(slot, slot, f_s.at[at], f_x.at[at], partner).wait_recv()
        remote(slot, slot, f_s.at[at], f_c.at[at], partner).start()

    def far_recv(at):
        buf, first, rows = far[at]
        slots = buf.at[pl.ds(0, 2), pl.ds(first, rows)]
        remote(slots, slots, f_s.at[at], f_c.at[at], partner).wait_recv()

    def far_drain(at):
        buf, first, rows = far[at]
        slots = buf.at[pl.ds(0, 3), pl.ds(first, rows)]
        remote(slots, slots, f_s.at[at], f_c.at[at], partner).wait_send()

    split_row = FIRST_FOLDS * 16
    far = (
        (fq, 0, fq.shape[1]),
        (fg, 0, split_row),
        (fg, split_row, fg.shape[1] - split_row),
        (fd, 0, fd.shape[1]),
    )

    def on_core(which):
        return pl.when(core == which)

    def dp_send(at):
        slot = gat.at[at, lo, hi]
        other = lo + core * (1 - 2 * lo)

        def send(k):
            to_dev = (lax.rem(hi + k, half_dp) * 2 + other, m)
            remote(slot, slot, g_s.at[at], g_r.at[at], to_dev).start()

        for k in range(1, half_dp):
            send(k)
        on_core(1)(lambda: send(0))

    def dp_forward(at):
        @on_core(1)
        def _():
            slots = gat.at[at, 1 - lo]
            remote(slots, slots, g_f.at[at], g_r.at[at], partner).wait_recv()
            remote(slots, slots, g_f.at[at], g_c.at[at], partner).start()

        @on_core(0)
        def _():
            slots = gat.at[at, 0, pl.ds(0, half_dp - 1)]
            remote(slots, slots, g_f.at[at], g_r.at[at], partner).wait_recv()
            for k in range(1, half_dp):
                slot = gat.at[at, lo, lax.rem(hi + k, half_dp)]
                remote(slot, slot, g_f.at[at], g_c.at[at], partner).start()

    def dp_wait(at, first, wait):
        for which in (0, 1):

            @on_core(which)
            def _(which=which):
                slots = gat.at[at, 0, pl.ds(0, half_dp - (1 if which == first else 0))]
                wait(slots)

    def dp_recv(at):
        dp_wait(
            at,
            1,
            lambda slots: remote(slots, slots, g_f.at[at], g_c.at[at], partner).wait_recv(),
        )

    def dp_drain(at):
        def wait(slots):
            remote(slots, slots, g_s.at[at], g_c.at[at], partner).wait_send()
            remote(slots, slots, g_f.at[at], g_c.at[at], partner).wait_send()

        dp_wait(at, 0, wait)

    def gathered(at):
        talls = [gat[at, i % 2, i // 2].astype(F32) for i in range(n_dp)]
        left = jnp.concatenate([t[:pairs] for t in talls], axis=0)
        right = jnp.concatenate([t[pairs:] for t in talls], axis=0)
        return jnp.concatenate([left, right], axis=1)

    def small_send(at, buf):
        @pl.loop(1, n_dp)
        def _(i):
            to_dev = (lax.rem(d + i, n_dp), m)
            remote(buf.at[d], buf.at[d], sm_s.at[at], sm_r.at[at], to_dev).start()

    def small_recv(at, buf):
        slots = buf.at[pl.ds(0, n_dp - 1)]
        remote(slots, slots, sm_s.at[at], sm_r.at[at], partner).wait_recv()

    def small_drain(at, buf):
        slots = buf.at[pl.ds(0, n_dp - 1)]
        remote(slots, slots, sm_s.at[at], sm_r.at[at], partner).wait_send()

    part_rows = tokens // (2 * TOKEN_PARTS)

    def split_hi(mine, body):
        for k in range(half_dp // 2 - 1):
            body(2 * k + (2 - core if mine else 1 + core))

        @pl.when(core == (1 if mine else 0))
        def _():
            body(half_dp - 1)

    def near_slot(i):
        return lax.rem(hi + half_dp - i, half_dp) * 2 + lo

    def far_slot(i):
        return lax.rem(hi + half_dp - i, half_dp) * 2 + 1 - lo

    def split_far(body):
        split_hi(True, lambda i: body(far_slot(i)))

    def split_near(body):
        split_hi(True, lambda i: body(near_slot(i)))

    def rows_of(slot, part, which):
        start = (which * TOKEN_PARTS + part) * part_rows
        return tok.at[slot, pl.ds(pl.multiple_of(start, 16), part_rows)]

    def tok_push(rows, recv, device):
        remote(rows, rows, t_s.at[0], recv, device).start()

    def tok_wait(recv, counts):
        for which in (0, 1):
            if counts[which]:

                @on_core(which)
                def _(which=which):
                    rows = tok.at[0, pl.ds(0, counts[which] * part_rows)]
                    remote(rows, rows, t_s.at[0], recv, partner).wait_recv()

    quarter = half_dp // 2
    counts = (quarter - 1, quarter)

    def tok_start(part):
        rows = rows_of(d, part, side)

        def body(i):
            tok_push(rows, tz_r.at[part], (lax.rem(hi + i, half_dp) * 2 + lo, m))

        split_hi(True, body)

        @on_core(0)
        def _():
            for which in (0, 1):
                tok_push(rows_of(d, part, which), to_r.at[part], beside)

    def tok_own(part):
        tok_wait(to_r.at[part], (2, 0))

        @on_core(0)
        def _():
            for which in (0, 1):
                tok_push(rows_of(far_slot(0), part, which), tl_r.at[0], partner)

    def tok_second(part):
        tok_wait(tz_r.at[part], counts)

        def body(slot):
            rows = rows_of(slot, part, side)
            tok_push(rows, ty_r.at[part], beside)
            tok_push(rows, tl_r.at[0], partner)

        split_near(body)

    def tok_third(part):
        tok_wait(ty_r.at[part], counts)
        split_far(lambda slot: tok_push(rows_of(slot, part, side), tl_r.at[0], partner))

    def tok_near(part):
        split_near(lambda slot: tok_push(rows_of(slot, part, side), tx_r.at[part, 0], across))

    def tok_far(part):
        split_far(lambda slot: tok_push(rows_of(slot, part, side), tx_r.at[part, 1], across))

    def tok_pass_near(part):
        tok_wait(tx_r.at[part, 0], counts)
        split_near(lambda slot: tok_push(rows_of(slot, part, 1 - side), tl_r.at[0], partner))

    def tok_pass_far(part):
        tok_wait(tx_r.at[part, 1], counts)
        split_far(lambda slot: tok_push(rows_of(slot, part, 1 - side), tl_r.at[0], partner))

    def tok_last():
        for which, count in ((0, 2 * quarter), (1, 2 * quarter - 1)):

            @on_core(which)
            def _(count=count):
                slots = tok.at[pl.ds(0, count)]
                remote(slots, slots, t_s.at[0], tl_r.at[0], partner).wait_recv()

    def tok_drain():
        for which, count in ((0, n_dp - 2), (1, n_dp)):

            @on_core(which)
            def _(count=count):
                slots = tok.at[pl.ds(0, count)]
                remote(slots, slots, t_s.at[0], tl_r.at[0], partner).wait_send()

    def token_steps(at):
        steps = {
            "start": tok_start,
            "own": tok_own,
            "second": tok_second,
            "third": tok_third,
            "near": tok_near,
            "far": tok_far,
            "pass": tok_pass_near,
            "last": tok_pass_far,
        }
        for name, part in STEPS.get(at, ()):
            steps[name](part)

    def attend_rows(queries, normed, allowed, weights):
        stacked = head_blocks(queries.astype(F32), width).astype(BF16)
        folded = dot(stacked, weights[1]).astype(BF16)
        scores = dot_nt(folded, normed) * scale
        probs = softmax_rows(scores, allowed)
        mixed = dot(probs.astype(BF16), normed).astype(BF16)
        context = head_pick(dot_nt(mixed, weights[2]), width).astype(BF16)
        return folded, probs, context

    for k in range(chunk):
        image_load(k).wait()
    gain, shift = vector("ig1", ig1_ref), vector("ib1", ib1_ref)
    loads["iw"].wait()
    hats = [
        normalized(xi[k * chunk_rows : (k + 1) * chunk_rows, :].astype(F32))[0].astype(BF16)
        for k in range(chunk)
    ]
    firsts = [i * IMG_LEN for i in range(pairs)]
    image_first = jnp.concatenate([xi[r : r + 1, :].astype(F32) for r in firsts], axis=0)
    first_n = (normalized(image_first)[0] * gain + shift).astype(BF16)
    image_fold = dot(head_blocks(dot_nt(first_n, iw[0]), width).astype(BF16), iw[1])
    shifted = jnp.sum(image_fold * shift, axis=-1, keepdims=True)
    image_fold = image_fold * gain
    group = pairs // chunk
    shape = (group, chunk_rows)
    place = lax.broadcasted_iota(jnp.int32, shape, 1)
    begin = lax.broadcasted_iota(jnp.int32, shape, 0) * IMG_LEN
    inside = jnp.concatenate([(place >= begin) & (place < begin + IMG_LEN)] * heads, axis=0)

    def of_group(rows, k):
        spots = [h * pairs + k * group for h in range(heads)]
        return jnp.concatenate([rows[at : at + group] for at in spots], axis=0)

    image_scores = [
        (dot_nt(of_group(image_fold, k).astype(BF16), hats[k]) + of_group(shifted, k)) * scale
        for k in range(chunk)
    ]
    image_probs = [softmax_rows(scores, inside).astype(BF16) for scores in image_scores]
    image_mixed = [dot(image_probs[k], hats[k]) for k in range(chunk)]
    image_mixed = jnp.concatenate(
        [mixed[h * group : (h + 1) * group] for h in range(heads) for mixed in image_mixed], axis=0
    )
    image_mixed = image_mixed * gain + shift
    image_context = head_pick(dot_nt(image_mixed.astype(BF16), iw[2]), width).astype(BF16)
    loads["io"].wait()
    ar[0, m] = to_tall(dot(image_context, io[...]))

    pl.semaphore_wait(barrier, n_mp - 1 + n_dp - 1)
    mp_send(ar.at[0], ar_s.at[0], ar_r.at[0])

    loads["text"].wait()
    gain_one = vector("tg1", tg1_ref)
    hat_one, factor_one = normalized(xt[...].astype(F32))
    tok[d] = (hat_one * gain_one + vector("tb1", tb1_ref)).astype(BF16)
    token_steps(0)
    seg = vector("seg", seg_ref)
    seg_rows = tokens // 128
    for i in range(seg_rows):
        ids[d, i : i + 1, :] = seg[:, i * 128 : (i + 1) * 128]
    ids[d, seg_rows : seg_rows + 1, 0:pairs] = vector("lab", lab_ref)

    normed = tok[d]
    mine, pick = caption_masks(seg, d * pairs, pairs)
    allowed = jnp.concatenate([mine] * heads, axis=0)
    loads["tw"].wait()
    queries = dot_nt(dot(pick, normed).astype(BF16), tw[0]).astype(BF16)
    folded, probs, context = attend_rows(queries, normed, allowed, tw)
    loads["to"].wait()
    ar[1, m] = to_tall(dot(context, to[...]))
    mp_send(ar.at[1], ar_s.at[1], ar_r.at[1])
    text_last = dot(pick, xt[...])

    def head_rows(blocks):
        rows = [
            jnp.sum(blocks[h * pairs : (h + 1) * pairs], axis=0, keepdims=True)
            for h in range(heads)
        ]
        return jnp.concatenate(rows + [jnp.zeros((8 - heads, tokens), F32)], axis=0)

    def padded(rows, foot):
        foot = jnp.concatenate([foot, jnp.zeros((8, features - tokens), F32)], axis=1)
        return jnp.concatenate([rows, foot], axis=0).astype(BF16)

    no_foot = jnp.zeros((8, tokens), F32)
    prob_rows = head_rows(probs)
    fq[m] = padded(folded.astype(F32), prob_rows)
    prow[d] = stats_pack([prob_rows[h : h + 1] for h in range(heads)])
    token_steps(1)

    def summed(at):
        mp_recv(ar.at[at], ar_s.at[at], ar_r.at[at])
        full = ar[at, 0].astype(F32)
        for i in range(1, n_mp):
            full = full + ar[at, i].astype(F32)
        count = full.shape[0] // 2
        return jnp.concatenate([full[:count], full[count:]], axis=1)

    image_middle = image_first + summed(0)
    gain, shift = vector("ig2", ig2_ref), vector("ib2", ib2_ref)
    image_n2 = (normalized(image_middle)[0] * gain + shift).astype(BF16)
    loads["iu"].wait()
    image_hidden = dot(image_n2, iu[...]) + vector("iub", iub_ref)
    image_active = gelu_parts(image_hidden)[0].astype(BF16)
    loads["id"].wait()
    ar[2, m] = to_tall(dot(image_active, idn[...]))
    mp_send(ar.at[2], ar_s.at[2], ar_r.at[2])
    token_steps(2)

    middle = text_last + summed(1)
    gat[0, lo, hi] = to_tall(middle)
    gain_two, shift_two = vector("tg2", tg2_ref), vector("tb2", tb2_ref)
    hat_two, factor_two = normalized(middle)
    normed_two = (hat_two * gain_two + shift_two).astype(BF16)
    loads["tu"].wait()
    up_shift = vector("tub", tub_ref)
    active, slope = gelu_parts(dot(normed_two, tu[...]) + up_shift)
    loads["td"].wait()
    ar[3, m] = to_tall(dot(active.astype(BF16), td[...]))
    mp_send(ar.at[3], ar_s.at[3], ar_r.at[3])
    token_steps(3)

    gat[1, lo, hi] = to_tall(unit(image_middle + summed(2)))
    dp_send(1)
    gat[2, lo, hi] = to_tall(middle + summed(3))
    dp_send(2)
    far_send(0)

    token_steps(4)
    dp_forward(1)
    token_steps(9)
    dp_forward(2)
    dp_send(0)
    small_send(0, ids)
    far_pass(0)
    token_steps(5)
    dp_recv(1)
    image_low = gathered(1).astype(BF16)
    own_labels = column_of(ids[d, seg_rows : seg_rows + 1, :], pairs)
    dp_recv(2)


    def embedded(rows):
        shrink = lax.rsqrt(jnp.sum(rows * rows, axis=-1, keepdims=True) + 1e-06)
        text_unit = rows * shrink
        return shrink, text_unit, 64.0 * dot_nt(text_unit.astype(BF16), image_low)

    def final_grad(shrink, text_unit, logits, labels):
        lanes = lax.broadcasted_iota(jnp.int32, logits.shape, 1)
        onehot = (labels == lanes).astype(F32)
        top = jnp.max(logits, axis=1, keepdims=True)
        lse = top + jnp.log(jnp.sum(jnp.exp(logits - top), axis=1, keepdims=True))
        grads = 0.5 * (jnp.exp(logits - lse) + jnp.exp(logits - col_lse)) - onehot
        grads = 64.0 * dot(grads.astype(BF16), image_low)
        along = jnp.sum(text_unit * grads, axis=-1, keepdims=True)
        positive = jnp.sum(logits * onehot, axis=1, keepdims=True)
        return shrink * (grads - text_unit * along), lse, positive

    shrink_all, unit_all, logits = embedded(gathered(2))
    col_top = jnp.max(logits, axis=0, keepdims=True)
    col_lse = col_top + jnp.log(jnp.sum(jnp.exp(logits - col_top), axis=0, keepdims=True))
    grad_final, own_lse, positive = final_grad(*embedded(from_tall(gat[2, lo, hi])), own_labels)
    grad_hidden = (dot_nt(grad_final.astype(BF16), td[...]) * slope).astype(BF16)
    ar[4, m] = to_tall(dot_nt(grad_hidden, tu[...]))
    mp_send(ar.at[4], ar_s.at[4], ar_r.at[4])
    small_send(1, prow)

    token_steps(6)
    lanes = lax.broadcasted_iota(jnp.int32, (pairs, total), 1)
    mine_first = lax.broadcasted_iota(jnp.int32, (pairs, total), 0) + d * pairs
    own_col = jnp.sum(jnp.where(lanes == mine_first, col_lse, 0.0), axis=1, keepdims=True)
    pair_loss = 0.5 * (own_lse + own_col) - positive
    shape = (pairs, loss_o.shape[1])
    diagonal = lax.broadcasted_iota(jnp.int32, shape, 0) == lax.broadcasted_iota(
        jnp.int32, shape, 1
    )
    loss_o[...] = jnp.sum(jnp.where(diagonal, pair_loss, 0.0), axis=0, keepdims=True)
    small_recv(0, ids)
    labels = jnp.concatenate(
        [column_of(ids[i, seg_rows : seg_rows + 1, :], pairs) for i in range(n_dp)], axis=0
    )
    fin_all = final_grad(shrink_all, unit_all, logits, labels)[0].astype(BF16)
    dp_forward(0)

    def spread(slots, ref, at):
        parts = []
        for i in slots:
            foot = ref[i, at : at + 8, 0:tokens].astype(F32)
            for h in range(heads):
                parts.append(jnp.where(mine, foot[h : h + 1], 0.0))
            parts.append(jnp.zeros((8, tokens), F32))
        return jnp.concatenate(parts, axis=0).astype(BF16)

    def placed(count):
        spots = jnp.concatenate([pick.astype(F32), jnp.zeros((8, tokens), F32)], axis=0)
        return jnp.concatenate([spots] * count, axis=0).astype(BF16)

    own_probs = spread([m], fq, pairs * heads)
    own_spots = placed(1)

    grad_n2 = summed(4)
    grad_middle = grad_final + norm_back(grad_n2, hat_two, factor_two, gain_two)
    gat[3, lo, hi] = to_tall(grad_middle)
    dp_send(3)
    middle_low = grad_middle.astype(BF16)
    grad_context = dot_nt(middle_low, to[...]).astype(BF16)
    grad_folded = dot(head_blocks(grad_context.astype(F32), width).astype(BF16), tw[2])
    fg[m] = padded(grad_folded, no_foot)
    far_send(1)
    grad_probs = dot_nt(grad_folded.astype(BF16), normed)
    grad_scores = probs * (grad_probs - jnp.sum(grad_probs * probs, axis=-1, keepdims=True))
    scaled = grad_scores * scale
    score_rows = head_rows(scaled)
    mixed_back = dot(scaled.astype(BF16), normed).astype(BF16)
    grad_queries = head_pick(dot_nt(mixed_back, tw[1]), width).astype(BF16)
    fd[m] = padded(dot(grad_queries, tw[0]), score_rows)

    part = dot_tn(spread([m], fd, pairs), fq[m])
    part = part + dot_tn(own_probs, fg[m])
    part = part + dot_tn(own_spots, fd[m])
    stm[m] = stats_pack(
        [jnp.sum(part * hat_one, axis=0, keepdims=True), jnp.sum(part, axis=0, keepdims=True)]
    )
    mp_send(stm, st_s.at[0], st_r.at[0])
    far_send(2)
    far_send(3)
    stats_two = [
        jnp.sum(grad_n2 * hat_two, axis=0, keepdims=True),
        jnp.sum(grad_n2, axis=0, keepdims=True),
    ]
    drow[d] = stats_pack([score_rows[h : h + 1] for h in range(heads)] + stats_two, 16).astype(BF16)
    small_send(3, drow)

    token_steps(7)
    dp_recv(0)
    n2_all = (normalized(gathered(0))[0] * gain_two + shift_two).astype(BF16)
    act_all, slope_all = gelu_parts(dot(n2_all, tu[...]) + up_shift)
    gh_all = (dot_nt(fin_all, td[...]) * slope_all).astype(BF16)
    up_bias = jnp.sum(gh_all.astype(F32), axis=0, keepdims=True)
    up_o[...] = dot_tn(n2_all, gh_all)
    down_o[...] = dot_tn(act_all.astype(BF16), fin_all)
    mp_recv(stm, st_s.at[0], st_r.at[0])
    one = stm[0]
    for i in range(1, n_mp):
        one = one + stm[i]
    std[d] = stats_pack(stats_unpack(one, 2, features), 16).astype(BF16)
    small_send(2, std)
    far_pass(1)
    far_pass(2)
    dp_forward(3)
    far_pass(3)
    token_steps(8)

    everyone = list(range(n_mp))

    def flat(ref):
        return ref[...].reshape(n_mp * ref.shape[1], features)

    for at in range(3):
        far_recv(at)
    from_probs = dot_tn(spread(everyone, fq, pairs * heads), flat(fg))
    far_recv(3)
    grad_normed = dot_tn(spread(everyone, fd, pairs), flat(fq)) + from_probs
    grad_normed = grad_normed + dot_tn(placed(n_mp), flat(fd))
    text_grad = norm_back(grad_normed, hat_one, factor_one, gain_one)
    tg_o[...] = text_grad + dot_tn(pick, middle_low)

    small_recv(1, prow)
    tok_last()
    twice = 2 * pairs
    pair_masks = []
    for j in range(half_dp):
        seg = jnp.concatenate(
            [ids[i, k : k + 1, :] for i in (2 * j, 2 * j + 1) for k in range(seg_rows)], axis=1
        )
        pair_masks.append(caption_masks(seg, j * twice, twice))

    def pair_at(j):
        return slice(j * twice, (j + 1) * twice)

    def pair_rows(j):
        return tok[2 * j : 2 * j + 2].reshape(2 * tokens, features)

    def spread_pair(j, rows, h):
        values = jnp.concatenate([rows[2 * j][h], rows[2 * j + 1][h]], axis=1)
        return jnp.where(pair_masks[j][0], values, 0.0).astype(BF16)

    early_rows = [stats_unpack(prow[i], heads, tokens) for i in range(n_dp)]
    for j in range(half_dp):
        parts = [spread_pair(j, early_rows, h) for h in range(heads)] + [pair_masks[j][1]]
        mixed = dot(jnp.concatenate(parts, axis=0), pair_rows(j)).astype(BF16)
        for h in range(heads):
            xv_o[h, pair_at(j), :] = mixed[h * twice : (h + 1) * twice]
        nsel_o[pair_at(j), :] = mixed[heads * twice :]

    small_recv(3, drow)
    late_rows = [stats_unpack(drow[i].astype(F32), heads, tokens) for i in range(n_dp)]
    for j in range(half_dp):
        parts = [spread_pair(j, late_rows, h) for h in range(heads)]
        mixed = dot(jnp.concatenate(parts, axis=0), pair_rows(j)).astype(BF16)
        for h in range(heads):
            xk_o[h, pair_at(j), :] = mixed[h * twice : (h + 1) * twice]
    dp_recv(3)
    mid_o[...] = gathered(3).astype(BF16)

    small_recv(2, std)
    stats = std[0].astype(F32)
    for i in range(1, n_dp):
        stats = stats + std[i].astype(F32)
    late = drow[0].astype(F32)
    for i in range(1, n_dp):
        late = late + drow[i].astype(F32)
    rows = stats_unpack(stats, 2, features)
    rows += stats_unpack(late[heads * seg_rows :], 2, features)
    vec_o[...] = jnp.concatenate(rows + [up_bias, jnp.zeros((3, features), F32)], axis=0)

    for at in range(ar.shape[0]):
        mp_drain(ar.at[at], ar_s.at[at], ar_r.at[at])
    mp_drain(stm, st_s.at[0], st_r.at[0])
    for at in range(len(far)):
        far_drain(at)
    for at in range(gat.shape[0]):
        dp_drain(at)
    for at, buf in enumerate((ids, prow, std, drow)):
        small_drain(at, buf)
    tok_drain()


def weights_kernel(
    up,
    down,
    tw,
    to,
    mid,
    nsel,
    xk,
    xv,
    tg,
    vec,
    loss,
    tg_out,
    qkv_out,
    out_out,
    up_out,
    down_out,
    loss_out,
    g1_out,
    b1_out,
    g2_out,
    b2_out,
    ub_out,
    qkv_buf,
    out_buf,
    sem,
    *vec_bufs,
):
    heads, total, features = xk.shape
    width = to.shape[0]
    started = []

    def ship(src, dst):
        copy = pltpu.make_async_copy(src, dst, sem.at[len(started)])
        copy.start()
        started.append(copy)

    for src, dst in ((up, up_out), (down, down_out)):
        step = src.shape[0] // SHIP_PARTS
        for at in range(0, src.shape[0], step):
            rows = pl.ds(at, step)
            ship(src.at[rows], dst.at[rows])
    ship(tg, tg_out)
    for at, dst in enumerate((g1_out, b1_out, g2_out, b2_out, ub_out)):
        vec_bufs[at][...] = vec[at, :]
        ship(vec_bufs[at], dst)
    vec_bufs[5][...] = loss[0, 0 : loss_out.shape[0]]
    ship(vec_bufs[5], loss_out)
    flat_k = xk[...].reshape(heads * total, features)
    flat_v = xv[...].reshape(heads * total, features)
    queries = dot_nt(nsel[...], tw[0])
    grad_context = dot_nt(mid[...], to[...])
    for at, rows, flat in ((1, queries, flat_k), (2, grad_context, flat_v)):
        stacked = head_blocks(rows.astype(BF16).astype(F32), width).astype(BF16)
        qkv_buf[at] = dot_tn(stacked, flat)
        ship(qkv_buf.at[at], qkv_out.at[at])
    grad_queries = head_pick(dot_nt(flat_k, tw[1]), width).astype(BF16)
    qkv_buf[0] = dot_tn(grad_queries, nsel[...])
    ship(qkv_buf.at[0], qkv_out.at[0])
    context = head_pick(dot_nt(flat_v, tw[2]), width).astype(BF16)
    out_buf[...] = dot_tn(context, mid[...])
    ship(out_buf, out_out)
    for copy in started:
        copy.wait()


def kernel_device(
    n_dp,
    n_mp,
    text_tokens,
    segment_ids,
    labels,
    image_tokens,
    image_gain_one,
    image_bias_one,
    image_qkv,
    image_out,
    image_gain_two,
    image_bias_two,
    image_up,
    image_up_bias,
    image_down,
    text_gain_one,
    text_bias_one,
    text_qkv,
    text_out,
    text_gain_two,
    text_bias_two,
    text_up,
    text_up_bias,
    text_down,
):
    pairs = labels.shape[0]
    tokens, features = text_tokens.shape
    width = text_out.shape[0]
    hidden = text_up.shape[1]
    heads = width // HEAD
    total = n_dp * pairs
    half_dp = n_dp // 2
    vmem = pltpu.VMEM
    whole = pl.BlockSpec(memory_space=pltpu.VMEM)
    anywhere = pl.BlockSpec(memory_space=pl.ANY)

    def sems(*shape):
        return pltpu.SemaphoreType.DMA(shape)

    outs = [
        ((features, hidden), F32),
        ((hidden, features), F32),
        ((3, width, features), BF16),
        ((width, features), BF16),
        ((total, features), BF16),
        ((total, features), BF16),
        ((heads, total, features), BF16),
        ((heads, total, features), BF16),
        ((tokens, features), F32),
        ((8, features), F32),
        ((1, 128), F32),
    ]
    tall = (2 * pairs, features // 2)
    fold_rows = heads * pairs + 8
    vectors = (
        segment_ids,
        labels,
        image_gain_one,
        image_bias_one,
        image_gain_two,
        image_bias_two,
        image_up_bias,
        text_gain_one,
        text_bias_one,
        text_gain_two,
        text_bias_two,
        text_up_bias,
    )
    operands = (
        text_tokens,
        image_tokens,
        jnp.transpose(image_qkv, (1, 2, 0)),
        image_out,
        image_up,
        image_down,
        jnp.transpose(text_qkv, (1, 2, 0)),
        text_out,
        text_up,
        text_down,
    ) + vectors
    factors = pl.pallas_call(
        functools.partial(step_kernel, (n_dp, n_mp, pairs, tokens, features, width)),
        out_shape=[vmem(shape, dtype) for shape, dtype in outs],
        in_specs=[anywhere] * len(operands),
        out_specs=[whole] * len(outs),
        scratch_shapes=[
            vmem(text_tokens.shape, BF16),
            vmem(image_tokens.shape, BF16),
            vmem((3, width, features), BF16),
            vmem(image_out.shape, BF16),
            vmem(image_up.shape, BF16),
            vmem(image_down.shape, BF16),
            vmem(text_up.shape, BF16),
            vmem(text_down.shape, BF16),
        ]
        + [vmem(array.shape, array.dtype) for array in vectors]
        + [
            vmem((n_dp, tokens, features), BF16),
            vmem((n_dp, 8, 128), jnp.int32),
            vmem((n_dp, 8, 128), F32),
            vmem((n_dp, 32, 128), BF16),
            vmem((n_mp, 16, 128), F32),
            vmem((n_dp, 16, 128), BF16),
            vmem((5, n_mp) + tall, BF16),
            vmem((4, 2, half_dp) + tall, BF16),
            vmem((n_mp, fold_rows, features), BF16),
            vmem((n_mp, fold_rows, features), BF16),
            vmem((n_mp, pairs + 8, features), BF16),
            sems(22),
            sems(pairs // 8),
            sems(1),
            sems(TOKEN_PARTS),
            sems(TOKEN_PARTS),
            sems(TOKEN_PARTS),
            sems(TOKEN_PARTS, 2),
            sems(1),
            sems(5),
            sems(5),
            sems(4),
            sems(4),
            sems(4),
            sems(4),
            sems(4),
            sems(4),
            sems(4),
            sems(1),
            sems(1),
            sems(4),
            sems(4),
        ],
        compiler_params=pltpu.CompilerParams(
            collective_id=0, has_side_effects=True, vmem_limit_bytes=48 * 2**20
        ),
        name="step",
    )(*[pltpu.with_memory_space_constraint(operand, pltpu.HBM) for operand in operands])
    vector = jax.ShapeDtypeStruct((features,), F32)
    results = pl.pallas_call(
        weights_kernel,
        out_shape=[
            jax.ShapeDtypeStruct((tokens, features), F32),
            jax.ShapeDtypeStruct((3, width, features), F32),
            jax.ShapeDtypeStruct((width, features), F32),
            jax.ShapeDtypeStruct((features, hidden), F32),
            jax.ShapeDtypeStruct((hidden, features), F32),
            jax.ShapeDtypeStruct((pairs,), F32),
            vector,
            vector,
            vector,
            vector,
            jax.ShapeDtypeStruct((hidden,), F32),
        ],
        in_specs=[whole] * len(outs),
        out_specs=[anywhere] * 11,
        scratch_shapes=[
            vmem((3, width, features), F32),
            vmem((width, features), F32),
            sems(2 * SHIP_PARTS + 11),
        ]
        + [vmem((features,), F32)] * 4
        + [vmem((hidden,), F32), vmem((pairs,), F32)],
        compiler_params=pltpu.CompilerParams(vmem_limit_bytes=32 * 2**20),
        name="weights",
    )(*[pltpu.with_memory_space_constraint(factor, pltpu.VMEM) for factor in factors])
    text_grad, qkv, out, up, down, loss, gain_one, bias_one, gain_two, bias_two, up_bias = results
    return (
        loss,
        text_grad,
        gain_one,
        bias_one,
        jnp.transpose(qkv, (2, 0, 1)),
        out,
        gain_two,
        bias_two,
        up,
        up_bias,
        down,
    )


def solution(mesh):
    placed = (
        P("dp", None),
        P("dp"),
        P("dp"),
        P("dp", None),
        P(),
        P(),
        P(None, None, "mp"),
        P("mp", None),
        P(),
        P(),
        P(None, "mp"),
        P("mp"),
        P("mp", None),
        P(),
        P(),
        P(None, None, "mp"),
        P("mp", None),
        P(),
        P(),
        P(None, "mp"),
        P("mp"),
        P("mp", None),
    )
    n_dp, n_mp = mesh.shape["dp"], mesh.shape["mp"]
    body = plain_device
    if n_dp <= 16 and n_dp % 4 == 0 and n_mp == 4:
        body = functools.partial(kernel_device, n_dp, n_mp)
    return jax.shard_map(
        body,
        mesh=mesh,
        in_specs=placed,
        out_specs=(
            P("dp"),
            P("dp", None),
            P(),
            P(),
            P(None, None, "mp"),
            P("mp", None),
            P(),
            P(),
            P(None, "mp"),
            P("mp"),
            P("mp", None),
        ),
        check_vma=False,
    )
```

```python
import functools

import jax
import jax.numpy as jnp
from jax import lax
from jax.experimental import pallas as pl
from jax.experimental.pallas import tpu as pltpu
from jax.sharding import PartitionSpec as P

HEAD = 64
IMG_LEN = 50
F32 = jnp.float32
BF16 = jnp.bfloat16


def dot(a, b):
    return lax.dot_general(a, b, (((1,), (0,)), ((), ())), preferred_element_type=F32)


def dot_nt(a, b):
    return lax.dot_general(a, b, (((1,), (1,)), ((), ())), preferred_element_type=F32)


def dot_tn(a, b):
    return lax.dot_general(a, b, (((0,), (0,)), ((), ())), preferred_element_type=F32)


def normalized(values):
    center = values - jnp.mean(values, axis=-1, keepdims=True)
    factor = lax.rsqrt(jnp.mean(center * center, axis=-1, keepdims=True) + 1e-05)
    return center * factor, factor


def norm_back(grad, hat, factor, gain):
    scaled = grad * gain
    along = jnp.mean(scaled * hat, axis=-1, keepdims=True)
    return factor * (scaled - jnp.mean(scaled, axis=-1, keepdims=True) - hat * along)


def unit(rows):
    return rows * lax.rsqrt(jnp.sum(rows * rows, axis=-1, keepdims=True) + 1e-06)


def gelu_parts(hidden):
    cdf = 0.5 * (1.0 + lax.erf(hidden * 0.7071067811865476))
    slope = cdf + hidden * jnp.exp(-0.5 * hidden * hidden) * 0.3989422804014327
    return hidden * cdf, slope


def head_blocks(rows, width):
    lanes = lax.broadcasted_iota(jnp.int32, (1, width), 1)
    return jnp.concatenate(
        [
            jnp.where((lanes >= h * HEAD) & (lanes < (h + 1) * HEAD), rows, 0.0)
            for h in range(width // HEAD)
        ],
        axis=0,
    )


def head_pick(blocks, width):
    heads = width // HEAD
    count = blocks.shape[0] // heads
    lanes = lax.broadcasted_iota(jnp.int32, (1, width), 1)
    total = jnp.zeros((count, width), F32)
    for h in range(heads):
        own = (lanes >= h * HEAD) & (lanes < (h + 1) * HEAD)
        total = total + jnp.where(own, blocks[h * count : (h + 1) * count], 0.0)
    return total


def attend(normed_rows, normed, allowed, weights):
    width = weights.shape[1]
    heads = width // HEAD
    queries = dot_nt(normed_rows, weights[0]).astype(BF16)
    folded = dot(head_blocks(queries.astype(F32), width).astype(BF16), weights[1]).astype(BF16)
    scores = dot_nt(folded, normed) * HEAD**-0.5
    scores = jnp.where(jnp.concatenate([allowed] * heads, axis=0), scores, -1e30)
    expo = jnp.exp(scores - jnp.max(scores, axis=-1, keepdims=True))
    probs = expo / jnp.sum(expo, axis=-1, keepdims=True)
    mixed = dot(probs.astype(BF16), normed).astype(BF16)
    context = head_pick(dot_nt(mixed, weights[2]), width).astype(BF16)
    return queries, folded, probs, mixed, context


def plain_device(
    text_tokens,
    segment_ids,
    labels,
    image_tokens,
    image_gain_one,
    image_bias_one,
    image_qkv,
    image_out,
    image_gain_two,
    image_bias_two,
    image_up,
    image_up_bias,
    image_down,
    text_gain_one,
    text_bias_one,
    text_qkv,
    text_out,
    text_gain_two,
    text_bias_two,
    text_up,
    text_up_bias,
    text_down,
):
    rank = lax.axis_index("dp")
    pairs = labels.shape[0]
    tokens = segment_ids.shape[0]
    width = text_out.shape[0]
    heads = width // HEAD
    features = text_tokens.shape[1]
    image_weights = jnp.transpose(image_qkv, (1, 2, 0))
    text_weights = jnp.transpose(text_qkv, (1, 2, 0))

    image_x = image_tokens.astype(F32)
    image_n = (normalized(image_x)[0] * image_gain_one + image_bias_one).astype(BF16)
    image_first = image_x.reshape(pairs, IMG_LEN, features)[:, 0]
    first_n = (normalized(image_first)[0] * image_gain_one + image_bias_one).astype(BF16)
    owner = lax.broadcasted_iota(jnp.int32, (pairs, pairs * IMG_LEN), 0)
    place = lax.broadcasted_iota(jnp.int32, (pairs, pairs * IMG_LEN), 1)
    inside = (place >= owner * IMG_LEN) & (place < (owner + 1) * IMG_LEN)
    image_context = attend(first_n, image_n, inside, image_weights)[4]

    text_x = text_tokens.astype(F32)
    hat_one, factor_one = normalized(text_x)
    normed = (hat_one * text_gain_one + text_bias_one).astype(BF16)
    captions = rank * pairs + jnp.arange(pairs)
    mine = segment_ids[None, :] == captions[:, None]
    spot = lax.broadcasted_iota(jnp.int32, (pairs, tokens), 1)
    last = jnp.max(jnp.where(mine, spot, -1), axis=1, keepdims=True)
    pick = (spot == last).astype(BF16)
    normed_last = dot(pick, normed).astype(BF16)
    queries, folded, probs, mixed, context = attend(normed_last, normed, mine, text_weights)

    attended = jnp.concatenate([dot(image_context, image_out), dot(context, text_out)], axis=0)
    attended = lax.psum(attended.astype(BF16), "mp").astype(F32)
    middle = jnp.concatenate([image_first, dot(pick, text_tokens)], axis=0) + attended
    hat_two, factor_two = normalized(middle)
    image_n2 = (hat_two[:pairs] * image_gain_two + image_bias_two).astype(BF16)
    normed_two = (hat_two[pairs:] * text_gain_two + text_bias_two).astype(BF16)
    image_active = gelu_parts(dot(image_n2, image_up) + image_up_bias)[0].astype(BF16)
    active, slope = gelu_parts(dot(normed_two, text_up) + text_up_bias)
    active = active.astype(BF16)
    branch = jnp.concatenate([dot(image_active, image_down), dot(active, text_down)], axis=0)
    final = middle + lax.psum(branch.astype(BF16), "mp").astype(F32)

    everyone = lax.all_gather(final.astype(BF16), "dp").astype(F32)
    total = everyone.shape[0] * pairs
    image_low = unit(everyone[:, :pairs].reshape(total, features)).astype(BF16)
    pooled = final[pairs:]
    text_low = unit(everyone[:, pairs:].reshape(total, features)).astype(BF16)
    logits = 64.0 * dot_nt(text_low, image_low)
    column_lse = jax.nn.logsumexp(logits, axis=0)
    own = lax.dynamic_slice_in_dim(logits, rank * pairs, pairs, axis=0)
    row_lse = jax.nn.logsumexp(own, axis=1)
    own_columns = lax.dynamic_slice_in_dim(column_lse, rank * pairs, pairs)
    onehot = (labels[:, None] == jnp.arange(total)[None, :]).astype(F32)
    pair_loss = 0.5 * (row_lse + own_columns) - jnp.sum(own * onehot, axis=1)
    grad_logits = (
        0.5 * (jnp.exp(own - row_lse[:, None]) + jnp.exp(own - column_lse[None, :])) - onehot
    )
    grad_embed = 64.0 * dot(grad_logits.astype(BF16), image_low)
    scale = lax.rsqrt(jnp.sum(pooled * pooled, axis=-1, keepdims=True) + 1e-06)
    text_unit = pooled * scale
    grad_final = scale * (
        grad_embed - text_unit * jnp.sum(text_unit * grad_embed, axis=-1, keepdims=True)
    )

    final_low = grad_final.astype(BF16)
    grad_hidden = (dot_nt(final_low, text_down) * slope).astype(BF16)
    grad_normed_two = lax.psum(dot_nt(grad_hidden, text_up).astype(BF16), "mp").astype(F32)
    hat_two = hat_two[pairs:]
    grad_middle = grad_final + norm_back(grad_normed_two, hat_two, factor_two[pairs:], text_gain_two)
    middle_low = grad_middle.astype(BF16)
    grad_context = dot_nt(middle_low, text_out).astype(BF16)
    grad_folded = dot(head_blocks(grad_context.astype(F32), width).astype(BF16), text_weights[2])
    grad_folded = grad_folded.astype(BF16)
    grad_probs = dot_nt(grad_folded, normed)
    grad_scores = probs * (grad_probs - jnp.sum(grad_probs * probs, axis=-1, keepdims=True))
    grad_scores = (grad_scores * HEAD**-0.5).astype(BF16)
    mixed_back = dot(grad_scores, normed).astype(BF16)
    grad_queries = head_pick(dot_nt(mixed_back, text_weights[1]), width).astype(BF16)
    grad_normed = dot_tn(grad_scores, folded) + dot_tn(probs.astype(BF16), grad_folded)
    grad_normed = grad_normed + dot_tn(pick, dot(grad_queries, text_weights[0]).astype(BF16))
    grad_normed = lax.psum(grad_normed.astype(BF16), "mp").astype(F32)
    text_grad = norm_back(grad_normed, hat_one, factor_one, text_gain_one)
    text_grad = text_grad + dot_tn(pick, middle_low)

    vectors = jnp.concatenate(
        [
            jnp.sum(grad_normed * hat_one, axis=0),
            jnp.sum(grad_normed, axis=0),
            jnp.sum(grad_normed_two * hat_two, axis=0),
            jnp.sum(grad_normed_two, axis=0),
            jnp.sum(grad_hidden.astype(F32), axis=0),
        ]
    )
    vectors = jnp.sum(lax.all_gather(vectors, "dp"), axis=0)
    cuts = [features, 2 * features, 3 * features, 4 * features]
    gain_one, bias_one, gain_two, bias_two, up_bias = jnp.split(vectors, cuts)

    def by_head(blocks):
        return [blocks[h * pairs : (h + 1) * pairs] for h in range(heads)]

    pieces = [active, final_low, normed_two, grad_hidden, context, middle_low, normed_last]
    pieces += [grad_queries, queries, grad_context] + by_head(mixed_back) + by_head(mixed)
    sent = lax.all_gather(jnp.concatenate(pieces, axis=1), "dp").reshape(total, -1)
    got = []
    at = 0
    for piece in pieces:
        got.append(sent[:, at : at + piece.shape[1]])
        at += piece.shape[1]
    active, final_low, normed_two, grad_hidden, context, middle_low, normed_last = got[:7]
    grad_queries, queries, grad_context = got[7:10]
    mixed_back = got[10 : 10 + heads]
    mixed = got[10 + heads :]

    def per_head(rows, blocks):
        return jnp.concatenate(
            [dot_tn(rows[:, h * HEAD : (h + 1) * HEAD], blocks[h]) for h in range(heads)], axis=0
        )

    grad_qkv = jnp.stack(
        [
            dot_tn(grad_queries, normed_last),
            per_head(queries, mixed_back),
            per_head(grad_context, mixed),
        ]
    )
    return (
        pair_loss,
        text_grad,
        gain_one,
        bias_one,
        jnp.transpose(grad_qkv, (2, 0, 1)),
        dot_tn(context, middle_low),
        gain_two,
        bias_two,
        dot_tn(normed_two, grad_hidden),
        up_bias,
        dot_tn(active, final_low),
    )


MESH = pl.DeviceIdType.MESH
TOKEN_PARTS = 2
SHIP_PARTS = 1
FIRST_FOLDS = 2
STEPS = {
    0: (("start", 0), ("start", 1)),
    3: (("second", 0), ("near", 0), ("own", 0)),
    4: (("second", 1), ("near", 1), ("own", 1)),
    9: (("pass", 0),),
    6: (("pass", 1),),
    7: (("third", 0), ("third", 1)),
    8: (("fourth", 0), ("fourth", 1)),
}


def to_tall(rows):
    half = rows.shape[1] // 2
    return jnp.concatenate([rows[:, :half], rows[:, half:]], axis=0).astype(BF16)


def from_tall(tall):
    count = tall.shape[0] // 2
    wide = tall.astype(F32)
    return jnp.concatenate([wide[:count], wide[count:]], axis=1)


def column_of(row, count):
    shape = (count, row.shape[1])
    same = lax.broadcasted_iota(jnp.int32, shape, 0) == lax.broadcasted_iota(jnp.int32, shape, 1)
    return jnp.sum(jnp.where(same, row, 0), axis=1, keepdims=True)


def caption_masks(seg, first, count):
    captions = first + lax.broadcasted_iota(jnp.int32, (count, seg.shape[1]), 0)
    mine = seg == captions
    spot = lax.broadcasted_iota(jnp.int32, (count, seg.shape[1]), 1)
    last = jnp.max(jnp.where(mine, spot, -1), axis=1, keepdims=True)
    return mine, (spot == last).astype(F32).astype(BF16)


def softmax_rows(scores, allowed):
    scores = jnp.where(allowed, scores, -1e30)
    expo = jnp.exp(scores - jnp.max(scores, axis=-1, keepdims=True))
    return expo / jnp.sum(expo, axis=-1, keepdims=True)


def stats_pack(rows, multiple=8):
    pieces = []
    for row in rows:
        pieces += [row[:, at : at + 128] for at in range(0, row.shape[1], 128)]
    if len(pieces) % multiple:
        pieces.append(jnp.zeros((-len(pieces) % multiple, 128), F32))
    return jnp.concatenate(pieces, axis=0)


def stats_unpack(packed, count, features):
    per = features // 128
    return [
        jnp.concatenate([packed[at * per + i : at * per + i + 1] for i in range(per)], axis=1)
        for at in range(count)
    ]


def step_kernel(
    sizes,
    text_hbm,
    image_hbm,
    iw_hbm,
    io_hbm,
    iu_hbm,
    id_hbm,
    tw_hbm,
    to_hbm,
    tu_hbm,
    td_hbm,
    seg_hbm,
    lab_hbm,
    ig1_hbm,
    ib1_hbm,
    ig2_hbm,
    ib2_hbm,
    iub_hbm,
    tg1_hbm,
    tb1_hbm,
    tg2_hbm,
    tb2_hbm,
    tub_hbm,
    up_o,
    down_o,
    tw,
    to,
    mid_o,
    nsel_o,
    xk_o,
    xv_o,
    tg_o,
    vec_o,
    loss_o,
    xt,
    xi,
    iw,
    io,
    iu,
    idn,
    tu,
    td,
    seg_ref,
    lab_ref,
    ig1_ref,
    ib1_ref,
    ig2_ref,
    ib2_ref,
    iub_ref,
    tg1_ref,
    tb1_ref,
    tg2_ref,
    tb2_ref,
    tub_ref,
    tok,
    ids,
    prow,
    drow,
    stm,
    std,
    ar,
    gat,
    fq,
    fg,
    fd,
    load_sem,
    img_sem,
    t_s,
    tz_r,
    ty_r,
    to_r,
    tx_r,
    tw_r,
    tl_r,
    ar_s,
    ar_r,
    g_s,
    g_r,
    g_f,
    g_c,
    f_s,
    f_x,
    f_c,
    st_s,
    st_r,
    sm_s,
    sm_r,
):
    n_dp, n_mp, pairs, tokens, features, width = sizes
    heads = width // HEAD
    half_dp = n_dp // 2
    total = n_dp * pairs
    scale = HEAD**-0.5
    d = lax.axis_index("dp")
    m = lax.axis_index("mp")
    core = lax.rem(m, 2)
    side = lax.div(m, 2)
    hi = lax.div(d, 2)
    lo = lax.rem(d, 2)
    partner = (d, m + 1 - 2 * core)
    across = (d, lax.rem(m + 2, 4))
    beside = (hi * 2 + 1 - lo, m)

    chunk = img_sem.shape[0]
    chunk_rows = xi.shape[0] // chunk

    def image_load(k):
        rows = pl.ds(k * chunk_rows, chunk_rows)
        return pltpu.make_async_copy(image_hbm.at[rows], xi.at[rows], img_sem.at[k])

    loads = {}

    def load(name, src, dst):
        loads[name] = pltpu.make_async_copy(src, dst, load_sem.at[len(loads)])
        loads[name].start()

    for k in range(chunk):
        image_load(k).start()
    load("ig1", ig1_hbm, ig1_ref)
    load("ib1", ib1_hbm, ib1_ref)
    load("iw", iw_hbm, iw)
    load("io", io_hbm, io)

    def vector(name, ref):
        loads[name].wait()
        return ref[...].reshape(1, ref.shape[0])

    barrier = pltpu.get_barrier_semaphore()
    for i in range(1, n_mp):
        pl.semaphore_signal(
            barrier, inc=1, device_id=(d, lax.rem(m + i, n_mp)), device_id_type=MESH
        )

    @pl.loop(1, n_dp)
    def _(i):
        pl.semaphore_signal(
            barrier, inc=1, device_id=(lax.rem(d + i, n_dp), m), device_id_type=MESH
        )

    load("text", text_hbm, xt)
    load("tg1", tg1_hbm, tg1_ref)
    load("tb1", tb1_hbm, tb1_ref)
    load("seg", seg_hbm, seg_ref)
    load("lab", lab_hbm, lab_ref)
    load("tw", tw_hbm, tw)
    load("to", to_hbm, to)
    load("ig2", ig2_hbm, ig2_ref)
    load("ib2", ib2_hbm, ib2_ref)
    load("iub", iub_hbm, iub_ref)
    load("iu", iu_hbm, iu)
    load("id", id_hbm, idn)
    load("tg2", tg2_hbm, tg2_ref)
    load("tb2", tb2_hbm, tb2_ref)
    load("tub", tub_hbm, tub_ref)
    load("tu", tu_hbm, tu)
    load("td", td_hbm, td)

    def remote(src, dst, send, recv, device):
        return pltpu.make_async_remote_copy(
            src_ref=src,
            dst_ref=dst,
            send_sem=send,
            recv_sem=recv,
            device_id=device,
            device_id_type=MESH,
        )

    def mp_send(buf, send, recv):
        for i in range(1, n_mp):
            remote(buf.at[m], buf.at[m], send, recv, (d, lax.rem(m + i, n_mp))).start()

    def mp_recv(buf, send, recv):
        slots = buf.at[pl.ds(0, n_mp - 1)]
        remote(slots, slots, send, recv, partner).wait_recv()

    def mp_drain(buf, send, recv):
        slots = buf.at[pl.ds(0, n_mp - 1)]
        remote(slots, slots, send, recv, partner).wait_send()

    def far_send(at):
        buf, first, rows = far[at]
        slot = buf.at[m, pl.ds(first, rows)]
        remote(slot, slot, f_s.at[at], f_x.at[at], across).start()
        remote(slot, slot, f_s.at[at], f_c.at[at], partner).start()

    def far_pass(at):
        buf, first, rows = far[at]
        slot = buf.at[lax.rem(m + 2, 4), pl.ds(first, rows)]
        remote(slot, slot, f_s.at[at], f_x.at[at], partner).wait_recv()
        remote(slot, slot, f_s.at[at], f_c.at[at], partner).start()

    def far_recv(at):
        buf, first, rows = far[at]
        slots = buf.at[pl.ds(0, 2), pl.ds(first, rows)]
        remote(slots, slots, f_s.at[at], f_c.at[at], partner).wait_recv()

    def far_drain(at):
        buf, first, rows = far[at]
        slots = buf.at[pl.ds(0, 3), pl.ds(first, rows)]
        remote(slots, slots, f_s.at[at], f_c.at[at], partner).wait_send()

    split_row = FIRST_FOLDS * 16
    far = (
        (fq, 0, fq.shape[1]),
        (fg, 0, split_row),
        (fg, split_row, fg.shape[1] - split_row),
        (fd, 0, fd.shape[1]),
    )

    def on_core(which):
        return pl.when(core == which)

    def dp_send(at):
        slot = gat.at[at, lo, hi]
        other = lo + core * (1 - 2 * lo)

        def send(k):
            to_dev = (lax.rem(hi + k, half_dp) * 2 + other, m)
            remote(slot, slot, g_s.at[at], g_r.at[at], to_dev).start()

        for k in range(1, half_dp):
            send(k)
        on_core(1)(lambda: send(0))

    def dp_forward(at):
        @on_core(1)
        def _():
            slots = gat.at[at, 1 - lo]
            remote(slots, slots, g_f.at[at], g_r.at[at], partner).wait_recv()
            remote(slots, slots, g_f.at[at], g_c.at[at], partner).start()

        @on_core(0)
        def _():
            slots = gat.at[at, 0, pl.ds(0, half_dp - 1)]
            remote(slots, slots, g_f.at[at], g_r.at[at], partner).wait_recv()
            for k in range(1, half_dp):
                slot = gat.at[at, lo, lax.rem(hi + k, half_dp)]
                remote(slot, slot, g_f.at[at], g_c.at[at], partner).start()

    def dp_wait(at, first, wait):
        for which in (0, 1):

            @on_core(which)
            def _(which=which):
                slots = gat.at[at, 0, pl.ds(0, half_dp - (1 if which == first else 0))]
                wait(slots)

    def dp_recv(at):
        dp_wait(
            at,
            1,
            lambda slots: remote(slots, slots, g_f.at[at], g_c.at[at], partner).wait_recv(),
        )

    def dp_drain(at):
        def wait(slots):
            remote(slots, slots, g_s.at[at], g_c.at[at], partner).wait_send()
            remote(slots, slots, g_f.at[at], g_c.at[at], partner).wait_send()

        dp_wait(at, 0, wait)

    def gathered(at):
        talls = [gat[at, i % 2, i // 2].astype(F32) for i in range(n_dp)]
        left = jnp.concatenate([t[:pairs] for t in talls], axis=0)
        right = jnp.concatenate([t[pairs:] for t in talls], axis=0)
        return jnp.concatenate([left, right], axis=1)

    def small_send(at, buf):
        @pl.loop(1, n_dp)
        def _(i):
            to_dev = (lax.rem(d + i, n_dp), m)
            remote(buf.at[d], buf.at[d], sm_s.at[at], sm_r.at[at], to_dev).start()

    def small_recv(at, buf):
        slots = buf.at[pl.ds(0, n_dp - 1)]
        remote(slots, slots, sm_s.at[at], sm_r.at[at], partner).wait_recv()

    def small_drain(at, buf):
        slots = buf.at[pl.ds(0, n_dp - 1)]
        remote(slots, slots, sm_s.at[at], sm_r.at[at], partner).wait_send()

    part_rows = tokens // (2 * TOKEN_PARTS)

    def split_hi(mine, body):
        for k in range(half_dp // 2 - 1):
            body(2 * k + (2 - core if mine else 1 + core))

        @pl.when(core == (1 if mine else 0))
        def _():
            body(half_dp - 1)

    def near_slot(i):
        return lax.rem(hi + half_dp - i, half_dp) * 2 + lo

    def far_slot(i):
        return lax.rem(hi + half_dp - i, half_dp) * 2 + 1 - lo

    def split_far(body):
        split_hi(True, lambda i: body(far_slot(i)))

    def split_near(body):
        split_hi(True, lambda i: body(near_slot(i)))

    def rows_of(slot, part, which):
        start = (which * TOKEN_PARTS + part) * part_rows
        return tok.at[slot, pl.ds(pl.multiple_of(start, 16), part_rows)]

    def tok_push(rows, recv, device):
        remote(rows, rows, t_s.at[0], recv, device).start()

    def tok_wait(recv, counts):
        for which in (0, 1):
            if counts[which]:

                @on_core(which)
                def _(which=which):
                    rows = tok.at[0, pl.ds(0, counts[which] * part_rows)]
                    remote(rows, rows, t_s.at[0], recv, partner).wait_recv()

    quarter = half_dp // 2
    counts = (quarter - 1, quarter)

    def tok_start(part):
        rows = rows_of(d, part, side)

        def body(i):
            tok_push(rows, tz_r.at[part], (lax.rem(hi + i, half_dp) * 2 + lo, m))

        split_hi(True, body)

        @on_core(0)
        def _():
            for which in (0, 1):
                tok_push(rows_of(d, part, which), to_r.at[part], beside)

    def tok_own(part):
        tok_wait(to_r.at[part], (2, 0))

        @on_core(0)
        def _():
            for which in (0, 1):
                tok_push(rows_of(far_slot(0), part, which), tl_r.at[0], partner)

    def tok_second(part):
        tok_wait(tz_r.at[part], counts)

        def body(slot):
            rows = rows_of(slot, part, side)
            tok_push(rows, ty_r.at[part], beside)
            tok_push(rows, tl_r.at[0], partner)

        split_near(body)

    def tok_third(part):
        tok_wait(ty_r.at[part], counts)
        split_far(lambda slot: tok_push(rows_of(slot, part, side), tl_r.at[0], partner))

    def tok_near(part):
        split_near(lambda slot: tok_push(rows_of(slot, part, side), tx_r.at[part], across))

    def tok_pass(part):
        tok_wait(tx_r.at[part], counts)

        def body(slot):
            rows = rows_of(slot, part, 1 - side)
            tok_push(rows, tw_r.at[part], beside)
            tok_push(rows, tl_r.at[0], partner)

        split_near(body)

    def tok_fourth(part):
        tok_wait(tw_r.at[part], counts)
        split_far(lambda slot: tok_push(rows_of(slot, part, 1 - side), tl_r.at[0], partner))

    def tok_last():
        for which, count in ((0, 2 * quarter), (1, 2 * quarter - 1)):

            @on_core(which)
            def _(count=count):
                slots = tok.at[pl.ds(0, count)]
                remote(slots, slots, t_s.at[0], tl_r.at[0], partner).wait_recv()

    def tok_drain():
        for which, count in ((0, n_dp - 2), (1, n_dp)):

            @on_core(which)
            def _(count=count):
                slots = tok.at[pl.ds(0, count)]
                remote(slots, slots, t_s.at[0], tl_r.at[0], partner).wait_send()

    def token_steps(at):
        steps = {
            "start": tok_start,
            "own": tok_own,
            "second": tok_second,
            "third": tok_third,
            "near": tok_near,
            "pass": tok_pass,
            "fourth": tok_fourth,
        }
        for name, part in STEPS.get(at, ()):
            steps[name](part)

    def attend_rows(queries, normed, allowed, weights):
        stacked = head_blocks(queries.astype(F32), width).astype(BF16)
        folded = dot(stacked, weights[1]).astype(BF16)
        scores = dot_nt(folded, normed) * scale
        probs = softmax_rows(scores, allowed)
        mixed = dot(probs.astype(BF16), normed).astype(BF16)
        context = head_pick(dot_nt(mixed, weights[2]), width).astype(BF16)
        return folded, probs, context

    for k in range(chunk):
        image_load(k).wait()
    gain, shift = vector("ig1", ig1_ref), vector("ib1", ib1_ref)
    loads["iw"].wait()
    hats = [
        normalized(xi[k * chunk_rows : (k + 1) * chunk_rows, :].astype(F32))[0].astype(BF16)
        for k in range(chunk)
    ]
    firsts = [i * IMG_LEN for i in range(pairs)]
    image_first = jnp.concatenate([xi[r : r + 1, :].astype(F32) for r in firsts], axis=0)
    first_n = (normalized(image_first)[0] * gain + shift).astype(BF16)
    image_fold = dot(head_blocks(dot_nt(first_n, iw[0]), width).astype(BF16), iw[1])
    shifted = jnp.sum(image_fold * shift, axis=-1, keepdims=True)
    image_fold = image_fold * gain
    group = pairs // chunk
    shape = (group, chunk_rows)
    place = lax.broadcasted_iota(jnp.int32, shape, 1)
    begin = lax.broadcasted_iota(jnp.int32, shape, 0) * IMG_LEN
    inside = jnp.concatenate([(place >= begin) & (place < begin + IMG_LEN)] * heads, axis=0)

    def of_group(rows, k):
        spots = [h * pairs + k * group for h in range(heads)]
        return jnp.concatenate([rows[at : at + group] for at in spots], axis=0)

    image_scores = [
        (dot_nt(of_group(image_fold, k).astype(BF16), hats[k]) + of_group(shifted, k)) * scale
        for k in range(chunk)
    ]
    image_probs = [softmax_rows(scores, inside).astype(BF16) for scores in image_scores]
    image_mixed = [dot(image_probs[k], hats[k]) for k in range(chunk)]
    image_mixed = jnp.concatenate(
        [mixed[h * group : (h + 1) * group] for h in range(heads) for mixed in image_mixed], axis=0
    )
    image_mixed = image_mixed * gain + shift
    image_context = head_pick(dot_nt(image_mixed.astype(BF16), iw[2]), width).astype(BF16)
    loads["io"].wait()
    ar[0, m] = to_tall(dot(image_context, io[...]))

    pl.semaphore_wait(barrier, n_mp - 1 + n_dp - 1)
    mp_send(ar.at[0], ar_s.at[0], ar_r.at[0])

    loads["text"].wait()
    gain_one = vector("tg1", tg1_ref)
    hat_one, factor_one = normalized(xt[...].astype(F32))
    tok[d] = (hat_one * gain_one + vector("tb1", tb1_ref)).astype(BF16)
    token_steps(0)
    seg = vector("seg", seg_ref)
    seg_rows = tokens // 128
    for i in range(seg_rows):
        ids[d, i : i + 1, :] = seg[:, i * 128 : (i + 1) * 128]
    ids[d, seg_rows : seg_rows + 1, 0:pairs] = vector("lab", lab_ref)

    normed = tok[d]
    mine, pick = caption_masks(seg, d * pairs, pairs)
    allowed = jnp.concatenate([mine] * heads, axis=0)
    loads["tw"].wait()
    queries = dot_nt(dot(pick, normed).astype(BF16), tw[0]).astype(BF16)
    folded, probs, context = attend_rows(queries, normed, allowed, tw)
    loads["to"].wait()
    ar[1, m] = to_tall(dot(context, to[...]))
    mp_send(ar.at[1], ar_s.at[1], ar_r.at[1])
    text_last = dot(pick, xt[...])

    def head_rows(blocks):
        rows = [
            jnp.sum(blocks[h * pairs : (h + 1) * pairs], axis=0, keepdims=True)
            for h in range(heads)
        ]
        return jnp.concatenate(rows + [jnp.zeros((8 - heads, tokens), F32)], axis=0)

    def padded(rows, foot):
        foot = jnp.concatenate([foot, jnp.zeros((8, features - tokens), F32)], axis=1)
        return jnp.concatenate([rows, foot], axis=0).astype(BF16)

    no_foot = jnp.zeros((8, tokens), F32)
    prob_rows = head_rows(probs)
    fq[m] = padded(folded.astype(F32), prob_rows)
    prow[d] = stats_pack([prob_rows[h : h + 1] for h in range(heads)])
    token_steps(1)

    def summed(at):
        mp_recv(ar.at[at], ar_s.at[at], ar_r.at[at])
        full = ar[at, 0].astype(F32)
        for i in range(1, n_mp):
            full = full + ar[at, i].astype(F32)
        count = full.shape[0] // 2
        return jnp.concatenate([full[:count], full[count:]], axis=1)

    image_middle = image_first + summed(0)
    gain, shift = vector("ig2", ig2_ref), vector("ib2", ib2_ref)
    image_n2 = (normalized(image_middle)[0] * gain + shift).astype(BF16)
    loads["iu"].wait()
    image_hidden = dot(image_n2, iu[...]) + vector("iub", iub_ref)
    image_active = gelu_parts(image_hidden)[0].astype(BF16)
    loads["id"].wait()
    ar[2, m] = to_tall(dot(image_active, idn[...]))
    mp_send(ar.at[2], ar_s.at[2], ar_r.at[2])
    token_steps(2)

    middle = text_last + summed(1)
    gat[0, lo, hi] = to_tall(middle)
    gain_two, shift_two = vector("tg2", tg2_ref), vector("tb2", tb2_ref)
    hat_two, factor_two = normalized(middle)
    normed_two = (hat_two * gain_two + shift_two).astype(BF16)
    loads["tu"].wait()
    up_shift = vector("tub", tub_ref)
    active, slope = gelu_parts(dot(normed_two, tu[...]) + up_shift)
    loads["td"].wait()
    ar[3, m] = to_tall(dot(active.astype(BF16), td[...]))
    mp_send(ar.at[3], ar_s.at[3], ar_r.at[3])
    token_steps(3)

    gat[1, lo, hi] = to_tall(unit(image_middle + summed(2)))
    dp_send(1)
    gat[2, lo, hi] = to_tall(middle + summed(3))
    dp_send(2)
    far_send(0)

    token_steps(4)
    dp_forward(1)
    token_steps(9)
    dp_forward(2)
    far_pass(0)
    token_steps(5)
    dp_recv(1)
    image_low = gathered(1).astype(BF16)
    own_labels = column_of(ids[d, seg_rows : seg_rows + 1, :], pairs)
    dp_recv(2)


    def embedded(rows):
        shrink = lax.rsqrt(jnp.sum(rows * rows, axis=-1, keepdims=True) + 1e-06)
        text_unit = rows * shrink
        return shrink, text_unit, 64.0 * dot_nt(text_unit.astype(BF16), image_low)

    def final_grad(shrink, text_unit, logits, labels):
        lanes = lax.broadcasted_iota(jnp.int32, logits.shape, 1)
        onehot = (labels == lanes).astype(F32)
        top = jnp.max(logits, axis=1, keepdims=True)
        lse = top + jnp.log(jnp.sum(jnp.exp(logits - top), axis=1, keepdims=True))
        grads = 0.5 * (jnp.exp(logits - lse) + jnp.exp(logits - col_lse)) - onehot
        grads = 64.0 * dot(grads.astype(BF16), image_low)
        along = jnp.sum(text_unit * grads, axis=-1, keepdims=True)
        positive = jnp.sum(logits * onehot, axis=1, keepdims=True)
        return shrink * (grads - text_unit * along), lse, positive

    shrink_all, unit_all, logits = embedded(gathered(2))
    col_top = jnp.max(logits, axis=0, keepdims=True)
    col_lse = col_top + jnp.log(jnp.sum(jnp.exp(logits - col_top), axis=0, keepdims=True))
    grad_final, own_lse, positive = final_grad(*embedded(from_tall(gat[2, lo, hi])), own_labels)
    grad_hidden = (dot_nt(grad_final.astype(BF16), td[...]) * slope).astype(BF16)
    ar[4, m] = to_tall(dot_nt(grad_hidden, tu[...]))
    mp_send(ar.at[4], ar_s.at[4], ar_r.at[4])
    small_send(0, ids)
    dp_send(0)
    small_send(1, prow)

    token_steps(6)
    lanes = lax.broadcasted_iota(jnp.int32, (pairs, total), 1)
    mine_first = lax.broadcasted_iota(jnp.int32, (pairs, total), 0) + d * pairs
    own_col = jnp.sum(jnp.where(lanes == mine_first, col_lse, 0.0), axis=1, keepdims=True)
    pair_loss = 0.5 * (own_lse + own_col) - positive
    shape = (pairs, loss_o.shape[1])
    diagonal = lax.broadcasted_iota(jnp.int32, shape, 0) == lax.broadcasted_iota(
        jnp.int32, shape, 1
    )
    loss_o[...] = jnp.sum(jnp.where(diagonal, pair_loss, 0.0), axis=0, keepdims=True)

    def spread(slots, ref, at):
        parts = []
        for i in slots:
            foot = ref[i, at : at + 8, 0:tokens].astype(F32)
            for h in range(heads):
                parts.append(jnp.where(mine, foot[h : h + 1], 0.0))
            parts.append(jnp.zeros((8, tokens), F32))
        return jnp.concatenate(parts, axis=0).astype(BF16)

    def placed(count):
        spots = jnp.concatenate([pick.astype(F32), jnp.zeros((8, tokens), F32)], axis=0)
        return jnp.concatenate([spots] * count, axis=0).astype(BF16)

    own_probs = spread([m], fq, pairs * heads)
    own_spots = placed(1)

    grad_n2 = summed(4)
    grad_middle = grad_final + norm_back(grad_n2, hat_two, factor_two, gain_two)
    gat[3, lo, hi] = to_tall(grad_middle)
    dp_send(3)
    middle_low = grad_middle.astype(BF16)
    grad_context = dot_nt(middle_low, to[...]).astype(BF16)
    grad_folded = dot(head_blocks(grad_context.astype(F32), width).astype(BF16), tw[2])
    fg[m] = padded(grad_folded, no_foot)
    far_send(1)
    grad_probs = dot_nt(grad_folded.astype(BF16), normed)
    grad_scores = probs * (grad_probs - jnp.sum(grad_probs * probs, axis=-1, keepdims=True))
    scaled = grad_scores * scale
    score_rows = head_rows(scaled)
    mixed_back = dot(scaled.astype(BF16), normed).astype(BF16)
    grad_queries = head_pick(dot_nt(mixed_back, tw[1]), width).astype(BF16)
    fd[m] = padded(dot(grad_queries, tw[0]), score_rows)

    part = dot_tn(spread([m], fd, pairs), fq[m])
    part = part + dot_tn(own_probs, fg[m])
    part = part + dot_tn(own_spots, fd[m])
    stm[m] = stats_pack(
        [jnp.sum(part * hat_one, axis=0, keepdims=True), jnp.sum(part, axis=0, keepdims=True)]
    )
    mp_send(stm, st_s.at[0], st_r.at[0])
    far_send(2)
    far_send(3)
    stats_two = [
        jnp.sum(grad_n2 * hat_two, axis=0, keepdims=True),
        jnp.sum(grad_n2, axis=0, keepdims=True),
    ]
    drow[d] = stats_pack([score_rows[h : h + 1] for h in range(heads)] + stats_two, 16).astype(BF16)
    small_send(3, drow)

    token_steps(7)
    small_recv(0, ids)
    labels = jnp.concatenate(
        [column_of(ids[i, seg_rows : seg_rows + 1, :], pairs) for i in range(n_dp)], axis=0
    )
    fin_all = final_grad(shrink_all, unit_all, logits, labels)[0].astype(BF16)
    dp_forward(0)
    dp_recv(0)
    n2_all = (normalized(gathered(0))[0] * gain_two + shift_two).astype(BF16)
    act_all, slope_all = gelu_parts(dot(n2_all, tu[...]) + up_shift)
    gh_all = (dot_nt(fin_all, td[...]) * slope_all).astype(BF16)
    up_bias = jnp.sum(gh_all.astype(F32), axis=0, keepdims=True)
    up_o[...] = dot_tn(n2_all, gh_all)
    down_o[...] = dot_tn(act_all.astype(BF16), fin_all)
    mp_recv(stm, st_s.at[0], st_r.at[0])
    one = stm[0]
    for i in range(1, n_mp):
        one = one + stm[i]
    std[d] = stats_pack(stats_unpack(one, 2, features), 16).astype(BF16)
    small_send(2, std)
    far_pass(1)
    far_pass(2)
    dp_forward(3)
    far_pass(3)
    token_steps(8)

    everyone = list(range(n_mp))

    def flat(ref):
        return ref[...].reshape(n_mp * ref.shape[1], features)

    for at in range(3):
        far_recv(at)
    from_probs = dot_tn(spread(everyone, fq, pairs * heads), flat(fg))
    far_recv(3)
    grad_normed = dot_tn(spread(everyone, fd, pairs), flat(fq)) + from_probs
    grad_normed = grad_normed + dot_tn(placed(n_mp), flat(fd))
    text_grad = norm_back(grad_normed, hat_one, factor_one, gain_one)
    tg_o[...] = text_grad + dot_tn(pick, middle_low)

    small_recv(1, prow)
    tok_last()
    twice = 2 * pairs
    pair_masks = []
    for j in range(half_dp):
        seg = jnp.concatenate(
            [ids[i, k : k + 1, :] for i in (2 * j, 2 * j + 1) for k in range(seg_rows)], axis=1
        )
        pair_masks.append(caption_masks(seg, j * twice, twice))

    def pair_at(j):
        return slice(j * twice, (j + 1) * twice)

    def pair_rows(j):
        return tok[2 * j : 2 * j + 2].reshape(2 * tokens, features)

    def spread_pair(j, rows, h):
        values = jnp.concatenate([rows[2 * j][h], rows[2 * j + 1][h]], axis=1)
        return jnp.where(pair_masks[j][0], values, 0.0).astype(BF16)

    early_rows = [stats_unpack(prow[i], heads, tokens) for i in range(n_dp)]
    for j in range(half_dp):
        parts = [spread_pair(j, early_rows, h) for h in range(heads)] + [pair_masks[j][1]]
        mixed = dot(jnp.concatenate(parts, axis=0), pair_rows(j)).astype(BF16)
        for h in range(heads):
            xv_o[h, pair_at(j), :] = mixed[h * twice : (h + 1) * twice]
        nsel_o[pair_at(j), :] = mixed[heads * twice :]

    small_recv(3, drow)
    late_rows = [stats_unpack(drow[i].astype(F32), heads, tokens) for i in range(n_dp)]
    for j in range(half_dp):
        parts = [spread_pair(j, late_rows, h) for h in range(heads)]
        mixed = dot(jnp.concatenate(parts, axis=0), pair_rows(j)).astype(BF16)
        for h in range(heads):
            xk_o[h, pair_at(j), :] = mixed[h * twice : (h + 1) * twice]
    dp_recv(3)
    mid_o[...] = gathered(3).astype(BF16)

    small_recv(2, std)
    stats = std[0].astype(F32)
    for i in range(1, n_dp):
        stats = stats + std[i].astype(F32)
    late = drow[0].astype(F32)
    for i in range(1, n_dp):
        late = late + drow[i].astype(F32)
    rows = stats_unpack(stats, 2, features)
    rows += stats_unpack(late[heads * seg_rows :], 2, features)
    vec_o[...] = jnp.concatenate(rows + [up_bias, jnp.zeros((3, features), F32)], axis=0)

    for at in range(ar.shape[0]):
        mp_drain(ar.at[at], ar_s.at[at], ar_r.at[at])
    mp_drain(stm, st_s.at[0], st_r.at[0])
    for at in range(len(far)):
        far_drain(at)
    for at in range(gat.shape[0]):
        dp_drain(at)
    for at, buf in enumerate((ids, prow, std, drow)):
        small_drain(at, buf)
    tok_drain()


def weights_kernel(
    up,
    down,
    tw,
    to,
    mid,
    nsel,
    xk,
    xv,
    tg,
    vec,
    loss,
    tg_out,
    qkv_out,
    out_out,
    up_out,
    down_out,
    loss_out,
    g1_out,
    b1_out,
    g2_out,
    b2_out,
    ub_out,
    qkv_buf,
    out_buf,
    sem,
    *vec_bufs,
):
    heads, total, features = xk.shape
    width = to.shape[0]
    started = []

    def ship(src, dst):
        copy = pltpu.make_async_copy(src, dst, sem.at[len(started)])
        copy.start()
        started.append(copy)

    for src, dst in ((up, up_out), (down, down_out)):
        step = src.shape[0] // SHIP_PARTS
        for at in range(0, src.shape[0], step):
            rows = pl.ds(at, step)
            ship(src.at[rows], dst.at[rows])
    ship(tg, tg_out)
    for at, dst in enumerate((g1_out, b1_out, g2_out, b2_out, ub_out)):
        vec_bufs[at][...] = vec[at, :]
        ship(vec_bufs[at], dst)
    vec_bufs[5][...] = loss[0, 0 : loss_out.shape[0]]
    ship(vec_bufs[5], loss_out)
    flat_k = xk[...].reshape(heads * total, features)
    flat_v = xv[...].reshape(heads * total, features)
    queries = dot_nt(nsel[...], tw[0])
    grad_context = dot_nt(mid[...], to[...])
    for at, rows, flat in ((1, queries, flat_k), (2, grad_context, flat_v)):
        stacked = head_blocks(rows.astype(BF16).astype(F32), width).astype(BF16)
        qkv_buf[at] = dot_tn(stacked, flat)
        ship(qkv_buf.at[at], qkv_out.at[at])
    grad_queries = head_pick(dot_nt(flat_k, tw[1]), width).astype(BF16)
    qkv_buf[0] = dot_tn(grad_queries, nsel[...])
    ship(qkv_buf.at[0], qkv_out.at[0])
    context = head_pick(dot_nt(flat_v, tw[2]), width).astype(BF16)
    out_buf[...] = dot_tn(context, mid[...])
    ship(out_buf, out_out)
    for copy in started:
        copy.wait()


def kernel_device(
    n_dp,
    n_mp,
    text_tokens,
    segment_ids,
    labels,
    image_tokens,
    image_gain_one,
    image_bias_one,
    image_qkv,
    image_out,
    image_gain_two,
    image_bias_two,
    image_up,
    image_up_bias,
    image_down,
    text_gain_one,
    text_bias_one,
    text_qkv,
    text_out,
    text_gain_two,
    text_bias_two,
    text_up,
    text_up_bias,
    text_down,
):
    pairs = labels.shape[0]
    tokens, features = text_tokens.shape
    width = text_out.shape[0]
    hidden = text_up.shape[1]
    heads = width // HEAD
    total = n_dp * pairs
    half_dp = n_dp // 2
    vmem = pltpu.VMEM
    whole = pl.BlockSpec(memory_space=pltpu.VMEM)
    anywhere = pl.BlockSpec(memory_space=pl.ANY)

    def sems(*shape):
        return pltpu.SemaphoreType.DMA(shape)

    outs = [
        ((features, hidden), F32),
        ((hidden, features), F32),
        ((3, width, features), BF16),
        ((width, features), BF16),
        ((total, features), BF16),
        ((total, features), BF16),
        ((heads, total, features), BF16),
        ((heads, total, features), BF16),
        ((tokens, features), F32),
        ((8, features), F32),
        ((1, 128), F32),
    ]
    tall = (2 * pairs, features // 2)
    fold_rows = heads * pairs + 8
    vectors = (
        segment_ids,
        labels,
        image_gain_one,
        image_bias_one,
        image_gain_two,
        image_bias_two,
        image_up_bias,
        text_gain_one,
        text_bias_one,
        text_gain_two,
        text_bias_two,
        text_up_bias,
    )
    operands = (
        text_tokens,
        image_tokens,
        jnp.transpose(image_qkv, (1, 2, 0)),
        image_out,
        image_up,
        image_down,
        jnp.transpose(text_qkv, (1, 2, 0)),
        text_out,
        text_up,
        text_down,
    ) + vectors
    factors = pl.pallas_call(
        functools.partial(step_kernel, (n_dp, n_mp, pairs, tokens, features, width)),
        out_shape=[vmem(shape, dtype) for shape, dtype in outs],
        in_specs=[anywhere] * len(operands),
        out_specs=[whole] * len(outs),
        scratch_shapes=[
            vmem(text_tokens.shape, BF16),
            vmem(image_tokens.shape, BF16),
            vmem((3, width, features), BF16),
            vmem(image_out.shape, BF16),
            vmem(image_up.shape, BF16),
            vmem(image_down.shape, BF16),
            vmem(text_up.shape, BF16),
            vmem(text_down.shape, BF16),
        ]
        + [vmem(array.shape, array.dtype) for array in vectors]
        + [
            vmem((n_dp, tokens, features), BF16),
            vmem((n_dp, 8, 128), jnp.int32),
            vmem((n_dp, 8, 128), F32),
            vmem((n_dp, 32, 128), BF16),
            vmem((n_mp, 16, 128), F32),
            vmem((n_dp, 16, 128), BF16),
            vmem((5, n_mp) + tall, BF16),
            vmem((4, 2, half_dp) + tall, BF16),
            vmem((n_mp, fold_rows, features), BF16),
            vmem((n_mp, fold_rows, features), BF16),
            vmem((n_mp, pairs + 8, features), BF16),
            sems(22),
            sems(pairs // 8),
            sems(1),
            sems(TOKEN_PARTS),
            sems(TOKEN_PARTS),
            sems(TOKEN_PARTS),
            sems(TOKEN_PARTS),
            sems(TOKEN_PARTS),
            sems(1),
            sems(5),
            sems(5),
            sems(4),
            sems(4),
            sems(4),
            sems(4),
            sems(4),
            sems(4),
            sems(4),
            sems(1),
            sems(1),
            sems(4),
            sems(4),
        ],
        compiler_params=pltpu.CompilerParams(
            collective_id=0, has_side_effects=True, vmem_limit_bytes=48 * 2**20
        ),
        name="step",
    )(*[pltpu.with_memory_space_constraint(operand, pltpu.HBM) for operand in operands])
    vector = jax.ShapeDtypeStruct((features,), F32)
    results = pl.pallas_call(
        weights_kernel,
        out_shape=[
            jax.ShapeDtypeStruct((tokens, features), F32),
            jax.ShapeDtypeStruct((3, width, features), F32),
            jax.ShapeDtypeStruct((width, features), F32),
            jax.ShapeDtypeStruct((features, hidden), F32),
            jax.ShapeDtypeStruct((hidden, features), F32),
            jax.ShapeDtypeStruct((pairs,), F32),
            vector,
            vector,
            vector,
            vector,
            jax.ShapeDtypeStruct((hidden,), F32),
        ],
        in_specs=[whole] * len(outs),
        out_specs=[anywhere] * 11,
        scratch_shapes=[
            vmem((3, width, features), F32),
            vmem((width, features), F32),
            sems(2 * SHIP_PARTS + 11),
        ]
        + [vmem((features,), F32)] * 4
        + [vmem((hidden,), F32), vmem((pairs,), F32)],
        compiler_params=pltpu.CompilerParams(vmem_limit_bytes=32 * 2**20),
        name="weights",
    )(*[pltpu.with_memory_space_constraint(factor, pltpu.VMEM) for factor in factors])
    text_grad, qkv, out, up, down, loss, gain_one, bias_one, gain_two, bias_two, up_bias = results
    return (
        loss,
        text_grad,
        gain_one,
        bias_one,
        jnp.transpose(qkv, (2, 0, 1)),
        out,
        gain_two,
        bias_two,
        up,
        up_bias,
        down,
    )


def solution(mesh):
    placed = (
        P("dp", None),
        P("dp"),
        P("dp"),
        P("dp", None),
        P(),
        P(),
        P(None, None, "mp"),
        P("mp", None),
        P(),
        P(),
        P(None, "mp"),
        P("mp"),
        P("mp", None),
        P(),
        P(),
        P(None, None, "mp"),
        P("mp", None),
        P(),
        P(),
        P(None, "mp"),
        P("mp"),
        P("mp", None),
    )
    n_dp, n_mp = mesh.shape["dp"], mesh.shape["mp"]
    body = plain_device
    if n_dp <= 16 and n_dp % 4 == 0 and n_mp == 4:
        body = functools.partial(kernel_device, n_dp, n_mp)
    return jax.shard_map(
        body,
        mesh=mesh,
        in_specs=placed,
        out_specs=(
            P("dp"),
            P("dp", None),
            P(),
            P(),
            P(None, None, "mp"),
            P("mp", None),
            P(),
            P(),
            P(None, "mp"),
            P("mp"),
            P("mp", None),
        ),
        check_vma=False,
    )
```

```python
import functools

import jax
import jax.numpy as jnp
from jax import lax
from jax.experimental import pallas as pl
from jax.experimental.pallas import tpu as pltpu
from jax.sharding import PartitionSpec as P

HEAD = 64
IMG_LEN = 50
F32 = jnp.float32
BF16 = jnp.bfloat16


def dot(a, b):
    return lax.dot_general(a, b, (((1,), (0,)), ((), ())), preferred_element_type=F32)


def dot_nt(a, b):
    return lax.dot_general(a, b, (((1,), (1,)), ((), ())), preferred_element_type=F32)


def dot_tn(a, b):
    return lax.dot_general(a, b, (((0,), (0,)), ((), ())), preferred_element_type=F32)


def normalized(values):
    center = values - jnp.mean(values, axis=-1, keepdims=True)
    factor = lax.rsqrt(jnp.mean(center * center, axis=-1, keepdims=True) + 1e-05)
    return center * factor, factor


def norm_back(grad, hat, factor, gain):
    scaled = grad * gain
    along = jnp.mean(scaled * hat, axis=-1, keepdims=True)
    return factor * (scaled - jnp.mean(scaled, axis=-1, keepdims=True) - hat * along)


def unit(rows):
    return rows * lax.rsqrt(jnp.sum(rows * rows, axis=-1, keepdims=True) + 1e-06)


def gelu_parts(hidden):
    cdf = 0.5 * (1.0 + lax.erf(hidden * 0.7071067811865476))
    slope = cdf + hidden * jnp.exp(-0.5 * hidden * hidden) * 0.3989422804014327
    return hidden * cdf, slope


def head_blocks(rows, width):
    lanes = lax.broadcasted_iota(jnp.int32, (1, width), 1)
    return jnp.concatenate(
        [
            jnp.where((lanes >= h * HEAD) & (lanes < (h + 1) * HEAD), rows, 0.0)
            for h in range(width // HEAD)
        ],
        axis=0,
    )


def head_pick(blocks, width):
    heads = width // HEAD
    count = blocks.shape[0] // heads
    lanes = lax.broadcasted_iota(jnp.int32, (1, width), 1)
    total = jnp.zeros((count, width), F32)
    for h in range(heads):
        own = (lanes >= h * HEAD) & (lanes < (h + 1) * HEAD)
        total = total + jnp.where(own, blocks[h * count : (h + 1) * count], 0.0)
    return total


def attend(normed_rows, normed, allowed, weights):
    width = weights.shape[1]
    heads = width // HEAD
    queries = dot_nt(normed_rows, weights[0]).astype(BF16)
    folded = dot(head_blocks(queries.astype(F32), width).astype(BF16), weights[1]).astype(BF16)
    scores = dot_nt(folded, normed) * HEAD**-0.5
    scores = jnp.where(jnp.concatenate([allowed] * heads, axis=0), scores, -1e30)
    expo = jnp.exp(scores - jnp.max(scores, axis=-1, keepdims=True))
    probs = expo / jnp.sum(expo, axis=-1, keepdims=True)
    mixed = dot(probs.astype(BF16), normed).astype(BF16)
    context = head_pick(dot_nt(mixed, weights[2]), width).astype(BF16)
    return queries, folded, probs, mixed, context


def plain_device(
    text_tokens,
    segment_ids,
    labels,
    image_tokens,
    image_gain_one,
    image_bias_one,
    image_qkv,
    image_out,
    image_gain_two,
    image_bias_two,
    image_up,
    image_up_bias,
    image_down,
    text_gain_one,
    text_bias_one,
    text_qkv,
    text_out,
    text_gain_two,
    text_bias_two,
    text_up,
    text_up_bias,
    text_down,
):
    rank = lax.axis_index("dp")
    pairs = labels.shape[0]
    tokens = segment_ids.shape[0]
    width = text_out.shape[0]
    heads = width // HEAD
    features = text_tokens.shape[1]
    image_weights = jnp.transpose(image_qkv, (1, 2, 0))
    text_weights = jnp.transpose(text_qkv, (1, 2, 0))

    image_x = image_tokens.astype(F32)
    image_n = (normalized(image_x)[0] * image_gain_one + image_bias_one).astype(BF16)
    image_first = image_x.reshape(pairs, IMG_LEN, features)[:, 0]
    first_n = (normalized(image_first)[0] * image_gain_one + image_bias_one).astype(BF16)
    owner = lax.broadcasted_iota(jnp.int32, (pairs, pairs * IMG_LEN), 0)
    place = lax.broadcasted_iota(jnp.int32, (pairs, pairs * IMG_LEN), 1)
    inside = (place >= owner * IMG_LEN) & (place < (owner + 1) * IMG_LEN)
    image_context = attend(first_n, image_n, inside, image_weights)[4]

    text_x = text_tokens.astype(F32)
    hat_one, factor_one = normalized(text_x)
    normed = (hat_one * text_gain_one + text_bias_one).astype(BF16)
    captions = rank * pairs + jnp.arange(pairs)
    mine = segment_ids[None, :] == captions[:, None]
    spot = lax.broadcasted_iota(jnp.int32, (pairs, tokens), 1)
    last = jnp.max(jnp.where(mine, spot, -1), axis=1, keepdims=True)
    pick = (spot == last).astype(BF16)
    normed_last = dot(pick, normed).astype(BF16)
    queries, folded, probs, mixed, context = attend(normed_last, normed, mine, text_weights)

    attended = jnp.concatenate([dot(image_context, image_out), dot(context, text_out)], axis=0)
    attended = lax.psum(attended.astype(BF16), "mp").astype(F32)
    middle = jnp.concatenate([image_first, dot(pick, text_tokens)], axis=0) + attended
    hat_two, factor_two = normalized(middle)
    image_n2 = (hat_two[:pairs] * image_gain_two + image_bias_two).astype(BF16)
    normed_two = (hat_two[pairs:] * text_gain_two + text_bias_two).astype(BF16)
    image_active = gelu_parts(dot(image_n2, image_up) + image_up_bias)[0].astype(BF16)
    active, slope = gelu_parts(dot(normed_two, text_up) + text_up_bias)
    active = active.astype(BF16)
    branch = jnp.concatenate([dot(image_active, image_down), dot(active, text_down)], axis=0)
    final = middle + lax.psum(branch.astype(BF16), "mp").astype(F32)

    everyone = lax.all_gather(final.astype(BF16), "dp").astype(F32)
    total = everyone.shape[0] * pairs
    image_low = unit(everyone[:, :pairs].reshape(total, features)).astype(BF16)
    pooled = final[pairs:]
    text_low = unit(everyone[:, pairs:].reshape(total, features)).astype(BF16)
    logits = 64.0 * dot_nt(text_low, image_low)
    column_lse = jax.nn.logsumexp(logits, axis=0)
    own = lax.dynamic_slice_in_dim(logits, rank * pairs, pairs, axis=0)
    row_lse = jax.nn.logsumexp(own, axis=1)
    own_columns = lax.dynamic_slice_in_dim(column_lse, rank * pairs, pairs)
    onehot = (labels[:, None] == jnp.arange(total)[None, :]).astype(F32)
    pair_loss = 0.5 * (row_lse + own_columns) - jnp.sum(own * onehot, axis=1)
    grad_logits = (
        0.5 * (jnp.exp(own - row_lse[:, None]) + jnp.exp(own - column_lse[None, :])) - onehot
    )
    grad_embed = 64.0 * dot(grad_logits.astype(BF16), image_low)
    scale = lax.rsqrt(jnp.sum(pooled * pooled, axis=-1, keepdims=True) + 1e-06)
    text_unit = pooled * scale
    grad_final = scale * (
        grad_embed - text_unit * jnp.sum(text_unit * grad_embed, axis=-1, keepdims=True)
    )

    final_low = grad_final.astype(BF16)
    grad_hidden = (dot_nt(final_low, text_down) * slope).astype(BF16)
    grad_normed_two = lax.psum(dot_nt(grad_hidden, text_up).astype(BF16), "mp").astype(F32)
    hat_two = hat_two[pairs:]
    grad_middle = grad_final + norm_back(grad_normed_two, hat_two, factor_two[pairs:], text_gain_two)
    middle_low = grad_middle.astype(BF16)
    grad_context = dot_nt(middle_low, text_out).astype(BF16)
    grad_folded = dot(head_blocks(grad_context.astype(F32), width).astype(BF16), text_weights[2])
    grad_folded = grad_folded.astype(BF16)
    grad_probs = dot_nt(grad_folded, normed)
    grad_scores = probs * (grad_probs - jnp.sum(grad_probs * probs, axis=-1, keepdims=True))
    grad_scores = (grad_scores * HEAD**-0.5).astype(BF16)
    mixed_back = dot(grad_scores, normed).astype(BF16)
    grad_queries = head_pick(dot_nt(mixed_back, text_weights[1]), width).astype(BF16)
    grad_normed = dot_tn(grad_scores, folded) + dot_tn(probs.astype(BF16), grad_folded)
    grad_normed = grad_normed + dot_tn(pick, dot(grad_queries, text_weights[0]).astype(BF16))
    grad_normed = lax.psum(grad_normed.astype(BF16), "mp").astype(F32)
    text_grad = norm_back(grad_normed, hat_one, factor_one, text_gain_one)
    text_grad = text_grad + dot_tn(pick, middle_low)

    vectors = jnp.concatenate(
        [
            jnp.sum(grad_normed * hat_one, axis=0),
            jnp.sum(grad_normed, axis=0),
            jnp.sum(grad_normed_two * hat_two, axis=0),
            jnp.sum(grad_normed_two, axis=0),
            jnp.sum(grad_hidden.astype(F32), axis=0),
        ]
    )
    vectors = jnp.sum(lax.all_gather(vectors, "dp"), axis=0)
    cuts = [features, 2 * features, 3 * features, 4 * features]
    gain_one, bias_one, gain_two, bias_two, up_bias = jnp.split(vectors, cuts)

    def by_head(blocks):
        return [blocks[h * pairs : (h + 1) * pairs] for h in range(heads)]

    pieces = [active, final_low, normed_two, grad_hidden, context, middle_low, normed_last]
    pieces += [grad_queries, queries, grad_context] + by_head(mixed_back) + by_head(mixed)
    sent = lax.all_gather(jnp.concatenate(pieces, axis=1), "dp").reshape(total, -1)
    got = []
    at = 0
    for piece in pieces:
        got.append(sent[:, at : at + piece.shape[1]])
        at += piece.shape[1]
    active, final_low, normed_two, grad_hidden, context, middle_low, normed_last = got[:7]
    grad_queries, queries, grad_context = got[7:10]
    mixed_back = got[10 : 10 + heads]
    mixed = got[10 + heads :]

    def per_head(rows, blocks):
        return jnp.concatenate(
            [dot_tn(rows[:, h * HEAD : (h + 1) * HEAD], blocks[h]) for h in range(heads)], axis=0
        )

    grad_qkv = jnp.stack(
        [
            dot_tn(grad_queries, normed_last),
            per_head(queries, mixed_back),
            per_head(grad_context, mixed),
        ]
    )
    return (
        pair_loss,
        text_grad,
        gain_one,
        bias_one,
        jnp.transpose(grad_qkv, (2, 0, 1)),
        dot_tn(context, middle_low),
        gain_two,
        bias_two,
        dot_tn(normed_two, grad_hidden),
        up_bias,
        dot_tn(active, final_low),
    )


MESH = pl.DeviceIdType.MESH
TOKEN_PARTS = 2
SHIP_PARTS = 1
FIRST_FOLDS = 2
STEPS = {
    0: (("start", 0), ("start", 1)),
    3: (("second", 0), ("near", 0), ("own", 0)),
    4: (("second", 1), ("near", 1), ("own", 1)),
    9: (("pass", 0),),
    6: (("pass", 1),),
    7: (("third", 0), ("third", 1)),
    8: (("fourth", 0), ("fourth", 1)),
}


def to_tall(rows):
    half = rows.shape[1] // 2
    return jnp.concatenate([rows[:, :half], rows[:, half:]], axis=0).astype(BF16)


def from_tall(tall):
    count = tall.shape[0] // 2
    wide = tall.astype(F32)
    return jnp.concatenate([wide[:count], wide[count:]], axis=1)


def column_of(row, count):
    shape = (count, row.shape[1])
    same = lax.broadcasted_iota(jnp.int32, shape, 0) == lax.broadcasted_iota(jnp.int32, shape, 1)
    return jnp.sum(jnp.where(same, row, 0), axis=1, keepdims=True)


def caption_masks(seg, first, count):
    captions = first + lax.broadcasted_iota(jnp.int32, (count, seg.shape[1]), 0)
    mine = seg == captions
    spot = lax.broadcasted_iota(jnp.int32, (count, seg.shape[1]), 1)
    last = jnp.max(jnp.where(mine, spot, -1), axis=1, keepdims=True)
    return mine, (spot == last).astype(F32).astype(BF16)


def softmax_rows(scores, allowed):
    scores = jnp.where(allowed, scores, -1e30)
    expo = jnp.exp(scores - jnp.max(scores, axis=-1, keepdims=True))
    return expo / jnp.sum(expo, axis=-1, keepdims=True)


def stats_pack(rows, multiple=8):
    pieces = []
    for row in rows:
        pieces += [row[:, at : at + 128] for at in range(0, row.shape[1], 128)]
    if len(pieces) % multiple:
        pieces.append(jnp.zeros((-len(pieces) % multiple, 128), F32))
    return jnp.concatenate(pieces, axis=0)


def stats_unpack(packed, count, features):
    per = features // 128
    return [
        jnp.concatenate([packed[at * per + i : at * per + i + 1] for i in range(per)], axis=1)
        for at in range(count)
    ]


def step_kernel(
    sizes,
    text_hbm,
    image_hbm,
    iw_hbm,
    io_hbm,
    iu_hbm,
    id_hbm,
    tw_hbm,
    to_hbm,
    tu_hbm,
    td_hbm,
    seg_hbm,
    lab_hbm,
    ig1_hbm,
    ib1_hbm,
    ig2_hbm,
    ib2_hbm,
    iub_hbm,
    tg1_hbm,
    tb1_hbm,
    tg2_hbm,
    tb2_hbm,
    tub_hbm,
    up_o,
    down_o,
    tw,
    to,
    mid_o,
    nsel_o,
    xk_o,
    xv_o,
    tg_o,
    vec_o,
    loss_o,
    xt,
    xi,
    iw,
    io,
    iu,
    idn,
    tu,
    td,
    seg_ref,
    lab_ref,
    ig1_ref,
    ib1_ref,
    ig2_ref,
    ib2_ref,
    iub_ref,
    tg1_ref,
    tb1_ref,
    tg2_ref,
    tb2_ref,
    tub_ref,
    tok,
    ids,
    prow,
    drow,
    stm,
    std,
    ar,
    gat,
    fq,
    fg,
    fd,
    load_sem,
    img_sem,
    t_s,
    tz_r,
    ty_r,
    to_r,
    tx_r,
    tw_r,
    tl_r,
    ar_s,
    ar_r,
    g_s,
    g_r,
    g_f,
    g_c,
    f_s,
    f_x,
    f_c,
    st_s,
    st_r,
    sm_s,
    sm_r,
):
    n_dp, n_mp, pairs, tokens, features, width = sizes
    heads = width // HEAD
    half_dp = n_dp // 2
    total = n_dp * pairs
    scale = HEAD**-0.5
    d = lax.axis_index("dp")
    m = lax.axis_index("mp")
    core = lax.rem(m, 2)
    side = lax.div(m, 2)
    hi = lax.div(d, 2)
    lo = lax.rem(d, 2)
    partner = (d, m + 1 - 2 * core)
    across = (d, lax.rem(m + 2, 4))
    beside = (hi * 2 + 1 - lo, m)

    chunk = img_sem.shape[0]
    chunk_rows = xi.shape[0] // chunk

    def image_load(k):
        rows = pl.ds(k * chunk_rows, chunk_rows)
        return pltpu.make_async_copy(image_hbm.at[rows], xi.at[rows], img_sem.at[k])

    loads = {}

    def load(name, src, dst):
        loads[name] = pltpu.make_async_copy(src, dst, load_sem.at[len(loads)])
        loads[name].start()

    for k in range(chunk):
        image_load(k).start()
    load("ig1", ig1_hbm, ig1_ref)
    load("ib1", ib1_hbm, ib1_ref)
    load("iw", iw_hbm, iw)
    load("io", io_hbm, io)

    def vector(name, ref):
        loads[name].wait()
        return ref[...].reshape(1, ref.shape[0])

    barrier = pltpu.get_barrier_semaphore()
    for i in range(1, n_mp):
        pl.semaphore_signal(
            barrier, inc=1, device_id=(d, lax.rem(m + i, n_mp)), device_id_type=MESH
        )

    @pl.loop(1, n_dp)
    def _(i):
        pl.semaphore_signal(
            barrier, inc=1, device_id=(lax.rem(d + i, n_dp), m), device_id_type=MESH
        )

    load("text", text_hbm, xt)
    load("tg1", tg1_hbm, tg1_ref)
    load("tb1", tb1_hbm, tb1_ref)
    load("seg", seg_hbm, seg_ref)
    load("lab", lab_hbm, lab_ref)
    load("tw", tw_hbm, tw)
    load("to", to_hbm, to)
    load("ig2", ig2_hbm, ig2_ref)
    load("ib2", ib2_hbm, ib2_ref)
    load("iub", iub_hbm, iub_ref)
    load("iu", iu_hbm, iu)
    load("id", id_hbm, idn)
    load("tg2", tg2_hbm, tg2_ref)
    load("tb2", tb2_hbm, tb2_ref)
    load("tub", tub_hbm, tub_ref)
    load("tu", tu_hbm, tu)
    load("td", td_hbm, td)

    def remote(src, dst, send, recv, device):
        return pltpu.make_async_remote_copy(
            src_ref=src,
            dst_ref=dst,
            send_sem=send,
            recv_sem=recv,
            device_id=device,
            device_id_type=MESH,
        )

    def mp_send(buf, send, recv):
        for i in range(1, n_mp):
            remote(buf.at[m], buf.at[m], send, recv, (d, lax.rem(m + i, n_mp))).start()

    def mp_recv(buf, send, recv):
        slots = buf.at[pl.ds(0, n_mp - 1)]
        remote(slots, slots, send, recv, partner).wait_recv()

    def mp_drain(buf, send, recv):
        slots = buf.at[pl.ds(0, n_mp - 1)]
        remote(slots, slots, send, recv, partner).wait_send()

    def far_send(at):
        buf, first, rows = far[at]
        slot = buf.at[m, pl.ds(first, rows)]
        remote(slot, slot, f_s.at[at], f_x.at[at], across).start()
        remote(slot, slot, f_s.at[at], f_c.at[at], partner).start()

    def far_pass(at):
        buf, first, rows = far[at]
        slot = buf.at[lax.rem(m + 2, 4), pl.ds(first, rows)]
        remote(slot, slot, f_s.at[at], f_x.at[at], partner).wait_recv()
        remote(slot, slot, f_s.at[at], f_c.at[at], partner).start()

    def far_recv(at):
        buf, first, rows = far[at]
        slots = buf.at[pl.ds(0, 2), pl.ds(first, rows)]
        remote(slots, slots, f_s.at[at], f_c.at[at], partner).wait_recv()

    def far_drain(at):
        buf, first, rows = far[at]
        slots = buf.at[pl.ds(0, 3), pl.ds(first, rows)]
        remote(slots, slots, f_s.at[at], f_c.at[at], partner).wait_send()

    split_row = FIRST_FOLDS * 16
    far = (
        (fq, 0, fq.shape[1]),
        (fg, 0, split_row),
        (fg, split_row, fg.shape[1] - split_row),
        (fd, 0, fd.shape[1]),
    )

    def on_core(which):
        return pl.when(core == which)

    def dp_send(at):
        slot = gat.at[at, lo, hi]
        other = lo + core * (1 - 2 * lo)

        def send(k):
            to_dev = (lax.rem(hi + k, half_dp) * 2 + other, m)
            remote(slot, slot, g_s.at[at], g_r.at[at], to_dev).start()

        for k in range(1, half_dp):
            send(k)
        on_core(1)(lambda: send(0))

    def dp_forward(at):
        @on_core(1)
        def _():
            slots = gat.at[at, 1 - lo]
            remote(slots, slots, g_f.at[at], g_r.at[at], partner).wait_recv()
            remote(slots, slots, g_f.at[at], g_c.at[at], partner).start()

        @on_core(0)
        def _():
            slots = gat.at[at, 0, pl.ds(0, half_dp - 1)]
            remote(slots, slots, g_f.at[at], g_r.at[at], partner).wait_recv()
            for k in range(1, half_dp):
                slot = gat.at[at, lo, lax.rem(hi + k, half_dp)]
                remote(slot, slot, g_f.at[at], g_c.at[at], partner).start()

    def dp_wait(at, first, wait):
        for which in (0, 1):

            @on_core(which)
            def _(which=which):
                slots = gat.at[at, 0, pl.ds(0, half_dp - (1 if which == first else 0))]
                wait(slots)

    def dp_recv(at):
        dp_wait(
            at,
            1,
            lambda slots: remote(slots, slots, g_f.at[at], g_c.at[at], partner).wait_recv(),
        )

    def dp_drain(at):
        def wait(slots):
            remote(slots, slots, g_s.at[at], g_c.at[at], partner).wait_send()
            remote(slots, slots, g_f.at[at], g_c.at[at], partner).wait_send()

        dp_wait(at, 0, wait)

    def gathered(at):
        talls = [gat[at, i % 2, i // 2].astype(F32) for i in range(n_dp)]
        left = jnp.concatenate([t[:pairs] for t in talls], axis=0)
        right = jnp.concatenate([t[pairs:] for t in talls], axis=0)
        return jnp.concatenate([left, right], axis=1)

    def small_send(at, buf):
        @pl.loop(1, n_dp)
        def _(i):
            to_dev = (lax.rem(d + i, n_dp), m)
            remote(buf.at[d], buf.at[d], sm_s.at[at], sm_r.at[at], to_dev).start()

    def small_recv(at, buf):
        slots = buf.at[pl.ds(0, n_dp - 1)]
        remote(slots, slots, sm_s.at[at], sm_r.at[at], partner).wait_recv()

    def small_drain(at, buf):
        slots = buf.at[pl.ds(0, n_dp - 1)]
        remote(slots, slots, sm_s.at[at], sm_r.at[at], partner).wait_send()

    part_rows = tokens // (2 * TOKEN_PARTS)

    def split_hi(mine, body):
        for k in range(half_dp // 2 - 1):
            body(2 * k + (2 - core if mine else 1 + core))

        @pl.when(core == (1 if mine else 0))
        def _():
            body(half_dp - 1)

    def near_slot(i):
        return lax.rem(hi + half_dp - i, half_dp) * 2 + lo

    def far_slot(i):
        return lax.rem(hi + half_dp - i, half_dp) * 2 + 1 - lo

    def split_far(body):
        split_hi(True, lambda i: body(far_slot(i)))

    def split_near(body):
        split_hi(True, lambda i: body(near_slot(i)))

    def rows_of(slot, part, which):
        start = (which * TOKEN_PARTS + part) * part_rows
        return tok.at[slot, pl.ds(pl.multiple_of(start, 16), part_rows)]

    def tok_push(rows, recv, device):
        remote(rows, rows, t_s.at[0], recv, device).start()

    def tok_wait(recv, counts):
        for which in (0, 1):
            if counts[which]:

                @on_core(which)
                def _(which=which):
                    rows = tok.at[0, pl.ds(0, counts[which] * part_rows)]
                    remote(rows, rows, t_s.at[0], recv, partner).wait_recv()

    quarter = half_dp // 2
    counts = (quarter - 1, quarter)

    def tok_start(part):
        rows = rows_of(d, part, side)

        def body(i):
            tok_push(rows, tz_r.at[part], (lax.rem(hi + i, half_dp) * 2 + lo, m))

        split_hi(True, body)

        @on_core(0)
        def _():
            for which in (0, 1):
                tok_push(rows_of(d, part, which), to_r.at[part], beside)

    def tok_own(part):
        tok_wait(to_r.at[part], (2, 0))

        @on_core(0)
        def _():
            for which in (0, 1):
                tok_push(rows_of(far_slot(0), part, which), tl_r.at[0], partner)

    def tok_second(part):
        tok_wait(tz_r.at[part], counts)

        def body(slot):
            rows = rows_of(slot, part, side)
            tok_push(rows, ty_r.at[part], beside)
            tok_push(rows, tl_r.at[0], partner)

        split_near(body)

    def tok_third(part):
        tok_wait(ty_r.at[part], counts)
        split_far(lambda slot: tok_push(rows_of(slot, part, side), tl_r.at[0], partner))

    def tok_near(part):
        split_near(lambda slot: tok_push(rows_of(slot, part, side), tx_r.at[part], across))

    def tok_pass(part):
        tok_wait(tx_r.at[part], counts)

        def body(slot):
            rows = rows_of(slot, part, 1 - side)
            tok_push(rows, tw_r.at[part], beside)
            tok_push(rows, tl_r.at[0], partner)

        split_near(body)

    def tok_fourth(part):
        tok_wait(tw_r.at[part], counts)
        split_far(lambda slot: tok_push(rows_of(slot, part, 1 - side), tl_r.at[0], partner))

    def tok_last():
        for which, count in ((0, 2 * quarter), (1, 2 * quarter - 1)):

            @on_core(which)
            def _(count=count):
                slots = tok.at[pl.ds(0, count)]
                remote(slots, slots, t_s.at[0], tl_r.at[0], partner).wait_recv()

    def tok_drain():
        for which, count in ((0, n_dp - 2), (1, n_dp)):

            @on_core(which)
            def _(count=count):
                slots = tok.at[pl.ds(0, count)]
                remote(slots, slots, t_s.at[0], tl_r.at[0], partner).wait_send()

    def token_steps(at):
        steps = {
            "start": tok_start,
            "own": tok_own,
            "second": tok_second,
            "third": tok_third,
            "near": tok_near,
            "pass": tok_pass,
            "fourth": tok_fourth,
        }
        for name, part in STEPS.get(at, ()):
            steps[name](part)

    def attend_rows(queries, normed, allowed, weights):
        stacked = head_blocks(queries.astype(F32), width).astype(BF16)
        folded = dot(stacked, weights[1]).astype(BF16)
        scores = dot_nt(folded, normed) * scale
        probs = softmax_rows(scores, allowed)
        mixed = dot(probs.astype(BF16), normed).astype(BF16)
        context = head_pick(dot_nt(mixed, weights[2]), width).astype(BF16)
        return folded, probs, context

    for k in range(chunk):
        image_load(k).wait()
    gain, shift = vector("ig1", ig1_ref), vector("ib1", ib1_ref)
    loads["iw"].wait()
    hats = [
        normalized(xi[k * chunk_rows : (k + 1) * chunk_rows, :].astype(F32))[0].astype(BF16)
        for k in range(chunk)
    ]
    firsts = [i * IMG_LEN for i in range(pairs)]
    image_first = jnp.concatenate([xi[r : r + 1, :].astype(F32) for r in firsts], axis=0)
    first_n = (normalized(image_first)[0] * gain + shift).astype(BF16)
    image_fold = dot(head_blocks(dot_nt(first_n, iw[0]), width).astype(BF16), iw[1])
    shifted = jnp.sum(image_fold * shift, axis=-1, keepdims=True)
    image_fold = image_fold * gain
    group = pairs // chunk
    shape = (group, chunk_rows)
    place = lax.broadcasted_iota(jnp.int32, shape, 1)
    begin = lax.broadcasted_iota(jnp.int32, shape, 0) * IMG_LEN
    inside = jnp.concatenate([(place >= begin) & (place < begin + IMG_LEN)] * heads, axis=0)

    def of_group(rows, k):
        spots = [h * pairs + k * group for h in range(heads)]
        return jnp.concatenate([rows[at : at + group] for at in spots], axis=0)

    image_scores = [
        (dot_nt(of_group(image_fold, k).astype(BF16), hats[k]) + of_group(shifted, k)) * scale
        for k in range(chunk)
    ]
    image_probs = [softmax_rows(scores, inside).astype(BF16) for scores in image_scores]
    image_mixed = [dot(image_probs[k], hats[k]) for k in range(chunk)]
    image_mixed = jnp.concatenate(
        [mixed[h * group : (h + 1) * group] for h in range(heads) for mixed in image_mixed], axis=0
    )
    image_mixed = image_mixed * gain + shift
    image_context = head_pick(dot_nt(image_mixed.astype(BF16), iw[2]), width).astype(BF16)
    loads["io"].wait()
    ar[0, m] = to_tall(dot(image_context, io[...]))

    loads["text"].wait()
    gain_one = vector("tg1", tg1_ref)
    hat_one, factor_one = normalized(xt[...].astype(F32))
    tok[d] = (hat_one * gain_one + vector("tb1", tb1_ref)).astype(BF16)
    pl.semaphore_wait(barrier, n_mp - 1 + n_dp - 1)
    mp_send(ar.at[0], ar_s.at[0], ar_r.at[0])

    token_steps(0)
    seg = vector("seg", seg_ref)
    seg_rows = tokens // 128
    for i in range(seg_rows):
        ids[d, i : i + 1, :] = seg[:, i * 128 : (i + 1) * 128]
    ids[d, seg_rows : seg_rows + 1, 0:pairs] = vector("lab", lab_ref)

    normed = tok[d]
    mine, pick = caption_masks(seg, d * pairs, pairs)
    allowed = jnp.concatenate([mine] * heads, axis=0)
    loads["tw"].wait()
    queries = dot_nt(dot(pick, normed).astype(BF16), tw[0]).astype(BF16)
    folded, probs, context = attend_rows(queries, normed, allowed, tw)
    loads["to"].wait()
    ar[1, m] = to_tall(dot(context, to[...]))
    mp_send(ar.at[1], ar_s.at[1], ar_r.at[1])
    text_last = dot(pick, xt[...])

    def head_rows(blocks):
        rows = [
            jnp.sum(blocks[h * pairs : (h + 1) * pairs], axis=0, keepdims=True)
            for h in range(heads)
        ]
        return jnp.concatenate(rows + [jnp.zeros((8 - heads, tokens), F32)], axis=0)

    def padded(rows, foot):
        foot = jnp.concatenate([foot, jnp.zeros((8, features - tokens), F32)], axis=1)
        return jnp.concatenate([rows, foot], axis=0).astype(BF16)

    no_foot = jnp.zeros((8, tokens), F32)
    prob_rows = head_rows(probs)
    fq[m] = padded(folded.astype(F32), prob_rows)
    prow[d] = stats_pack([prob_rows[h : h + 1] for h in range(heads)])
    token_steps(1)

    def summed(at):
        mp_recv(ar.at[at], ar_s.at[at], ar_r.at[at])
        full = ar[at, 0].astype(F32)
        for i in range(1, n_mp):
            full = full + ar[at, i].astype(F32)
        count = full.shape[0] // 2
        return jnp.concatenate([full[:count], full[count:]], axis=1)

    image_middle = image_first + summed(0)
    gain, shift = vector("ig2", ig2_ref), vector("ib2", ib2_ref)
    image_n2 = (normalized(image_middle)[0] * gain + shift).astype(BF16)
    loads["iu"].wait()
    image_hidden = dot(image_n2, iu[...]) + vector("iub", iub_ref)
    image_active = gelu_parts(image_hidden)[0].astype(BF16)
    loads["id"].wait()
    ar[2, m] = to_tall(dot(image_active, idn[...]))
    mp_send(ar.at[2], ar_s.at[2], ar_r.at[2])
    token_steps(2)

    middle = text_last + summed(1)
    gat[0, lo, hi] = to_tall(middle)
    gain_two, shift_two = vector("tg2", tg2_ref), vector("tb2", tb2_ref)
    hat_two, factor_two = normalized(middle)
    normed_two = (hat_two * gain_two + shift_two).astype(BF16)
    loads["tu"].wait()
    up_shift = vector("tub", tub_ref)
    active, slope = gelu_parts(dot(normed_two, tu[...]) + up_shift)
    loads["td"].wait()
    ar[3, m] = to_tall(dot(active.astype(BF16), td[...]))
    mp_send(ar.at[3], ar_s.at[3], ar_r.at[3])
    token_steps(3)

    gat[1, lo, hi] = to_tall(unit(image_middle + summed(2)))
    dp_send(1)
    gat[2, lo, hi] = to_tall(middle + summed(3))
    dp_send(2)
    far_send(0)

    token_steps(4)
    dp_forward(1)
    token_steps(9)
    dp_forward(2)
    far_pass(0)
    token_steps(5)
    dp_recv(1)
    image_low = gathered(1).astype(BF16)
    own_labels = column_of(ids[d, seg_rows : seg_rows + 1, :], pairs)
    dp_recv(2)


    def embedded(rows):
        shrink = lax.rsqrt(jnp.sum(rows * rows, axis=-1, keepdims=True) + 1e-06)
        text_unit = rows * shrink
        return shrink, text_unit, 64.0 * dot_nt(text_unit.astype(BF16), image_low)

    def final_grad(shrink, text_unit, logits, labels):
        lanes = lax.broadcasted_iota(jnp.int32, logits.shape, 1)
        onehot = (labels == lanes).astype(F32)
        top = jnp.max(logits, axis=1, keepdims=True)
        lse = top + jnp.log(jnp.sum(jnp.exp(logits - top), axis=1, keepdims=True))
        grads = 0.5 * (jnp.exp(logits - lse) + jnp.exp(logits - col_lse)) - onehot
        grads = 64.0 * dot(grads.astype(BF16), image_low)
        along = jnp.sum(text_unit * grads, axis=-1, keepdims=True)
        positive = jnp.sum(logits * onehot, axis=1, keepdims=True)
        return shrink * (grads - text_unit * along), lse, positive

    shrink_all, unit_all, logits = embedded(gathered(2))
    col_top = jnp.max(logits, axis=0, keepdims=True)
    col_lse = col_top + jnp.log(jnp.sum(jnp.exp(logits - col_top), axis=0, keepdims=True))
    grad_final, own_lse, positive = final_grad(*embedded(from_tall(gat[2, lo, hi])), own_labels)
    grad_hidden = (dot_nt(grad_final.astype(BF16), td[...]) * slope).astype(BF16)
    ar[4, m] = to_tall(dot_nt(grad_hidden, tu[...]))
    mp_send(ar.at[4], ar_s.at[4], ar_r.at[4])
    small_send(0, ids)
    dp_send(0)
    small_send(1, prow)

    token_steps(6)
    lanes = lax.broadcasted_iota(jnp.int32, (pairs, total), 1)
    mine_first = lax.broadcasted_iota(jnp.int32, (pairs, total), 0) + d * pairs
    own_col = jnp.sum(jnp.where(lanes == mine_first, col_lse, 0.0), axis=1, keepdims=True)
    pair_loss = 0.5 * (own_lse + own_col) - positive
    shape = (pairs, loss_o.shape[1])
    diagonal = lax.broadcasted_iota(jnp.int32, shape, 0) == lax.broadcasted_iota(
        jnp.int32, shape, 1
    )
    loss_o[...] = jnp.sum(jnp.where(diagonal, pair_loss, 0.0), axis=0, keepdims=True)

    def spread(slots, ref, at):
        parts = []
        for i in slots:
            foot = ref[i, at : at + 8, 0:tokens].astype(F32)
            for h in range(heads):
                parts.append(jnp.where(mine, foot[h : h + 1], 0.0))
            parts.append(jnp.zeros((8, tokens), F32))
        return jnp.concatenate(parts, axis=0).astype(BF16)

    def placed(count):
        spots = jnp.concatenate([pick.astype(F32), jnp.zeros((8, tokens), F32)], axis=0)
        return jnp.concatenate([spots] * count, axis=0).astype(BF16)

    own_probs = spread([m], fq, pairs * heads)
    own_spots = placed(1)

    grad_n2 = summed(4)
    grad_middle = grad_final + norm_back(grad_n2, hat_two, factor_two, gain_two)
    gat[3, lo, hi] = to_tall(grad_middle)
    dp_send(3)
    middle_low = grad_middle.astype(BF16)
    grad_context = dot_nt(middle_low, to[...]).astype(BF16)
    grad_folded = dot(head_blocks(grad_context.astype(F32), width).astype(BF16), tw[2])
    fg[m] = padded(grad_folded, no_foot)
    far_send(1)
    grad_probs = dot_nt(grad_folded.astype(BF16), normed)
    grad_scores = probs * (grad_probs - jnp.sum(grad_probs * probs, axis=-1, keepdims=True))
    scaled = grad_scores * scale
    score_rows = head_rows(scaled)
    mixed_back = dot(scaled.astype(BF16), normed).astype(BF16)
    grad_queries = head_pick(dot_nt(mixed_back, tw[1]), width).astype(BF16)
    fd[m] = padded(dot(grad_queries, tw[0]), score_rows)

    part = dot_tn(spread([m], fd, pairs), fq[m])
    part = part + dot_tn(own_probs, fg[m])
    part = part + dot_tn(own_spots, fd[m])
    stm[m] = stats_pack(
        [jnp.sum(part * hat_one, axis=0, keepdims=True), jnp.sum(part, axis=0, keepdims=True)]
    )
    mp_send(stm, st_s.at[0], st_r.at[0])
    far_send(2)
    far_send(3)
    stats_two = [
        jnp.sum(grad_n2 * hat_two, axis=0, keepdims=True),
        jnp.sum(grad_n2, axis=0, keepdims=True),
    ]
    drow[d] = stats_pack([score_rows[h : h + 1] for h in range(heads)] + stats_two, 16).astype(BF16)
    small_send(3, drow)

    token_steps(7)
    small_recv(0, ids)
    labels = jnp.concatenate(
        [column_of(ids[i, seg_rows : seg_rows + 1, :], pairs) for i in range(n_dp)], axis=0
    )
    fin_all = final_grad(shrink_all, unit_all, logits, labels)[0].astype(BF16)
    dp_forward(0)
    dp_recv(0)
    n2_all = (normalized(gathered(0))[0] * gain_two + shift_two).astype(BF16)
    act_all, slope_all = gelu_parts(dot(n2_all, tu[...]) + up_shift)
    gh_all = (dot_nt(fin_all, td[...]) * slope_all).astype(BF16)
    up_bias = jnp.sum(gh_all.astype(F32), axis=0, keepdims=True)
    up_o[...] = dot_tn(n2_all, gh_all)
    down_o[...] = dot_tn(act_all.astype(BF16), fin_all)
    mp_recv(stm, st_s.at[0], st_r.at[0])
    one = stm[0]
    for i in range(1, n_mp):
        one = one + stm[i]
    std[d] = stats_pack(stats_unpack(one, 2, features), 16).astype(BF16)
    small_send(2, std)
    far_pass(1)
    far_pass(2)
    dp_forward(3)
    far_pass(3)
    token_steps(8)

    everyone = list(range(n_mp))

    def flat(ref):
        return ref[...].reshape(n_mp * ref.shape[1], features)

    for at in range(3):
        far_recv(at)
    from_probs = dot_tn(spread(everyone, fq, pairs * heads), flat(fg))
    far_recv(3)
    grad_normed = dot_tn(spread(everyone, fd, pairs), flat(fq)) + from_probs
    grad_normed = grad_normed + dot_tn(placed(n_mp), flat(fd))
    text_grad = norm_back(grad_normed, hat_one, factor_one, gain_one)
    tg_o[...] = text_grad + dot_tn(pick, middle_low)

    small_recv(1, prow)
    tok_last()
    twice = 2 * pairs
    pair_masks = []
    for j in range(half_dp):
        seg = jnp.concatenate(
            [ids[i, k : k + 1, :] for i in (2 * j, 2 * j + 1) for k in range(seg_rows)], axis=1
        )
        pair_masks.append(caption_masks(seg, j * twice, twice))

    def pair_at(j):
        return slice(j * twice, (j + 1) * twice)

    def pair_rows(j):
        return tok[2 * j : 2 * j + 2].reshape(2 * tokens, features)

    def spread_pair(j, rows, h):
        values = jnp.concatenate([rows[2 * j][h], rows[2 * j + 1][h]], axis=1)
        return jnp.where(pair_masks[j][0], values, 0.0).astype(BF16)

    early_rows = [stats_unpack(prow[i], heads, tokens) for i in range(n_dp)]
    for j in range(half_dp):
        parts = [spread_pair(j, early_rows, h) for h in range(heads)] + [pair_masks[j][1]]
        mixed = dot(jnp.concatenate(parts, axis=0), pair_rows(j)).astype(BF16)
        for h in range(heads):
            xv_o[h, pair_at(j), :] = mixed[h * twice : (h + 1) * twice]
        nsel_o[pair_at(j), :] = mixed[heads * twice :]

    small_recv(3, drow)
    late_rows = [stats_unpack(drow[i].astype(F32), heads, tokens) for i in range(n_dp)]
    for j in range(half_dp):
        parts = [spread_pair(j, late_rows, h) for h in range(heads)]
        mixed = dot(jnp.concatenate(parts, axis=0), pair_rows(j)).astype(BF16)
        for h in range(heads):
            xk_o[h, pair_at(j), :] = mixed[h * twice : (h + 1) * twice]
    dp_recv(3)
    mid_o[...] = gathered(3).astype(BF16)

    small_recv(2, std)
    stats = std[0].astype(F32)
    for i in range(1, n_dp):
        stats = stats + std[i].astype(F32)
    late = drow[0].astype(F32)
    for i in range(1, n_dp):
        late = late + drow[i].astype(F32)
    rows = stats_unpack(stats, 2, features)
    rows += stats_unpack(late[heads * seg_rows :], 2, features)
    vec_o[...] = jnp.concatenate(rows + [up_bias, jnp.zeros((3, features), F32)], axis=0)

    for at in range(ar.shape[0]):
        mp_drain(ar.at[at], ar_s.at[at], ar_r.at[at])
    mp_drain(stm, st_s.at[0], st_r.at[0])
    for at in range(len(far)):
        far_drain(at)
    for at in range(gat.shape[0]):
        dp_drain(at)
    for at, buf in enumerate((ids, prow, std, drow)):
        small_drain(at, buf)
    tok_drain()


def weights_kernel(
    up,
    down,
    tw,
    to,
    mid,
    nsel,
    xk,
    xv,
    tg,
    vec,
    loss,
    tg_out,
    qkv_out,
    out_out,
    up_out,
    down_out,
    loss_out,
    g1_out,
    b1_out,
    g2_out,
    b2_out,
    ub_out,
    qkv_buf,
    out_buf,
    sem,
    *vec_bufs,
):
    heads, total, features = xk.shape
    width = to.shape[0]
    started = []

    def ship(src, dst):
        copy = pltpu.make_async_copy(src, dst, sem.at[len(started)])
        copy.start()
        started.append(copy)

    for src, dst in ((up, up_out), (down, down_out)):
        step = src.shape[0] // SHIP_PARTS
        for at in range(0, src.shape[0], step):
            rows = pl.ds(at, step)
            ship(src.at[rows], dst.at[rows])
    ship(tg, tg_out)
    for at, dst in enumerate((g1_out, b1_out, g2_out, b2_out, ub_out)):
        vec_bufs[at][...] = vec[at, :]
        ship(vec_bufs[at], dst)
    vec_bufs[5][...] = loss[0, 0 : loss_out.shape[0]]
    ship(vec_bufs[5], loss_out)
    flat_k = xk[...].reshape(heads * total, features)
    flat_v = xv[...].reshape(heads * total, features)
    queries = dot_nt(nsel[...], tw[0])
    grad_context = dot_nt(mid[...], to[...])
    for at, rows, flat in ((1, queries, flat_k), (2, grad_context, flat_v)):
        stacked = head_blocks(rows.astype(BF16).astype(F32), width).astype(BF16)
        qkv_buf[at] = dot_tn(stacked, flat)
        ship(qkv_buf.at[at], qkv_out.at[at])
    grad_queries = head_pick(dot_nt(flat_k, tw[1]), width).astype(BF16)
    qkv_buf[0] = dot_tn(grad_queries, nsel[...])
    ship(qkv_buf.at[0], qkv_out.at[0])
    context = head_pick(dot_nt(flat_v, tw[2]), width).astype(BF16)
    out_buf[...] = dot_tn(context, mid[...])
    ship(out_buf, out_out)
    for copy in started:
        copy.wait()


def kernel_device(
    n_dp,
    n_mp,
    text_tokens,
    segment_ids,
    labels,
    image_tokens,
    image_gain_one,
    image_bias_one,
    image_qkv,
    image_out,
    image_gain_two,
    image_bias_two,
    image_up,
    image_up_bias,
    image_down,
    text_gain_one,
    text_bias_one,
    text_qkv,
    text_out,
    text_gain_two,
    text_bias_two,
    text_up,
    text_up_bias,
    text_down,
):
    pairs = labels.shape[0]
    tokens, features = text_tokens.shape
    width = text_out.shape[0]
    hidden = text_up.shape[1]
    heads = width // HEAD
    total = n_dp * pairs
    half_dp = n_dp // 2
    vmem = pltpu.VMEM
    whole = pl.BlockSpec(memory_space=pltpu.VMEM)
    anywhere = pl.BlockSpec(memory_space=pl.ANY)

    def sems(*shape):
        return pltpu.SemaphoreType.DMA(shape)

    outs = [
        ((features, hidden), F32),
        ((hidden, features), F32),
        ((3, width, features), BF16),
        ((width, features), BF16),
        ((total, features), BF16),
        ((total, features), BF16),
        ((heads, total, features), BF16),
        ((heads, total, features), BF16),
        ((tokens, features), F32),
        ((8, features), F32),
        ((1, 128), F32),
    ]
    tall = (2 * pairs, features // 2)
    fold_rows = heads * pairs + 8
    vectors = (
        segment_ids,
        labels,
        image_gain_one,
        image_bias_one,
        image_gain_two,
        image_bias_two,
        image_up_bias,
        text_gain_one,
        text_bias_one,
        text_gain_two,
        text_bias_two,
        text_up_bias,
    )
    operands = (
        text_tokens,
        image_tokens,
        jnp.transpose(image_qkv, (1, 2, 0)),
        image_out,
        image_up,
        image_down,
        jnp.transpose(text_qkv, (1, 2, 0)),
        text_out,
        text_up,
        text_down,
    ) + vectors
    factors = pl.pallas_call(
        functools.partial(step_kernel, (n_dp, n_mp, pairs, tokens, features, width)),
        out_shape=[vmem(shape, dtype) for shape, dtype in outs],
        in_specs=[anywhere] * len(operands),
        out_specs=[whole] * len(outs),
        scratch_shapes=[
            vmem(text_tokens.shape, BF16),
            vmem(image_tokens.shape, BF16),
            vmem((3, width, features), BF16),
            vmem(image_out.shape, BF16),
            vmem(image_up.shape, BF16),
            vmem(image_down.shape, BF16),
            vmem(text_up.shape, BF16),
            vmem(text_down.shape, BF16),
        ]
        + [vmem(array.shape, array.dtype) for array in vectors]
        + [
            vmem((n_dp, tokens, features), BF16),
            vmem((n_dp, 8, 128), jnp.int32),
            vmem((n_dp, 8, 128), F32),
            vmem((n_dp, 32, 128), BF16),
            vmem((n_mp, 16, 128), F32),
            vmem((n_dp, 16, 128), BF16),
            vmem((5, n_mp) + tall, BF16),
            vmem((4, 2, half_dp) + tall, BF16),
            vmem((n_mp, fold_rows, features), BF16),
            vmem((n_mp, fold_rows, features), BF16),
            vmem((n_mp, pairs + 8, features), BF16),
            sems(22),
            sems(pairs // 8),
            sems(1),
            sems(TOKEN_PARTS),
            sems(TOKEN_PARTS),
            sems(TOKEN_PARTS),
            sems(TOKEN_PARTS),
            sems(TOKEN_PARTS),
            sems(1),
            sems(5),
            sems(5),
            sems(4),
            sems(4),
            sems(4),
            sems(4),
            sems(4),
            sems(4),
            sems(4),
            sems(1),
            sems(1),
            sems(4),
            sems(4),
        ],
        compiler_params=pltpu.CompilerParams(
            collective_id=0, has_side_effects=True, vmem_limit_bytes=48 * 2**20
        ),
        name="step",
    )(*[pltpu.with_memory_space_constraint(operand, pltpu.HBM) for operand in operands])
    vector = jax.ShapeDtypeStruct((features,), F32)
    results = pl.pallas_call(
        weights_kernel,
        out_shape=[
            jax.ShapeDtypeStruct((tokens, features), F32),
            jax.ShapeDtypeStruct((3, width, features), F32),
            jax.ShapeDtypeStruct((width, features), F32),
            jax.ShapeDtypeStruct((features, hidden), F32),
            jax.ShapeDtypeStruct((hidden, features), F32),
            jax.ShapeDtypeStruct((pairs,), F32),
            vector,
            vector,
            vector,
            vector,
            jax.ShapeDtypeStruct((hidden,), F32),
        ],
        in_specs=[whole] * len(outs),
        out_specs=[anywhere] * 11,
        scratch_shapes=[
            vmem((3, width, features), F32),
            vmem((width, features), F32),
            sems(2 * SHIP_PARTS + 11),
        ]
        + [vmem((features,), F32)] * 4
        + [vmem((hidden,), F32), vmem((pairs,), F32)],
        compiler_params=pltpu.CompilerParams(vmem_limit_bytes=32 * 2**20),
        name="weights",
    )(*[pltpu.with_memory_space_constraint(factor, pltpu.VMEM) for factor in factors])
    text_grad, qkv, out, up, down, loss, gain_one, bias_one, gain_two, bias_two, up_bias = results
    return (
        loss,
        text_grad,
        gain_one,
        bias_one,
        jnp.transpose(qkv, (2, 0, 1)),
        out,
        gain_two,
        bias_two,
        up,
        up_bias,
        down,
    )


def solution(mesh):
    placed = (
        P("dp", None),
        P("dp"),
        P("dp"),
        P("dp", None),
        P(),
        P(),
        P(None, None, "mp"),
        P("mp", None),
        P(),
        P(),
        P(None, "mp"),
        P("mp"),
        P("mp", None),
        P(),
        P(),
        P(None, None, "mp"),
        P("mp", None),
        P(),
        P(),
        P(None, "mp"),
        P("mp"),
        P("mp", None),
    )
    n_dp, n_mp = mesh.shape["dp"], mesh.shape["mp"]
    body = plain_device
    if n_dp <= 16 and n_dp % 4 == 0 and n_mp == 4:
        body = functools.partial(kernel_device, n_dp, n_mp)
    return jax.shard_map(
        body,
        mesh=mesh,
        in_specs=placed,
        out_specs=(
            P("dp"),
            P("dp", None),
            P(),
            P(),
            P(None, None, "mp"),
            P("mp", None),
            P(),
            P(),
            P(None, "mp"),
            P("mp"),
            P("mp", None),
        ),
        check_vma=False,
    )
```
